32 devices in a mesh: wide: 8 (over y, x, core), narrow: 4 (over z).
Axes of the slice: x: 2, y: 2, z: 4, core: 2. Of those that a mesh axis runs over, the one named last changes fastest.
Arguments:
- tokens: bfloat16 [32768, 1024], P(('wide', 'narrow')), may hold values from -6 to 6
- memory: bfloat16 [16384, 1024], P(('wide', 'narrow')), may hold values from -6 to 6
- cotangent: bfloat16 [32768, 1024], P(('wide', 'narrow')), may hold values from -6 to 6
- live_length: int32 [32], P(('wide', 'narrow')), may hold values from 278 to 1024, as said below
- pair_starts: int32 [32, 8], P(('wide', 'narrow')), may hold values from 0 to 1023, as said below
- source_starts: int32 [32, 8], P(('wide', 'narrow')), may hold values from 0 to 511, as said below
- group_bounds: int32 [9], replicated, may hold values from 0 to 32, as said below
- group_counts: int32 [8], replicated, may hold values from 500 to 1499
- self_query: bfloat16 [1024, 1024], P(('wide', 'narrow')), may hold values from -0.1875 to 0.1875
- self_key: bfloat16 [1024, 1024], P(('wide', 'narrow')), may hold values from -0.1875 to 0.1875
- self_value: bfloat16 [1024, 1024], P(('wide', 'narrow')), may hold values from -0.1875 to 0.1875
- self_output: bfloat16 [1024, 1024], P(('wide', 'narrow')), may hold values from -1.5 to 1.5
- cross_query: bfloat16 [1024, 1024], P(('wide', 'narrow')), may hold values from -0.1875 to 0.1875
- cross_key: bfloat16 [1024, 1024], P(('wide', 'narrow')), may hold values from -0.1875 to 0.1875
- cross_value: bfloat16 [1024, 1024], P(('wide', 'narrow')), may hold values from -0.1875 to 0.1875
- cross_output: bfloat16 [1024, 1024], P(('wide', 'narrow')), may hold values from -1.5 to 1.5
- hidden_in: bfloat16 [1024, 4096], P(('wide', 'narrow')), may hold values from -0.1875 to 0.1875
- hidden_out: bfloat16 [4096, 1024], P(('wide', 'narrow')), may hold values from -0.09375 to 0.09375
- first_gain: bfloat16 [1024], P(('wide', 'narrow')), may hold values from 0.099609375 to 1.8984375
- first_shift: bfloat16 [1024], P(('wide', 'narrow')), may hold values from -3 to 3
- second_gain: bfloat16 [1024], P(('wide', 'narrow')), may hold values from 0.099609375 to 1.8984375
- second_shift: bfloat16 [1024], P(('wide', 'narrow')), may hold values from -3 to 3
- third_gain: bfloat16 [1024], P(('wide', 'narrow')), may hold values from 0.099609375 to 1.8984375
- third_shift: bfloat16 [1024], P(('wide', 'narrow')), may hold values from -3 to 3
Outputs:
- layer_output: bfloat16 [32768, 1024], P(('wide', 'narrow'))
- tokens_grad: bfloat16 [32768, 1024], P(('wide', 'narrow'))
- memory_grad: bfloat16 [16384, 1024], P(('wide', 'narrow'))
- self_query_grad: float32 [1024, 1024], P(('wide', 'narrow'))
- self_key_grad: float32 [1024, 1024], P(('wide', 'narrow'))
- self_value_grad: float32 [1024, 1024], P(('wide', 'narrow'))
- self_output_grad: float32 [1024, 1024], P(('wide', 'narrow'))
- cross_query_grad: float32 [1024, 1024], P(('wide', 'narrow'))
- cross_key_grad: float32 [1024, 1024], P(('wide', 'narrow'))
- cross_value_grad: float32 [1024, 1024], P(('wide', 'narrow'))
- cross_output_grad: float32 [1024, 1024], P(('wide', 'narrow'))
- hidden_in_grad: float32 [1024, 4096], P(('wide', 'narrow'))
- hidden_out_grad: float32 [4096, 1024], P(('wide', 'narrow'))
- first_gain_grad: float32 [1024], P(('wide', 'narrow'))
- first_shift_grad: float32 [1024], P(('wide', 'narrow'))
- second_gain_grad: float32 [1024], P(('wide', 'narrow'))
- second_shift_grad: float32 [1024], P(('wide', 'narrow'))
- third_gain_grad: float32 [1024], P(('wide', 'narrow'))
- third_shift_grad: float32 [1024], P(('wide', 'narrow'))
The draws below stay inside these ranges and needn't reach their ends.
Inputs may be any that keep to these rules, and one draw needn't show every extreme that they name: `live_length`: positions at or after a row's live length are padding; the rows of the last device are full. `pair_starts`: strictly rising, the first 0, all below the row's live length; a sentence pair runs to the next start or to the live length. `source_starts`: strictly rising, the first 0, all below 512; a source runs to the next start or to 512. Strictly rising, the first 0, the last the number of devices; language pair g holds the devices group_bounds[g] to group_bounds[g + 1] - 1 of the joined index wide+narrow.
All inputs are finite; a program needn't handle non-finite values.
Results may differ from the reference program's by a relative error of at most 0.017.
Values may be sent and summed in bfloat16 or wider, within the bound.
A program may use at most 384 MiB of HBM per device.

```python
import jax
import jax.numpy as jnp
from jax import lax

D = 1024
HEADS = 16
HEAD_DIM = 64
FF = 4096
SEQ = 1024
MEM = 512
NSEG = 8
GROUPS = 8
ROWS_DEV = 1
ROWS = 32
TOKENS = 32768
MEM_TOKENS = 16384
DEVICES = 32


def live_lengths(key):
    length_key = jax.random.fold_in(key, 11)
    row_index = jnp.arange(ROWS, dtype=jnp.int32)
    device = row_index // ROWS_DEV
    rising = SEQ // 3 + (SEQ - SEQ // 3) * device // (DEVICES - 1)
    removed = jax.random.randint(length_key, (ROWS,), 0, SEQ // 16)
    return (rising - removed * (device < DEVICES - 1).astype(jnp.int32)).astype(jnp.int32)


def split_points(key, lengths):
    counter = jnp.arange(NSEG, dtype=jnp.int32)
    evenly = counter[None, :] * lengths[:, None] // NSEG
    spread = jnp.maximum(lengths // (2 * NSEG), 1)
    jitter = jax.random.randint(key, (ROWS, NSEG), 0, 1 << 20) % spread[:, None]
    jitter = jitter * (counter[None, :] > 0).astype(jnp.int32)
    return (evenly + jitter).astype(jnp.int32)


def draw_live_length(key, part):
    return live_lengths(key)


def draw_pair_starts(key, part):
    lengths = live_lengths(key)
    key = jax.random.fold_in(key, 2)
    return split_points(key, lengths)


def draw_source_starts(key, part):
    key = jax.random.fold_in(key, 3)
    lengths = jnp.full((ROWS,), MEM, jnp.int32)
    return split_points(key, lengths)


def draw_group_bounds(key, part):
    key = jax.random.fold_in(key, 4)
    shuffled = jax.random.permutation(key, DEVICES - 1)
    cuts = jnp.sort(shuffled[:GROUPS - 1] + 1)
    return jnp.concatenate([jnp.zeros((1,), jnp.int32), cuts.astype(jnp.int32), jnp.full((1,), DEVICES, jnp.int32)])


def plant(array, rng, least, largest):
    index_at = [jax.random.randint(jax.random.fold_in(rng, axis), (), 0, length) for axis, length in enumerate(array.shape)]
    longest = array.shape.index(max(array.shape))
    neighbour = index_at[:longest] + [(index_at[longest] + 1) % array.shape[longest]] + index_at[longest + 1:]
    return array.at[tuple(index_at)].set(least).at[tuple(neighbour)].set(largest)


def level_of(key, shape, shards, low, top_value):
    gain, own = 1.0, jax.random.fold_in(key, 6)
    for position, parts in shards:
        steps = jnp.exp(jax.random.uniform(jax.random.fold_in(own, position), (parts,), jnp.float32, low / len(shards), top_value / len(shards)))
        gain = gain * jnp.repeat(steps, shape[position] // parts).reshape([-1 if axis == position else 1 for axis in range(len(shape))])
    return gain


def bell_draw(stream_key, shape, scale, reach, shards=(), held_as=jnp.bfloat16):
    drawn = jax.random.normal(stream_key, shape, jnp.float32) * scale
    if len(shards) > 0:
        drawn = level_of(stream_key, shape, shards, -0.22, 0.18) * drawn
    return jnp.clip(drawn, min=-reach, max=reach).astype(held_as)


def setup_inputs(seed: int = 0) -> dict:
    splits = jax.random.split(jax.random.key(seed), 25)
    tokens = bell_draw(splits[0], (TOKENS, D), 1.0, 6.0, ((0, 32),))
    memory = bell_draw(splits[1], (MEM_TOKENS, D), 1.0, 6.0, ((0, 32),))
    cotangent = bell_draw(splits[2], (TOKENS, D), 1.0, 6.0, ((0, 32),))
    live_length = draw_live_length(jax.random.fold_in(splits[24], 71), 0)
    pair_starts = draw_pair_starts(jax.random.fold_in(splits[24], 71), 0)
    source_starts = draw_source_starts(jax.random.fold_in(splits[24], 71), 0)
    group_bounds = draw_group_bounds(jax.random.fold_in(splits[24], 71), 0)
    group_counts = plant(jax.random.randint(splits[7], (GROUPS,), 500, 1500), jax.random.fold_in(splits[7], 1), 500, 1499).astype(jnp.int32)
    self_query = bell_draw(splits[8], (D, D), D ** -0.5, 0.1875, ((0, 32),))
    self_key = bell_draw(splits[9], (D, D), D ** -0.5, 0.1875, ((0, 32),))
    self_value = bell_draw(splits[10], (D, D), D ** -0.5, 0.1875, ((0, 32),))
    self_output = bell_draw(splits[11], (D, D), (max(D // 64, 4)) ** -0.5, 1.5, ((0, 32),))
    cross_query = bell_draw(splits[12], (D, D), D ** -0.5, 0.1875, ((0, 32),))
    cross_key = bell_draw(splits[13], (D, D), D ** -0.5, 0.1875, ((0, 32),))
    cross_value = bell_draw(splits[14], (D, D), D ** -0.5, 0.1875, ((0, 32),))
    cross_output = bell_draw(splits[15], (D, D), (max(D // 64, 4)) ** -0.5, 1.5, ((0, 32),))
    hidden_in = bell_draw(splits[16], (D, FF), D ** -0.5, 0.1875, ((0, 32),))
    hidden_out = bell_draw(splits[17], (FF, D), FF ** -0.5, 0.09375, ((0, 32),))
    first_gain = jnp.clip(1.0 + 0.18 * jax.random.normal(splits[18], (D,), jnp.float32), 0.099609375, 1.8984375).astype(jnp.bfloat16)
    first_shift = bell_draw(splits[19], (D,), 0.5, 3.0, ((0, 32),))
    second_gain = jnp.clip(1.0 + 0.18 * jax.random.normal(splits[20], (D,), jnp.float32), 0.099609375, 1.8984375).astype(jnp.bfloat16)
    second_shift = bell_draw(splits[21], (D,), 0.5, 3.0, ((0, 32),))
    third_gain = jnp.clip(1.0 + 0.18 * jax.random.normal(splits[22], (D,), jnp.float32), 0.099609375, 1.8984375).astype(jnp.bfloat16)
    third_shift = bell_draw(splits[23], (D,), 0.5, 3.0, ((0, 32),))
    return dict(tokens=tokens, memory=memory, cotangent=cotangent, live_length=live_length, pair_starts=pair_starts, source_starts=source_starts, group_bounds=group_bounds, group_counts=group_counts, self_query=self_query, self_key=self_key, self_value=self_value, self_output=self_output, cross_query=cross_query, cross_key=cross_key, cross_value=cross_value, cross_output=cross_output, hidden_in=hidden_in, hidden_out=hidden_out, first_gain=first_gain, first_shift=first_shift, second_gain=second_gain, second_shift=second_shift, third_gain=third_gain, third_shift=third_shift)


HIGH = lax.Precision.HIGHEST
EPSILON = 1e-05
FILLER = -1e+30

@jax.custom_vjp
def low(v):
    return lax.optimization_barrier(v.astype(jnp.bfloat16)).astype(jnp.float32)

@jax.custom_vjp
def low_back(v):
    return v

def low_keep(v):
    return (low(v), None)

def low_pass(kept, grad):
    return (grad,)

def back_keep(v):
    return (v, None)

def back_low(kept, grad):
    return (low(grad),)
low.defvjp(low_keep, low_pass)
low_back.defvjp(back_keep, back_low)

def layer_norm(values, gain_vector, shift_vector):
    center = values - lax.optimization_barrier(jnp.mean(values, axis=-1, keepdims=True))
    inverse = lax.rsqrt(lax.optimization_barrier(jnp.mean(center * center, axis=-1, keepdims=True)) + EPSILON)
    return center * inverse * gain_vector + shift_vector

def product(left_side, right_side):
    return jnp.dot(left_side, right_side, precision=HIGH)

def rounded(values):
    return low_back(low(values))

def attention(query_rows, key_rows, value_rows, allowed):
    length = query_rows.shape[0]
    block_rows = min(512, length)
    block_count = length // block_rows
    query_heads = query_rows.reshape(block_count, block_rows, HEADS, HEAD_DIM)
    key_heads = key_rows.reshape(-1, HEADS, HEAD_DIM)
    value_heads = value_rows.reshape(-1, HEADS, HEAD_DIM)
    allowed_blocks = allowed.reshape(block_count, block_rows, -1)
    score_scale = HEAD_DIM ** (-0.5)

    def one_block(block_input):
        query_part, allowed_part = block_input
        scores = jnp.einsum('qhd,khd->hqk', query_part, key_heads, precision=HIGH) * score_scale
        scores = jnp.where(allowed_part[None], low_back(scores), FILLER)
        weights = low(jax.nn.softmax(scores, axis=-1))
        mixed_heads = jnp.einsum('hqk,khd->qhd', weights, value_heads, precision=HIGH)
        return mixed_heads.reshape(block_rows, HEADS * HEAD_DIM)
    mixed_blocks = lax.map(jax.checkpoint(one_block), (query_heads, allowed_blocks))
    return mixed_blocks.reshape(length, HEADS * HEAD_DIM)

def decoder(params, tokens, memory, self_allowed, cross_allowed):
    query_self, key_self, value_self, output_self, query_cross, key_cross, value_cross, output_cross, expand_whole, reduce_whole, gain_one, shift_one, gain_two, shift_two, gain_three, shift_three = params
    normed = low(layer_norm(tokens, gain_one, shift_one))
    mixed = rounded(attention(rounded(product(normed, query_self)), rounded(product(normed, key_self)), rounded(product(normed, value_self)), self_allowed))
    after_self = tokens + low_back(product(mixed, output_self))
    normed = low(layer_norm(after_self, gain_two, shift_two))
    mixed = rounded(attention(rounded(product(normed, query_cross)), rounded(product(memory, key_cross)), rounded(product(memory, value_cross)), cross_allowed))
    after_cross = after_self + low_back(product(mixed, output_cross))
    normed = low(layer_norm(after_cross, gain_three, shift_three))
    activated = low(jax.nn.gelu(low_back(product(normed, expand_whole))))
    return after_cross + low_back(product(activated, reduce_whole))

def segment_ids(starts, length, extent):
    places = jnp.arange(extent, dtype=jnp.int32)
    counted = lax.optimization_barrier(jnp.sum((starts[None, :] <= places[:, None]).astype(jnp.int32), axis=1)) - 1
    return jnp.where(places < length, counted, NSEG)

def masks_of(pair_row, source_row, length):
    places = jnp.arange(SEQ, dtype=jnp.int32)
    target_segment = segment_ids(pair_row, length, SEQ)
    memory_segment = segment_ids(source_row, MEM, MEM)
    self_allowed = (target_segment[:, None] == target_segment[None, :]) & (places[None, :] <= places[:, None])
    cross_allowed = (target_segment[:, None] == memory_segment[None, :]) | (target_segment[:, None] == NSEG)
    return (self_allowed, cross_allowed)

def reference(tokens, memory, cotangent, live_length, pair_starts, source_starts, group_bounds, group_counts, self_query, self_key, self_value, self_output, cross_query, cross_key, cross_value, cross_output, hidden_in, hidden_out, first_gain, first_shift, second_gain, second_shift, third_gain, third_shift):
    params = tuple((weight.astype(jnp.float32) for weight in (self_query, self_key, self_value, self_output, cross_query, cross_key, cross_value, cross_output, hidden_in, hidden_out, first_gain, first_shift, second_gain, second_shift, third_gain, third_shift)))
    row_index = jnp.arange(ROWS, dtype=jnp.int32)
    device = row_index // ROWS_DEV
    member = (group_bounds[None, :-1] <= device[:, None]) & (device[:, None] < group_bounds[None, 1:])
    pair_tokens = lax.optimization_barrier(jnp.sum(jnp.where(member, group_counts[None, :], 0), axis=1))
    live_total = jnp.sum(live_length)
    row_weight = pair_tokens.astype(jnp.float32) * (TOKENS / 1000.0) / live_total.astype(jnp.float32)
    token_rows = tokens.reshape(ROWS, SEQ, D).astype(jnp.float32)
    memory_rows = memory.reshape(ROWS, MEM, D).astype(jnp.float32)
    cotangent_rows = cotangent.reshape(ROWS, SEQ, D).astype(jnp.float32)

    def row_step(totals, inputs):
        row_tokens, row_memory, row_cotangent, row_length, pair_row, source_row, weight_row = inputs
        self_allowed, cross_allowed = masks_of(pair_row, source_row, row_length)

        def local(layer_params, layer_tokens, layer_memory):
            return decoder(layer_params, layer_tokens, layer_memory, self_allowed, cross_allowed)
        output, pullback = jax.vjp(local, params, row_tokens, row_memory)
        live_mask = (jnp.arange(SEQ, dtype=jnp.int32) < row_length).astype(jnp.float32)
        param_grads, token_grads, memory_grads = pullback(row_cotangent * live_mask[:, None] * weight_row)
        totals = jax.tree.map(lambda summed, addend: summed + addend, totals, param_grads)
        return (totals, (output.astype(jnp.bfloat16), token_grads.astype(jnp.bfloat16), memory_grads.astype(jnp.bfloat16)))
    starting = tuple((jnp.zeros(weight.shape, jnp.float32) for weight in params))
    totals, (outputs, token_grads, memory_grads) = lax.scan(row_step, starting, (token_rows, memory_rows, cotangent_rows, live_length, pair_starts, source_starts, row_weight))
    return (outputs.reshape(TOKENS, D), token_grads.reshape(TOKENS, D), memory_grads.reshape(MEM_TOKENS, D), totals[0], totals[1], totals[2], totals[3], totals[4], totals[5], totals[6], totals[7], totals[8], totals[9], totals[10], totals[11], totals[12], totals[13], totals[14], totals[15])
```

```python
import functools
import jax
import jax.numpy as jnp
from jax import lax
from jax.experimental import pallas as pl
from jax.experimental.pallas import tpu as pltpu
from jax.sharding import PartitionSpec as P

SEQ = 1024
MEM = 512
HEADS = 16
HEAD_DIM = 64
EPSILON = 1e-05
BQ = 256
LOG2E = 1.4426950408889634
SCALE2 = HEAD_DIM**-0.5 * LOG2E
FILLER = -1e30
F32, BF16 = jnp.float32, jnp.bfloat16


def mm(a, b):
    return jnp.dot(a, b, preferred_element_type=F32)


def halves(x):
    low = lax.broadcasted_iota(jnp.int32, x.shape, 1) < HEAD_DIM
    zero = jnp.zeros_like(x)
    return (jnp.where(low, x, zero), jnp.where(low, zero, x))


def self_allowed_of(i, j, first_row):
    shape = (BQ, BQ)
    key = lax.broadcasted_iota(jnp.int32, shape, 0)
    allowed = key >= first_row - j * BQ
    if i == j:
        allowed = allowed & (key <= lax.broadcasted_iota(jnp.int32, shape, 1))
    return allowed


def self_forward_kernel(low_ref, first_ref, qkv_ref, out_ref, log_ref, m_ref, l_ref, acc_ref):
    row = pl.program_id(0)
    blocks = SEQ // BQ
    for i in range(blocks):
        rows = slice(i * BQ, (i + 1) * BQ)
        q_t = qkv_ref[rows, 0:128].T
        first_row = first_ref[0, :, rows]

        def step(j, fresh):
            keys = slice(j * BQ, (j + 1) * BQ)
            k_parts = halves(qkv_ref[keys, 128:256])
            v_t = qkv_ref[keys, 256:384].T
            allowed = self_allowed_of(i, j, first_row)
            for h in range(2):
                feats = slice(h * 64, (h + 1) * 64)
                s = jnp.where(allowed, mm(k_parts[h], q_t) * SCALE2, FILLER)
                peak = jnp.max(s, axis=0, keepdims=True)
                if fresh:
                    p = jnp.exp2(s - peak)
                    m_ref[h : h + 1, :] = peak
                    l_ref[h : h + 1, :] = jnp.sum(p, axis=0, keepdims=True)
                    acc_ref[feats, :] = mm(v_t[feats, :], p.astype(BF16))
                else:
                    old = m_ref[h : h + 1, :]
                    peak = jnp.maximum(old, peak)
                    p = jnp.exp2(s - peak)
                    fade = jnp.exp2(old - peak)
                    m_ref[h : h + 1, :] = peak
                    l_ref[h : h + 1, :] = l_ref[h : h + 1, :] * fade + jnp.sum(p, axis=0, keepdims=True)
                    acc_ref[feats, :] = acc_ref[feats, :] * fade + mm(v_t[feats, :], p.astype(BF16))

        step(i, True)
        for j in reversed(range(i)):
            pl.when(j >= low_ref[row * blocks + i])(functools.partial(step, j, False))
        total = l_ref[0:2, :]
        log_ref[0, 0, 0:2, rows] = m_ref[0:2, :] + jnp.log2(total)
        inv = 1.0 / total
        o_t = jnp.concatenate([acc_ref[0:64, :] * inv[0:1], acc_ref[64:128, :] * inv[1:2]], axis=0)
        out_ref[rows, :] = o_t.T.astype(BF16)


def self_forward(low, first, qkv, row_count):
    pairs = HEADS // 2
    return pl.pallas_call(
        self_forward_kernel,
        grid_spec=pltpu.PrefetchScalarGridSpec(
            num_scalar_prefetch=1,
            grid=(row_count, pairs),
            in_specs=[
                pl.BlockSpec((1, 1, SEQ), lambda r, p, low: (r, 0, 0)),
                pl.BlockSpec((SEQ, 384), lambda r, p, low: (r, p)),
            ],
            out_specs=[
                pl.BlockSpec((SEQ, 128), lambda r, p, low: (r, p)),
                pl.BlockSpec((1, 1, 8, SEQ), lambda r, p, low: (r, p, 0, 0)),
            ],
            scratch_shapes=[pltpu.VMEM((8, BQ), F32), pltpu.VMEM((8, BQ), F32), pltpu.VMEM((128, BQ), F32)],
        ),
        out_shape=[
            jax.ShapeDtypeStruct((row_count * SEQ, HEADS * HEAD_DIM), BF16),
            jax.ShapeDtypeStruct((row_count, pairs, 8, SEQ), F32),
        ],
        name="self_forward",
        compiler_params=pltpu.CompilerParams(vmem_limit_bytes=32 << 20),
        cost_estimate=pl.CostEstimate(flops=20 << 30, bytes_accessed=row_count * (8 << 20), transcendentals=8 << 20),
    )(low, first, qkv)


def self_backward_kernel(low_ref, first_ref, log_ref, qkv_ref, out_ref, grad_ref, dqkv_ref, dk_ref, dv_ref, dq_ref):
    row = pl.program_id(0)
    blocks = SEQ // BQ
    dk_ref[...] = jnp.zeros_like(dk_ref)
    dv_ref[...] = jnp.zeros_like(dv_ref)
    for i in range(blocks):
        rows = slice(i * BQ, (i + 1) * BQ)
        q, g = qkv_ref[rows, 0:128], grad_ref[rows, :]
        q_t, g_t = q.T, g.T
        prod = g_t.astype(F32) * out_ref[rows, :].T.astype(F32)
        delta = [jnp.sum(prod[h * 64 : (h + 1) * 64], axis=0, keepdims=True) for h in range(2)]
        q_parts, g_parts = halves(q), halves(g)
        first_row = first_ref[0, :, rows]

        def step(j, fresh):
            keys = slice(j * BQ, (j + 1) * BQ)
            k = qkv_ref[keys, 128:256]
            k_parts, k_t = halves(k), k.T
            v_parts = halves(qkv_ref[keys, 256:384])
            allowed = self_allowed_of(i, j, first_row)
            dv, dk = [], []
            for h in range(2):
                feats = slice(h * 64, (h + 1) * 64)
                s = jnp.where(allowed, mm(k_parts[h], q_t) * SCALE2, FILLER)
                p = jnp.exp2(s - log_ref[0, 0, h : h + 1, rows])
                dp = mm(v_parts[h], g_t)
                ds = (p * (dp - delta[h])).astype(BF16)
                dv.append(mm(p.astype(BF16), g_parts[h]))
                dk.append(mm(ds, q_parts[h]))
                part = mm(k_t[feats, :], ds)
                dq_ref[feats, :] = part if fresh else dq_ref[feats, :] + part
            dv_ref[keys, :] += dv[0] + dv[1]
            dk_ref[keys, :] += dk[0] + dk[1]

        step(i, True)
        for j in reversed(range(i)):
            pl.when(j >= low_ref[row * blocks + i])(functools.partial(step, j, False))
        dqkv_ref[rows, 0:128] = (dq_ref[...] * HEAD_DIM**-0.5).T.astype(BF16)
    dqkv_ref[:, 128:256] = (dk_ref[...] * HEAD_DIM**-0.5).astype(BF16)
    dqkv_ref[:, 256:384] = dv_ref[...].astype(BF16)


def self_backward(low, first, logs, qkv, out, grad, row_count):
    pairs = HEADS // 2
    return pl.pallas_call(
        self_backward_kernel,
        grid_spec=pltpu.PrefetchScalarGridSpec(
            num_scalar_prefetch=1,
            grid=(row_count, pairs),
            in_specs=[
                pl.BlockSpec((1, 1, SEQ), lambda r, p, low: (r, 0, 0)),
                pl.BlockSpec((1, 1, 8, SEQ), lambda r, p, low: (r, p, 0, 0)),
                pl.BlockSpec((SEQ, 384), lambda r, p, low: (r, p)),
                pl.BlockSpec((SEQ, 128), lambda r, p, low: (r, p)),
                pl.BlockSpec((SEQ, 128), lambda r, p, low: (r, p)),
            ],
            out_specs=pl.BlockSpec((SEQ, 384), lambda r, p, low: (r, p)),
            scratch_shapes=[pltpu.VMEM((SEQ, 128), F32), pltpu.VMEM((SEQ, 128), F32), pltpu.VMEM((128, BQ), F32)],
        ),
        out_shape=jax.ShapeDtypeStruct((row_count * SEQ, 3 * HEADS * HEAD_DIM), BF16),
        name="self_backward",
        compiler_params=pltpu.CompilerParams(vmem_limit_bytes=32 << 20),
        cost_estimate=pl.CostEstimate(flops=40 << 30, bytes_accessed=row_count * (16 << 20), transcendentals=8 << 20),
    )(low, first, logs, qkv, out, grad)


def cross_allowed_of(bounds_ref, rows):
    key = lax.broadcasted_iota(jnp.int32, (MEM, BQ), 0)
    return (key >= bounds_ref[0, 0:1, rows]) & (key < bounds_ref[0, 1:2, rows])


def cross_forward_kernel(bounds_ref, q_ref, kv_ref, out_ref, log_ref):
    k_parts = halves(kv_ref[:, 0:128])
    v_t = kv_ref[:, 128:256].T
    for i in range(SEQ // BQ):
        rows = slice(i * BQ, (i + 1) * BQ)
        q_t = q_ref[rows, :].T
        allowed = cross_allowed_of(bounds_ref, rows)
        outs = []
        for h in range(2):
            s = jnp.where(allowed, mm(k_parts[h], q_t) * SCALE2, FILLER)
            peak = jnp.max(s, axis=0, keepdims=True)
            p = jnp.exp2(s - peak)
            total = jnp.sum(p, axis=0, keepdims=True)
            log_ref[0, 0, h : h + 1, rows] = peak + jnp.log2(total)
            outs.append(mm(v_t[h * 64 : (h + 1) * 64, :], p.astype(BF16)) * (1.0 / total))
        out_ref[rows, :] = jnp.concatenate(outs, axis=0).T.astype(BF16)


def cross_forward(bounds, q, kv, row_count):
    pairs = HEADS // 2
    return pl.pallas_call(
        cross_forward_kernel,
        grid=(row_count, pairs),
        in_specs=[
            pl.BlockSpec((1, 8, SEQ), lambda r, p: (r, 0, 0)),
            pl.BlockSpec((SEQ, 128), lambda r, p: (r, p)),
            pl.BlockSpec((MEM, 256), lambda r, p: (r, p)),
        ],
        out_specs=[
            pl.BlockSpec((SEQ, 128), lambda r, p: (r, p)),
            pl.BlockSpec((1, 1, 8, SEQ), lambda r, p: (r, p, 0, 0)),
        ],
        out_shape=[
            jax.ShapeDtypeStruct((row_count * SEQ, HEADS * HEAD_DIM), BF16),
            jax.ShapeDtypeStruct((row_count, pairs, 8, SEQ), F32),
        ],
        name="cross_forward",
        compiler_params=pltpu.CompilerParams(vmem_limit_bytes=32 << 20),
        cost_estimate=pl.CostEstimate(flops=20 << 30, bytes_accessed=row_count * (6 << 20), transcendentals=8 << 20),
    )(bounds, q, kv)


def cross_backward_kernel(bounds_ref, log_ref, q_ref, kv_ref, out_ref, grad_ref, dq_ref, dkv_ref, dk_ref, dv_ref):
    k = kv_ref[:, 0:128]
    k_parts, k_t = halves(k), k.T
    v_parts = halves(kv_ref[:, 128:256])
    for i in range(SEQ // BQ):
        rows = slice(i * BQ, (i + 1) * BQ)
        q, g = q_ref[rows, :], grad_ref[rows, :]
        q_t, g_t = q.T, g.T
        prod = g_t.astype(F32) * out_ref[rows, :].T.astype(F32)
        q_parts, g_parts = halves(q), halves(g)
        allowed = cross_allowed_of(bounds_ref, rows)
        dv, dk, dq = [], [], []
        for h in range(2):
            feats = slice(h * 64, (h + 1) * 64)
            delta = jnp.sum(prod[feats], axis=0, keepdims=True)
            s = jnp.where(allowed, mm(k_parts[h], q_t) * SCALE2, FILLER)
            p = jnp.exp2(s - log_ref[0, 0, h : h + 1, rows])
            dp = mm(v_parts[h], g_t)
            ds = (p * (dp - delta)).astype(BF16)
            dv.append(mm(p.astype(BF16), g_parts[h]))
            dk.append(mm(ds, q_parts[h]))
            dq.append(mm(k_t[feats, :], ds))
        if i == 0:
            dv_ref[...] = dv[0] + dv[1]
            dk_ref[...] = dk[0] + dk[1]
        else:
            dv_ref[...] += dv[0] + dv[1]
            dk_ref[...] += dk[0] + dk[1]
        dq_ref[rows, :] = (jnp.concatenate(dq, axis=0) * HEAD_DIM**-0.5).T.astype(BF16)
    dkv_ref[:, 0:128] = (dk_ref[...] * HEAD_DIM**-0.5).astype(BF16)
    dkv_ref[:, 128:256] = dv_ref[...].astype(BF16)


def cross_backward(bounds, logs, q, kv, out, grad, row_count):
    pairs = HEADS // 2
    return pl.pallas_call(
        cross_backward_kernel,
        grid=(row_count, pairs),
        in_specs=[
            pl.BlockSpec((1, 8, SEQ), lambda r, p: (r, 0, 0)),
            pl.BlockSpec((1, 1, 8, SEQ), lambda r, p: (r, p, 0, 0)),
            pl.BlockSpec((SEQ, 128), lambda r, p: (r, p)),
            pl.BlockSpec((MEM, 256), lambda r, p: (r, p)),
            pl.BlockSpec((SEQ, 128), lambda r, p: (r, p)),
            pl.BlockSpec((SEQ, 128), lambda r, p: (r, p)),
        ],
        out_specs=[
            pl.BlockSpec((SEQ, 128), lambda r, p: (r, p)),
            pl.BlockSpec((MEM, 256), lambda r, p: (r, p)),
        ],
        scratch_shapes=[pltpu.VMEM((MEM, 128), F32), pltpu.VMEM((MEM, 128), F32)],
        out_shape=[
            jax.ShapeDtypeStruct((row_count * SEQ, HEADS * HEAD_DIM), BF16),
            jax.ShapeDtypeStruct((row_count * MEM, 2 * HEADS * HEAD_DIM), BF16),
        ],
        name="cross_backward",
        compiler_params=pltpu.CompilerParams(vmem_limit_bytes=32 << 20),
        cost_estimate=pl.CostEstimate(flops=40 << 30, bytes_accessed=row_count * (12 << 20), transcendentals=8 << 20),
    )(bounds, logs, q, kv, out, grad)


def row_bounds(pair_starts, source_starts, live_length):
    places = jnp.arange(SEQ, dtype=jnp.int32)
    counted = jnp.sum((pair_starts[:, :, None] <= places).astype(jnp.int32), axis=1)
    live = places < live_length[:, None]
    begun = jnp.max(jnp.where(pair_starts[:, :, None] <= places, pair_starts[:, :, None], 0), axis=1)
    first = jnp.where(live, begun, live_length[:, None])
    nseg = pair_starts.shape[1]
    pick = jnp.arange(nseg)[None, :, None] == (counted - 1)[:, None, :]
    ends = jnp.concatenate([source_starts[:, 1:], jnp.full_like(source_starts[:, :1], MEM)], axis=1)
    start = jnp.sum(jnp.where(pick, source_starts[:, :, None], 0), axis=1)
    end = jnp.sum(jnp.where(pick, ends[:, :, None], 0), axis=1)
    start = jnp.where(live, start, 0)
    end = jnp.where(live, end, MEM)
    bounds = jnp.pad(jnp.stack([start, end], axis=1), ((0, 0), (0, 6), (0, 0)))
    low = (first[:, ::BQ] // BQ).reshape(-1)
    return low, first[:, None, :], bounds


def stages_of(mesh_axes):
    plan = []
    for axis, size in mesh_axes:
        bits = size.bit_length() - 1
        at = 0
        while at < bits:
            take = 1 if (bits - at) % 2 else 2
            plan.append((axis, at, take))
            at += take
    return plan


def trade(value, axis, size, mask):
    return lax.ppermute(value, axis, [(i, i ^ mask) for i in range(size)])


def digit_of(axis, at, take):
    return (lax.axis_index(axis) >> at) & ((1 << take) - 1)


def sum_to_owner(partial, mesh_axes):
    rows, columns = partial.shape
    sizes = dict(mesh_axes)
    plan = stages_of(mesh_axes)
    groups = []
    for axis, _ in mesh_axes:
        groups += sorted((s for s in plan if s[0] == axis), key=lambda s: -s[1])
    extents = [1 << s[2] for s in groups]
    value = partial.reshape(*extents, -1, columns)
    for number, stage in enumerate(plan):
        axis, at, take = stage
        place = groups.index(stage)
        digit = digit_of(axis, at, take)

        def chunk(mask):
            return lax.dynamic_index_in_dim(value, digit ^ mask, place, keepdims=False)

        arrived = [trade(chunk(mask), axis, sizes[axis], mask << at) for mask in range(1, 1 << take)]
        total = chunk(0).astype(F32)
        for piece in arrived:
            total = total + piece.astype(F32)
        groups = [g for g in groups if g != stage]
        value = total if number == len(plan) - 1 else total.astype(BF16)
    return value.reshape(-1, columns)


def sum_everywhere(value, mesh_axes):
    sizes = dict(mesh_axes)
    for axis, at, take in stages_of(mesh_axes):
        arrived = [trade(value, axis, sizes[axis], mask << at) for mask in range(1, 1 << take)]
        for piece in arrived:
            value = value + piece
    return value


def norm_parts(values):
    center = values - jnp.mean(values, axis=-1, keepdims=True)
    inverse = lax.rsqrt(jnp.mean(center * center, axis=-1, keepdims=True) + EPSILON)
    return center * inverse, inverse


def norm_back(values, gain, gradient):
    unit, inverse = norm_parts(values)
    gain_grad = jnp.sum(gradient * unit, axis=0)
    shift_grad = jnp.sum(gradient, axis=0)
    scaled = gradient * gain
    back = inverse * (
        scaled
        - jnp.mean(scaled, axis=-1, keepdims=True)
        - unit * jnp.mean(scaled * unit, axis=-1, keepdims=True)
    )
    return back, gain_grad, shift_grad


def by_pairs(*parts):
    rows = parts[0].shape[0]
    return jnp.stack([p.reshape(rows, -1, 128) for p in parts], axis=2).reshape(rows, -1)


def from_pairs(value, count):
    rows = value.shape[0]
    split = value.reshape(rows, -1, count, 128)
    return [split[:, :, c].reshape(rows, -1) for c in range(count)]


def linear_back(gradient, weight):
    return jnp.einsum("te,de->td", gradient, weight, preferred_element_type=F32)


def outer_sum(left_side, gradient):
    return jnp.einsum("td,te->de", left_side, gradient, preferred_element_type=F32).astype(BF16)


def on_device(
    mesh_axes,
    tokens,
    memory,
    cotangent,
    live_length,
    pair_starts,
    source_starts,
    group_bounds,
    group_counts,
    self_query,
    self_key,
    self_value,
    self_output,
    cross_query,
    cross_key,
    cross_value,
    cross_output,
    hidden_in,
    hidden_out,
    first_gain,
    first_shift,
    second_gain,
    second_shift,
    third_gain,
    third_shift,
):
    names = tuple(axis for axis, _ in mesh_axes)
    row_count = live_length.shape[0]
    shard_rows = self_query.shape[0]
    reduce_sum = functools.partial(sum_to_owner, mesh_axes=mesh_axes)

    def gather(shard):
        return lax.all_gather(shard, names, axis=0, tiled=True)

    digits = jnp.stack([live_length // 256, live_length % 256], axis=1).astype(BF16)
    digits = jnp.pad(digits, ((0, shard_rows - row_count), (0, 0)))
    norms = jnp.stack([first_gain, first_shift, second_gain, second_shift, third_gain, third_shift], axis=1)
    extra = jnp.pad(jnp.concatenate([norms, digits], axis=1), ((0, 0), (0, 120)))
    early = gather(jnp.concatenate([by_pairs(self_query, self_key, self_value), extra], axis=1))
    d = early.shape[0]
    qkv_weight = early[:, : 3 * d]
    extra = early[:, 3 * d : 3 * d + 8].astype(F32).T
    gain_one, shift_one, gain_two, shift_two, gain_three, shift_three = [extra[n] for n in range(6)]
    live_total = jnp.sum(extra[6]) * 256.0 + jnp.sum(extra[7])
    later = gather(
        jnp.concatenate([self_output, cross_query, by_pairs(cross_key, cross_value), cross_output, hidden_in], axis=1)
    )
    output_self = later[:, :d]
    query_cross = later[:, d : 2 * d]
    kv_cross = later[:, 2 * d : 4 * d]
    output_cross = later[:, 4 * d : 5 * d]
    expand_whole = later[:, 5 * d :]
    reduce_whole = gather(hidden_out)

    low, first, bounds = row_bounds(pair_starts, source_starts, live_length)
    resident = tokens.astype(F32)
    normed_one = (norm_parts(resident)[0] * gain_one + shift_one).astype(BF16)
    qkv = mm(normed_one, qkv_weight).astype(BF16)
    self_mixed, self_logs = self_forward(low, first, qkv, row_count)
    after_self = resident + mm(self_mixed, output_self)
    normed_two = (norm_parts(after_self)[0] * gain_two + shift_two).astype(BF16)
    cross_q = mm(normed_two, query_cross).astype(BF16)
    cross_kv = mm(memory, kv_cross).astype(BF16)
    cross_mixed, cross_logs = cross_forward(bounds, cross_q, cross_kv, row_count)
    after_cross = after_self + mm(cross_mixed, output_cross)
    normed_three = (norm_parts(after_cross)[0] * gain_three + shift_three).astype(BF16)
    hidden = mm(normed_three, expand_whole)
    activated, gelu_back = jax.vjp(jax.nn.gelu, hidden)
    activated = activated.astype(BF16)
    layer_output = (after_cross + mm(activated, reduce_whole)).astype(BF16)

    device = lax.axis_index(names)
    member = (group_bounds[:-1] <= device) & (device < group_bounds[1:])
    pair_tokens = jnp.sum(jnp.where(member, group_counts, 0))
    device_count = 1
    for _, size in mesh_axes:
        device_count *= size
    token_all = row_count * SEQ * device_count
    row_weight = pair_tokens.astype(F32) * (token_all / 1000.0) / live_total
    places = jnp.arange(SEQ, dtype=jnp.int32)
    live_mask = (places[None, :] < live_length[:, None]).astype(F32).reshape(-1, 1)
    out_grad = cotangent.astype(F32) * live_mask * row_weight

    branch_three = out_grad.astype(BF16)
    reduce_shard = reduce_sum(outer_sum(activated, branch_three))
    hidden_grad = gelu_back(linear_back(branch_three, reduce_whole))[0].astype(BF16)
    expand_shard = reduce_sum(outer_sum(normed_three, hidden_grad))
    cross_part, gain_three_grad, shift_three_grad = norm_back(
        after_cross, gain_three, linear_back(hidden_grad, expand_whole)
    )
    cross_total = out_grad + cross_part

    branch_two = cross_total.astype(BF16)
    mixed_grad = linear_back(branch_two, output_cross).astype(BF16)
    cq_grad, ckv_grad = cross_backward(bounds, cross_logs, cross_q, cross_kv, cross_mixed, mixed_grad, row_count)
    cross_shard = reduce_sum(
        jnp.concatenate(
            [outer_sum(cross_mixed, branch_two), outer_sum(normed_two, cq_grad), outer_sum(memory, ckv_grad)], axis=1
        )
    )
    memory_grad = linear_back(ckv_grad, kv_cross).astype(BF16)
    self_part, gain_two_grad, shift_two_grad = norm_back(after_self, gain_two, linear_back(cq_grad, query_cross))
    self_total = cross_total + self_part

    branch_one = self_total.astype(BF16)
    self_output_shard = reduce_sum(outer_sum(self_mixed, branch_one))
    mixed_grad = linear_back(branch_one, output_self).astype(BF16)
    qkv_grad = self_backward(low, first, self_logs, qkv, self_mixed, mixed_grad, row_count)
    qkv_shard = reduce_sum(outer_sum(normed_one, qkv_grad))
    input_part, gain_one_grad, shift_one_grad = norm_back(resident, gain_one, linear_back(qkv_grad, qkv_weight))
    tokens_grad = (self_total + input_part).astype(BF16)

    norm_grads = sum_everywhere(
        jnp.stack([gain_one_grad, shift_one_grad, gain_two_grad, shift_two_grad, gain_three_grad, shift_three_grad]),
        mesh_axes,
    )
    norm_shards = lax.dynamic_slice_in_dim(norm_grads, device * shard_rows, shard_rows, axis=1)
    query_shard, key_shard, value_shard = from_pairs(qkv_shard, 3)
    cross_key_shard, cross_value_shard = from_pairs(cross_shard[:, 2 * d :], 2)
    return (
        layer_output,
        tokens_grad,
        memory_grad,
        query_shard,
        key_shard,
        value_shard,
        self_output_shard,
        cross_shard[:, d : 2 * d],
        cross_key_shard,
        cross_value_shard,
        cross_shard[:, :d],
        expand_shard,
        reduce_shard,
        *[norm_shards[n] for n in range(6)],
    )


def solution(mesh):
    names = ("wide", "narrow")
    mesh_axes = tuple((axis, mesh.shape[axis]) for axis in names)
    split, vector = P(names, None), P(names)
    return jax.shard_map(
        functools.partial(on_device, mesh_axes),
        mesh=mesh,
        in_specs=(split,) * 3 + (vector,) + (split,) * 2 + (P(), P()) + (split,) * 10 + (vector,) * 6,
        out_specs=(split,) * 13 + (vector,) * 6,
        check_vma=False,
    )
```

```python
import functools
import jax
import jax.numpy as jnp
from jax import lax
from jax.experimental import pallas as pl
from jax.experimental.pallas import tpu as pltpu
from jax.sharding import PartitionSpec as P

SEQ = 1024
MEM = 512
HEADS = 16
HEAD_DIM = 64
WIDTH = HEADS * HEAD_DIM
EPSILON = 1e-05
BQ = 256
LOG2E = 1.4426950408889634
SCALE2 = HEAD_DIM**-0.5 * LOG2E
FILLER = -1e30
F32, BF16 = jnp.float32, jnp.bfloat16


def mm(a, b):
    return jnp.dot(a, b, preferred_element_type=F32)


def halves(x):
    low = lax.broadcasted_iota(jnp.int32, x.shape, 1) < HEAD_DIM
    zero = jnp.zeros_like(x)
    return (jnp.where(low, x, zero), jnp.where(low, zero, x))


def self_allowed_of(i, j, first_row):
    shape = (BQ, BQ)
    key = lax.broadcasted_iota(jnp.int32, shape, 0)
    allowed = key >= first_row - j * BQ
    if i == j:
        allowed = allowed & (key <= lax.broadcasted_iota(jnp.int32, shape, 1))
    return allowed


def self_forward_kernel(low_ref, first_ref, qkv_ref, out_ref, log_ref, m_ref, l_ref, acc_ref):
    row = pl.program_id(0)
    blocks = SEQ // BQ
    for i in range(blocks):
        rows = slice(i * BQ, (i + 1) * BQ)
        q_t = qkv_ref[rows, 0:128].T
        first_row = first_ref[0, :, rows]

        def step(j, fresh):
            keys = slice(j * BQ, (j + 1) * BQ)
            k_parts = halves(qkv_ref[keys, 128:256])
            v_t = qkv_ref[keys, 256:384].T
            allowed = self_allowed_of(i, j, first_row)
            for h in range(2):
                feats = slice(h * 64, (h + 1) * 64)
                s = jnp.where(allowed, mm(k_parts[h], q_t) * SCALE2, FILLER)
                peak = jnp.max(s, axis=0, keepdims=True)
                if fresh:
                    p = jnp.exp2(s - peak)
                    m_ref[h : h + 1, :] = peak
                    l_ref[h : h + 1, :] = jnp.sum(p, axis=0, keepdims=True)
                    acc_ref[feats, :] = mm(v_t[feats, :], p.astype(BF16))
                else:
                    old = m_ref[h : h + 1, :]
                    peak = jnp.maximum(old, peak)
                    p = jnp.exp2(s - peak)
                    fade = jnp.exp2(old - peak)
                    m_ref[h : h + 1, :] = peak
                    l_ref[h : h + 1, :] = l_ref[h : h + 1, :] * fade + jnp.sum(p, axis=0, keepdims=True)
                    acc_ref[feats, :] = acc_ref[feats, :] * fade + mm(v_t[feats, :], p.astype(BF16))

        step(i, True)
        for j in reversed(range(i)):
            pl.when(j >= low_ref[row * blocks + i])(functools.partial(step, j, False))
        total = l_ref[0:2, :]
        log_ref[0, 0, 0:2, rows] = m_ref[0:2, :] + jnp.log2(total)
        inv = 1.0 / total
        o_t = jnp.concatenate([acc_ref[0:64, :] * inv[0:1], acc_ref[64:128, :] * inv[1:2]], axis=0)
        out_ref[rows, :] = o_t.T.astype(BF16)


def self_forward(low, first, qkv, row_count):
    pairs = HEADS // 2
    return pl.pallas_call(
        self_forward_kernel,
        grid_spec=pltpu.PrefetchScalarGridSpec(
            num_scalar_prefetch=1,
            grid=(row_count, pairs),
            in_specs=[
                pl.BlockSpec((1, 1, SEQ), lambda r, p, low: (r, 0, 0)),
                pl.BlockSpec((SEQ, 384), lambda r, p, low: (r, p)),
            ],
            out_specs=[
                pl.BlockSpec((SEQ, 128), lambda r, p, low: (r, p)),
                pl.BlockSpec((1, 1, 8, SEQ), lambda r, p, low: (r, p, 0, 0)),
            ],
            scratch_shapes=[pltpu.VMEM((8, BQ), F32), pltpu.VMEM((8, BQ), F32), pltpu.VMEM((128, BQ), F32)],
        ),
        out_shape=[
            jax.ShapeDtypeStruct((row_count * SEQ, HEADS * HEAD_DIM), BF16),
            jax.ShapeDtypeStruct((row_count, pairs, 8, SEQ), F32),
        ],
        name="self_forward",
        compiler_params=pltpu.CompilerParams(vmem_limit_bytes=32 << 20),
        cost_estimate=pl.CostEstimate(flops=20 << 30, bytes_accessed=row_count * (8 << 20), transcendentals=8 << 20),
    )(low, first, qkv)


def self_backward_kernel(low_ref, first_ref, log_ref, qkv_ref, out_ref, grad_ref, dqkv_ref, dk_ref, dv_ref, dq_ref):
    row = pl.program_id(0)
    blocks = SEQ // BQ
    dk_ref[...] = jnp.zeros_like(dk_ref)
    dv_ref[...] = jnp.zeros_like(dv_ref)
    for i in range(blocks):
        rows = slice(i * BQ, (i + 1) * BQ)
        q, g = qkv_ref[rows, 0:128], grad_ref[rows, :]
        q_t, g_t = q.T, g.T
        prod = g_t.astype(F32) * out_ref[rows, :].T.astype(F32)
        delta = [jnp.sum(prod[h * 64 : (h + 1) * 64], axis=0, keepdims=True) for h in range(2)]
        q_parts, g_parts = halves(q), halves(g)
        first_row = first_ref[0, :, rows]

        def step(j, fresh):
            keys = slice(j * BQ, (j + 1) * BQ)
            k = qkv_ref[keys, 128:256]
            k_parts, k_t = halves(k), k.T
            v_parts = halves(qkv_ref[keys, 256:384])
            allowed = self_allowed_of(i, j, first_row)
            dv, dk = [], []
            for h in range(2):
                feats = slice(h * 64, (h + 1) * 64)
                s = jnp.where(allowed, mm(k_parts[h], q_t) * SCALE2, FILLER)
                p = jnp.exp2(s - log_ref[0, 0, h : h + 1, rows])
                dp = mm(v_parts[h], g_t)
                ds = (p * (dp - delta[h])).astype(BF16)
                dv.append(mm(p.astype(BF16), g_parts[h]))
                dk.append(mm(ds, q_parts[h]))
                part = mm(k_t[feats, :], ds)
                dq_ref[feats, :] = part if fresh else dq_ref[feats, :] + part
            dv_ref[keys, :] += dv[0] + dv[1]
            dk_ref[keys, :] += dk[0] + dk[1]

        step(i, True)
        for j in reversed(range(i)):
            pl.when(j >= low_ref[row * blocks + i])(functools.partial(step, j, False))
        dqkv_ref[rows, 0:128] = (dq_ref[...] * HEAD_DIM**-0.5).T.astype(BF16)
    dqkv_ref[:, 128:256] = (dk_ref[...] * HEAD_DIM**-0.5).astype(BF16)
    dqkv_ref[:, 256:384] = dv_ref[...].astype(BF16)


def self_backward(low, first, logs, qkv, out, grad, row_count, part):
    pairs = HEADS // 4
    skip = part * pairs
    return pl.pallas_call(
        self_backward_kernel,
        grid_spec=pltpu.PrefetchScalarGridSpec(
            num_scalar_prefetch=1,
            grid=(row_count, pairs),
            in_specs=[
                pl.BlockSpec((1, 1, SEQ), lambda r, p, low: (r, 0, 0)),
                pl.BlockSpec((1, 1, 8, SEQ), lambda r, p, low: (r, p + skip, 0, 0)),
                pl.BlockSpec((SEQ, 384), lambda r, p, low: (r, p + skip)),
                pl.BlockSpec((SEQ, 128), lambda r, p, low: (r, p + skip)),
                pl.BlockSpec((SEQ, 128), lambda r, p, low: (r, p + skip)),
            ],
            out_specs=pl.BlockSpec((SEQ, 384), lambda r, p, low: (r, p)),
            scratch_shapes=[pltpu.VMEM((SEQ, 128), F32), pltpu.VMEM((SEQ, 128), F32), pltpu.VMEM((128, BQ), F32)],
        ),
        out_shape=jax.ShapeDtypeStruct((row_count * SEQ, pairs * 384), BF16),
        name="self_backward",
        compiler_params=pltpu.CompilerParams(vmem_limit_bytes=32 << 20),
        cost_estimate=pl.CostEstimate(flops=(5 << 30) * pairs, bytes_accessed=row_count * (16 << 20), transcendentals=8 << 20),
    )(low, first, logs, qkv, out, grad)


def cross_allowed_of(bounds_ref, rows):
    key = lax.broadcasted_iota(jnp.int32, (MEM, BQ), 0)
    return (key >= bounds_ref[0, 0:1, rows]) & (key < bounds_ref[0, 1:2, rows])


def cross_forward_kernel(bounds_ref, q_ref, kv_ref, out_ref, log_ref):
    k_parts = halves(kv_ref[:, 0:128])
    v_t = kv_ref[:, 128:256].T
    for i in range(SEQ // BQ):
        rows = slice(i * BQ, (i + 1) * BQ)
        q_t = q_ref[rows, :].T
        allowed = cross_allowed_of(bounds_ref, rows)
        outs = []
        for h in range(2):
            s = jnp.where(allowed, mm(k_parts[h], q_t) * SCALE2, FILLER)
            peak = jnp.max(s, axis=0, keepdims=True)
            p = jnp.exp2(s - peak)
            total = jnp.sum(p, axis=0, keepdims=True)
            log_ref[0, 0, h : h + 1, rows] = peak + jnp.log2(total)
            outs.append(mm(v_t[h * 64 : (h + 1) * 64, :], p.astype(BF16)) * (1.0 / total))
        out_ref[rows, :] = jnp.concatenate(outs, axis=0).T.astype(BF16)


def cross_forward(bounds, q, kv, row_count):
    pairs = HEADS // 2
    return pl.pallas_call(
        cross_forward_kernel,
        grid=(row_count, pairs),
        in_specs=[
            pl.BlockSpec((1, 8, SEQ), lambda r, p: (r, 0, 0)),
            pl.BlockSpec((SEQ, 128), lambda r, p: (r, p)),
            pl.BlockSpec((MEM, 256), lambda r, p: (r, p)),
        ],
        out_specs=[
            pl.BlockSpec((SEQ, 128), lambda r, p: (r, p)),
            pl.BlockSpec((1, 1, 8, SEQ), lambda r, p: (r, p, 0, 0)),
        ],
        out_shape=[
            jax.ShapeDtypeStruct((row_count * SEQ, HEADS * HEAD_DIM), BF16),
            jax.ShapeDtypeStruct((row_count, pairs, 8, SEQ), F32),
        ],
        name="cross_forward",
        compiler_params=pltpu.CompilerParams(vmem_limit_bytes=32 << 20),
        cost_estimate=pl.CostEstimate(flops=20 << 30, bytes_accessed=row_count * (6 << 20), transcendentals=8 << 20),
    )(bounds, q, kv)


def cross_backward_kernel(bounds_ref, log_ref, q_ref, kv_ref, out_ref, grad_ref, dq_ref, dkv_ref, dk_ref, dv_ref):
    k = kv_ref[:, 0:128]
    k_parts, k_t = halves(k), k.T
    v_parts = halves(kv_ref[:, 128:256])
    for i in range(SEQ // BQ):
        rows = slice(i * BQ, (i + 1) * BQ)
        q, g = q_ref[rows, :], grad_ref[rows, :]
        q_t, g_t = q.T, g.T
        prod = g_t.astype(F32) * out_ref[rows, :].T.astype(F32)
        q_parts, g_parts = halves(q), halves(g)
        allowed = cross_allowed_of(bounds_ref, rows)
        dv, dk, dq = [], [], []
        for h in range(2):
            feats = slice(h * 64, (h + 1) * 64)
            delta = jnp.sum(prod[feats], axis=0, keepdims=True)
            s = jnp.where(allowed, mm(k_parts[h], q_t) * SCALE2, FILLER)
            p = jnp.exp2(s - log_ref[0, 0, h : h + 1, rows])
            dp = mm(v_parts[h], g_t)
            ds = (p * (dp - delta)).astype(BF16)
            dv.append(mm(p.astype(BF16), g_parts[h]))
            dk.append(mm(ds, q_parts[h]))
            dq.append(mm(k_t[feats, :], ds))
        if i == 0:
            dv_ref[...] = dv[0] + dv[1]
            dk_ref[...] = dk[0] + dk[1]
        else:
            dv_ref[...] += dv[0] + dv[1]
            dk_ref[...] += dk[0] + dk[1]
        dq_ref[rows, :] = (jnp.concatenate(dq, axis=0) * HEAD_DIM**-0.5).T.astype(BF16)
    dkv_ref[:, 0:128] = (dk_ref[...] * HEAD_DIM**-0.5).astype(BF16)
    dkv_ref[:, 128:256] = dv_ref[...].astype(BF16)


def cross_backward(bounds, logs, q, kv, out, grad, row_count):
    pairs = HEADS // 2
    return pl.pallas_call(
        cross_backward_kernel,
        grid=(row_count, pairs),
        in_specs=[
            pl.BlockSpec((1, 8, SEQ), lambda r, p: (r, 0, 0)),
            pl.BlockSpec((1, 1, 8, SEQ), lambda r, p: (r, p, 0, 0)),
            pl.BlockSpec((SEQ, 128), lambda r, p: (r, p)),
            pl.BlockSpec((MEM, 256), lambda r, p: (r, p)),
            pl.BlockSpec((SEQ, 128), lambda r, p: (r, p)),
            pl.BlockSpec((SEQ, 128), lambda r, p: (r, p)),
        ],
        out_specs=[
            pl.BlockSpec((SEQ, 128), lambda r, p: (r, p)),
            pl.BlockSpec((MEM, 256), lambda r, p: (r, p)),
        ],
        scratch_shapes=[pltpu.VMEM((MEM, 128), F32), pltpu.VMEM((MEM, 128), F32)],
        out_shape=[
            jax.ShapeDtypeStruct((row_count * SEQ, HEADS * HEAD_DIM), BF16),
            jax.ShapeDtypeStruct((row_count * MEM, 2 * HEADS * HEAD_DIM), BF16),
        ],
        name="cross_backward",
        compiler_params=pltpu.CompilerParams(vmem_limit_bytes=32 << 20),
        cost_estimate=pl.CostEstimate(flops=40 << 30, bytes_accessed=row_count * (12 << 20), transcendentals=8 << 20),
    )(bounds, logs, q, kv, out, grad)


def row_bounds(pair_starts, source_starts, live_length):
    places = jnp.arange(SEQ, dtype=jnp.int32)
    counted = jnp.sum((pair_starts[:, :, None] <= places).astype(jnp.int32), axis=1)
    live = places < live_length[:, None]
    begun = jnp.max(jnp.where(pair_starts[:, :, None] <= places, pair_starts[:, :, None], 0), axis=1)
    first = jnp.where(live, begun, live_length[:, None])
    nseg = pair_starts.shape[1]
    pick = jnp.arange(nseg)[None, :, None] == (counted - 1)[:, None, :]
    ends = jnp.concatenate([source_starts[:, 1:], jnp.full_like(source_starts[:, :1], MEM)], axis=1)
    start = jnp.sum(jnp.where(pick, source_starts[:, :, None], 0), axis=1)
    end = jnp.sum(jnp.where(pick, ends[:, :, None], 0), axis=1)
    start = jnp.where(live, start, 0)
    end = jnp.where(live, end, MEM)
    bounds = jnp.pad(jnp.stack([start, end], axis=1), ((0, 0), (0, 6), (0, 0)))
    low = (first[:, ::BQ] // BQ).reshape(-1)
    return low, first[:, None, :], bounds


TB = 256


def mm_t(a, b):
    return lax.dot_general(a, b, (((1,), (1,)), ((), ())), preferred_element_type=F32)


def norm_parts(values):
    center = values - jnp.mean(values, axis=-1, keepdims=True)
    inverse = lax.rsqrt(jnp.mean(center * center, axis=-1, keepdims=True) + EPSILON)
    return center * inverse, inverse


def norm_back(unit, inverse, gain, gradient):
    scaled = gradient * gain
    return inverse * (
        scaled
        - jnp.mean(scaled, axis=-1, keepdims=True)
        - unit * jnp.mean(scaled * unit, axis=-1, keepdims=True)
    )


def add_norm_grads(ref, unit, gradient):
    @pl.when(pl.program_id(0) == 0)
    def _():
        ref[...] = jnp.zeros_like(ref)

    ref[0:1, :] += jnp.sum(gradient * unit, axis=0, keepdims=True)
    ref[1:2, :] += jnp.sum(gradient, axis=0, keepdims=True)


def tile(rows, columns, at=0):
    return pl.BlockSpec((rows, columns), lambda b: (b, at))


def whole(rows, columns, at=0):
    return pl.BlockSpec((rows, columns), lambda b: (0, at), pipeline_mode=pl.Buffered(1))


def shape(rows, columns, dtype):
    return jax.ShapeDtypeStruct((rows, columns), dtype)


def params(mib):
    return pltpu.CompilerParams(vmem_limit_bytes=mib << 20)


def cost(flops, moved):
    return pl.CostEstimate(flops=int(flops), bytes_accessed=int(moved), transcendentals=0)


def project_kernel(tokens_ref, norms_ref, weight_ref, normed_ref, out_ref):
    unit, _ = norm_parts(tokens_ref[...].astype(F32))
    normed = (unit * norms_ref[0:1, :] + norms_ref[1:2, :]).astype(BF16)
    normed_ref[...] = normed
    for part in range(3):
        at = slice(part * 1024, (part + 1) * 1024)
        out_ref[:, at] = mm(normed, weight_ref[:, at]).astype(BF16)


def project(tokens, norms, early):
    rows, d = tokens.shape
    return pl.pallas_call(
        project_kernel,
        grid=(rows // TB,),
        in_specs=[tile(TB, d), whole(8, d), whole(d, 3 * d)],
        out_specs=[tile(TB, d), tile(TB, 3 * d)],
        out_shape=[shape(rows, d, BF16), shape(rows, 3 * d, BF16)],
        name="project",
        compiler_params=params(40),
        cost_estimate=cost(6 * rows * d * d, 16 << 20),
    )(tokens, norms, early)


def middle_kernel(
    mixed_ref, tokens_ref, memory_ref, norms_ref, wo_ref, wq_ref, wkv_ref, after_ref, normed_ref, q_ref, kv_ref
):
    after = tokens_ref[...].astype(F32) + mm(mixed_ref[...], wo_ref[...])
    after_ref[...] = after
    kv_ref[...] = mm(memory_ref[...], wkv_ref[...]).astype(BF16)
    unit, _ = norm_parts(after)
    normed = (unit * norms_ref[2:3, :] + norms_ref[3:4, :]).astype(BF16)
    normed_ref[...] = normed
    q_ref[...] = mm(normed, wq_ref[...]).astype(BF16)


def middle(mixed, tokens, memory, norms, early):
    rows, d = tokens.shape
    mem_rows = memory.shape[0]
    steps = rows // TB
    mb = mem_rows // steps
    return pl.pallas_call(
        middle_kernel,
        grid=(steps,),
        in_specs=[
            tile(TB, d),
            tile(TB, d),
            tile(mb, d),
            whole(8, d),
            whole(d, d, OUT_SELF),
            whole(d, d, QUERY_CROSS),
            whole(d, 2 * d, KV_CROSS),
        ],
        out_specs=[tile(TB, d), tile(TB, d), tile(TB, d), tile(mb, 2 * d)],
        out_shape=[shape(rows, d, F32), shape(rows, d, BF16), shape(rows, d, BF16), shape(mem_rows, 2 * d, BF16)],
        name="middle",
        compiler_params=params(40),
        cost_estimate=cost(6 * rows * d * d, 20 << 20),
    )(mixed, tokens, memory, norms, early, early, early)


GELU_A = 0.7978845608028654
GELU_B = 0.044715


def feed_kernel(
    live_ref,
    weight_ref,
    mixed_ref,
    before_ref,
    cot_ref,
    norms_ref,
    wo_ref,
    win_ref,
    wout_ref,
    out_ref,
    normed_ref,
    act_ref,
    hid_ref,
    b3_ref,
    total_ref,
    b2_ref,
    grad_ref,
    ngrad_ref,
):
    block = pl.program_id(0)
    per_row = SEQ // TB
    row = block // per_row
    places = lax.broadcasted_iota(jnp.int32, (TB, 1), 0) + (block % per_row) * TB
    live = (places < live_ref[row]).astype(F32)
    out_grad = cot_ref[...].astype(F32) * live * weight_ref[0]
    branch = out_grad.astype(BF16)
    b3_ref[...] = branch
    after = before_ref[...] + mm(mixed_ref[...], wo_ref[...])
    unit, inverse = norm_parts(after)
    normed = (unit * norms_ref[4:5, :] + norms_ref[5:6, :]).astype(BF16)
    normed_ref[...] = normed
    d = normed.shape[1]
    result, back = after, None
    for part in range(win_ref.shape[1] // d):
        at = slice(part * d, (part + 1) * d)
        x = mm(normed, win_ref[:, at])
        square = x * x
        t = jnp.tanh(GELU_A * x * (1.0 + GELU_B * square))
        half = 0.5 * (1.0 + t)
        act = (x * half).astype(BF16)
        slope = half + (0.5 * GELU_A) * x * (1.0 - t * t) * (1.0 + (3.0 * GELU_B) * square)
        act_ref[:, at] = act
        hid = (mm_t(branch, wout_ref[:, at]) * slope).astype(BF16)
        hid_ref[:, at] = hid
        result = result + mm(act, wout_ref[:, at])
        term = mm_t(hid, win_ref[:, at])
        back = term if back is None else back + term
    out_ref[...] = result.astype(BF16)
    total = out_grad + norm_back(unit, inverse, norms_ref[4:5, :], back)
    total_ref[...] = total
    b2 = total.astype(BF16)
    b2_ref[...] = b2
    grad_ref[...] = mm_t(b2, wo_ref[...]).astype(BF16)
    add_norm_grads(ngrad_ref, unit, back)


def feed(live_length, row_weight, mixed, before, cotangent, norms, early, late):
    rows, d = cotangent.shape
    ff = late.shape[1] // 2
    smem = pl.BlockSpec(memory_space=pltpu.SMEM)
    return pl.pallas_call(
        feed_kernel,
        grid=(rows // TB,),
        in_specs=[
            smem,
            smem,
            tile(TB, d),
            tile(TB, d),
            tile(TB, d),
            whole(8, d),
            whole(d, d, OUT_CROSS),
            whole(d, ff, 0),
            whole(d, ff, 1),
        ],
        out_specs=[
            tile(TB, d),
            tile(TB, d),
            tile(TB, ff),
            tile(TB, ff),
            tile(TB, d),
            tile(TB, d),
            tile(TB, d),
            tile(TB, d),
            whole(8, d),
        ],
        out_shape=[
            shape(rows, d, BF16),
            shape(rows, d, BF16),
            shape(rows, ff, BF16),
            shape(rows, ff, BF16),
            shape(rows, d, BF16),
            shape(rows, d, F32),
            shape(rows, d, BF16),
            shape(rows, d, BF16),
            shape(8, d, F32),
        ],
        name="feed",
        compiler_params=params(58),
        cost_estimate=cost(38 * rows * d * d, 50 << 20),
    )(live_length, row_weight, mixed, before, cotangent, norms, early, late, late)


def cross_close_kernel(
    dq_ref, dkv_ref, before_ref, total_ref, norms_ref, wq_ref, wkv_ref, wo_ref, out_ref, b1_ref, grad_ref, mem_ref, ngrad_ref
):
    gradient = mm_t(dq_ref[...], wq_ref[...])
    mem_ref[...] = mm_t(dkv_ref[...], wkv_ref[...]).astype(BF16)
    unit, inverse = norm_parts(before_ref[...])
    total = total_ref[...] + norm_back(unit, inverse, norms_ref[2:3, :], gradient)
    out_ref[...] = total
    b1 = total.astype(BF16)
    b1_ref[...] = b1
    grad_ref[...] = mm_t(b1, wo_ref[...]).astype(BF16)
    add_norm_grads(ngrad_ref, unit, gradient)


def cross_close(dq, dkv, before, total, norms, early):
    rows, d = dq.shape
    mem_rows = dkv.shape[0]
    steps = rows // TB
    mb = mem_rows // steps
    return pl.pallas_call(
        cross_close_kernel,
        grid=(steps,),
        in_specs=[
            tile(TB, d),
            tile(mb, 2 * d),
            tile(TB, d),
            tile(TB, d),
            whole(8, d),
            whole(d, d, QUERY_CROSS),
            whole(d, 2 * d, KV_CROSS),
            whole(d, d, OUT_SELF),
        ],
        out_specs=[tile(TB, d), tile(TB, d), tile(TB, d), tile(mb, d), whole(8, d)],
        out_shape=[
            shape(rows, d, F32),
            shape(rows, d, BF16),
            shape(rows, d, BF16),
            shape(mem_rows, d, BF16),
            shape(8, d, F32),
        ],
        name="cross_close",
        compiler_params=params(40),
        cost_estimate=cost(6 * rows * d * d, 24 << 20),
    )(dq, dkv, before, total, norms, early, early, early)


def self_close_kernel(dqkv_ref, before_ref, total_ref, norms_ref, w_ref, out_ref, ngrad_ref):
    gradient = mm_t(dqkv_ref[...], w_ref[...])
    unit, inverse = norm_parts(before_ref[...].astype(F32))
    total = total_ref[...] + norm_back(unit, inverse, norms_ref[0:1, :], gradient)
    out_ref[...] = total.astype(BF16)
    add_norm_grads(ngrad_ref, unit, gradient)


def self_close(dqkv, before, total, norms, early):
    rows, d = total.shape
    return pl.pallas_call(
        self_close_kernel,
        grid=(rows // TB,),
        in_specs=[tile(TB, 3 * d), tile(TB, d), tile(TB, d), whole(8, d), whole(d, 3 * d)],
        out_specs=[tile(TB, d), whole(8, d)],
        out_shape=[shape(rows, d, BF16), shape(8, d, F32)],
        name="self_close",
        compiler_params=params(40),
        cost_estimate=cost(6 * rows * d * d, 20 << 20),
    )(dqkv, before, total, norms, early)


OUT_SELF, KV_CROSS, QUERY_CROSS, OUT_CROSS, EXTRA = 3, 2, 6, 7, 64


def greet_all(narrow):
    w, z = lax.axis_index("wide"), lax.axis_index("narrow")
    barrier = pltpu.get_barrier_semaphore()
    others = [(w ^ 1, z), (w ^ 2, z), (w ^ 4, z)] + [(w, z ^ mask) for mask in range(1, narrow)]
    for other in others:
        pl.semaphore_signal(barrier, inc=1, device_id=other, device_id_type=pl.DeviceIdType.MESH)
    pl.semaphore_wait(barrier, len(others))


def early_gather_kernel(wide, narrow, shard_ref, out_ref, send_sems, recv_sems, own_sem):
    rows = shard_ref.shape[0]
    half = rows // 2
    w, z = lax.axis_index("wide"), lax.axis_index("narrow")
    core, x, y = w ^ 1, w ^ 2, w ^ 4
    up, down, to_x, to_y, on_y, on_x, to_core = [k * narrow for k in range(7)]

    def start_of(holder, s):
        return pl.multiple_of((holder * narrow + s) * rows, rows)

    def move(holder, s, number, target, first=0, count=rows, own=False):
        at = pl.multiple_of(start_of(holder, s) + first, half)
        place = out_ref.at[pl.ds(at, count)]
        return pltpu.make_async_remote_copy(
            src_ref=shard_ref.at[pl.ds(first, count)] if own else place,
            dst_ref=place,
            send_sem=send_sems.at[number],
            recv_sem=recv_sems.at[number],
            device_id=target,
            device_id_type=pl.DeviceIdType.MESH,
        )

    above, below = (w, z + 1), (w, z - 1)
    greet_all(narrow)

    keep = pltpu.make_async_copy(shard_ref, out_ref.at[pl.ds(start_of(w, z), rows)], own_sem)
    keep.start()

    def spread(s, own=False):
        move(w, s, to_x + s, (x, z), own=own).start()
        move(w, s, to_y + s, (y, z), own=own).start()
        move(w, s, to_core + s, (core, z), own=own).start()

    def relay(s):
        move(x, s, to_x + s, (x, z)).wait_recv()
        move(x, s, on_y + s, (y, z), 0, half).start()
        move(x, s, to_core + narrow + s, (core, z)).start()
        move(y, s, to_y + s, (y, z)).wait_recv()
        move(y, s, on_x + s, (x, z), half, half).start()
        move(y, s, to_core + 2 * narrow + s, (core, z)).start()

    def at_distance(r, action):
        if r == 0:
            action(z)
        else:
            pl.when(z - r >= 0)(lambda: action(z - r))
            pl.when(z + r < narrow)(lambda: action(z + r))

    pl.when(z < narrow - 1)(lambda: move(w, z, up + z, above, own=True).start())
    pl.when(z > 0)(lambda: move(w, z, down + z, below, own=True).start())
    spread(z, own=True)
    for r in range(1, narrow):

        def from_below(r=r):
            s = z - r
            move(w, s, up + s, above).wait_recv()
            pl.when(z < narrow - 1)(lambda: move(w, s, up + s, above).start())
            spread(s)

        def from_above(r=r):
            s = z + r
            move(w, s, down + s, below).wait_recv()
            pl.when(z > 0)(lambda: move(w, s, down + s, below).start())
            spread(s)

        pl.when(z - r >= 0)(from_below)
        pl.when(z + r < narrow)(from_above)
        at_distance(r - 1, relay)
    at_distance(narrow - 1, relay)

    def corner(s):
        move(x ^ 4, s, on_y + s, (y, z), 0, half).wait_recv()
        move(x ^ 4, s, on_x + s, (x, z), half, half).wait_recv()
        move(x ^ 4, s, to_core + 3 * narrow + s, (core, z)).start()

    for r in range(narrow):
        at_distance(r, corner)
    for s in range(narrow):
        for k, holder in enumerate((w, x, y, x ^ 4)):
            move(holder ^ 1, s, to_core + k * narrow + s, (core, z)).wait_recv()
    for s in range(narrow):
        pl.when((s <= z) & (z < narrow - 1))(lambda s=s: move(w, s, up + s, above).wait_send())
        pl.when((s >= z) & (z > 0))(lambda s=s: move(w, s, down + s, below).wait_send())
        move(w, s, to_x + s, (x, z)).wait_send()
        move(w, s, to_y + s, (y, z)).wait_send()
        move(x, s, on_y + s, (y, z), 0, half).wait_send()
        move(y, s, on_x + s, (x, z), half, half).wait_send()
        for k, holder in enumerate((w, x, y, x ^ 4)):
            move(holder, s, to_core + k * narrow + s, (core, z)).wait_send()
    keep.wait()


def early_gather(shard, mesh_axes):
    (_, wide), (_, narrow) = mesh_axes
    rows, columns = shard.shape
    if wide != 8 or rows % 32:
        return lax.all_gather(shard, tuple(axis for axis, _ in mesh_axes), axis=0, tiled=True)
    return pl.pallas_call(
        functools.partial(early_gather_kernel, wide, narrow),
        in_specs=[pl.BlockSpec(memory_space=pl.ANY)],
        out_specs=pl.BlockSpec(memory_space=pl.ANY),
        out_shape=jax.ShapeDtypeStruct((rows * wide * narrow, columns), BF16),
        scratch_shapes=[
            pltpu.SemaphoreType.DMA((10 * narrow,)),
            pltpu.SemaphoreType.DMA((10 * narrow,)),
            pltpu.SemaphoreType.DMA,
        ],
        name="early_gather",
        compiler_params=pltpu.CompilerParams(collective_id=0, has_side_effects=True),
        cost_estimate=pl.CostEstimate(flops=0, bytes_accessed=200 << 20, transcendentals=0),
    )(shard)


def stages_of(mesh_axes):
    plan = []
    for axis, size in mesh_axes:
        bits = size.bit_length() - 1
        at = 0
        while at < bits:
            take = 1 if (bits - at) % 2 else 2
            plan.append((axis, at, take))
            at += take
    return plan


def trade(value, axis, size, mask):
    return lax.ppermute(value, axis, [(i, i ^ mask) for i in range(size)])


def digit_of(axis, at, take):
    return (lax.axis_index(axis) >> at) & ((1 << take) - 1)


def pick(value, digit, place):
    if isinstance(value, list):
        return jnp.concatenate([pick(v, digit, place) for v in value], axis=0)
    return lax.dynamic_index_in_dim(value, digit, place, keepdims=False)


def add_up(own, pieces):
    total = own.astype(F32)
    for piece in pieces:
        total = total + piece.astype(F32)
    return total


def sum_steps(partial, mesh_axes):
    sizes = dict(mesh_axes)
    plan = stages_of(mesh_axes)
    groups = []
    for axis, _ in mesh_axes:
        groups += sorted((s for s in plan if s[0] == axis), key=lambda s: -s[1])
    devices = 1
    for _, size in mesh_axes:
        devices *= size
    columns = partial[0].shape[1]
    extents = [1 << s[2] for s in groups]
    value = [p.reshape(p.shape[0] // WIDTH, *extents, -1, columns) for p in partial]
    for number, stage in enumerate(plan):
        axis, at, take = stage
        place = 1 + groups.index(stage)
        groups.remove(stage)
        if axis == "wide" and take == 2:
            if isinstance(value, list):
                value = jnp.concatenate(value, axis=0)
            split = value.reshape(*value.shape[:place], 2, 2, *value.shape[place + 1 :])
            a, b = split[..., : columns // 2], split[..., columns // 2 :]
            low, high = digit_of(axis, at, 1), digit_of(axis, at + 1, 1)
            step = ((high, place, 2 << at), (low, place + 1, 1 << at))
            for (digit_a, place_a, mask_a), (digit_b, place_b, mask_b) in (
                step,
                ((low, place, 1 << at), (high, place, 2 << at)),
            ):
                pieces = yield [
                    trade(pick(a, digit_a ^ 1, place_a), axis, sizes[axis], mask_a),
                    trade(pick(b, digit_b ^ 1, place_b), axis, sizes[axis], mask_b),
                ]
                a = add_up(pick(a, digit_a, place_a), pieces[:1]).astype(BF16)
                b = add_up(pick(b, digit_b, place_b), pieces[1:]).astype(BF16)
            value = jnp.concatenate([a, b], axis=-1)
            continue
        digit = digit_of(axis, at, take)
        pieces = yield [
            trade(pick(value, digit ^ mask, place), axis, sizes[axis], mask << at) for mask in range(1, 1 << take)
        ]
        value = add_up(pick(value, digit, place), pieces)
        if number < len(plan) - 1:
            value = value.astype(BF16)
    return value.astype(F32).reshape(-1, columns)


class StagedSum:
    def __init__(self, partial, mesh_axes):
        self.steps = sum_steps(partial, mesh_axes)
        self.under_way = next(self.steps)
        self.value = None

    def go_on(self, pieces):
        try:
            self.under_way = self.steps.send(pieces)
        except StopIteration as stop:
            self.under_way, self.value = None, stop.value

    def result(self):
        while self.under_way is not None:
            self.go_on(self.under_way)
        return self.value


def fence(value, *sums):
    held = [s for s in sums if s.under_way is not None]
    value, arrived = lax.optimization_barrier((value, [s.under_way for s in held]))
    for s, pieces in zip(held, arrived):
        s.go_on(pieces)
    return value


def sum_everywhere(value, mesh_axes):
    sizes = dict(mesh_axes)
    for axis, at, take in stages_of(mesh_axes):
        arrived = [trade(value, axis, sizes[axis], mask << at) for mask in range(1, 1 << take)]
        for piece in arrived:
            value = value + piece
    return value


def by_pairs(*parts):
    rows = parts[0].shape[0]
    return jnp.stack([p.reshape(rows, -1, 128) for p in parts], axis=2).reshape(rows, -1)


def from_pairs(value, count):
    rows = value.shape[0]
    split = value.reshape(rows, -1, count, 128)
    return [split[:, :, c].reshape(rows, -1) for c in range(count)]


def outer_sum(left_side, gradient):
    return jnp.einsum("td,te->de", left_side, gradient, preferred_element_type=F32).astype(BF16)


CHUNKS = 4


class Scatter:
    def __init__(self, share, buffers, out_ref, send_sems, recv_sems, narrow, base=0):
        self.share, self.out_ref = share, out_ref
        self.from_core, self.a1, self.b1, self.a2, self.b2, self.from_line = buffers
        self.send_sems, self.recv_sems, self.base = send_sems, recv_sems, base
        self.narrow = narrow
        self.half = share.shape[-1] // 2
        self.w, self.z = lax.axis_index("wide"), lax.axis_index("narrow")
        self.c, self.x, self.y = self.w & 1, (self.w >> 1) & 1, (self.w >> 2) & 1
        self.per_chunk = 4 + narrow

    def move(self, i, number, src, dst, target):
        at = self.base + i * self.per_chunk + number
        return pltpu.make_async_remote_copy(
            src_ref=src,
            dst_ref=dst,
            send_sem=self.send_sems.at[at],
            recv_sem=self.recv_sems.at[at],
            device_id=target,
            device_id_type=pl.DeviceIdType.MESH,
        )

    def to_core(self, i):
        return self.move(i, 0, self.share.at[i, :, :, 1 - self.c], self.from_core.at[i], (self.w ^ 1, self.z))

    def first(self, i):
        left, right = pl.ds(0, self.half), pl.ds(self.half, self.half)
        return (
            self.move(
                i, 1, self.share.at[i, :, 1 - self.x, self.c, :, :, left], self.a1.at[i], (self.w ^ 2, self.z)
            ),
            self.move(
                i, 2, self.share.at[i, 1 - self.y, :, self.c, :, :, right], self.b1.at[i], (self.w ^ 4, self.z)
            ),
        )

    def second(self, i):
        left, right = pl.ds(0, self.half), pl.ds(self.half, self.half)
        return (
            self.move(
                i, 3, self.share.at[i, 1 - self.y, self.x, self.c, :, :, left], self.a2.at[i], (self.w ^ 4, self.z)
            ),
            self.move(
                i, 4, self.share.at[i, self.y, 1 - self.x, self.c, :, :, right], self.b2.at[i], (self.w ^ 2, self.z)
            ),
        )

    def along(self, i):
        return [
            self.move(
                i,
                4 + mask,
                self.share.at[i, self.y, self.x, self.c, self.z ^ mask],
                self.from_line.at[i, mask - 1],
                (self.w, self.z ^ mask),
            )
            for mask in range(1, self.narrow)
        ]

    def begin(self, i):
        self.to_core(i).start()

    def add(self, place, columns, piece):
        now = self.share[(*place, slice(None), slice(None), columns)]
        self.share[(*place, slice(None), slice(None), columns)] = (now.astype(F32) + piece.astype(F32)).astype(BF16)

    def step(self, i, stage):
        both, left, right = slice(None), slice(0, self.half), slice(self.half, None)
        if stage == 0:
            self.to_core(i).wait_recv()
            for a in range(2):
                for b in range(2):
                    self.add((i, a, b, self.c), both, self.from_core[i, a, b])
            for copy in self.first(i):
                copy.start()
        elif stage == 1:
            for copy in self.first(i):
                copy.wait_recv()
            for a in range(2):
                self.add((i, a, self.x, self.c), left, self.a1[i, a])
                self.add((i, self.y, a, self.c), right, self.b1[i, a])
            for copy in self.second(i):
                copy.start()
        elif stage == 2:
            for copy in self.second(i):
                copy.wait_recv()
            self.add((i, self.y, self.x, self.c), left, self.a2[i])
            self.add((i, self.y, self.x, self.c), right, self.b2[i])
            for copy in self.along(i):
                copy.start()
        else:
            for copy in self.along(i):
                copy.wait_recv()
            total = self.share[i, self.y, self.x, self.c, self.z].astype(F32)
            for mask in range(1, self.narrow):
                total = total + self.from_line[i, mask - 1].astype(F32)
            width = 2 * self.half
            self.out_ref[:, i * width : (i + 1) * width] = total

    def close(self, i):
        for copy in (self.to_core(i), *self.first(i), *self.second(i), *self.along(i)):
            copy.wait_send()


def scatter_scratch(chunks, narrow, rows, width):
    return [
        pltpu.VMEM((chunks, 2, 2, narrow, rows, width), BF16),
        pltpu.VMEM((chunks, 2, narrow, rows, width // 2), BF16),
        pltpu.VMEM((chunks, 2, narrow, rows, width // 2), BF16),
        pltpu.VMEM((chunks, narrow, rows, width // 2), BF16),
        pltpu.VMEM((chunks, narrow, rows, width // 2), BF16),
        pltpu.VMEM((chunks, narrow - 1, rows, width), BF16),
    ]


def tail_kernel(
    narrow,
    share_any,
    normed_any,
    low_any,
    high_any,
    weight_any,
    tokens_any,
    total_any,
    norms_ref,
    norm_two_ref,
    norm_three_ref,
    out_ref,
    shard_ref,
    norm_out_ref,
    normed,
    normed_t,
    grads,
    weight,
    tokens,
    total,
    share,
    from_core,
    a1,
    b1,
    a2,
    b2,
    from_line,
    nval,
    nin,
    send_sems,
    recv_sems,
    load_sems,
):
    d = normed.shape[1]
    width = share.shape[-1]
    part = low_any.shape[1]
    loads = [
        pltpu.make_async_copy(share_any, share.at[0], load_sems.at[0]),
        pltpu.make_async_copy(normed_any, normed, load_sems.at[1]),
        pltpu.make_async_copy(low_any, grads.at[:, pl.ds(0, part)], load_sems.at[2]),
        pltpu.make_async_copy(high_any, grads.at[:, pl.ds(part, part)], load_sems.at[3]),
        pltpu.make_async_copy(weight_any.at[:, pl.ds(0, 3 * d)], weight, load_sems.at[4]),
        pltpu.make_async_copy(tokens_any, tokens, load_sems.at[5]),
        pltpu.make_async_copy(total_any, total, load_sems.at[6]),
    ]
    for load in loads:
        load.start()
    greet_all(narrow)
    scatter = Scatter(share, (from_core, a1, b1, a2, b2, from_line), shard_ref, send_sems, recv_sems, narrow)
    w, z = scatter.w, scatter.z
    rows = share.shape[5]
    group = 2 * narrow * rows

    loads[0].wait()
    scatter.begin(0)
    loads[1].wait()
    for t in range(d // TB):
        normed_t[:, t * TB : (t + 1) * TB] = normed[t * TB : (t + 1) * TB, :].T

    def multiply(i):
        if i < 3:
            loads[1 + i].wait()
        for a in range(2):
            for b in range(2):
                at = (2 * a + b) * group
                product = mm(normed_t[at : at + group, :], grads[:, (i - 1) * width : i * width])
                share[i, a, b] = product.astype(BF16).reshape(2, narrow, rows, width)
        scatter.begin(i)

    def close_tokens(t):
        if t == 0:
            for load in loads[4:]:
                load.wait()
        at = slice(t * TB, (t + 1) * TB)
        gradient = mm_t(grads[at, :], weight[...])
        unit, inverse = norm_parts(tokens[at, :].astype(F32))
        out_ref[at, :] = (total[at, :] + norm_back(unit, inverse, norms_ref[0:1, :], gradient)).astype(BF16)
        gain, shift = jnp.sum(gradient * unit, axis=0, keepdims=True), jnp.sum(gradient, axis=0, keepdims=True)
        if t == 0:
            nval[0, 0:1, :] = gain
            nval[0, 1:2, :] = shift
        else:
            nval[0, 0:1, :] += gain
            nval[0, 1:2, :] += shift

    first_sem = CHUNKS * scatter.per_chunk

    def norm_copy(stage, number, target):
        return pltpu.make_async_remote_copy(
            src_ref=nval.at[stage],
            dst_ref=nin.at[number],
            send_sem=send_sems.at[first_sem + number],
            recv_sem=recv_sems.at[first_sem + number],
            device_id=target,
            device_id_type=pl.DeviceIdType.MESH,
        )

    norm_copies = [[norm_copy(0, 0, (w ^ 1, z))], [norm_copy(1, 1, (w ^ 2, z))], [norm_copy(2, 2, (w ^ 4, z))]]
    norm_copies.append([norm_copy(3, 2 + mask, (w, z ^ mask)) for mask in range(1, narrow)])

    def norm_step(stage):
        if stage == 0:
            nval[0, 2:4, :] = norm_two_ref[0:2, :]
            nval[0, 4:6, :] = norm_three_ref[0:2, :]
            nval[0, 6:8, :] = jnp.zeros_like(norm_two_ref[0:2, :])
        else:
            for copy in norm_copies[stage - 1]:
                copy.wait_recv()
            value = nval[stage - 1]
            if stage < 4:
                nval[stage] = value + nin[stage - 1]
            else:
                for mask in range(1, narrow):
                    value = value + nin[2 + mask]
                norm_out_ref[...] = value
        if stage < 4:
            for copy in norm_copies[stage]:
                copy.start()

    multiply(1)
    scatter.step(0, 0)
    multiply(2)
    scatter.step(1, 0)
    multiply(3)
    scatter.step(2, 0)
    scatter.step(0, 1)
    close_tokens(0)
    scatter.step(3, 0)
    scatter.step(1, 1)
    scatter.step(0, 2)
    close_tokens(1)
    scatter.step(2, 1)
    scatter.step(1, 2)
    close_tokens(2)
    scatter.step(3, 1)
    scatter.step(0, 3)
    close_tokens(3)
    norm_step(0)
    scatter.step(2, 2)
    norm_step(1)
    scatter.step(1, 3)
    norm_step(2)
    scatter.step(3, 2)
    norm_step(3)
    scatter.step(2, 3)
    norm_step(4)
    scatter.step(3, 3)
    for i in range(CHUNKS):
        scatter.close(i)
    for copies in norm_copies:
        for copy in copies:
            copy.wait_send()


def tail(output_share, normed, low_grads, high_grads, tokens, total, norms, norm_two, norm_three, early, mesh_axes):
    (_, wide), (_, narrow) = mesh_axes
    rows, d = tokens.shape
    shard_rows = d // (wide * narrow)
    width = 4 * d // CHUNKS
    anywhere, vmem = pl.BlockSpec(memory_space=pl.ANY), pl.BlockSpec(memory_space=pltpu.VMEM)
    copies = CHUNKS * (4 + narrow) + 2 + narrow
    return pl.pallas_call(
        functools.partial(tail_kernel, narrow),
        in_specs=[anywhere] * 7 + [vmem] * 3,
        out_specs=[vmem] * 3,
        out_shape=[shape(rows, d, BF16), shape(shard_rows, 4 * d, F32), shape(8, d, F32)],
        scratch_shapes=[
            pltpu.VMEM((rows, d), BF16),
            pltpu.VMEM((d, rows), BF16),
            pltpu.VMEM((rows, 3 * d), BF16),
            pltpu.VMEM((d, 3 * d), BF16),
            pltpu.VMEM((rows, d), BF16),
            pltpu.VMEM((rows, d), F32),
            pltpu.VMEM((CHUNKS, 2, 2, 2, narrow, shard_rows, width), BF16),
            *scatter_scratch(CHUNKS, narrow, shard_rows, width),
            pltpu.VMEM((4, 8, d), F32),
            pltpu.VMEM((2 + narrow, 8, d), F32),
            pltpu.SemaphoreType.DMA((copies,)),
            pltpu.SemaphoreType.DMA((copies,)),
            pltpu.SemaphoreType.DMA((7,)),
        ],
        name="tail",
        compiler_params=pltpu.CompilerParams(collective_id=1, has_side_effects=True, vmem_limit_bytes=58 << 20),
        cost_estimate=cost(12 * rows * d * d, 100 << 20),
    )(
        output_share.reshape(2, 2, 2, narrow, shard_rows, d),
        normed,
        low_grads,
        high_grads,
        early,
        tokens,
        total,
        norms,
        norm_two,
        norm_three,
    )


def on_device(
    mesh_axes,
    tokens,
    memory,
    cotangent,
    live_length,
    pair_starts,
    source_starts,
    group_bounds,
    group_counts,
    self_query,
    self_key,
    self_value,
    self_output,
    cross_query,
    cross_key,
    cross_value,
    cross_output,
    hidden_in,
    hidden_out,
    first_gain,
    first_shift,
    second_gain,
    second_shift,
    third_gain,
    third_shift,
):
    names = tuple(axis for axis, _ in mesh_axes)
    row_count = live_length.shape[0]
    shard_rows = self_query.shape[0]
    device_count = 1
    for _, size in mesh_axes:
        device_count *= size

    def staged(*partial):
        return StagedSum(partial, mesh_axes)

    digits = jnp.stack([live_length // 256, live_length % 256], axis=1).astype(BF16)
    digits = jnp.pad(digits, ((0, shard_rows - row_count), (0, 0)))
    norms = jnp.stack([first_gain, first_shift, second_gain, second_shift, third_gain, third_shift], axis=1)
    extra = jnp.pad(jnp.concatenate([norms, digits], axis=1), ((0, 0), (0, 120)))
    early = early_gather(
        jnp.concatenate(
            [
                by_pairs(self_query, self_key, self_value),
                self_output,
                by_pairs(cross_key, cross_value),
                cross_query,
                cross_output,
                extra,
            ],
            axis=1,
        ),
        mesh_axes,
    )
    quarters = hidden_out.shape[0] // shard_rows
    late = lax.all_gather(
        jnp.concatenate(
            [hidden_in.reshape(shard_rows, device_count, quarters, -1).transpose(0, 2, 1, 3).reshape(shard_rows, -1)]
            + [hidden_out[n * shard_rows : (n + 1) * shard_rows] for n in range(quarters)],
            axis=1,
        ),
        names,
        axis=0,
        tiled=True,
    )

    norms = early[:, EXTRA * 128 : EXTRA * 128 + 8].astype(F32).T
    live_total = jnp.sum(norms[6]) * 256.0 + jnp.sum(norms[7])
    device = lax.axis_index(names)
    member = (group_bounds[:-1] <= device) & (device < group_bounds[1:])
    pair_tokens = jnp.sum(jnp.where(member, group_counts, 0))
    token_all = row_count * SEQ * device_count
    row_weight = pair_tokens.astype(F32) * (token_all / 1000.0) / live_total
    low, first, bounds = row_bounds(pair_starts, source_starts, live_length)

    normed_one, qkv = project(tokens, norms, early)
    self_mixed, self_logs = self_forward(low, first, qkv, row_count)
    after_self, normed_two, cross_q, cross_kv = middle(self_mixed, tokens, memory, norms, early)
    cross_mixed, cross_logs = cross_forward(bounds, cross_q, cross_kv, row_count)
    layer_output, normed_three, activated, hidden_grad, branch_three, cross_total, branch_two, mixed_grad, norm_three = feed(
        live_length, row_weight[None], cross_mixed, after_self, cotangent, norms, early, late
    )

    reduce_sum = staged(outer_sum(activated, branch_three))
    mixed_grad, expand_share = lax.optimization_barrier((mixed_grad, outer_sum(normed_three, hidden_grad)))
    mixed_grad = fence(mixed_grad, reduce_sum)
    expand_sum = staged(expand_share)
    cq_grad, ckv_grad = cross_backward(bounds, cross_logs, cross_q, cross_kv, cross_mixed, mixed_grad, row_count)
    cq_grad, ckv_grad = fence((cq_grad, ckv_grad), reduce_sum, expand_sum)
    shares = [outer_sum(cross_mixed, branch_two), outer_sum(normed_two, cq_grad)]
    shares += [outer_sum(memory, part) for part in (ckv_grad[:, :WIDTH], ckv_grad[:, WIDTH:])]
    cq_grad, shares = lax.optimization_barrier((cq_grad, shares))
    cross_sum = staged(*shares)
    self_total, branch_one, mixed_grad, memory_grad, norm_two = cross_close(
        cq_grad, ckv_grad, after_self, cross_total, norms, early
    )
    mixed_grad = fence(mixed_grad, reduce_sum, expand_sum, cross_sum)
    output_share = outer_sum(self_mixed, branch_one)
    low_grads = self_backward(low, first, self_logs, qkv, self_mixed, mixed_grad, row_count, 0)
    low_grads, mixed_grad = fence((low_grads, mixed_grad), reduce_sum, expand_sum)
    high_grads = self_backward(low, first, self_logs, qkv, self_mixed, mixed_grad, row_count, 1)
    high_grads = fence(high_grads, expand_sum, cross_sum)
    if mesh_axes[0][1] == 8 and row_count == 1:
        high_grads = fence(high_grads, cross_sum)
        tokens_grad, last_shard, norm_grads = tail(
            output_share, normed_one, low_grads, high_grads, tokens, self_total, norms, norm_two, norm_three, early, mesh_axes
        )
        output_shard, qkv_shard = last_shard[:, :WIDTH], last_shard[:, WIDTH:]
    else:
        qkv_grad = jnp.concatenate([low_grads, high_grads], axis=1)
        last_sum = staged(output_share, *[outer_sum(normed_one, qkv_grad[:, n * WIDTH : (n + 1) * WIDTH]) for n in range(3)])
        tokens_grad, norm_one = self_close(qkv_grad, tokens, self_total, norms, early)
        norm_grads = sum_everywhere(jnp.concatenate([norm_one[:2], norm_two[:2], norm_three[:2]]), mesh_axes)
        output_shard, *qkv_shards = last_sum.result().reshape(4, shard_rows, WIDTH)
        qkv_shard = jnp.concatenate(qkv_shards, axis=1)
    norm_shards = lax.dynamic_slice_in_dim(norm_grads, device * shard_rows, shard_rows, axis=1)
    reduce_shard = reduce_sum.result()
    expand_shard = expand_sum.result()
    expand_shard = (
        expand_shard.reshape(shard_rows, quarters, device_count, -1).transpose(0, 2, 1, 3).reshape(shard_rows, -1)
    )
    cross_shards = cross_sum.result().reshape(4, shard_rows, WIDTH)
    cross_key_shard, cross_value_shard = from_pairs(jnp.concatenate([cross_shards[2], cross_shards[3]], axis=1), 2)
    query_shard, key_shard, value_shard = from_pairs(qkv_shard, 3)
    return (
        layer_output,
        tokens_grad,
        memory_grad,
        query_shard,
        key_shard,
        value_shard,
        output_shard,
        cross_shards[1],
        cross_key_shard,
        cross_value_shard,
        cross_shards[0],
        expand_shard,
        reduce_shard,
        *[norm_shards[n] for n in range(6)],
    )


def solution(mesh):
    names = ("wide", "narrow")
    mesh_axes = tuple((axis, mesh.shape[axis]) for axis in names)
    split, vector = P(names, None), P(names)
    return jax.shard_map(
        functools.partial(on_device, mesh_axes),
        mesh=mesh,
        in_specs=(split,) * 3 + (vector,) + (split,) * 2 + (P(), P()) + (split,) * 10 + (vector,) * 6,
        out_specs=(split,) * 13 + (vector,) * 6,
        check_vma=False,
    )
```

```python
import functools
import jax
import jax.numpy as jnp
from jax import lax
from jax.experimental import pallas as pl
from jax.experimental.pallas import tpu as pltpu
from jax.sharding import PartitionSpec as P

SEQ = 1024
MEM = 512
HEADS = 16
HEAD_DIM = 64
WIDTH = HEADS * HEAD_DIM
EPSILON = 1e-05
BQ = 256
LOG2E = 1.4426950408889634
SCALE2 = HEAD_DIM**-0.5 * LOG2E
FILLER = -1e30
F32, BF16 = jnp.float32, jnp.bfloat16


def mm(a, b):
    return jnp.dot(a, b, preferred_element_type=F32)


def mm_t(a, b):
    return lax.dot_general(a, b, (((1,), (1,)), ((), ())), preferred_element_type=F32)


def halves(x):
    low = lax.broadcasted_iota(jnp.int32, x.shape, 1) < HEAD_DIM
    zero = jnp.zeros_like(x)
    return (jnp.where(low, x, zero), jnp.where(low, zero, x))


def in_turn(tasks, front, back, ahead):
    waiting = []
    for task in tasks:
        waiting.append((task, front(*task)))
        if len(waiting) > ahead:
            task, held = waiting.pop(0)
            back(*task, *held)
    for task, held in waiting:
        back(*task, *held)


BLOCKS = [slice(i * BQ, (i + 1) * BQ) for i in range(SEQ // BQ)]
TASKS = [(i, h) for i in range(SEQ // BQ) for h in range(2)]


def self_extent(i):
    return (i + 1) * BQ


def cross_extent(i):
    return MEM


def self_visible(first_ref, i):
    shape = (self_extent(i), BQ)
    key = lax.broadcasted_iota(jnp.int32, shape, 0)
    return (key >= first_ref[0, :, BLOCKS[i]]) & (key <= lax.broadcasted_iota(jnp.int32, shape, 1) + i * BQ)


def cross_visible(bounds_ref, i):
    key = lax.broadcasted_iota(jnp.int32, (MEM, BQ), 0)
    return (key >= bounds_ref[0, 0:1, BLOCKS[i]]) & (key < bounds_ref[0, 1:2, BLOCKS[i]])


def attend(q_of, k, v, visible, extent, out_ref, log_ref):
    k_parts, v_t = halves(k), v.T
    outs = {}

    def front(i, h):
        s = jnp.where(visible(i), mm_t(k_parts[h][: extent(i)], q_of(BLOCKS[i])) * SCALE2, FILLER)
        return s, jnp.max(s, axis=0, keepdims=True)

    def back(i, h, s, peak):
        p = jnp.exp2(s - peak)
        total = jnp.sum(p, axis=0, keepdims=True)
        log_ref[0, 0, h : h + 1, BLOCKS[i]] = peak + jnp.log2(total)
        outs[h] = mm(v_t[h * 64 : (h + 1) * 64, : extent(i)], p.astype(BF16)) * (1.0 / total)
        if h == 1:
            out_ref[BLOCKS[i], :] = jnp.concatenate([outs[0], outs[1]], axis=0).T.astype(BF16)

    in_turn(TASKS, front, back, 3)


def attend_back(q_of, k, v, g_ref, out_ref, log_ref, visible, extent, keep_dq, dk_ref, dv_ref):
    k_parts, k_t, v_parts = halves(k), k.T, halves(v)
    deltas, dq = {}, {}
    dk_ref[...] = jnp.zeros_like(dk_ref)
    dv_ref[...] = jnp.zeros_like(dv_ref)

    def front(i, h):
        q, g = q_of(BLOCKS[i]), g_ref[BLOCKS[i], :]
        if h == 0:
            prod = (g.astype(F32) * out_ref[BLOCKS[i], :].astype(F32)).T
            deltas[i] = [jnp.sum(prod[n * 64 : (n + 1) * 64], axis=0, keepdims=True) for n in range(2)]
        s = jnp.where(visible(i), mm_t(k_parts[h][: extent(i)], q) * SCALE2, FILLER)
        p = jnp.exp2(s - log_ref[0, 0, h : h + 1, BLOCKS[i]])
        dp = mm_t(v_parts[h][: extent(i)], g)
        return p.astype(BF16), (p * (dp - deltas[i][h])).astype(BF16)

    def back(i, h, p, ds):
        n = extent(i)
        dv_ref[:n, :] += mm(p, halves(g_ref[BLOCKS[i], :])[h])
        dk_ref[:n, :] += mm(ds, halves(q_of(BLOCKS[i]))[h])
        dq[h] = mm(k_t[h * 64 : (h + 1) * 64, :n], ds)
        if h == 1:
            keep_dq(BLOCKS[i], (jnp.concatenate([dq[0], dq[1]], axis=0) * HEAD_DIM**-0.5).T.astype(BF16))

    in_turn(TASKS, front, back, 2)


def self_forward_kernel(first_ref, qkv_ref, out_ref, log_ref):
    attend(
        lambda rows: qkv_ref[rows, 0:128],
        qkv_ref[:, 128:256],
        qkv_ref[:, 256:384],
        functools.partial(self_visible, first_ref),
        self_extent,
        out_ref,
        log_ref,
    )


def cross_forward_kernel(bounds_ref, q_ref, kv_ref, out_ref, log_ref):
    attend(
        lambda rows: q_ref[rows, :],
        kv_ref[:, 0:128],
        kv_ref[:, 128:256],
        functools.partial(cross_visible, bounds_ref),
        cross_extent,
        out_ref,
        log_ref,
    )


PAIRS = HEADS // 2
LOG_SPEC = pl.BlockSpec((1, 1, 8, SEQ), lambda r, p: (r, p, 0, 0))
ROW_SPEC = pl.BlockSpec((SEQ, 128), lambda r, p: (r, p))
QKV_SPEC = pl.BlockSpec((SEQ, 384), lambda r, p: (r, p))
KV_SPEC = pl.BlockSpec((MEM, 256), lambda r, p: (r, p))
FIRST_SPEC = pl.BlockSpec((1, 1, SEQ), lambda r, p: (r, 0, 0))
BOUNDS_SPEC = pl.BlockSpec((1, 8, SEQ), lambda r, p: (r, 0, 0))


def attention_call(kernel, name, in_specs, args, row_count):
    return pl.pallas_call(
        kernel,
        grid=(row_count, PAIRS),
        in_specs=in_specs,
        out_specs=[ROW_SPEC, LOG_SPEC],
        out_shape=[
            jax.ShapeDtypeStruct((row_count * SEQ, WIDTH), BF16),
            jax.ShapeDtypeStruct((row_count, PAIRS, 8, SEQ), F32),
        ],
        name=name,
        compiler_params=pltpu.CompilerParams(vmem_limit_bytes=40 << 20),
        cost_estimate=pl.CostEstimate(flops=20 << 30, bytes_accessed=row_count * (8 << 20), transcendentals=8 << 20),
    )(*args)


def self_forward(first, qkv, row_count):
    return attention_call(self_forward_kernel, "self_forward", [FIRST_SPEC, QKV_SPEC], (first, qkv), row_count)


def cross_forward(bounds, q, kv, row_count):
    return attention_call(
        cross_forward_kernel, "cross_forward", [BOUNDS_SPEC, ROW_SPEC, KV_SPEC], (bounds, q, kv), row_count
    )


def self_backward_kernel(first_ref, log_ref, qkv_ref, out_ref, grad_ref, dqkv_ref, dk_ref, dv_ref):
    def keep_dq(rows, value):
        dqkv_ref[rows, 0:128] = value

    attend_back(
        lambda rows: qkv_ref[rows, 0:128],
        qkv_ref[:, 128:256],
        qkv_ref[:, 256:384],
        grad_ref,
        out_ref,
        log_ref,
        functools.partial(self_visible, first_ref),
        self_extent,
        keep_dq,
        dk_ref,
        dv_ref,
    )
    dqkv_ref[:, 128:256] = (dk_ref[...] * HEAD_DIM**-0.5).astype(BF16)
    dqkv_ref[:, 256:384] = dv_ref[...].astype(BF16)


def self_backward(first, logs, qkv, out, grad, row_count):
    return pl.pallas_call(
        self_backward_kernel,
        grid=(row_count, PAIRS),
        in_specs=[FIRST_SPEC, LOG_SPEC, QKV_SPEC, ROW_SPEC, ROW_SPEC],
        out_specs=QKV_SPEC,
        scratch_shapes=[pltpu.VMEM((SEQ, 128), F32), pltpu.VMEM((SEQ, 128), F32)],
        out_shape=jax.ShapeDtypeStruct((row_count * SEQ, 3 * WIDTH), BF16),
        name="self_backward",
        compiler_params=pltpu.CompilerParams(vmem_limit_bytes=40 << 20),
        cost_estimate=pl.CostEstimate(flops=40 << 30, bytes_accessed=row_count * (16 << 20), transcendentals=8 << 20),
    )(first, logs, qkv, out, grad)


def cross_backward_pair(bounds_ref, log_ref, q_ref, kv_ref, out_ref, grad_ref, keep_dq, dkv_ref, dk_ref, dv_ref):
    attend_back(
        lambda rows: q_ref[rows, :],
        kv_ref[:, 0:128],
        kv_ref[:, 128:256],
        grad_ref,
        out_ref,
        log_ref,
        functools.partial(cross_visible, bounds_ref),
        cross_extent,
        keep_dq,
        dk_ref,
        dv_ref,
    )


def cross_backward_kernel(bounds_ref, log_ref, q_ref, kv_ref, out_ref, grad_ref, dq_ref, dkv_ref, dk_ref, dv_ref):
    def keep_dq(rows, value):
        dq_ref[rows, :] = value

    cross_backward_pair(bounds_ref, log_ref, q_ref, kv_ref, out_ref, grad_ref, keep_dq, dkv_ref, dk_ref, dv_ref)
    dkv_ref[:, 0:128] = (dk_ref[...] * HEAD_DIM**-0.5).astype(BF16)
    dkv_ref[:, 128:256] = dv_ref[...].astype(BF16)


def cross_backward(bounds, logs, q, kv, out, grad, row_count):
    return pl.pallas_call(
        cross_backward_kernel,
        grid=(row_count, PAIRS),
        in_specs=[BOUNDS_SPEC, LOG_SPEC, ROW_SPEC, KV_SPEC, ROW_SPEC, ROW_SPEC],
        out_specs=[ROW_SPEC, KV_SPEC],
        scratch_shapes=[pltpu.VMEM((MEM, 128), F32), pltpu.VMEM((MEM, 128), F32)],
        out_shape=[
            jax.ShapeDtypeStruct((row_count * SEQ, WIDTH), BF16),
            jax.ShapeDtypeStruct((row_count * MEM, 2 * WIDTH), BF16),
        ],
        name="cross_backward",
        compiler_params=pltpu.CompilerParams(vmem_limit_bytes=40 << 20),
        cost_estimate=pl.CostEstimate(flops=40 << 30, bytes_accessed=row_count * (12 << 20), transcendentals=8 << 20),
    )(bounds, logs, q, kv, out, grad)


def row_bounds(pair_starts, source_starts, live_length):
    places = jnp.arange(SEQ, dtype=jnp.int32)
    counted = jnp.sum((pair_starts[:, :, None] <= places).astype(jnp.int32), axis=1)
    live = places < live_length[:, None]
    begun = jnp.max(jnp.where(pair_starts[:, :, None] <= places, pair_starts[:, :, None], 0), axis=1)
    first = jnp.where(live, begun, live_length[:, None])
    nseg = pair_starts.shape[1]
    pick = jnp.arange(nseg)[None, :, None] == (counted - 1)[:, None, :]
    ends = jnp.concatenate([source_starts[:, 1:], jnp.full_like(source_starts[:, :1], MEM)], axis=1)
    start = jnp.sum(jnp.where(pick, source_starts[:, :, None], 0), axis=1)
    end = jnp.sum(jnp.where(pick, ends[:, :, None], 0), axis=1)
    start = jnp.where(live, start, 0)
    end = jnp.where(live, end, MEM)
    bounds = jnp.pad(jnp.stack([start, end], axis=1), ((0, 0), (0, 6), (0, 0)))
    return first[:, None, :], bounds


TB = 256


def norm_parts(values):
    center = values - jnp.mean(values, axis=-1, keepdims=True)
    inverse = lax.rsqrt(jnp.mean(center * center, axis=-1, keepdims=True) + EPSILON)
    return center * inverse, inverse


def norm_back(unit, inverse, gain, gradient):
    scaled = gradient * gain
    return inverse * (
        scaled
        - jnp.mean(scaled, axis=-1, keepdims=True)
        - unit * jnp.mean(scaled * unit, axis=-1, keepdims=True)
    )


def add_norm_grads(ref, unit, gradient):
    @pl.when(pl.program_id(0) == 0)
    def _():
        ref[...] = jnp.zeros_like(ref)

    ref[0:1, :] += jnp.sum(gradient * unit, axis=0, keepdims=True)
    ref[1:2, :] += jnp.sum(gradient, axis=0, keepdims=True)


def tile(rows, columns, at=0):
    return pl.BlockSpec((rows, columns), lambda b: (b, at))


def whole(rows, columns, at=0):
    return pl.BlockSpec((rows, columns), lambda b: (0, at), pipeline_mode=pl.Buffered(1))


def shape(rows, columns, dtype):
    return jax.ShapeDtypeStruct((rows, columns), dtype)


def params(mib):
    return pltpu.CompilerParams(vmem_limit_bytes=mib << 20)


def cost(flops, moved):
    return pl.CostEstimate(flops=int(flops), bytes_accessed=int(moved), transcendentals=0)


def project_kernel(tokens_ref, norms_ref, weight_ref, normed_ref, out_ref):
    unit, _ = norm_parts(tokens_ref[...].astype(F32))
    normed = (unit * norms_ref[0:1, :] + norms_ref[1:2, :]).astype(BF16)
    normed_ref[...] = normed
    for part in range(3):
        at = slice(part * 1024, (part + 1) * 1024)
        out_ref[:, at] = mm(normed, weight_ref[:, at]).astype(BF16)


def project(tokens, norms, early):
    rows, d = tokens.shape
    return pl.pallas_call(
        project_kernel,
        grid=(rows // TB,),
        in_specs=[tile(TB, d), whole(8, d), whole(d, 3 * d)],
        out_specs=[tile(TB, d), tile(TB, 3 * d)],
        out_shape=[shape(rows, d, BF16), shape(rows, 3 * d, BF16)],
        name="project",
        compiler_params=params(40),
        cost_estimate=cost(6 * rows * d * d, 16 << 20),
    )(tokens, norms, early)


def middle_kernel(
    mixed_ref, tokens_ref, memory_ref, norms_ref, wo_ref, wq_ref, wkv_ref, after_ref, normed_ref, q_ref, kv_ref
):
    after = tokens_ref[...].astype(F32) + mm(mixed_ref[...], wo_ref[...])
    after_ref[...] = after
    kv_ref[...] = mm(memory_ref[...], wkv_ref[...]).astype(BF16)
    unit, _ = norm_parts(after)
    normed = (unit * norms_ref[2:3, :] + norms_ref[3:4, :]).astype(BF16)
    normed_ref[...] = normed
    q_ref[...] = mm(normed, wq_ref[...]).astype(BF16)


def middle(mixed, tokens, memory, norms, early):
    rows, d = tokens.shape
    mem_rows = memory.shape[0]
    steps = rows // TB
    mb = mem_rows // steps
    return pl.pallas_call(
        middle_kernel,
        grid=(steps,),
        in_specs=[
            tile(TB, d),
            tile(TB, d),
            tile(mb, d),
            whole(8, d),
            whole(d, d, OUT_SELF),
            whole(d, d, QUERY_CROSS),
            whole(d, 2 * d, KV_CROSS),
        ],
        out_specs=[tile(TB, d), tile(TB, d), tile(TB, d), tile(mb, 2 * d)],
        out_shape=[shape(rows, d, F32), shape(rows, d, BF16), shape(rows, d, BF16), shape(mem_rows, 2 * d, BF16)],
        name="middle",
        compiler_params=params(40),
        cost_estimate=cost(6 * rows * d * d, 20 << 20),
    )(mixed, tokens, memory, norms, early, early, early)


GELU_A = 0.7978845608028654
GELU_B = 0.044715


def feed_kernel(
    live_ref,
    weight_ref,
    mixed_ref,
    before_ref,
    cot_ref,
    norms_ref,
    wo_ref,
    win_ref,
    wout_ref,
    out_ref,
    normed_ref,
    act_ref,
    hid_ref,
    b3_ref,
    total_ref,
    b2_ref,
    grad_ref,
    ngrad_ref,
):
    block = pl.program_id(0)
    per_row = SEQ // TB
    row = block // per_row
    places = lax.broadcasted_iota(jnp.int32, (TB, 1), 0) + (block % per_row) * TB
    live = (places < live_ref[row]).astype(F32)
    out_grad = cot_ref[...].astype(F32) * live * weight_ref[0]
    branch = out_grad.astype(BF16)
    b3_ref[...] = branch
    after = before_ref[...] + mm(mixed_ref[...], wo_ref[...])
    unit, inverse = norm_parts(after)
    normed = (unit * norms_ref[4:5, :] + norms_ref[5:6, :]).astype(BF16)
    normed_ref[...] = normed
    d = normed.shape[1]
    result, back = after, None
    for part in range(win_ref.shape[1] // d):
        at = slice(part * d, (part + 1) * d)
        x = mm(normed, win_ref[:, at])
        square = x * x
        t = jnp.tanh(GELU_A * x * (1.0 + GELU_B * square))
        half = 0.5 * (1.0 + t)
        act = (x * half).astype(BF16)
        slope = half + (0.5 * GELU_A) * x * (1.0 - t * t) * (1.0 + (3.0 * GELU_B) * square)
        act_ref[:, at] = act
        hid = (mm_t(branch, wout_ref[:, at]) * slope).astype(BF16)
        hid_ref[:, at] = hid
        result = result + mm(act, wout_ref[:, at])
        term = mm_t(hid, win_ref[:, at])
        back = term if back is None else back + term
    out_ref[...] = result.astype(BF16)
    total = out_grad + norm_back(unit, inverse, norms_ref[4:5, :], back)
    total_ref[...] = total
    b2 = total.astype(BF16)
    b2_ref[...] = b2
    grad_ref[...] = mm_t(b2, wo_ref[...]).astype(BF16)
    add_norm_grads(ngrad_ref, unit, back)


def feed(live_length, row_weight, mixed, before, cotangent, norms, early, late):
    rows, d = cotangent.shape
    ff = late.shape[1] // 2
    smem = pl.BlockSpec(memory_space=pltpu.SMEM)
    return pl.pallas_call(
        feed_kernel,
        grid=(rows // TB,),
        in_specs=[
            smem,
            smem,
            tile(TB, d),
            tile(TB, d),
            tile(TB, d),
            whole(8, d),
            whole(d, d, OUT_CROSS),
            whole(d, ff, 0),
            whole(d, ff, 1),
        ],
        out_specs=[
            tile(TB, d),
            tile(TB, d),
            tile(TB, ff),
            tile(TB, ff),
            tile(TB, d),
            tile(TB, d),
            tile(TB, d),
            tile(TB, d),
            whole(8, d),
        ],
        out_shape=[
            shape(rows, d, BF16),
            shape(rows, d, BF16),
            shape(rows, ff, BF16),
            shape(rows, ff, BF16),
            shape(rows, d, BF16),
            shape(rows, d, F32),
            shape(rows, d, BF16),
            shape(rows, d, BF16),
            shape(8, d, F32),
        ],
        name="feed",
        compiler_params=params(58),
        cost_estimate=cost(38 * rows * d * d, 50 << 20),
    )(live_length, row_weight, mixed, before, cotangent, norms, early, late, late)


def cross_close_kernel(
    dq_ref, dkv_ref, before_ref, total_ref, norms_ref, wq_ref, wkv_ref, wo_ref, out_ref, b1_ref, grad_ref, mem_ref, ngrad_ref
):
    gradient = mm_t(dq_ref[...], wq_ref[...])
    mem_ref[...] = mm_t(dkv_ref[...], wkv_ref[...]).astype(BF16)
    unit, inverse = norm_parts(before_ref[...])
    total = total_ref[...] + norm_back(unit, inverse, norms_ref[2:3, :], gradient)
    out_ref[...] = total
    b1 = total.astype(BF16)
    b1_ref[...] = b1
    grad_ref[...] = mm_t(b1, wo_ref[...]).astype(BF16)
    add_norm_grads(ngrad_ref, unit, gradient)


def cross_close(dq, dkv, before, total, norms, early):
    rows, d = dq.shape
    mem_rows = dkv.shape[0]
    steps = rows // TB
    mb = mem_rows // steps
    return pl.pallas_call(
        cross_close_kernel,
        grid=(steps,),
        in_specs=[
            tile(TB, d),
            tile(mb, 2 * d),
            tile(TB, d),
            tile(TB, d),
            whole(8, d),
            whole(d, d, QUERY_CROSS),
            whole(d, 2 * d, KV_CROSS),
            whole(d, d, OUT_SELF),
        ],
        out_specs=[tile(TB, d), tile(TB, d), tile(TB, d), tile(mb, d), whole(8, d)],
        out_shape=[
            shape(rows, d, F32),
            shape(rows, d, BF16),
            shape(rows, d, BF16),
            shape(mem_rows, d, BF16),
            shape(8, d, F32),
        ],
        name="cross_close",
        compiler_params=params(40),
        cost_estimate=cost(6 * rows * d * d, 24 << 20),
    )(dq, dkv, before, total, norms, early, early, early)


def self_close_kernel(dqkv_ref, before_ref, total_ref, norms_ref, w_ref, out_ref, ngrad_ref):
    gradient = mm_t(dqkv_ref[...], w_ref[...])
    unit, inverse = norm_parts(before_ref[...].astype(F32))
    total = total_ref[...] + norm_back(unit, inverse, norms_ref[0:1, :], gradient)
    out_ref[...] = total.astype(BF16)
    add_norm_grads(ngrad_ref, unit, gradient)


def self_close(dqkv, before, total, norms, early):
    rows, d = total.shape
    return pl.pallas_call(
        self_close_kernel,
        grid=(rows // TB,),
        in_specs=[tile(TB, 3 * d), tile(TB, d), tile(TB, d), whole(8, d), whole(d, 3 * d)],
        out_specs=[tile(TB, d), whole(8, d)],
        out_shape=[shape(rows, d, BF16), shape(8, d, F32)],
        name="self_close",
        compiler_params=params(40),
        cost_estimate=cost(6 * rows * d * d, 20 << 20),
    )(dqkv, before, total, norms, early)


OUT_SELF, KV_CROSS, QUERY_CROSS, OUT_CROSS, EXTRA = 3, 2, 6, 7, 64


def greet_all(narrow):
    w, z = lax.axis_index("wide"), lax.axis_index("narrow")
    barrier = pltpu.get_barrier_semaphore()
    others = [(w ^ 1, z), (w ^ 2, z), (w ^ 4, z)] + [(w, z ^ mask) for mask in range(1, narrow)]
    for other in others:
        pl.semaphore_signal(barrier, inc=1, device_id=other, device_id_type=pl.DeviceIdType.MESH)
    pl.semaphore_wait(barrier, len(others))


def early_gather_kernel(wide, narrow, shard_ref, out_ref, send_sems, recv_sems, own_sem):
    rows = shard_ref.shape[0]
    half = rows // 2
    w, z = lax.axis_index("wide"), lax.axis_index("narrow")
    core, x, y = w ^ 1, w ^ 2, w ^ 4
    up, down, to_x, to_y, on_y, on_x, to_core = [k * narrow for k in range(7)]

    def start_of(holder, s):
        return pl.multiple_of((holder * narrow + s) * rows, rows)

    def move(holder, s, number, target, first=0, count=rows, own=False):
        at = pl.multiple_of(start_of(holder, s) + first, half)
        place = out_ref.at[pl.ds(at, count)]
        return pltpu.make_async_remote_copy(
            src_ref=shard_ref.at[pl.ds(first, count)] if own else place,
            dst_ref=place,
            send_sem=send_sems.at[number],
            recv_sem=recv_sems.at[number],
            device_id=target,
            device_id_type=pl.DeviceIdType.MESH,
        )

    above, below = (w, z + 1), (w, z - 1)
    greet_all(narrow)

    keep = pltpu.make_async_copy(shard_ref, out_ref.at[pl.ds(start_of(w, z), rows)], own_sem)
    keep.start()

    def spread(s, own=False):
        move(w, s, to_x + s, (x, z), own=own).start()
        move(w, s, to_y + s, (y, z), own=own).start()
        move(w, s, to_core + s, (core, z), own=own).start()

    def relay(s):
        move(x, s, to_x + s, (x, z)).wait_recv()
        move(x, s, on_y + s, (y, z), 0, half).start()
        move(x, s, to_core + narrow + s, (core, z)).start()
        move(y, s, to_y + s, (y, z)).wait_recv()
        move(y, s, on_x + s, (x, z), half, half).start()
        move(y, s, to_core + 2 * narrow + s, (core, z)).start()

    def at_distance(r, action):
        if r == 0:
            action(z)
        else:
            pl.when(z - r >= 0)(lambda: action(z - r))
            pl.when(z + r < narrow)(lambda: action(z + r))

    pl.when(z < narrow - 1)(lambda: move(w, z, up + z, above, own=True).start())
    pl.when(z > 0)(lambda: move(w, z, down + z, below, own=True).start())
    spread(z, own=True)
    for r in range(1, narrow):

        def from_below(r=r):
            s = z - r
            move(w, s, up + s, above).wait_recv()
            pl.when(z < narrow - 1)(lambda: move(w, s, up + s, above).start())
            spread(s)

        def from_above(r=r):
            s = z + r
            move(w, s, down + s, below).wait_recv()
            pl.when(z > 0)(lambda: move(w, s, down + s, below).start())
            spread(s)

        pl.when(z - r >= 0)(from_below)
        pl.when(z + r < narrow)(from_above)
        at_distance(r - 1, relay)
    at_distance(narrow - 1, relay)

    def corner(s):
        move(x ^ 4, s, on_y + s, (y, z), 0, half).wait_recv()
        move(x ^ 4, s, on_x + s, (x, z), half, half).wait_recv()
        move(x ^ 4, s, to_core + 3 * narrow + s, (core, z)).start()

    for r in range(narrow):
        at_distance(r, corner)
    for s in range(narrow):
        for k, holder in enumerate((w, x, y, x ^ 4)):
            move(holder ^ 1, s, to_core + k * narrow + s, (core, z)).wait_recv()
    for s in range(narrow):
        pl.when((s <= z) & (z < narrow - 1))(lambda s=s: move(w, s, up + s, above).wait_send())
        pl.when((s >= z) & (z > 0))(lambda s=s: move(w, s, down + s, below).wait_send())
        move(w, s, to_x + s, (x, z)).wait_send()
        move(w, s, to_y + s, (y, z)).wait_send()
        move(x, s, on_y + s, (y, z), 0, half).wait_send()
        move(y, s, on_x + s, (x, z), half, half).wait_send()
        for k, holder in enumerate((w, x, y, x ^ 4)):
            move(holder, s, to_core + k * narrow + s, (core, z)).wait_send()
    keep.wait()


def early_gather(shard, mesh_axes):
    (_, wide), (_, narrow) = mesh_axes
    rows, columns = shard.shape
    if wide != 8 or rows % 32:
        return lax.all_gather(shard, tuple(axis for axis, _ in mesh_axes), axis=0, tiled=True)
    return pl.pallas_call(
        functools.partial(early_gather_kernel, wide, narrow),
        in_specs=[pl.BlockSpec(memory_space=pl.ANY)],
        out_specs=pl.BlockSpec(memory_space=pl.ANY),
        out_shape=jax.ShapeDtypeStruct((rows * wide * narrow, columns), BF16),
        scratch_shapes=[
            pltpu.SemaphoreType.DMA((10 * narrow,)),
            pltpu.SemaphoreType.DMA((10 * narrow,)),
            pltpu.SemaphoreType.DMA,
        ],
        name="early_gather",
        compiler_params=pltpu.CompilerParams(collective_id=0, has_side_effects=True),
        cost_estimate=pl.CostEstimate(flops=0, bytes_accessed=200 << 20, transcendentals=0),
    )(shard)


def stages_of(mesh_axes):
    plan = []
    for axis, size in mesh_axes:
        bits = size.bit_length() - 1
        at = 0
        while at < bits:
            take = 1 if (bits - at) % 2 else 2
            plan.append((axis, at, take))
            at += take
    return plan


def trade(value, axis, size, mask):
    return lax.ppermute(value, axis, [(i, i ^ mask) for i in range(size)])


def digit_of(axis, at, take):
    return (lax.axis_index(axis) >> at) & ((1 << take) - 1)


def pick(value, digit, place):
    if isinstance(value, list):
        return jnp.concatenate([pick(v, digit, place) for v in value], axis=0)
    return lax.dynamic_index_in_dim(value, digit, place, keepdims=False)


def add_up(own, pieces):
    total = own.astype(F32)
    for piece in pieces:
        total = total + piece.astype(F32)
    return total


def sum_steps(partial, mesh_axes):
    sizes = dict(mesh_axes)
    plan = stages_of(mesh_axes)
    groups = []
    for axis, _ in mesh_axes:
        groups += sorted((s for s in plan if s[0] == axis), key=lambda s: -s[1])
    devices = 1
    for _, size in mesh_axes:
        devices *= size
    columns = partial[0].shape[1]
    extents = [1 << s[2] for s in groups]
    value = [p.reshape(p.shape[0] // WIDTH, *extents, -1, columns) for p in partial]
    for number, stage in enumerate(plan):
        axis, at, take = stage
        place = 1 + groups.index(stage)
        groups.remove(stage)
        if axis == "wide" and take == 2:
            if isinstance(value, list):
                value = jnp.concatenate(value, axis=0)
            split = value.reshape(*value.shape[:place], 2, 2, *value.shape[place + 1 :])
            a, b = split[..., : columns // 2], split[..., columns // 2 :]
            low, high = digit_of(axis, at, 1), digit_of(axis, at + 1, 1)
            step = ((high, place, 2 << at), (low, place + 1, 1 << at))
            for (digit_a, place_a, mask_a), (digit_b, place_b, mask_b) in (
                step,
                ((low, place, 1 << at), (high, place, 2 << at)),
            ):
                pieces = yield [
                    trade(pick(a, digit_a ^ 1, place_a), axis, sizes[axis], mask_a),
                    trade(pick(b, digit_b ^ 1, place_b), axis, sizes[axis], mask_b),
                ]
                a = add_up(pick(a, digit_a, place_a), pieces[:1]).astype(BF16)
                b = add_up(pick(b, digit_b, place_b), pieces[1:]).astype(BF16)
            value = jnp.concatenate([a, b], axis=-1)
            continue
        digit = digit_of(axis, at, take)
        pieces = yield [
            trade(pick(value, digit ^ mask, place), axis, sizes[axis], mask << at) for mask in range(1, 1 << take)
        ]
        value = add_up(pick(value, digit, place), pieces)
        if number < len(plan) - 1:
            value = value.astype(BF16)
    return value.astype(F32).reshape(-1, columns)


class StagedSum:
    def __init__(self, partial, mesh_axes):
        self.steps = sum_steps(partial, mesh_axes)
        self.under_way = next(self.steps)
        self.value = None

    def go_on(self, pieces):
        try:
            self.under_way = self.steps.send(pieces)
        except StopIteration as stop:
            self.under_way, self.value = None, stop.value

    def result(self):
        while self.under_way is not None:
            self.go_on(self.under_way)
        return self.value


def fence(value, *sums):
    held = [s for s in sums if s.under_way is not None]
    value, arrived = lax.optimization_barrier((value, [s.under_way for s in held]))
    for s, pieces in zip(held, arrived):
        s.go_on(pieces)
    return value


def sum_everywhere(value, mesh_axes):
    sizes = dict(mesh_axes)
    for axis, at, take in stages_of(mesh_axes):
        arrived = [trade(value, axis, sizes[axis], mask << at) for mask in range(1, 1 << take)]
        for piece in arrived:
            value = value + piece
    return value


def by_pairs(*parts):
    rows = parts[0].shape[0]
    return jnp.stack([p.reshape(rows, -1, 128) for p in parts], axis=2).reshape(rows, -1)


def from_pairs(value, count):
    rows = value.shape[0]
    split = value.reshape(rows, -1, count, 128)
    return [split[:, :, c].reshape(rows, -1) for c in range(count)]


def outer_sum(left_side, gradient):
    return jnp.einsum("td,te->de", left_side, gradient, preferred_element_type=F32).astype(BF16)


CHUNKS = 4


class Scatter:
    def __init__(self, own, theirs, buffers, out_ref, send_sems, recv_sems, narrow):
        self.own, self.theirs, self.out_ref = own, theirs, out_ref
        self.from_core, self.a1, self.b1, self.a2, self.b2, self.from_line = buffers
        self.send_sems, self.recv_sems = send_sems, recv_sems
        self.narrow = narrow
        self.half = self.a1.shape[-1]
        self.w, self.z = lax.axis_index("wide"), lax.axis_index("narrow")
        self.c, self.x, self.y = self.w & 1, (self.w >> 1) & 1, (self.w >> 2) & 1
        self.per_chunk = 4 + narrow

    def move(self, i, number, src, dst, target):
        at = i * self.per_chunk + number
        return pltpu.make_async_remote_copy(
            src_ref=src,
            dst_ref=dst,
            send_sem=self.send_sems.at[at],
            recv_sem=self.recv_sems.at[at],
            device_id=target,
            device_id_type=pl.DeviceIdType.MESH,
        )

    def to_core(self, i):
        return self.move(i, 0, self.theirs(i), self.from_core.at[i], (self.w ^ 1, self.z))

    def first(self, i):
        left, right = pl.ds(0, self.half), pl.ds(self.half, self.half)
        to_x, to_y = (self.w ^ 2, self.z), (self.w ^ 4, self.z)
        return (
            self.move(i, 1, self.own.at[i, :, 1 - self.x, :, :, left], self.a1.at[i], to_x),
            self.move(i, 2, self.own.at[i, 1 - self.y, :, :, :, right], self.b1.at[i], to_y),
        )

    def second(self, i):
        left, right = pl.ds(0, self.half), pl.ds(self.half, self.half)
        to_x, to_y = (self.w ^ 2, self.z), (self.w ^ 4, self.z)
        return (
            self.move(i, 3, self.own.at[i, 1 - self.y, self.x, :, :, left], self.a2.at[i], to_y),
            self.move(i, 4, self.own.at[i, self.y, 1 - self.x, :, :, right], self.b2.at[i], to_x),
        )

    def along(self, i):
        return [
            self.move(
                i,
                4 + mask,
                self.own.at[i, self.y, self.x, self.z ^ mask],
                self.from_line.at[i, mask - 1],
                (self.w, self.z ^ mask),
            )
            for mask in range(1, self.narrow)
        ]

    def begin(self, i):
        self.to_core(i).start()

    def add(self, i, y, x, columns, piece):
        now = self.own[i, y, x, :, :, columns]
        self.own[i, y, x, :, :, columns] = (now.astype(F32) + piece.astype(F32)).astype(BF16)

    def step(self, i, stage):
        both, left, right = slice(None), slice(0, self.half), slice(self.half, None)
        if stage == 0:
            self.to_core(i).wait_recv()
            for a in range(2):
                for b in range(2):
                    self.add(i, a, b, both, self.from_core[i, a, b])
            for copy in self.first(i):
                copy.start()
        elif stage == 1:
            for copy in self.first(i):
                copy.wait_recv()
            for a in range(2):
                self.add(i, a, self.x, left, self.a1[i, a])
                self.add(i, self.y, a, right, self.b1[i, a])
            for copy in self.second(i):
                copy.start()
        elif stage == 2:
            for copy in self.second(i):
                copy.wait_recv()
            self.add(i, self.y, self.x, left, self.a2[i])
            self.add(i, self.y, self.x, right, self.b2[i])
            for copy in self.along(i):
                copy.start()
        else:
            for copy in self.along(i):
                copy.wait_recv()
            total = self.own[i, self.y, self.x, self.z].astype(F32)
            for mask in range(1, self.narrow):
                total = total + self.from_line[i, mask - 1].astype(F32)
            self.out_ref[i] = total

    def close(self, i):
        for copy in (self.to_core(i), *self.first(i), *self.second(i), *self.along(i)):
            copy.wait_send()


def scatter_scratch(chunks, narrow, rows, width):
    copies = chunks * (4 + narrow)
    return [
        pltpu.VMEM((chunks, 2, 2, narrow, rows, width), BF16),
        pltpu.VMEM((chunks, 2, 2, narrow, rows, width), BF16),
        pltpu.VMEM((chunks, 2, narrow, rows, width // 2), BF16),
        pltpu.VMEM((chunks, 2, narrow, rows, width // 2), BF16),
        pltpu.VMEM((chunks, narrow, rows, width // 2), BF16),
        pltpu.VMEM((chunks, narrow, rows, width // 2), BF16),
        pltpu.VMEM((chunks, narrow - 1, rows, width), BF16),
        pltpu.SemaphoreType.DMA((copies,)),
        pltpu.SemaphoreType.DMA((copies,)),
        pltpu.SemaphoreType.DMA((chunks,)),
    ]


class Carried:
    def __init__(self, shares, scratch, out_ref, narrow):
        own, *buffers, send_sems, recv_sems, self.load_sems = scratch
        self.shares = shares
        self.scatter = Scatter(own, lambda i: self.part(i, 1 - self.scatter.c), buffers, out_ref, send_sems, recv_sems, narrow)
        self.chunks = own.shape[0]

    def part(self, i, core):
        ref, at, width = self.shares[i]
        return ref.at[:, :, core, :, :, pl.ds(at, width)]

    def load(self, i):
        return pltpu.make_async_copy(self.part(i, self.scatter.c), self.scatter.own.at[i], self.load_sems.at[i])

    def open(self):
        for i in range(self.chunks):
            self.load(i).start()
        greet_all(self.scatter.narrow)
        for i in range(self.chunks):
            self.scatter.begin(i)

    def steps(self, plan):
        for i, stage in plan:
            if stage == 0:
                self.load(i).wait()
            self.scatter.step(i, stage)

    def close(self):
        for i in range(self.chunks):
            self.scatter.close(i)


def share_views(array, narrow, rows):
    return array.reshape(2, 2, 2, narrow, rows, array.shape[1])


CROSS_PLAN = (
    ((0, 0), (1, 0)),
    ((2, 0),),
    ((0, 1),),
    ((3, 0),),
    ((1, 1),),
    ((2, 1), (0, 2)),
    ((1, 2),),
    ((3, 1),),
    ((2, 2), (0, 3)),
    ((1, 3),),
    ((3, 2),),
    ((2, 3), (3, 3)),
)


def cross_back_kernel(
    narrow,
    bounds_ref,
    log_ref,
    q_ref,
    kv_ref,
    mixed_ref,
    grad_ref,
    before_ref,
    total_ref,
    norms_ref,
    early_any,
    share_any,
    dq_ref,
    dkv_ref,
    out_ref,
    b1_ref,
    next_ref,
    mem_ref,
    ngrad_ref,
    shard_ref,
    dk_ref,
    dv_ref,
    wq,
    wkv,
    wo,
    weight_sems,
    *scratch,
):
    step = pl.program_id(0)
    d = wq.shape[0]
    width = shard_ref.shape[-1]
    chunks = shard_ref.shape[0]
    carried = Carried([(share_any.at[i], 0, width) for i in range(chunks)], scratch, shard_ref, narrow)
    loads = [
        pltpu.make_async_copy(early_any.at[:, pl.ds(QUERY_CROSS * d, d)], wq, weight_sems.at[0]),
        pltpu.make_async_copy(early_any.at[:, pl.ds(2 * KV_CROSS * d, 2 * d)], wkv, weight_sems.at[1]),
        pltpu.make_async_copy(early_any.at[:, pl.ds(OUT_SELF * d, d)], wo, weight_sems.at[2]),
    ]

    @pl.when(step == 0)
    def _():
        carried.open()
        for load in loads:
            load.start()

    @pl.when(step < PAIRS)
    def _():
        def keep_dq(rows, value):
            dq_ref[rows, pl.ds(pl.multiple_of(step * 128, 128), 128)] = value

        cross_backward_pair(bounds_ref, log_ref, q_ref, kv_ref, mixed_ref, grad_ref, keep_dq, None, dk_ref, dv_ref)
        at = pl.multiple_of(step * 256, 256)
        dkv_ref[:, pl.ds(at, 128)] = (dk_ref[...] * HEAD_DIM**-0.5).astype(BF16)
        dkv_ref[:, pl.ds(pl.multiple_of(at + 128, 128), 128)] = dv_ref[...].astype(BF16)

    @pl.when(step == PAIRS)
    def _():
        for load in loads:
            load.wait()
        ngrad_ref[...] = jnp.zeros_like(ngrad_ref)

    @pl.when(step >= PAIRS)
    def _():
        t = step - PAIRS
        mb = mem_ref.shape[0]
        gradient = mm_t(dq_ref[pl.ds(pl.multiple_of(t * TB, TB), TB), :], wq[...])
        mem_ref[...] = mm_t(dkv_ref[pl.ds(pl.multiple_of(t * mb, mb), mb), :], wkv[...]).astype(BF16)
        unit, inverse = norm_parts(before_ref[...])
        total = total_ref[...] + norm_back(unit, inverse, norms_ref[2:3, :], gradient)
        out_ref[...] = total
        b1 = total.astype(BF16)
        b1_ref[...] = b1
        next_ref[...] = mm_t(b1, wo[...]).astype(BF16)
        ngrad_ref[0:1, :] += jnp.sum(gradient * unit, axis=0, keepdims=True)
        ngrad_ref[1:2, :] += jnp.sum(gradient, axis=0, keepdims=True)

    for number, plan in enumerate(CROSS_PLAN):
        pl.when(step == number)(functools.partial(carried.steps, plan))
    pl.when(step == len(CROSS_PLAN) - 1)(carried.close)


def cross_back(bounds, logs, q, kv, mixed, grad, before, total, norms, early, share, narrow):
    rows, d = q.shape
    mem_rows = kv.shape[0]
    chunks = share.shape[0] // d
    shard_rows = d // (8 * narrow)
    steps = rows // TB
    mb = mem_rows // steps

    def pair(s):
        return jnp.minimum(s, PAIRS - 1)

    def token(s):
        return jnp.maximum(s - PAIRS, 0)

    anywhere = pl.BlockSpec(memory_space=pl.ANY)
    by_pair = pl.BlockSpec((SEQ, 128), lambda s: (0, pair(s)))
    by_token = pl.BlockSpec((TB, d), lambda s: (token(s), 0))
    return pl.pallas_call(
        functools.partial(cross_back_kernel, narrow),
        grid=(PAIRS + steps,),
        in_specs=[
            pl.BlockSpec((1, 8, SEQ), lambda s: (0, 0, 0)),
            pl.BlockSpec((1, 1, 8, SEQ), lambda s: (0, pair(s), 0, 0)),
            by_pair,
            pl.BlockSpec((MEM, 256), lambda s: (0, pair(s))),
            by_pair,
            by_pair,
            by_token,
            by_token,
            whole(8, d),
            anywhere,
            anywhere,
        ],
        out_specs=[
            whole(rows, d),
            whole(mem_rows, 2 * d),
            by_token,
            by_token,
            by_token,
            pl.BlockSpec((mb, d), lambda s: (token(s), 0)),
            whole(8, d),
            pl.BlockSpec((chunks, shard_rows, d), lambda s: (0, 0, 0), pipeline_mode=pl.Buffered(1)),
        ],
        out_shape=[
            shape(rows, d, BF16),
            shape(mem_rows, 2 * d, BF16),
            shape(rows, d, F32),
            shape(rows, d, BF16),
            shape(rows, d, BF16),
            shape(mem_rows, d, BF16),
            shape(8, d, F32),
            jax.ShapeDtypeStruct((chunks, shard_rows, d), F32),
        ],
        scratch_shapes=[
            pltpu.VMEM((MEM, 128), F32),
            pltpu.VMEM((MEM, 128), F32),
            pltpu.VMEM((d, d), BF16),
            pltpu.VMEM((d, 2 * d), BF16),
            pltpu.VMEM((d, d), BF16),
            pltpu.SemaphoreType.DMA((3,)),
            *scatter_scratch(chunks, narrow, shard_rows, d),
        ],
        name="cross_back",
        compiler_params=pltpu.CompilerParams(collective_id=2, has_side_effects=True, vmem_limit_bytes=58 << 20),
        cost_estimate=cost(40 * rows * d * d, 100 << 20),
    )(
        bounds,
        logs,
        q,
        kv,
        mixed,
        grad,
        before,
        total,
        norms,
        early,
        share.reshape(chunks, 2, 2, 2, narrow, shard_rows, d),
    )


SELF_PLAN = (
    ((0, 0), (1, 0)),
    ((2, 0),),
    ((0, 1),),
    ((3, 0), (1, 1)),
    ((4, 0),),
    ((2, 1), (0, 2)),
    ((5, 0), (1, 2)),
    (
        ((3, 1), (2, 2), (6, 0), (0, 3), (4, 1), (3, 2), (1, 3), (7, 0), (5, 1), (4, 2), (2, 3))
        + ((6, 1), (5, 2), (3, 3), (7, 1), (6, 2), (4, 3), (7, 2), (5, 3), (6, 3), (7, 3))
    ),
)


def self_back_kernel(
    narrow,
    first_ref,
    log_ref,
    qkv_ref,
    mixed_ref,
    grad_ref,
    wide_any,
    a_any,
    b_any,
    c_any,
    d_any,
    dqkv_ref,
    shard_ref,
    dk_ref,
    dv_ref,
    *scratch,
):
    step = pl.program_id(0)
    width = shard_ref.shape[-1]
    shares = [(wide_any, i * width, width) for i in range(4)]
    shares += [(ref, 0, width) for ref in (a_any, b_any, c_any, d_any)]
    carried = Carried(shares, scratch, shard_ref, narrow)
    pl.when(step == 0)(carried.open)
    self_backward_kernel(first_ref, log_ref, qkv_ref, mixed_ref, grad_ref, dqkv_ref, dk_ref, dv_ref)
    for number, plan in enumerate(SELF_PLAN):
        pl.when(step == number)(functools.partial(carried.steps, plan))
    pl.when(step == len(SELF_PLAN) - 1)(carried.close)


def self_back(first, logs, qkv, mixed, grad, wide_share, shares, narrow):
    rows, d = mixed.shape
    shard_rows = d // (8 * narrow)
    anywhere = pl.BlockSpec(memory_space=pl.ANY)
    by_pair = pl.BlockSpec((SEQ, 128), lambda s: (0, s))
    qkv_pair = pl.BlockSpec((SEQ, 384), lambda s: (0, s))
    return pl.pallas_call(
        functools.partial(self_back_kernel, narrow),
        grid=(PAIRS,),
        in_specs=[
            pl.BlockSpec((1, 1, SEQ), lambda s: (0, 0, 0)),
            pl.BlockSpec((1, 1, 8, SEQ), lambda s: (0, s, 0, 0)),
            qkv_pair,
            by_pair,
            by_pair,
            *[anywhere] * 5,
        ],
        out_specs=[qkv_pair, pl.BlockSpec((8, shard_rows, d), lambda s: (0, 0, 0), pipeline_mode=pl.Buffered(1))],
        out_shape=[shape(rows, 3 * d, BF16), jax.ShapeDtypeStruct((8, shard_rows, d), F32)],
        scratch_shapes=[
            pltpu.VMEM((SEQ, 128), F32),
            pltpu.VMEM((SEQ, 128), F32),
            *scatter_scratch(8, narrow, shard_rows, d),
        ],
        name="self_back",
        compiler_params=pltpu.CompilerParams(collective_id=3, has_side_effects=True, vmem_limit_bytes=58 << 20),
        cost_estimate=cost(40 * rows * d * d, 100 << 20),
    )(
        first,
        logs,
        qkv,
        mixed,
        grad,
        share_views(wide_share, narrow, shard_rows),
        *[share_views(s, narrow, shard_rows) for s in shares],
    )


def tail_kernel(
    narrow,
    share_any,
    normed_any,
    grads_any,
    weight_any,
    tokens_any,
    total_any,
    norms_ref,
    norm_two_ref,
    norm_three_ref,
    out_ref,
    shard_ref,
    norm_out_ref,
    normed,
    normed_t,
    grads,
    weight,
    tokens,
    total,
    share,
    from_core,
    a1,
    b1,
    a2,
    b2,
    from_line,
    send_sems,
    recv_sems,
    nval,
    nin,
    norm_send_sems,
    norm_recv_sems,
    load_sems,
):
    d = normed.shape[1]
    width = share.shape[-1]
    loads = [
        pltpu.make_async_copy(share_any, share.at[0], load_sems.at[0]),
        pltpu.make_async_copy(normed_any, normed, load_sems.at[1]),
        *[
            pltpu.make_async_copy(
                grads_any.at[:, pl.ds(i * width, width)], grads.at[:, pl.ds(i * width, width)], load_sems.at[2 + i]
            )
            for i in range(3)
        ],
        pltpu.make_async_copy(weight_any.at[:, pl.ds(0, 3 * d)], weight, load_sems.at[5]),
        pltpu.make_async_copy(tokens_any, tokens, load_sems.at[6]),
        pltpu.make_async_copy(total_any, total, load_sems.at[7]),
    ]
    for load in loads:
        load.start()
    greet_all(narrow)
    w, z = lax.axis_index("wide"), lax.axis_index("narrow")
    scatter = Scatter(
        share.at[:, :, :, w & 1],
        lambda i: share.at[i, :, :, 1 - (w & 1)],
        (from_core, a1, b1, a2, b2, from_line),
        shard_ref,
        send_sems,
        recv_sems,
        narrow,
    )
    rows = share.shape[5]
    group = 2 * narrow * rows

    loads[0].wait()
    scatter.begin(0)
    loads[1].wait()
    for t in range(d // TB):
        normed_t[:, t * TB : (t + 1) * TB] = normed[t * TB : (t + 1) * TB, :].T

    def multiply(i):
        loads[1 + i].wait()
        for a in range(2):
            for b in range(2):
                at = (2 * a + b) * group
                product = mm(normed_t[at : at + group, :], grads[:, (i - 1) * width : i * width])
                share[i, a, b] = product.astype(BF16).reshape(2, narrow, rows, width)
        scatter.begin(i)

    def close_tokens(t):
        if t == 0:
            for load in loads[5:]:
                load.wait()
        at = slice(t * TB, (t + 1) * TB)
        gradient = mm_t(grads[at, :], weight[...])
        unit, inverse = norm_parts(tokens[at, :].astype(F32))
        out_ref[at, :] = (total[at, :] + norm_back(unit, inverse, norms_ref[0:1, :], gradient)).astype(BF16)
        gain, shift = jnp.sum(gradient * unit, axis=0, keepdims=True), jnp.sum(gradient, axis=0, keepdims=True)
        if t == 0:
            nval[0, 0:1, :] = gain
            nval[0, 1:2, :] = shift
        else:
            nval[0, 0:1, :] += gain
            nval[0, 1:2, :] += shift

    def norm_copy(stage, number, target):
        return pltpu.make_async_remote_copy(
            src_ref=nval.at[stage],
            dst_ref=nin.at[number],
            send_sem=norm_send_sems.at[number],
            recv_sem=norm_recv_sems.at[number],
            device_id=target,
            device_id_type=pl.DeviceIdType.MESH,
        )

    norm_copies = [[norm_copy(0, 0, (w ^ 1, z))], [norm_copy(1, 1, (w ^ 2, z))], [norm_copy(2, 2, (w ^ 4, z))]]
    norm_copies.append([norm_copy(3, 2 + mask, (w, z ^ mask)) for mask in range(1, narrow)])

    def norm_step(stage):
        if stage == 0:
            nval[0, 2:4, :] = norm_two_ref[0:2, :]
            nval[0, 4:6, :] = norm_three_ref[0:2, :]
            nval[0, 6:8, :] = jnp.zeros_like(norm_two_ref[0:2, :])
        else:
            for copy in norm_copies[stage - 1]:
                copy.wait_recv()
            value = nval[stage - 1]
            if stage < 4:
                nval[stage] = value + nin[stage - 1]
            else:
                for mask in range(1, narrow):
                    value = value + nin[2 + mask]
                norm_out_ref[...] = value
        if stage < 4:
            for copy in norm_copies[stage]:
                copy.start()

    multiply(1)
    scatter.step(0, 0)
    multiply(2)
    scatter.step(1, 0)
    multiply(3)
    scatter.step(2, 0)
    scatter.step(0, 1)
    close_tokens(0)
    scatter.step(3, 0)
    scatter.step(1, 1)
    scatter.step(0, 2)
    close_tokens(1)
    scatter.step(2, 1)
    scatter.step(1, 2)
    close_tokens(2)
    scatter.step(3, 1)
    scatter.step(0, 3)
    close_tokens(3)
    norm_step(0)
    scatter.step(2, 2)
    norm_step(1)
    scatter.step(1, 3)
    norm_step(2)
    scatter.step(3, 2)
    norm_step(3)
    scatter.step(2, 3)
    norm_step(4)
    scatter.step(3, 3)
    for i in range(CHUNKS):
        scatter.close(i)
    for copies in norm_copies:
        for copy in copies:
            copy.wait_send()


def tail(output_share, normed, grads, tokens, total, norms, norm_two, norm_three, early, mesh_axes):
    (_, wide), (_, narrow) = mesh_axes
    rows, d = tokens.shape
    shard_rows = d // (wide * narrow)
    width = 4 * d // CHUNKS
    anywhere, vmem = pl.BlockSpec(memory_space=pl.ANY), pl.BlockSpec(memory_space=pltpu.VMEM)
    return pl.pallas_call(
        functools.partial(tail_kernel, narrow),
        in_specs=[anywhere] * 6 + [vmem] * 3,
        out_specs=[vmem] * 3,
        out_shape=[shape(rows, d, BF16), jax.ShapeDtypeStruct((CHUNKS, shard_rows, d), F32), shape(8, d, F32)],
        scratch_shapes=[
            pltpu.VMEM((rows, d), BF16),
            pltpu.VMEM((d, rows), BF16),
            pltpu.VMEM((rows, 3 * d), BF16),
            pltpu.VMEM((d, 3 * d), BF16),
            pltpu.VMEM((rows, d), BF16),
            pltpu.VMEM((rows, d), F32),
            pltpu.VMEM((CHUNKS, 2, 2, 2, narrow, shard_rows, width), BF16),
            *scatter_scratch(CHUNKS, narrow, shard_rows, width)[1:-1],
            pltpu.VMEM((4, 8, d), F32),
            pltpu.VMEM((2 + narrow, 8, d), F32),
            pltpu.SemaphoreType.DMA((2 + narrow,)),
            pltpu.SemaphoreType.DMA((2 + narrow,)),
            pltpu.SemaphoreType.DMA((8,)),
        ],
        name="tail",
        compiler_params=pltpu.CompilerParams(collective_id=1, has_side_effects=True, vmem_limit_bytes=58 << 20),
        cost_estimate=cost(12 * rows * d * d, 100 << 20),
    )(
        output_share.reshape(2, 2, 2, narrow, shard_rows, d),
        normed,
        grads,
        early,
        tokens,
        total,
        norms,
        norm_two,
        norm_three,
    )


def on_device(
    mesh_axes,
    tokens,
    memory,
    cotangent,
    live_length,
    pair_starts,
    source_starts,
    group_bounds,
    group_counts,
    self_query,
    self_key,
    self_value,
    self_output,
    cross_query,
    cross_key,
    cross_value,
    cross_output,
    hidden_in,
    hidden_out,
    first_gain,
    first_shift,
    second_gain,
    second_shift,
    third_gain,
    third_shift,
):
    names = tuple(axis for axis, _ in mesh_axes)
    row_count = live_length.shape[0]
    shard_rows = self_query.shape[0]
    device_count = 1
    for _, size in mesh_axes:
        device_count *= size

    def staged(*partial):
        return StagedSum(partial, mesh_axes)

    digits = jnp.stack([live_length // 256, live_length % 256], axis=1).astype(BF16)
    digits = jnp.pad(digits, ((0, shard_rows - row_count), (0, 0)))
    norms = jnp.stack([first_gain, first_shift, second_gain, second_shift, third_gain, third_shift], axis=1)
    extra = jnp.pad(jnp.concatenate([norms, digits], axis=1), ((0, 0), (0, 120)))
    early = early_gather(
        jnp.concatenate(
            [
                by_pairs(self_query, self_key, self_value),
                self_output,
                by_pairs(cross_key, cross_value),
                cross_query,
                cross_output,
                extra,
            ],
            axis=1,
        ),
        mesh_axes,
    )
    quarters = hidden_out.shape[0] // shard_rows
    late = lax.all_gather(
        jnp.concatenate(
            [hidden_in.reshape(shard_rows, device_count, quarters, -1).transpose(0, 2, 1, 3).reshape(shard_rows, -1)]
            + [hidden_out[n * shard_rows : (n + 1) * shard_rows] for n in range(quarters)],
            axis=1,
        ),
        names,
        axis=0,
        tiled=True,
    )

    norms = early[:, EXTRA * 128 : EXTRA * 128 + 8].astype(F32).T
    live_total = jnp.sum(norms[6]) * 256.0 + jnp.sum(norms[7])
    device = lax.axis_index(names)
    member = (group_bounds[:-1] <= device) & (device < group_bounds[1:])
    pair_tokens = jnp.sum(jnp.where(member, group_counts, 0))
    token_all = row_count * SEQ * device_count
    row_weight = pair_tokens.astype(F32) * (token_all / 1000.0) / live_total
    first, bounds = row_bounds(pair_starts, source_starts, live_length)

    normed_one, qkv = project(tokens, norms, early)
    self_mixed, self_logs = self_forward(first, qkv, row_count)
    after_self, normed_two, cross_q, cross_kv = middle(self_mixed, tokens, memory, norms, early)
    cross_mixed, cross_logs = cross_forward(bounds, cross_q, cross_kv, row_count)
    layer_output, normed_three, activated, hidden_grad, branch_three, cross_total, branch_two, mixed_grad, norm_three = feed(
        live_length, row_weight[None], cross_mixed, after_self, cotangent, norms, early, late
    )

    reduce_share, expand_share = outer_sum(activated, branch_three), outer_sum(normed_three, hidden_grad)
    if mesh_axes[0][1] == 8 and row_count == 1 and quarters == 4 and shard_rows % 32 == 0:
        narrow = mesh_axes[1][1]
        cq_grad, ckv_grad, self_total, branch_one, mixed_grad, memory_grad, norm_two, reduce_shard = cross_back(
            bounds, cross_logs, cross_q, cross_kv, cross_mixed, mixed_grad, after_self, cross_total, norms, early, reduce_share, narrow
        )
        cross_shares = [outer_sum(cross_mixed, branch_two), outer_sum(normed_two, cq_grad)]
        cross_shares += [outer_sum(memory, part) for part in (ckv_grad[:, :WIDTH], ckv_grad[:, WIDTH:])]
        qkv_grad, shards = self_back(first, self_logs, qkv, self_mixed, mixed_grad, expand_share, cross_shares, narrow)
        expand_shards, cross_shards = shards[:4], shards[4:]
        tokens_grad, last_shards, norm_grads = tail(
            outer_sum(self_mixed, branch_one),
            normed_one,
            qkv_grad,
            tokens,
            self_total,
            norms,
            norm_two,
            norm_three,
            early,
            mesh_axes,
        )
    else:
        reduce_sum, expand_sum = staged(reduce_share), staged(expand_share)
        cq_grad, ckv_grad = cross_backward(bounds, cross_logs, cross_q, cross_kv, cross_mixed, mixed_grad, row_count)
        cq_grad, ckv_grad = fence((cq_grad, ckv_grad), reduce_sum, expand_sum)
        cross_shares = [outer_sum(cross_mixed, branch_two), outer_sum(normed_two, cq_grad)]
        cross_shares += [outer_sum(memory, part) for part in (ckv_grad[:, :WIDTH], ckv_grad[:, WIDTH:])]
        cross_sum = staged(*cross_shares)
        self_total, branch_one, mixed_grad, memory_grad, norm_two = cross_close(
            cq_grad, ckv_grad, after_self, cross_total, norms, early
        )
        mixed_grad = fence(mixed_grad, reduce_sum, expand_sum, cross_sum)
        qkv_grad = self_backward(first, self_logs, qkv, self_mixed, mixed_grad, row_count)
        qkv_grad = fence(qkv_grad, reduce_sum, expand_sum, cross_sum)
        last_sum = staged(
            outer_sum(self_mixed, branch_one),
            *[outer_sum(normed_one, qkv_grad[:, n * WIDTH : (n + 1) * WIDTH]) for n in range(3)],
        )
        tokens_grad, norm_one = self_close(qkv_grad, tokens, self_total, norms, early)
        norm_grads = sum_everywhere(jnp.concatenate([norm_one[:2], norm_two[:2], norm_three[:2]]), mesh_axes)
        last_shards = last_sum.result().reshape(4, shard_rows, WIDTH)
        reduce_shard = reduce_sum.result()
        expand_shards = expand_sum.result().reshape(shard_rows, 4, -1).transpose(1, 0, 2)
        cross_shards = cross_sum.result().reshape(4, shard_rows, WIDTH)

    norm_shards = lax.dynamic_slice_in_dim(norm_grads, device * shard_rows, shard_rows, axis=1)
    reduce_shard = reduce_shard.reshape(-1, WIDTH)
    expand_shard = (
        expand_shards.reshape(quarters, shard_rows, device_count, -1).transpose(1, 2, 0, 3).reshape(shard_rows, -1)
    )
    output_shard = last_shards[0]
    query_shard, key_shard, value_shard = from_pairs(jnp.concatenate(list(last_shards[1:]), axis=1), 3)
    cross_key_shard, cross_value_shard = from_pairs(jnp.concatenate([cross_shards[2], cross_shards[3]], axis=1), 2)
    return (
        layer_output,
        tokens_grad,
        memory_grad,
        query_shard,
        key_shard,
        value_shard,
        output_shard,
        cross_shards[1],
        cross_key_shard,
        cross_value_shard,
        cross_shards[0],
        expand_shard,
        reduce_shard,
        *[norm_shards[n] for n in range(6)],
    )


def solution(mesh):
    names = ("wide", "narrow")
    mesh_axes = tuple((axis, mesh.shape[axis]) for axis in names)
    split, vector = P(names, None), P(names)
    return jax.shard_map(
        functools.partial(on_device, mesh_axes),
        mesh=mesh,
        in_specs=(split,) * 3 + (vector,) + (split,) * 2 + (P(), P()) + (split,) * 10 + (vector,) * 6,
        out_specs=(split,) * 13 + (vector,) * 6,
        check_vma=False,
    )
```

```python
import functools
import jax
import jax.numpy as jnp
from jax import lax
from jax.experimental import pallas as pl
from jax.experimental.pallas import tpu as pltpu
from jax.sharding import PartitionSpec as P

SEQ = 1024
MEM = 512
HEADS = 16
HEAD_DIM = 64
WIDTH = HEADS * HEAD_DIM
EPSILON = 1e-05
BQ = 256
LOG2E = 1.4426950408889634
SCALE2 = HEAD_DIM**-0.5 * LOG2E
FILLER = -1e30
F32, BF16 = jnp.float32, jnp.bfloat16


def mm(a, b):
    return jnp.dot(a, b, preferred_element_type=F32)


def mm_t(a, b):
    return lax.dot_general(a, b, (((1,), (1,)), ((), ())), preferred_element_type=F32)


def halves(x):
    low = lax.broadcasted_iota(jnp.int32, x.shape, 1) < HEAD_DIM
    zero = jnp.zeros_like(x)
    return (jnp.where(low, x, zero), jnp.where(low, zero, x))


def in_turn(tasks, front, back, ahead):
    waiting = []
    for task in tasks:
        waiting.append((task, front(*task)))
        if len(waiting) > ahead:
            task, held = waiting.pop(0)
            back(*task, *held)
    for task, held in waiting:
        back(*task, *held)


BLOCKS = [slice(i * BQ, (i + 1) * BQ) for i in range(SEQ // BQ)]
TASKS = [(i, h) for i in range(SEQ // BQ) for h in range(2)]


def self_extent(i):
    return (i + 1) * BQ


def cross_extent(i):
    return MEM


def self_visible(first_ref, i):
    shape = (self_extent(i), BQ)
    key = lax.broadcasted_iota(jnp.int32, shape, 0)
    return (key >= first_ref[0, :, BLOCKS[i]]) & (key <= lax.broadcasted_iota(jnp.int32, shape, 1) + i * BQ)


def cross_visible(bounds_ref, i):
    key = lax.broadcasted_iota(jnp.int32, (MEM, BQ), 0)
    return (key >= bounds_ref[0, 0:1, BLOCKS[i]]) & (key < bounds_ref[0, 1:2, BLOCKS[i]])


def attend(q_of, k, v, visible, extent, out_ref, log_ref):
    k_parts, v_t = halves(k), v.T
    outs = {}

    def front(i, h):
        s = jnp.where(visible(i), mm_t(k_parts[h][: extent(i)], q_of(BLOCKS[i])) * SCALE2, FILLER)
        return s, jnp.max(s, axis=0, keepdims=True)

    def back(i, h, s, peak):
        p = jnp.exp2(s - peak)
        total = jnp.sum(p, axis=0, keepdims=True)
        log_ref[0, 0, h : h + 1, BLOCKS[i]] = peak + jnp.log2(total)
        outs[h] = mm(v_t[h * 64 : (h + 1) * 64, : extent(i)], p.astype(BF16)) * (1.0 / total)
        if h == 1:
            out_ref[BLOCKS[i], :] = jnp.concatenate([outs[0], outs[1]], axis=0).T.astype(BF16)

    in_turn(TASKS, front, back, 3)


def attend_back(q_of, k, v, g_ref, out_ref, log_ref, visible, extent, keep_dq, dk_ref, dv_ref):
    k_parts, k_t, v_parts = halves(k), k.T, halves(v)
    deltas, dq = {}, {}
    dk_ref[...] = jnp.zeros_like(dk_ref)
    dv_ref[...] = jnp.zeros_like(dv_ref)

    def front(i, h):
        q, g = q_of(BLOCKS[i]), g_ref[BLOCKS[i], :]
        if h == 0:
            prod = (g.astype(F32) * out_ref[BLOCKS[i], :].astype(F32)).T
            deltas[i] = [jnp.sum(prod[n * 64 : (n + 1) * 64], axis=0, keepdims=True) for n in range(2)]
        s = jnp.where(visible(i), mm_t(k_parts[h][: extent(i)], q) * SCALE2, FILLER)
        p = jnp.exp2(s - log_ref[0, 0, h : h + 1, BLOCKS[i]])
        dp = mm_t(v_parts[h][: extent(i)], g)
        return p.astype(BF16), (p * (dp - deltas[i][h])).astype(BF16)

    def back(i, h, p, ds):
        n = extent(i)
        dv_ref[:n, :] += mm(p, halves(g_ref[BLOCKS[i], :])[h])
        dk_ref[:n, :] += mm(ds, halves(q_of(BLOCKS[i]))[h])
        dq[h] = mm(k_t[h * 64 : (h + 1) * 64, :n], ds)
        if h == 1:
            keep_dq(BLOCKS[i], (jnp.concatenate([dq[0], dq[1]], axis=0) * HEAD_DIM**-0.5).T.astype(BF16))

    in_turn(TASKS, front, back, 2)


def self_forward_kernel(first_ref, qkv_ref, out_ref, log_ref):
    attend(
        lambda rows: qkv_ref[rows, 0:128],
        qkv_ref[:, 128:256],
        qkv_ref[:, 256:384],
        functools.partial(self_visible, first_ref),
        self_extent,
        out_ref,
        log_ref,
    )


def cross_forward_kernel(bounds_ref, q_ref, kv_ref, out_ref, log_ref):
    attend(
        lambda rows: q_ref[rows, :],
        kv_ref[:, 0:128],
        kv_ref[:, 128:256],
        functools.partial(cross_visible, bounds_ref),
        cross_extent,
        out_ref,
        log_ref,
    )


PAIRS = HEADS // 2
LOG_SPEC = pl.BlockSpec((1, 1, 8, SEQ), lambda r, p: (r, p, 0, 0))
ROW_SPEC = pl.BlockSpec((SEQ, 128), lambda r, p: (r, p))
QKV_SPEC = pl.BlockSpec((SEQ, 384), lambda r, p: (r, p))
KV_SPEC = pl.BlockSpec((MEM, 256), lambda r, p: (r, p))
FIRST_SPEC = pl.BlockSpec((1, 1, SEQ), lambda r, p: (r, 0, 0))
BOUNDS_SPEC = pl.BlockSpec((1, 8, SEQ), lambda r, p: (r, 0, 0))


def attention_call(kernel, name, in_specs, args, row_count):
    return pl.pallas_call(
        kernel,
        grid=(row_count, PAIRS),
        in_specs=in_specs,
        out_specs=[ROW_SPEC, LOG_SPEC],
        out_shape=[
            jax.ShapeDtypeStruct((row_count * SEQ, WIDTH), BF16),
            jax.ShapeDtypeStruct((row_count, PAIRS, 8, SEQ), F32),
        ],
        name=name,
        compiler_params=pltpu.CompilerParams(vmem_limit_bytes=40 << 20),
        cost_estimate=pl.CostEstimate(flops=20 << 30, bytes_accessed=row_count * (8 << 20), transcendentals=8 << 20),
    )(*args)


def self_forward(first, qkv, row_count):
    return attention_call(self_forward_kernel, "self_forward", [FIRST_SPEC, QKV_SPEC], (first, qkv), row_count)


def cross_forward(bounds, q, kv, row_count):
    return attention_call(
        cross_forward_kernel, "cross_forward", [BOUNDS_SPEC, ROW_SPEC, KV_SPEC], (bounds, q, kv), row_count
    )


def self_backward_kernel(first_ref, log_ref, qkv_ref, out_ref, grad_ref, dqkv_ref, dk_ref, dv_ref):
    def keep_dq(rows, value):
        dqkv_ref[rows, 0:128] = value

    attend_back(
        lambda rows: qkv_ref[rows, 0:128],
        qkv_ref[:, 128:256],
        qkv_ref[:, 256:384],
        grad_ref,
        out_ref,
        log_ref,
        functools.partial(self_visible, first_ref),
        self_extent,
        keep_dq,
        dk_ref,
        dv_ref,
    )
    dqkv_ref[:, 128:256] = (dk_ref[...] * HEAD_DIM**-0.5).astype(BF16)
    dqkv_ref[:, 256:384] = dv_ref[...].astype(BF16)


def self_backward(first, logs, qkv, out, grad, row_count):
    return pl.pallas_call(
        self_backward_kernel,
        grid=(row_count, PAIRS),
        in_specs=[FIRST_SPEC, LOG_SPEC, QKV_SPEC, ROW_SPEC, ROW_SPEC],
        out_specs=QKV_SPEC,
        scratch_shapes=[pltpu.VMEM((SEQ, 128), F32), pltpu.VMEM((SEQ, 128), F32)],
        out_shape=jax.ShapeDtypeStruct((row_count * SEQ, 3 * WIDTH), BF16),
        name="self_backward",
        compiler_params=pltpu.CompilerParams(vmem_limit_bytes=40 << 20),
        cost_estimate=pl.CostEstimate(flops=40 << 30, bytes_accessed=row_count * (16 << 20), transcendentals=8 << 20),
    )(first, logs, qkv, out, grad)


def cross_backward_pair(bounds_ref, log_ref, q_ref, kv_ref, out_ref, grad_ref, keep_dq, dkv_ref, dk_ref, dv_ref):
    attend_back(
        lambda rows: q_ref[rows, :],
        kv_ref[:, 0:128],
        kv_ref[:, 128:256],
        grad_ref,
        out_ref,
        log_ref,
        functools.partial(cross_visible, bounds_ref),
        cross_extent,
        keep_dq,
        dk_ref,
        dv_ref,
    )


def cross_backward_kernel(bounds_ref, log_ref, q_ref, kv_ref, out_ref, grad_ref, dq_ref, dkv_ref, dk_ref, dv_ref):
    def keep_dq(rows, value):
        dq_ref[rows, :] = value

    cross_backward_pair(bounds_ref, log_ref, q_ref, kv_ref, out_ref, grad_ref, keep_dq, dkv_ref, dk_ref, dv_ref)
    dkv_ref[:, 0:128] = (dk_ref[...] * HEAD_DIM**-0.5).astype(BF16)
    dkv_ref[:, 128:256] = dv_ref[...].astype(BF16)


def cross_backward(bounds, logs, q, kv, out, grad, row_count):
    return pl.pallas_call(
        cross_backward_kernel,
        grid=(row_count, PAIRS),
        in_specs=[BOUNDS_SPEC, LOG_SPEC, ROW_SPEC, KV_SPEC, ROW_SPEC, ROW_SPEC],
        out_specs=[ROW_SPEC, KV_SPEC],
        scratch_shapes=[pltpu.VMEM((MEM, 128), F32), pltpu.VMEM((MEM, 128), F32)],
        out_shape=[
            jax.ShapeDtypeStruct((row_count * SEQ, WIDTH), BF16),
            jax.ShapeDtypeStruct((row_count * MEM, 2 * WIDTH), BF16),
        ],
        name="cross_backward",
        compiler_params=pltpu.CompilerParams(vmem_limit_bytes=40 << 20),
        cost_estimate=pl.CostEstimate(flops=40 << 30, bytes_accessed=row_count * (12 << 20), transcendentals=8 << 20),
    )(bounds, logs, q, kv, out, grad)


def row_bounds(pair_starts, source_starts, live_length):
    places = jnp.arange(SEQ, dtype=jnp.int32)
    counted = jnp.sum((pair_starts[:, :, None] <= places).astype(jnp.int32), axis=1)
    live = places < live_length[:, None]
    begun = jnp.max(jnp.where(pair_starts[:, :, None] <= places, pair_starts[:, :, None], 0), axis=1)
    first = jnp.where(live, begun, live_length[:, None])
    nseg = pair_starts.shape[1]
    pick = jnp.arange(nseg)[None, :, None] == (counted - 1)[:, None, :]
    ends = jnp.concatenate([source_starts[:, 1:], jnp.full_like(source_starts[:, :1], MEM)], axis=1)
    start = jnp.sum(jnp.where(pick, source_starts[:, :, None], 0), axis=1)
    end = jnp.sum(jnp.where(pick, ends[:, :, None], 0), axis=1)
    start = jnp.where(live, start, 0)
    end = jnp.where(live, end, MEM)
    bounds = jnp.pad(jnp.stack([start, end], axis=1), ((0, 0), (0, 6), (0, 0)))
    return first[:, None, :], bounds


TB = 256


def norm_parts(values):
    center = values - jnp.mean(values, axis=-1, keepdims=True)
    inverse = lax.rsqrt(jnp.mean(center * center, axis=-1, keepdims=True) + EPSILON)
    return center * inverse, inverse


def norm_back(unit, inverse, gain, gradient):
    scaled = gradient * gain
    return inverse * (
        scaled
        - jnp.mean(scaled, axis=-1, keepdims=True)
        - unit * jnp.mean(scaled * unit, axis=-1, keepdims=True)
    )


def add_norm_grads(ref, unit, gradient):
    @pl.when(pl.program_id(0) == 0)
    def _():
        ref[...] = jnp.zeros_like(ref)

    ref[0:1, :] += jnp.sum(gradient * unit, axis=0, keepdims=True)
    ref[1:2, :] += jnp.sum(gradient, axis=0, keepdims=True)


def tile(rows, columns, at=0):
    return pl.BlockSpec((rows, columns), lambda b: (b, at))


def whole(rows, columns, at=0):
    return pl.BlockSpec((rows, columns), lambda b: (0, at), pipeline_mode=pl.Buffered(1))


def shape(rows, columns, dtype):
    return jax.ShapeDtypeStruct((rows, columns), dtype)


def params(mib):
    return pltpu.CompilerParams(vmem_limit_bytes=mib << 20)


def cost(flops, moved):
    return pl.CostEstimate(flops=int(flops), bytes_accessed=int(moved), transcendentals=0)


def project_kernel(tokens_ref, norms_ref, weight_ref, normed_ref, out_ref):
    unit, _ = norm_parts(tokens_ref[...].astype(F32))
    normed = (unit * norms_ref[0:1, :] + norms_ref[1:2, :]).astype(BF16)
    normed_ref[...] = normed
    for part in range(3):
        at = slice(part * 1024, (part + 1) * 1024)
        out_ref[:, at] = mm(normed, weight_ref[:, at]).astype(BF16)


def project(tokens, norms, early):
    rows, d = tokens.shape
    return pl.pallas_call(
        project_kernel,
        grid=(rows // TB,),
        in_specs=[tile(TB, d), whole(8, d), whole(d, 3 * d)],
        out_specs=[tile(TB, d), tile(TB, 3 * d)],
        out_shape=[shape(rows, d, BF16), shape(rows, 3 * d, BF16)],
        name="project",
        compiler_params=params(40),
        cost_estimate=cost(6 * rows * d * d, 16 << 20),
    )(tokens, norms, early)


def middle_kernel(
    mixed_ref, tokens_ref, memory_ref, norms_ref, wo_ref, wq_ref, wkv_ref, after_ref, normed_ref, q_ref, kv_ref
):
    after = tokens_ref[...].astype(F32) + mm(mixed_ref[...], wo_ref[...])
    after_ref[...] = after
    kv_ref[...] = mm(memory_ref[...], wkv_ref[...]).astype(BF16)
    unit, _ = norm_parts(after)
    normed = (unit * norms_ref[2:3, :] + norms_ref[3:4, :]).astype(BF16)
    normed_ref[...] = normed
    q_ref[...] = mm(normed, wq_ref[...]).astype(BF16)


def middle(mixed, tokens, memory, norms, early):
    rows, d = tokens.shape
    mem_rows = memory.shape[0]
    steps = rows // TB
    mb = mem_rows // steps
    return pl.pallas_call(
        middle_kernel,
        grid=(steps,),
        in_specs=[
            tile(TB, d),
            tile(TB, d),
            tile(mb, d),
            whole(8, d),
            whole(d, d, OUT_SELF),
            whole(d, d, QUERY_CROSS),
            whole(d, 2 * d, KV_CROSS),
        ],
        out_specs=[tile(TB, d), tile(TB, d), tile(TB, d), tile(mb, 2 * d)],
        out_shape=[shape(rows, d, F32), shape(rows, d, BF16), shape(rows, d, BF16), shape(mem_rows, 2 * d, BF16)],
        name="middle",
        compiler_params=params(40),
        cost_estimate=cost(6 * rows * d * d, 20 << 20),
    )(mixed, tokens, memory, norms, early, early, early)


GELU_A = 0.7978845608028654
GELU_B = 0.044715


def feed_kernel(
    live_ref,
    weight_ref,
    mixed_ref,
    before_ref,
    cot_ref,
    norms_ref,
    wo_ref,
    win_ref,
    wout_ref,
    out_ref,
    normed_ref,
    act_ref,
    hid_ref,
    b3_ref,
    total_ref,
    b2_ref,
    grad_ref,
    ngrad_ref,
):
    block = pl.program_id(0)
    per_row = SEQ // TB
    row = block // per_row
    places = lax.broadcasted_iota(jnp.int32, (TB, 1), 0) + (block % per_row) * TB
    live = (places < live_ref[row]).astype(F32)
    out_grad = cot_ref[...].astype(F32) * live * weight_ref[0]
    branch = out_grad.astype(BF16)
    b3_ref[...] = branch
    after = before_ref[...] + mm(mixed_ref[...], wo_ref[...])
    unit, inverse = norm_parts(after)
    normed = (unit * norms_ref[4:5, :] + norms_ref[5:6, :]).astype(BF16)
    normed_ref[...] = normed
    d = normed.shape[1]
    result, back = after, None
    for part in range(win_ref.shape[1] // d):
        at = slice(part * d, (part + 1) * d)
        x = mm(normed, win_ref[:, at])
        square = x * x
        t = jnp.tanh(GELU_A * x * (1.0 + GELU_B * square))
        half = 0.5 * (1.0 + t)
        act = (x * half).astype(BF16)
        slope = half + (0.5 * GELU_A) * x * (1.0 - t * t) * (1.0 + (3.0 * GELU_B) * square)
        act_ref[:, at] = act
        hid = (mm_t(branch, wout_ref[at, :]) * slope).astype(BF16)
        hid_ref[:, at] = hid
        result = result + mm(act, wout_ref[at, :])
        term = mm_t(hid, win_ref[:, at])
        back = term if back is None else back + term
    out_ref[...] = result.astype(BF16)
    total = out_grad + norm_back(unit, inverse, norms_ref[4:5, :], back)
    total_ref[...] = total
    b2 = total.astype(BF16)
    b2_ref[...] = b2
    grad_ref[...] = mm_t(b2, wo_ref[...]).astype(BF16)
    add_norm_grads(ngrad_ref, unit, back)


def feed(live_length, row_weight, mixed, before, cotangent, norms, early, late):
    rows, d = cotangent.shape
    ff = late[0].shape[1]
    smem = pl.BlockSpec(memory_space=pltpu.SMEM)
    return pl.pallas_call(
        feed_kernel,
        grid=(rows // TB,),
        in_specs=[
            smem,
            smem,
            tile(TB, d),
            tile(TB, d),
            tile(TB, d),
            whole(8, d),
            whole(d, d, OUT_CROSS),
            whole(d, ff),
            whole(ff, d),
        ],
        out_specs=[
            tile(TB, d),
            tile(TB, d),
            tile(TB, ff),
            tile(TB, ff),
            tile(TB, d),
            tile(TB, d),
            tile(TB, d),
            tile(TB, d),
            whole(8, d),
        ],
        out_shape=[
            shape(rows, d, BF16),
            shape(rows, d, BF16),
            shape(rows, ff, BF16),
            shape(rows, ff, BF16),
            shape(rows, d, BF16),
            shape(rows, d, F32),
            shape(rows, d, BF16),
            shape(rows, d, BF16),
            shape(8, d, F32),
        ],
        name="feed",
        compiler_params=params(58),
        cost_estimate=cost(38 * rows * d * d, 50 << 20),
    )(live_length, row_weight, mixed, before, cotangent, norms, early, *late)


def cross_close_kernel(
    dq_ref, dkv_ref, before_ref, total_ref, norms_ref, wq_ref, wkv_ref, wo_ref, out_ref, b1_ref, grad_ref, mem_ref, ngrad_ref
):
    gradient = mm_t(dq_ref[...], wq_ref[...])
    mem_ref[...] = mm_t(dkv_ref[...], wkv_ref[...]).astype(BF16)
    unit, inverse = norm_parts(before_ref[...])
    total = total_ref[...] + norm_back(unit, inverse, norms_ref[2:3, :], gradient)
    out_ref[...] = total
    b1 = total.astype(BF16)
    b1_ref[...] = b1
    grad_ref[...] = mm_t(b1, wo_ref[...]).astype(BF16)
    add_norm_grads(ngrad_ref, unit, gradient)


def cross_close(dq, dkv, before, total, norms, early):
    rows, d = dq.shape
    mem_rows = dkv.shape[0]
    steps = rows // TB
    mb = mem_rows // steps
    return pl.pallas_call(
        cross_close_kernel,
        grid=(steps,),
        in_specs=[
            tile(TB, d),
            tile(mb, 2 * d),
            tile(TB, d),
            tile(TB, d),
            whole(8, d),
            whole(d, d, QUERY_CROSS),
            whole(d, 2 * d, KV_CROSS),
            whole(d, d, OUT_SELF),
        ],
        out_specs=[tile(TB, d), tile(TB, d), tile(TB, d), tile(mb, d), whole(8, d)],
        out_shape=[
            shape(rows, d, F32),
            shape(rows, d, BF16),
            shape(rows, d, BF16),
            shape(mem_rows, d, BF16),
            shape(8, d, F32),
        ],
        name="cross_close",
        compiler_params=params(40),
        cost_estimate=cost(6 * rows * d * d, 24 << 20),
    )(dq, dkv, before, total, norms, early, early, early)


def self_close_kernel(dqkv_ref, before_ref, total_ref, norms_ref, w_ref, out_ref, ngrad_ref):
    gradient = mm_t(dqkv_ref[...], w_ref[...])
    unit, inverse = norm_parts(before_ref[...].astype(F32))
    total = total_ref[...] + norm_back(unit, inverse, norms_ref[0:1, :], gradient)
    out_ref[...] = total.astype(BF16)
    add_norm_grads(ngrad_ref, unit, gradient)


def self_close(dqkv, before, total, norms, early):
    rows, d = total.shape
    return pl.pallas_call(
        self_close_kernel,
        grid=(rows // TB,),
        in_specs=[tile(TB, 3 * d), tile(TB, d), tile(TB, d), whole(8, d), whole(d, 3 * d)],
        out_specs=[tile(TB, d), whole(8, d)],
        out_shape=[shape(rows, d, BF16), shape(8, d, F32)],
        name="self_close",
        compiler_params=params(40),
        cost_estimate=cost(6 * rows * d * d, 20 << 20),
    )(dqkv, before, total, norms, early)


OUT_SELF, KV_CROSS, QUERY_CROSS, OUT_CROSS, EXTRA = 3, 2, 6, 7, 64


def greet_all(narrow):
    w, z = lax.axis_index("wide"), lax.axis_index("narrow")
    barrier = pltpu.get_barrier_semaphore()
    others = [(w ^ 1, z), (w ^ 2, z), (w ^ 4, z)] + [(w, z ^ mask) for mask in range(1, narrow)]
    for other in others:
        pl.semaphore_signal(barrier, inc=1, device_id=other, device_id_type=pl.DeviceIdType.MESH)
    pl.semaphore_wait(barrier, len(others))


def early_gather_kernel(wide, narrow, shard_ref, out_ref, send_sems, recv_sems, own_sem):
    rows = shard_ref.shape[0]
    half = rows // 2
    w, z = lax.axis_index("wide"), lax.axis_index("narrow")
    core, x, y = w ^ 1, w ^ 2, w ^ 4
    up, down, to_x, to_y, on_y, on_x, to_core = [k * narrow for k in range(7)]

    def start_of(holder, s):
        return pl.multiple_of((holder * narrow + s) * rows, rows)

    def move(holder, s, number, target, first=0, count=rows, own=False):
        at = pl.multiple_of(start_of(holder, s) + first, half)
        place = out_ref.at[pl.ds(at, count)]
        return pltpu.make_async_remote_copy(
            src_ref=shard_ref.at[pl.ds(first, count)] if own else place,
            dst_ref=place,
            send_sem=send_sems.at[number],
            recv_sem=recv_sems.at[number],
            device_id=target,
            device_id_type=pl.DeviceIdType.MESH,
        )

    above, below = (w, z + 1), (w, z - 1)
    greet_all(narrow)

    keep = pltpu.make_async_copy(shard_ref, out_ref.at[pl.ds(start_of(w, z), rows)], own_sem)
    keep.start()

    def spread(s, own=False):
        move(w, s, to_x + s, (x, z), own=own).start()
        move(w, s, to_y + s, (y, z), own=own).start()
        move(w, s, to_core + s, (core, z), own=own).start()

    def relay(s):
        move(x, s, to_x + s, (x, z)).wait_recv()
        move(x, s, on_y + s, (y, z), 0, half).start()
        move(x, s, to_core + narrow + s, (core, z)).start()
        move(y, s, to_y + s, (y, z)).wait_recv()
        move(y, s, on_x + s, (x, z), half, half).start()
        move(y, s, to_core + 2 * narrow + s, (core, z)).start()

    def at_distance(r, action):
        if r == 0:
            action(z)
        else:
            pl.when(z - r >= 0)(lambda: action(z - r))
            pl.when(z + r < narrow)(lambda: action(z + r))

    pl.when(z < narrow - 1)(lambda: move(w, z, up + z, above, own=True).start())
    pl.when(z > 0)(lambda: move(w, z, down + z, below, own=True).start())
    spread(z, own=True)
    for r in range(1, narrow):

        def from_below(r=r):
            s = z - r
            move(w, s, up + s, above).wait_recv()
            pl.when(z < narrow - 1)(lambda: move(w, s, up + s, above).start())
            spread(s)

        def from_above(r=r):
            s = z + r
            move(w, s, down + s, below).wait_recv()
            pl.when(z > 0)(lambda: move(w, s, down + s, below).start())
            spread(s)

        pl.when(z - r >= 0)(from_below)
        pl.when(z + r < narrow)(from_above)
        at_distance(r - 1, relay)
    at_distance(narrow - 1, relay)

    def corner(s):
        move(x ^ 4, s, on_y + s, (y, z), 0, half).wait_recv()
        move(x ^ 4, s, on_x + s, (x, z), half, half).wait_recv()
        move(x ^ 4, s, to_core + 3 * narrow + s, (core, z)).start()

    for r in range(narrow):
        at_distance(r, corner)
    for s in range(narrow):
        for k, holder in enumerate((w, x, y, x ^ 4)):
            move(holder ^ 1, s, to_core + k * narrow + s, (core, z)).wait_recv()
    for s in range(narrow):
        pl.when((s <= z) & (z < narrow - 1))(lambda s=s: move(w, s, up + s, above).wait_send())
        pl.when((s >= z) & (z > 0))(lambda s=s: move(w, s, down + s, below).wait_send())
        move(w, s, to_x + s, (x, z)).wait_send()
        move(w, s, to_y + s, (y, z)).wait_send()
        move(x, s, on_y + s, (y, z), 0, half).wait_send()
        move(y, s, on_x + s, (x, z), half, half).wait_send()
        for k, holder in enumerate((w, x, y, x ^ 4)):
            move(holder, s, to_core + k * narrow + s, (core, z)).wait_send()
    keep.wait()


def early_gather(shard, mesh_axes):
    (_, wide), (_, narrow) = mesh_axes
    rows, columns = shard.shape
    if wide != 8 or rows % 32:
        return lax.all_gather(shard, tuple(axis for axis, _ in mesh_axes), axis=0, tiled=True)
    return pl.pallas_call(
        functools.partial(early_gather_kernel, wide, narrow),
        in_specs=[pl.BlockSpec(memory_space=pl.ANY)],
        out_specs=pl.BlockSpec(memory_space=pl.ANY),
        out_shape=jax.ShapeDtypeStruct((rows * wide * narrow, columns), BF16),
        scratch_shapes=[
            pltpu.SemaphoreType.DMA((10 * narrow,)),
            pltpu.SemaphoreType.DMA((10 * narrow,)),
            pltpu.SemaphoreType.DMA,
        ],
        name="early_gather",
        compiler_params=pltpu.CompilerParams(collective_id=0, has_side_effects=True),
        cost_estimate=pl.CostEstimate(flops=0, bytes_accessed=200 << 20, transcendentals=0),
    )(shard)


def stages_of(mesh_axes):
    plan = []
    for axis, size in mesh_axes:
        bits = size.bit_length() - 1
        at = 0
        while at < bits:
            take = 1 if (bits - at) % 2 else 2
            plan.append((axis, at, take))
            at += take
    return plan


def trade(value, axis, size, mask):
    return lax.ppermute(value, axis, [(i, i ^ mask) for i in range(size)])


def digit_of(axis, at, take):
    return (lax.axis_index(axis) >> at) & ((1 << take) - 1)


def pick(value, digit, place):
    if isinstance(value, list):
        return jnp.concatenate([pick(v, digit, place) for v in value], axis=0)
    return lax.dynamic_index_in_dim(value, digit, place, keepdims=False)


def add_up(own, pieces):
    total = own.astype(F32)
    for piece in pieces:
        total = total + piece.astype(F32)
    return total


def sum_steps(partial, mesh_axes):
    sizes = dict(mesh_axes)
    plan = stages_of(mesh_axes)
    groups = []
    for axis, _ in mesh_axes:
        groups += sorted((s for s in plan if s[0] == axis), key=lambda s: -s[1])
    devices = 1
    for _, size in mesh_axes:
        devices *= size
    columns = partial[0].shape[1]
    extents = [1 << s[2] for s in groups]
    value = [p.reshape(p.shape[0] // WIDTH, *extents, -1, columns) for p in partial]
    for number, stage in enumerate(plan):
        axis, at, take = stage
        place = 1 + groups.index(stage)
        groups.remove(stage)
        if axis == "wide" and take == 2:
            if isinstance(value, list):
                value = jnp.concatenate(value, axis=0)
            split = value.reshape(*value.shape[:place], 2, 2, *value.shape[place + 1 :])
            a, b = split[..., : columns // 2], split[..., columns // 2 :]
            low, high = digit_of(axis, at, 1), digit_of(axis, at + 1, 1)
            step = ((high, place, 2 << at), (low, place + 1, 1 << at))
            for (digit_a, place_a, mask_a), (digit_b, place_b, mask_b) in (
                step,
                ((low, place, 1 << at), (high, place, 2 << at)),
            ):
                pieces = yield [
                    trade(pick(a, digit_a ^ 1, place_a), axis, sizes[axis], mask_a),
                    trade(pick(b, digit_b ^ 1, place_b), axis, sizes[axis], mask_b),
                ]
                a = add_up(pick(a, digit_a, place_a), pieces[:1]).astype(BF16)
                b = add_up(pick(b, digit_b, place_b), pieces[1:]).astype(BF16)
            value = jnp.concatenate([a, b], axis=-1)
            continue
        digit = digit_of(axis, at, take)
        pieces = yield [
            trade(pick(value, digit ^ mask, place), axis, sizes[axis], mask << at) for mask in range(1, 1 << take)
        ]
        value = add_up(pick(value, digit, place), pieces)
        if number < len(plan) - 1:
            value = value.astype(BF16)
    return value.astype(F32).reshape(-1, columns)


class StagedSum:
    def __init__(self, partial, mesh_axes):
        self.steps = sum_steps(partial, mesh_axes)
        self.under_way = next(self.steps)
        self.value = None

    def go_on(self, pieces):
        try:
            self.under_way = self.steps.send(pieces)
        except StopIteration as stop:
            self.under_way, self.value = None, stop.value

    def result(self):
        while self.under_way is not None:
            self.go_on(self.under_way)
        return self.value


def fence(value, *sums):
    held = [s for s in sums if s.under_way is not None]
    value, arrived = lax.optimization_barrier((value, [s.under_way for s in held]))
    for s, pieces in zip(held, arrived):
        s.go_on(pieces)
    return value


def sum_everywhere(value, mesh_axes):
    sizes = dict(mesh_axes)
    for axis, at, take in stages_of(mesh_axes):
        arrived = [trade(value, axis, sizes[axis], mask << at) for mask in range(1, 1 << take)]
        for piece in arrived:
            value = value + piece
    return value


def by_pairs(*parts):
    rows = parts[0].shape[0]
    return jnp.stack([p.reshape(rows, -1, 128) for p in parts], axis=2).reshape(rows, -1)


def from_pairs(value, count):
    rows = value.shape[0]
    split = value.reshape(rows, -1, count, 128)
    return [split[:, :, c].reshape(rows, -1) for c in range(count)]


def outer_sum(left_side, gradient):
    return jnp.einsum("td,te->de", left_side, gradient, preferred_element_type=F32).astype(BF16)


CHUNKS = 4


class Scatter:
    def __init__(self, own, theirs, buffers, keep, send_sems, recv_sems, narrow):
        self.own, self.theirs, self.keep = own, theirs, keep
        self.from_core, self.a1, self.b1, self.a2, self.b2, self.from_line = buffers
        self.send_sems, self.recv_sems = send_sems, recv_sems
        self.narrow = narrow
        self.half = self.a1.shape[-1]
        self.w, self.z = lax.axis_index("wide"), lax.axis_index("narrow")
        self.c, self.x, self.y = self.w & 1, (self.w >> 1) & 1, (self.w >> 2) & 1
        self.per_chunk = 4 + narrow

    def move(self, i, number, src, dst, target):
        at = i * self.per_chunk + number
        return pltpu.make_async_remote_copy(
            src_ref=src,
            dst_ref=dst,
            send_sem=self.send_sems.at[at],
            recv_sem=self.recv_sems.at[at],
            device_id=target,
            device_id_type=pl.DeviceIdType.MESH,
        )

    def to_core(self, i):
        return self.move(i, 0, self.theirs(i), self.from_core.at[i], (self.w ^ 1, self.z))

    def first(self, i):
        left, right = pl.ds(0, self.half), pl.ds(self.half, self.half)
        to_x, to_y = (self.w ^ 2, self.z), (self.w ^ 4, self.z)
        return (
            self.move(i, 1, self.own.at[i, :, 1 - self.x, :, :, left], self.a1.at[i], to_x),
            self.move(i, 2, self.own.at[i, 1 - self.y, :, :, :, right], self.b1.at[i], to_y),
        )

    def second(self, i):
        left, right = pl.ds(0, self.half), pl.ds(self.half, self.half)
        to_x, to_y = (self.w ^ 2, self.z), (self.w ^ 4, self.z)
        return (
            self.move(i, 3, self.own.at[i, 1 - self.y, self.x, :, :, left], self.a2.at[i], to_y),
            self.move(i, 4, self.own.at[i, self.y, 1 - self.x, :, :, right], self.b2.at[i], to_x),
        )

    def along(self, i):
        return [
            self.move(
                i,
                4 + mask,
                self.own.at[i, self.y, self.x, self.z ^ mask],
                self.from_line.at[i, mask - 1],
                (self.w, self.z ^ mask),
            )
            for mask in range(1, self.narrow)
        ]

    def begin(self, i):
        self.to_core(i).start()

    def add(self, i, y, x, columns, piece):
        now = self.own[i, y, x, :, :, columns]
        self.own[i, y, x, :, :, columns] = now + piece

    def step(self, i, stage):
        both, left, right = slice(None), slice(0, self.half), slice(self.half, None)
        if stage == 0:
            self.to_core(i).wait_recv()
            for a in range(2):
                for b in range(2):
                    self.add(i, a, b, both, self.from_core[i, a, b])
            for copy in self.first(i):
                copy.start()
        elif stage == 1:
            for copy in self.first(i):
                copy.wait_recv()
            for a in range(2):
                self.add(i, a, self.x, left, self.a1[i, a])
                self.add(i, self.y, a, right, self.b1[i, a])
            for copy in self.second(i):
                copy.start()
        elif stage == 2:
            for copy in self.second(i):
                copy.wait_recv()
            self.add(i, self.y, self.x, left, self.a2[i])
            self.add(i, self.y, self.x, right, self.b2[i])
            for copy in self.along(i):
                copy.start()
        else:
            for copy in self.along(i):
                copy.wait_recv()
            total = self.own[i, self.y, self.x, self.z].astype(F32)
            for mask in range(1, self.narrow):
                total = total + self.from_line[i, mask - 1].astype(F32)
            self.keep(i, total)

    def close(self, i):
        for copy in (self.to_core(i), *self.first(i), *self.second(i), *self.along(i)):
            copy.wait_send()


def scatter_scratch(chunks, narrow, rows, width):
    copies = chunks * (4 + narrow)
    return [
        pltpu.VMEM((chunks, 2, 2, narrow, rows, width), BF16),
        pltpu.VMEM((chunks, 2, 2, narrow, rows, width), BF16),
        pltpu.VMEM((chunks, 2, narrow, rows, width // 2), BF16),
        pltpu.VMEM((chunks, 2, narrow, rows, width // 2), BF16),
        pltpu.VMEM((chunks, narrow, rows, width // 2), BF16),
        pltpu.VMEM((chunks, narrow, rows, width // 2), BF16),
        pltpu.VMEM((chunks, narrow - 1, rows, width), BF16),
        pltpu.SemaphoreType.DMA((copies,)),
        pltpu.SemaphoreType.DMA((copies,)),
        pltpu.SemaphoreType.DMA((chunks,)),
    ]


class Carried:
    def __init__(self, shares, scratch, keep, narrow):
        own, *buffers, send_sems, recv_sems, self.load_sems = scratch
        self.shares = shares
        self.scatter = Scatter(own, self.other, buffers, keep, send_sems, recv_sems, narrow)
        self.chunks = own.shape[0]

    def part(self, i, core):
        return self.shares[i](core)

    def other(self, i):
        return self.part(i, 1 - self.scatter.c)

    def load(self, i):
        return pltpu.make_async_copy(self.part(i, self.scatter.c), self.scatter.own.at[i], self.load_sems.at[i])

    def open(self):
        for i in range(self.chunks):
            self.load(i).start()
        greet_all(self.scatter.narrow)
        for i in range(2):
            self.scatter.begin(i)

    def steps(self, plan):
        for i, stage in plan:
            if stage == 0:
                self.load(i).wait()
            self.scatter.step(i, stage)
            if stage == 0 and i + 2 < self.chunks:
                self.scatter.begin(i + 2)

    def close(self):
        for i in range(self.chunks):
            self.scatter.close(i)


def share_views(array, narrow, rows):
    return array.reshape(2, 2, 2, narrow, rows, array.shape[1])


def share_views(array, narrow, rows):
    return array.reshape(2, 2, 2, narrow, rows, array.shape[1])


def columns_of(ref, at, width):
    return lambda core: ref.at[:, :, core, :, :, pl.ds(at, width)]


def tn(a, b):
    return lax.dot_general(a, b, (((0,), (0,)), ((), ())), preferred_element_type=F32)


def outer_into(out_ref, left_ref, right):
    for at in range(0, left_ref.shape[1], 256):
        out_ref[at : at + 256, :] = tn(left_ref[:, at : at + 256], right).astype(BF16)


CROSS_PLAN = (
    ((0, 0), (1, 0)),
    ((2, 0),),
    ((0, 1),),
    ((3, 0),),
    ((1, 1),),
    ((0, 2), (4, 0)),
    ((2, 1),),
    ((1, 2),),
    ((0, 3), (3, 1), (5, 0)),
    ((2, 2),),
    ((1, 3), (4, 1)),
    ((3, 2),),
    ((2, 3),),
    ((5, 1),),
    ((4, 2),),
    ((3, 3),),
    ((5, 2), (4, 3), (5, 3)),
)
CROSS_WIDE = 2


def cross_back_kernel(
    narrow,
    bounds_ref,
    log_ref,
    q_ref,
    kv_ref,
    mixed_pair_ref,
    grad_ref,
    before_ref,
    total_ref,
    norms_ref,
    mixed_ref,
    b2_ref,
    normed_ref,
    memory_ref,
    self_mixed_ref,
    early_any,
    share_any,
    wide_any,
    out_ref,
    next_ref,
    mem_ref,
    ngrad_ref,
    shares_ref,
    shard_ref,
    wide_ref,
    dk_ref,
    dv_ref,
    dq_ref,
    dkv_ref,
    b1_ref,
    wq,
    wkv,
    wo,
    weight_sems,
    *scratch,
):
    step = pl.program_id(0)
    d = wq.shape[0]
    rows = shard_ref.shape[0] // 4

    def keep(i, value):
        if i < 4:
            shard_ref[i * rows : (i + 1) * rows, :] = value
        else:
            wide_ref[:, (i - 4) * d : (i - 3) * d] = value

    def piece(i):
        return lambda core: share_any.at[:, :, core, :, i]

    pieces = [piece(i) for i in range(4)] + [columns_of(wide_any, i * d, d) for i in range(CROSS_WIDE)]
    carried = Carried(pieces, scratch, keep, narrow)
    loads = [
        pltpu.make_async_copy(early_any.at[:, pl.ds(QUERY_CROSS * d, d)], wq, weight_sems.at[0]),
        pltpu.make_async_copy(early_any.at[:, pl.ds(2 * KV_CROSS * d, 2 * d)], wkv, weight_sems.at[1]),
        pltpu.make_async_copy(early_any.at[:, pl.ds(OUT_SELF * d, d)], wo, weight_sems.at[2]),
    ]

    @pl.when(step == 0)
    def _():
        carried.open()
        for load in loads:
            load.start()

    @pl.when(step < PAIRS)
    def _():
        def keep_dq(rows, value):
            dq_ref[rows, pl.ds(pl.multiple_of(step * 128, 128), 128)] = value

        cross_backward_pair(bounds_ref, log_ref, q_ref, kv_ref, mixed_pair_ref, grad_ref, keep_dq, None, dk_ref, dv_ref)
        at = pl.multiple_of(step * 256, 256)
        dkv_ref[:, pl.ds(at, 128)] = (dk_ref[...] * HEAD_DIM**-0.5).astype(BF16)
        dkv_ref[:, pl.ds(pl.multiple_of(at + 128, 128), 128)] = dv_ref[...].astype(BF16)

    @pl.when(step == PAIRS)
    def _():
        for load in loads:
            load.wait()
        ngrad_ref[...] = jnp.zeros_like(ngrad_ref)

    tokens_end = PAIRS + SEQ // TB

    @pl.when((step >= PAIRS) & (step < tokens_end))
    def _():
        t = step - PAIRS
        mb = mem_ref.shape[0]
        at = pl.ds(pl.multiple_of(t * TB, TB), TB)
        gradient = mm_t(dq_ref[at, :], wq[...])
        mem_ref[...] = mm_t(dkv_ref[pl.ds(pl.multiple_of(t * mb, mb), mb), :], wkv[...]).astype(BF16)
        unit, inverse = norm_parts(before_ref[...])
        total = total_ref[...] + norm_back(unit, inverse, norms_ref[2:3, :], gradient)
        out_ref[...] = total
        b1 = total.astype(BF16)
        b1_ref[at, :] = b1
        next_ref[...] = mm_t(b1, wo[...]).astype(BF16)
        ngrad_ref[0:1, :] += jnp.sum(gradient * unit, axis=0, keepdims=True)
        ngrad_ref[1:2, :] += jnp.sum(gradient, axis=0, keepdims=True)

    pl.when(step == tokens_end)(lambda: outer_into(shares_ref, mixed_ref, b2_ref[...]))
    pl.when(step == tokens_end + 1)(lambda: outer_into(shares_ref, normed_ref, dq_ref[...]))
    pl.when(step == tokens_end + 2)(lambda: outer_into(shares_ref, memory_ref, dkv_ref[:, :d]))
    pl.when(step == tokens_end + 3)(lambda: outer_into(shares_ref, memory_ref, dkv_ref[:, d:]))
    pl.when(step == tokens_end + 4)(lambda: outer_into(shares_ref, self_mixed_ref, b1_ref[...]))

    for number, plan in enumerate(CROSS_PLAN):
        pl.when(step == number)(functools.partial(carried.steps, plan))
    pl.when(step == len(CROSS_PLAN) - 1)(carried.close)


def cross_back(bounds, logs, q, kv, mixed, grad, before, total, norms, b2, normed, memory, self_mixed, early, share, wide_share, narrow):
    rows, d = q.shape
    mem_rows = kv.shape[0]
    shard_rows = d // (8 * narrow)
    steps = rows // TB
    mb = mem_rows // steps

    def pair(s):
        return jnp.minimum(s, PAIRS - 1)

    def token(s):
        return jnp.clip(s - PAIRS, 0, steps - 1)

    anywhere = pl.BlockSpec(memory_space=pl.ANY)
    by_pair = pl.BlockSpec((SEQ, 128), lambda s: (0, pair(s)))
    by_token = pl.BlockSpec((TB, d), lambda s: (token(s), 0))
    return pl.pallas_call(
        functools.partial(cross_back_kernel, narrow),
        grid=(PAIRS + steps + 5,),
        in_specs=[
            pl.BlockSpec((1, 8, SEQ), lambda s: (0, 0, 0)),
            pl.BlockSpec((1, 1, 8, SEQ), lambda s: (0, pair(s), 0, 0)),
            by_pair,
            pl.BlockSpec((MEM, 256), lambda s: (0, pair(s))),
            by_pair,
            by_pair,
            by_token,
            by_token,
            whole(8, d),
            whole(rows, d),
            whole(rows, d),
            whole(rows, d),
            whole(mem_rows, d),
            whole(rows, d),
            anywhere,
            anywhere,
            anywhere,
        ],
        out_specs=[
            by_token,
            by_token,
            pl.BlockSpec((mb, d), lambda s: (token(s), 0)),
            whole(8, d),
            pl.BlockSpec((d, d), lambda s: (jnp.maximum(s - PAIRS - steps, 0), 0)),
            whole(4 * shard_rows, d),
            whole(shard_rows, CROSS_WIDE * d),
        ],
        out_shape=[
            shape(rows, d, F32),
            shape(rows, d, BF16),
            shape(mem_rows, d, BF16),
            shape(8, d, F32),
            shape(5 * d, d, BF16),
            shape(4 * shard_rows, d, F32),
            shape(shard_rows, CROSS_WIDE * d, F32),
        ],
        scratch_shapes=[
            pltpu.VMEM((MEM, 128), F32),
            pltpu.VMEM((MEM, 128), F32),
            pltpu.VMEM((rows, d), BF16),
            pltpu.VMEM((mem_rows, 2 * d), BF16),
            pltpu.VMEM((rows, d), BF16),
            pltpu.VMEM((d, d), BF16),
            pltpu.VMEM((d, 2 * d), BF16),
            pltpu.VMEM((d, d), BF16),
            pltpu.SemaphoreType.DMA((3,)),
            *scatter_scratch(4 + CROSS_WIDE, narrow, shard_rows, d),
        ],
        name="cross_back",
        compiler_params=pltpu.CompilerParams(collective_id=2, has_side_effects=True, vmem_limit_bytes=60 << 20),
        cost_estimate=cost(40 * rows * d * d, 100 << 20),
    )(
        bounds,
        logs,
        q,
        kv,
        mixed,
        grad,
        before,
        total,
        norms,
        mixed,
        b2,
        normed,
        memory,
        self_mixed,
        early,
        share.reshape(2, 2, 2, narrow, 4, shard_rows, d),
        share_views(wide_share, narrow, shard_rows),
    )


SELF_PLAN = (
    ((0, 0), (1, 0)),
    ((2, 0),),
    ((0, 1),),
    ((3, 0),),
    ((1, 1),),
    ((0, 2), (4, 0)),
    ((2, 1),),
    ((1, 2), (5, 0), (3, 1)),
    ((0, 3),),
    ((2, 2), (6, 0)),
    ((1, 3), (4, 1)),
    ((3, 2),),
    ((2, 3), (5, 1)),
    ((4, 2),),
    ((3, 3), (6, 1), (5, 2), (4, 3), (6, 2), (5, 3), (6, 3)),
)
SELF_WIDE = 4 - CROSS_WIDE
SELF_CHUNKS = SELF_WIDE + 5


def self_back_kernel(
    narrow,
    first_ref,
    log_ref,
    qkv_ref,
    mixed_ref,
    grad_ref,
    normed_ref,
    tokens_ref,
    total_ref,
    norms_ref,
    early_any,
    wide_any,
    shares_any,
    qkv_share_ref,
    out_ref,
    ngrad_ref,
    expand_ref,
    cross_output_ref,
    cross_query_ref,
    cross_key_ref,
    cross_value_ref,
    self_output_ref,
    dk_ref,
    dv_ref,
    dqkv,
    weight,
    weight_sem,
    *scratch,
):
    step = pl.program_id(0)
    d = normed_ref.shape[1]

    def keep(i, value):
        i -= SELF_WIDE
        if i < 0:
            expand_ref[:, (i + SELF_WIDE) * d : (i + SELF_WIDE + 1) * d] = value
        elif i == 0:
            cross_output_ref[...] = value
        elif i == 1:
            cross_query_ref[...] = value
        elif i == 4:
            self_output_ref[...] = value
        else:
            for n in range(d // 256):
                at = (i - 2) * d // 2 + n * 128
                cross_key_ref[:, at : at + 128] = value[:, n * 256 : n * 256 + 128]
                cross_value_ref[:, at : at + 128] = value[:, n * 256 + 128 : n * 256 + 256]

    def piece(i):
        return lambda core: shares_any.at[i, :, :, core]

    pieces = [columns_of(wide_any, (CROSS_WIDE + i) * d, d) for i in range(SELF_WIDE)] + [piece(i) for i in range(5)]
    carried = Carried(pieces, scratch, keep, narrow)
    load = pltpu.make_async_copy(early_any.at[:, pl.ds(0, 3 * d)], weight, weight_sem)

    @pl.when(step == 0)
    def _():
        carried.open()
        load.start()

    @pl.when(step < PAIRS)
    def _():
        base = step * 384

        def keep_dq(rows, value):
            dqkv[rows, pl.ds(pl.multiple_of(base, 128), 128)] = value

        attend_back(
            lambda rows: qkv_ref[rows, 0:128],
            qkv_ref[:, 128:256],
            qkv_ref[:, 256:384],
            grad_ref,
            mixed_ref,
            log_ref,
            functools.partial(self_visible, first_ref),
            self_extent,
            keep_dq,
            dk_ref,
            dv_ref,
        )
        dqkv[:, pl.ds(pl.multiple_of(base + 128, 128), 128)] = (dk_ref[...] * HEAD_DIM**-0.5).astype(BF16)
        dqkv[:, pl.ds(pl.multiple_of(base + 256, 128), 128)] = dv_ref[...].astype(BF16)

    @pl.when((step >= PAIRS) & (step < PAIRS + 3))
    def _():
        at = pl.ds(pl.multiple_of((step - PAIRS) * d, d), d)
        outer_into(qkv_share_ref, normed_ref, dqkv[:, at])

    @pl.when(step == PAIRS + 3)
    def _():
        load.wait()
        ngrad_ref[...] = jnp.zeros_like(ngrad_ref)

    @pl.when(step >= PAIRS + 3)
    def _():
        at = pl.ds(pl.multiple_of((step - PAIRS - 3) * TB, TB), TB)
        gradient = mm_t(dqkv[at, :], weight[...])
        unit, inverse = norm_parts(tokens_ref[...].astype(F32))
        total = total_ref[...] + norm_back(unit, inverse, norms_ref[0:1, :], gradient)
        out_ref[...] = total.astype(BF16)
        ngrad_ref[0:1, :] += jnp.sum(gradient * unit, axis=0, keepdims=True)
        ngrad_ref[1:2, :] += jnp.sum(gradient, axis=0, keepdims=True)

    for number, plan in enumerate(SELF_PLAN):
        pl.when(step == number)(functools.partial(carried.steps, plan))
    pl.when(step == len(SELF_PLAN) - 1)(carried.close)


def self_back(first, logs, qkv, mixed, grad, normed, tokens, total, norms, early, wide_share, shares, narrow):
    rows, d = mixed.shape
    shard_rows = d // (8 * narrow)

    def pair(s):
        return jnp.minimum(s, PAIRS - 1)

    def token(s):
        return jnp.maximum(s - PAIRS - 3, 0)

    anywhere = pl.BlockSpec(memory_space=pl.ANY)
    by_pair = pl.BlockSpec((SEQ, 128), lambda s: (0, pair(s)))
    by_token = pl.BlockSpec((TB, d), lambda s: (token(s), 0))
    return pl.pallas_call(
        functools.partial(self_back_kernel, narrow),
        grid=(PAIRS + 3 + rows // TB,),
        in_specs=[
            pl.BlockSpec((1, 1, SEQ), lambda s: (0, 0, 0)),
            pl.BlockSpec((1, 1, 8, SEQ), lambda s: (0, pair(s), 0, 0)),
            pl.BlockSpec((SEQ, 384), lambda s: (0, pair(s))),
            by_pair,
            by_pair,
            whole(rows, d),
            by_token,
            by_token,
            whole(8, d),
            anywhere,
            anywhere,
            anywhere,
        ],
        out_specs=[
            pl.BlockSpec((d, d), lambda s: (0, jnp.clip(s - PAIRS, 0, 2))),
            by_token,
            whole(8, d),
            whole(shard_rows, SELF_WIDE * d),
            *[whole(shard_rows, d)] * 5,
        ],
        out_shape=[
            shape(d, 3 * d, BF16),
            shape(rows, d, BF16),
            shape(8, d, F32),
            shape(shard_rows, SELF_WIDE * d, F32),
            *[shape(shard_rows, d, F32)] * 5,
        ],
        scratch_shapes=[
            pltpu.VMEM((SEQ, 128), F32),
            pltpu.VMEM((SEQ, 128), F32),
            pltpu.VMEM((rows, 3 * d), BF16),
            pltpu.VMEM((d, 3 * d), BF16),
            pltpu.SemaphoreType.DMA,
            *scatter_scratch(SELF_CHUNKS, narrow, shard_rows, d),
        ],
        name="self_back",
        compiler_params=pltpu.CompilerParams(collective_id=3, has_side_effects=True, vmem_limit_bytes=60 << 20),
        cost_estimate=cost(40 * rows * d * d, 100 << 20),
    )(
        first,
        logs,
        qkv,
        mixed,
        grad,
        normed,
        tokens,
        total,
        norms,
        early,
        share_views(wide_share, narrow, shard_rows),
        shares.reshape(5, 2, 2, 2, narrow, shard_rows, d),
    )


TAIL_CHUNKS = 6
TAIL_PLAN = [(0, 0), (1, 0)]
for _k in range(TAIL_CHUNKS + 5):
    TAIL_PLAN += [(_k + 2, 0)] if _k + 2 < TAIL_CHUNKS else []
    TAIL_PLAN += [(_k, 1)] if _k < TAIL_CHUNKS else []
    TAIL_PLAN += [(_k - 1, 2)] if 0 <= _k - 1 < TAIL_CHUNKS else []
    TAIL_PLAN += [(_k - 3, 3)] if 0 <= _k - 3 < TAIL_CHUNKS else []


def tail_kernel(
    narrow,
    norm_refs,
    qkv_any,
    query_ref,
    key_ref,
    value_ref,
    norm_out_ref,
    nval,
    nin,
    norm_send_sems,
    norm_recv_sems,
    *scratch,
):
    width = scratch[0].shape[-1]
    outs = (query_ref, key_ref, value_ref)

    def keep(i, value):
        for n in range(width // 128):
            pair, kind = divmod(i * width // 128 + n, 3)
            outs[kind][:, pair * 128 : (pair + 1) * 128] = value[:, n * 128 : (n + 1) * 128]

    carried = Carried([columns_of(qkv_any, i * width, width) for i in range(TAIL_CHUNKS)], scratch, keep, narrow)
    w, z = carried.scatter.w, carried.scatter.z

    def norm_copy(stage, number, target):
        return pltpu.make_async_remote_copy(
            src_ref=nval.at[stage],
            dst_ref=nin.at[number],
            send_sem=norm_send_sems.at[number],
            recv_sem=norm_recv_sems.at[number],
            device_id=target,
            device_id_type=pl.DeviceIdType.MESH,
        )

    norm_copies = [[norm_copy(0, 0, (w ^ 1, z))], [norm_copy(1, 1, (w ^ 2, z))], [norm_copy(2, 2, (w ^ 4, z))]]
    norm_copies.append([norm_copy(3, 2 + mask, (w, z ^ mask)) for mask in range(1, narrow)])

    def norm_step(stage):
        if stage == 0:
            for n, ref in enumerate(norm_refs):
                nval[0, 2 * n : 2 * n + 2, :] = ref[0:2, :]
            nval[0, 6:8, :] = jnp.zeros_like(norm_refs[0][0:2, :])
        else:
            for copy in norm_copies[stage - 1]:
                copy.wait_recv()
            value = nval[stage - 1]
            if stage < 4:
                nval[stage] = value + nin[stage - 1]
            else:
                for mask in range(1, narrow):
                    value = value + nin[2 + mask]
                norm_out_ref[...] = value
        if stage < 4:
            for copy in norm_copies[stage]:
                copy.start()

    carried.open()
    for number, action in enumerate(TAIL_PLAN):
        carried.steps([action])
        if number % 4 == 0 and number // 4 <= 4:
            norm_step(number // 4)
    carried.close()
    for copies in norm_copies:
        for copy in copies:
            copy.wait_send()


def tail(qkv_share, norm_grads, narrow):
    d = qkv_share.shape[0]
    shard_rows = d // (8 * narrow)
    width = 3 * d // TAIL_CHUNKS
    anywhere, vmem = pl.BlockSpec(memory_space=pl.ANY), pl.BlockSpec(memory_space=pltpu.VMEM)

    def kernel(one, two, three, *refs):
        tail_kernel(narrow, (one, two, three), *refs)

    return pl.pallas_call(
        kernel,
        in_specs=[vmem] * 3 + [anywhere],
        out_specs=[vmem] * 4,
        out_shape=[*[shape(shard_rows, d, F32)] * 3, shape(8, d, F32)],
        scratch_shapes=[
            pltpu.VMEM((4, 8, d), F32),
            pltpu.VMEM((2 + narrow, 8, d), F32),
            pltpu.SemaphoreType.DMA((2 + narrow,)),
            pltpu.SemaphoreType.DMA((2 + narrow,)),
            *scatter_scratch(TAIL_CHUNKS, narrow, shard_rows, width),
        ],
        name="tail",
        compiler_params=pltpu.CompilerParams(collective_id=1, has_side_effects=True, vmem_limit_bytes=40 << 20),
        cost_estimate=cost(4 * d * d * d, 100 << 20),
    )(*norm_grads, share_views(qkv_share, narrow, shard_rows))


def on_device(
    mesh_axes,
    tokens,
    memory,
    cotangent,
    live_length,
    pair_starts,
    source_starts,
    group_bounds,
    group_counts,
    self_query,
    self_key,
    self_value,
    self_output,
    cross_query,
    cross_key,
    cross_value,
    cross_output,
    hidden_in,
    hidden_out,
    first_gain,
    first_shift,
    second_gain,
    second_shift,
    third_gain,
    third_shift,
):
    names = tuple(axis for axis, _ in mesh_axes)
    row_count = live_length.shape[0]
    shard_rows = self_query.shape[0]
    device_count = 1
    for _, size in mesh_axes:
        device_count *= size

    def staged(*partial):
        return StagedSum(partial, mesh_axes)

    digits = jnp.stack([live_length // 256, live_length % 256], axis=1).astype(BF16)
    digits = jnp.pad(digits, ((0, shard_rows - row_count), (0, 0)))
    norms = jnp.stack([first_gain, first_shift, second_gain, second_shift, third_gain, third_shift], axis=1)
    extra = jnp.pad(jnp.concatenate([norms, digits], axis=1), ((0, 0), (0, 120)))
    early = early_gather(
        jnp.concatenate(
            [
                by_pairs(self_query, self_key, self_value),
                self_output,
                by_pairs(cross_key, cross_value),
                cross_query,
                cross_output,
                extra,
            ],
            axis=1,
        ),
        mesh_axes,
    )
    late = [lax.all_gather(part, names, axis=0, tiled=True) for part in (hidden_in, hidden_out)]

    norms = early[:, EXTRA * 128 : EXTRA * 128 + 8].astype(F32).T
    live_total = jnp.sum(norms[6]) * 256.0 + jnp.sum(norms[7])
    device = lax.axis_index(names)
    member = (group_bounds[:-1] <= device) & (device < group_bounds[1:])
    pair_tokens = jnp.sum(jnp.where(member, group_counts, 0))
    token_all = row_count * SEQ * device_count
    row_weight = pair_tokens.astype(F32) * (token_all / 1000.0) / live_total
    first, bounds = row_bounds(pair_starts, source_starts, live_length)

    normed_one, qkv = project(tokens, norms, early)
    self_mixed, self_logs = self_forward(first, qkv, row_count)
    after_self, normed_two, cross_q, cross_kv = middle(self_mixed, tokens, memory, norms, early)
    cross_mixed, cross_logs = cross_forward(bounds, cross_q, cross_kv, row_count)
    layer_output, normed_three, activated, hidden_grad, branch_three, cross_total, branch_two, mixed_grad, norm_three = feed(
        live_length, row_weight[None], cross_mixed, after_self, cotangent, norms, early, late
    )

    reduce_share, expand_share = outer_sum(activated, branch_three), outer_sum(normed_three, hidden_grad)
    if mesh_axes[0][1] == 8 and row_count == 1 and shard_rows % 32 == 0:
        narrow = mesh_axes[1][1]
        self_total, mixed_grad, memory_grad, norm_two, shares, reduce_shard, expand_low = cross_back(
            bounds,
            cross_logs,
            cross_q,
            cross_kv,
            cross_mixed,
            mixed_grad,
            after_self,
            cross_total,
            norms,
            branch_two,
            normed_two,
            memory,
            self_mixed,
            early,
            reduce_share,
            expand_share,
            narrow,
        )
        (
            qkv_share,
            tokens_grad,
            norm_one,
            expand_high,
            cross_output_shard,
            cross_query_shard,
            cross_key_shard,
            cross_value_shard,
            output_shard,
        ) = self_back(
            first,
            self_logs,
            qkv,
            self_mixed,
            mixed_grad,
            normed_one,
            tokens,
            self_total,
            norms,
            early,
            expand_share,
            shares,
            narrow,
        )
        query_shard, key_shard, value_shard, norm_grads = tail(qkv_share, (norm_one, norm_two, norm_three), narrow)
        expand_shard = jnp.concatenate([expand_low, expand_high], axis=1)
    else:
        reduce_sum, expand_sum = staged(reduce_share), staged(expand_share)
        cq_grad, ckv_grad = cross_backward(bounds, cross_logs, cross_q, cross_kv, cross_mixed, mixed_grad, row_count)
        cq_grad, ckv_grad = fence((cq_grad, ckv_grad), reduce_sum, expand_sum)
        cross_shares = [outer_sum(cross_mixed, branch_two), outer_sum(normed_two, cq_grad)]
        cross_shares += [outer_sum(memory, part) for part in (ckv_grad[:, :WIDTH], ckv_grad[:, WIDTH:])]
        cross_sum = staged(*cross_shares)
        self_total, branch_one, mixed_grad, memory_grad, norm_two = cross_close(
            cq_grad, ckv_grad, after_self, cross_total, norms, early
        )
        mixed_grad = fence(mixed_grad, reduce_sum, expand_sum, cross_sum)
        qkv_grad = self_backward(first, self_logs, qkv, self_mixed, mixed_grad, row_count)
        qkv_grad = fence(qkv_grad, reduce_sum, expand_sum, cross_sum)
        last_sum = staged(
            outer_sum(self_mixed, branch_one),
            *[outer_sum(normed_one, qkv_grad[:, n * WIDTH : (n + 1) * WIDTH]) for n in range(3)],
        )
        tokens_grad, norm_one = self_close(qkv_grad, tokens, self_total, norms, early)
        norm_grads = sum_everywhere(jnp.concatenate([norm_one[:2], norm_two[:2], norm_three[:2]]), mesh_axes)
        output_shard, *qkv_shards = last_sum.result().reshape(4, shard_rows, WIDTH)
        query_shard, key_shard, value_shard = from_pairs(jnp.concatenate(qkv_shards, axis=1), 3)
        reduce_shard = reduce_sum.result()
        expand_shard = expand_sum.result()
        cross_output_shard, cross_query_shard, *cross_shards = cross_sum.result().reshape(4, shard_rows, WIDTH)
        cross_key_shard, cross_value_shard = from_pairs(jnp.concatenate(cross_shards, axis=1), 2)

    norm_shards = lax.dynamic_slice_in_dim(norm_grads, device * shard_rows, shard_rows, axis=1)
    return (
        layer_output,
        tokens_grad,
        memory_grad,
        query_shard,
        key_shard,
        value_shard,
        output_shard,
        cross_query_shard,
        cross_key_shard,
        cross_value_shard,
        cross_output_shard,
        expand_shard,
        reduce_shard,
        *[norm_shards[n] for n in range(6)],
    )


def solution(mesh):
    names = ("wide", "narrow")
    mesh_axes = tuple((axis, mesh.shape[axis]) for axis in names)
    split, vector = P(names, None), P(names)
    return jax.shard_map(
        functools.partial(on_device, mesh_axes),
        mesh=mesh,
        in_specs=(split,) * 3 + (vector,) + (split,) * 2 + (P(), P()) + (split,) * 10 + (vector,) * 6,
        out_specs=(split,) * 13 + (vector,) * 6,
        check_vma=False,
    )
```

```python
import functools
import jax
import jax.numpy as jnp
from jax import lax
from jax.experimental import pallas as pl
from jax.experimental.pallas import tpu as pltpu
from jax.sharding import PartitionSpec as P

SEQ = 1024
MEM = 512
HEADS = 16
HEAD_DIM = 64
WIDTH = HEADS * HEAD_DIM
EPSILON = 1e-05
BQ = 256
LOG2E = 1.4426950408889634
SCALE2 = HEAD_DIM**-0.5 * LOG2E
FILLER = -1e30
F32, BF16 = jnp.float32, jnp.bfloat16


def mm(a, b):
    return jnp.dot(a, b, preferred_element_type=F32)


def mm_t(a, b):
    return lax.dot_general(a, b, (((1,), (1,)), ((), ())), preferred_element_type=F32)


def halves(x):
    low = lax.broadcasted_iota(jnp.int32, x.shape, 1) < HEAD_DIM
    zero = jnp.zeros_like(x)
    return (jnp.where(low, x, zero), jnp.where(low, zero, x))


def in_turn(tasks, front, back, ahead):
    waiting = []
    for task in tasks:
        waiting.append((task, front(*task)))
        if len(waiting) > ahead:
            task, held = waiting.pop(0)
            back(*task, *held)
    for task, held in waiting:
        back(*task, *held)


BLOCKS = [slice(i * BQ, (i + 1) * BQ) for i in range(SEQ // BQ)]
TASKS = [(i, h) for i in range(SEQ // BQ) for h in range(2)]


def self_extent(i):
    return (i + 1) * BQ


def cross_extent(i):
    return MEM


def self_visible(first_ref, i):
    shape = (self_extent(i), BQ)
    key = lax.broadcasted_iota(jnp.int32, shape, 0)
    return (key >= first_ref[0, :, BLOCKS[i]]) & (key <= lax.broadcasted_iota(jnp.int32, shape, 1) + i * BQ)


def cross_visible(bounds_ref, i):
    key = lax.broadcasted_iota(jnp.int32, (MEM, BQ), 0)
    return (key >= bounds_ref[0, 0:1, BLOCKS[i]]) & (key < bounds_ref[0, 1:2, BLOCKS[i]])


def attend(q_of, k, v, visible, extent, keep_out, keep_log):
    k_parts, v_t = halves(k), v.T
    outs = {}

    def front(i, h):
        s = jnp.where(visible(i), mm_t(k_parts[h][: extent(i)], q_of(BLOCKS[i])) * SCALE2, FILLER)
        return s, jnp.max(s, axis=0, keepdims=True)

    def back(i, h, s, peak):
        p = jnp.exp2(s - peak)
        total = jnp.sum(p, axis=0, keepdims=True)
        keep_log(h, BLOCKS[i], peak + jnp.log2(total))
        outs[h] = mm(v_t[h * 64 : (h + 1) * 64, : extent(i)], p.astype(BF16)) * (1.0 / total)
        if h == 1:
            keep_out(BLOCKS[i], jnp.concatenate([outs[0], outs[1]], axis=0).T.astype(BF16))

    in_turn(TASKS, front, back, 3)


def attend_back(q_of, k, v, g_ref, out_ref, log_ref, visible, extent, keep_dq, dk_ref, dv_ref):
    k_parts, k_t, v_parts = halves(k), k.T, halves(v)
    deltas, dq = {}, {}
    dk_ref[...] = jnp.zeros_like(dk_ref)
    dv_ref[...] = jnp.zeros_like(dv_ref)

    def front(i, h):
        q, g = q_of(BLOCKS[i]), g_ref[BLOCKS[i], :]
        if h == 0:
            prod = (g.astype(F32) * out_ref[BLOCKS[i], :].astype(F32)).T
            deltas[i] = [jnp.sum(prod[n * 64 : (n + 1) * 64], axis=0, keepdims=True) for n in range(2)]
        s = jnp.where(visible(i), mm_t(k_parts[h][: extent(i)], q) * SCALE2, FILLER)
        p = jnp.exp2(s - log_ref[0, 0, h : h + 1, BLOCKS[i]])
        dp = mm_t(v_parts[h][: extent(i)], g)
        return p.astype(BF16), (p * (dp - deltas[i][h])).astype(BF16)

    def back(i, h, p, ds):
        n = extent(i)
        dv_ref[:n, :] += mm(p, halves(g_ref[BLOCKS[i], :])[h])
        dk_ref[:n, :] += mm(ds, halves(q_of(BLOCKS[i]))[h])
        dq[h] = mm(k_t[h * 64 : (h + 1) * 64, :n], ds)
        if h == 1:
            keep_dq(BLOCKS[i], (jnp.concatenate([dq[0], dq[1]], axis=0) * HEAD_DIM**-0.5).T.astype(BF16))

    in_turn(TASKS, front, back, 2)


def keepers(out_ref, log_ref):
    def keep_out(rows, value):
        out_ref[rows, :] = value

    def keep_log(h, rows, value):
        log_ref[0, 0, h : h + 1, rows] = value

    return keep_out, keep_log


def self_forward_kernel(first_ref, qkv_ref, out_ref, log_ref):
    attend(
        lambda rows: qkv_ref[rows, 0:128],
        qkv_ref[:, 128:256],
        qkv_ref[:, 256:384],
        functools.partial(self_visible, first_ref),
        self_extent,
        *keepers(out_ref, log_ref),
    )


def cross_forward_kernel(bounds_ref, q_ref, kv_ref, out_ref, log_ref):
    attend(
        lambda rows: q_ref[rows, :],
        kv_ref[:, 0:128],
        kv_ref[:, 128:256],
        functools.partial(cross_visible, bounds_ref),
        cross_extent,
        *keepers(out_ref, log_ref),
    )


PAIRS = HEADS // 2
LOG_SPEC = pl.BlockSpec((1, 1, 8, SEQ), lambda r, p: (r, p, 0, 0))
ROW_SPEC = pl.BlockSpec((SEQ, 128), lambda r, p: (r, p))
QKV_SPEC = pl.BlockSpec((SEQ, 384), lambda r, p: (r, p))
KV_SPEC = pl.BlockSpec((MEM, 256), lambda r, p: (r, p))
FIRST_SPEC = pl.BlockSpec((1, 1, SEQ), lambda r, p: (r, 0, 0))
BOUNDS_SPEC = pl.BlockSpec((1, 8, SEQ), lambda r, p: (r, 0, 0))


def attention_call(kernel, name, in_specs, args, row_count):
    return pl.pallas_call(
        kernel,
        grid=(row_count, PAIRS),
        in_specs=in_specs,
        out_specs=[ROW_SPEC, LOG_SPEC],
        out_shape=[
            jax.ShapeDtypeStruct((row_count * SEQ, WIDTH), BF16),
            jax.ShapeDtypeStruct((row_count, PAIRS, 8, SEQ), F32),
        ],
        name=name,
        compiler_params=pltpu.CompilerParams(vmem_limit_bytes=40 << 20),
        cost_estimate=pl.CostEstimate(flops=20 << 30, bytes_accessed=row_count * (8 << 20), transcendentals=8 << 20),
    )(*args)


def self_forward(first, qkv, row_count):
    return attention_call(self_forward_kernel, "self_forward", [FIRST_SPEC, QKV_SPEC], (first, qkv), row_count)


def cross_forward(bounds, q, kv, row_count):
    return attention_call(
        cross_forward_kernel, "cross_forward", [BOUNDS_SPEC, ROW_SPEC, KV_SPEC], (bounds, q, kv), row_count
    )


def self_backward_kernel(first_ref, log_ref, qkv_ref, out_ref, grad_ref, dqkv_ref, dk_ref, dv_ref):
    def keep_dq(rows, value):
        dqkv_ref[rows, 0:128] = value

    attend_back(
        lambda rows: qkv_ref[rows, 0:128],
        qkv_ref[:, 128:256],
        qkv_ref[:, 256:384],
        grad_ref,
        out_ref,
        log_ref,
        functools.partial(self_visible, first_ref),
        self_extent,
        keep_dq,
        dk_ref,
        dv_ref,
    )
    dqkv_ref[:, 128:256] = (dk_ref[...] * HEAD_DIM**-0.5).astype(BF16)
    dqkv_ref[:, 256:384] = dv_ref[...].astype(BF16)


def self_backward(first, logs, qkv, out, grad, row_count):
    return pl.pallas_call(
        self_backward_kernel,
        grid=(row_count, PAIRS),
        in_specs=[FIRST_SPEC, LOG_SPEC, QKV_SPEC, ROW_SPEC, ROW_SPEC],
        out_specs=QKV_SPEC,
        scratch_shapes=[pltpu.VMEM((SEQ, 128), F32), pltpu.VMEM((SEQ, 128), F32)],
        out_shape=jax.ShapeDtypeStruct((row_count * SEQ, 3 * WIDTH), BF16),
        name="self_backward",
        compiler_params=pltpu.CompilerParams(vmem_limit_bytes=40 << 20),
        cost_estimate=pl.CostEstimate(flops=40 << 30, bytes_accessed=row_count * (16 << 20), transcendentals=8 << 20),
    )(first, logs, qkv, out, grad)


def cross_backward_pair(bounds_ref, log_ref, q_ref, kv_ref, out_ref, grad_ref, keep_dq, dkv_ref, dk_ref, dv_ref):
    attend_back(
        lambda rows: q_ref[rows, :],
        kv_ref[:, 0:128],
        kv_ref[:, 128:256],
        grad_ref,
        out_ref,
        log_ref,
        functools.partial(cross_visible, bounds_ref),
        cross_extent,
        keep_dq,
        dk_ref,
        dv_ref,
    )


def cross_backward_kernel(bounds_ref, log_ref, q_ref, kv_ref, out_ref, grad_ref, dq_ref, dkv_ref, dk_ref, dv_ref):
    def keep_dq(rows, value):
        dq_ref[rows, :] = value

    cross_backward_pair(bounds_ref, log_ref, q_ref, kv_ref, out_ref, grad_ref, keep_dq, dkv_ref, dk_ref, dv_ref)
    dkv_ref[:, 0:128] = (dk_ref[...] * HEAD_DIM**-0.5).astype(BF16)
    dkv_ref[:, 128:256] = dv_ref[...].astype(BF16)


def cross_backward(bounds, logs, q, kv, out, grad, row_count):
    return pl.pallas_call(
        cross_backward_kernel,
        grid=(row_count, PAIRS),
        in_specs=[BOUNDS_SPEC, LOG_SPEC, ROW_SPEC, KV_SPEC, ROW_SPEC, ROW_SPEC],
        out_specs=[ROW_SPEC, KV_SPEC],
        scratch_shapes=[pltpu.VMEM((MEM, 128), F32), pltpu.VMEM((MEM, 128), F32)],
        out_shape=[
            jax.ShapeDtypeStruct((row_count * SEQ, WIDTH), BF16),
            jax.ShapeDtypeStruct((row_count * MEM, 2 * WIDTH), BF16),
        ],
        name="cross_backward",
        compiler_params=pltpu.CompilerParams(vmem_limit_bytes=40 << 20),
        cost_estimate=pl.CostEstimate(flops=40 << 30, bytes_accessed=row_count * (12 << 20), transcendentals=8 << 20),
    )(bounds, logs, q, kv, out, grad)


def row_bounds(pair_starts, source_starts, live_length):
    places = jnp.arange(SEQ, dtype=jnp.int32)
    counted = jnp.sum((pair_starts[:, :, None] <= places).astype(jnp.int32), axis=1)
    live = places < live_length[:, None]
    begun = jnp.max(jnp.where(pair_starts[:, :, None] <= places, pair_starts[:, :, None], 0), axis=1)
    first = jnp.where(live, begun, live_length[:, None])
    nseg = pair_starts.shape[1]
    pick = jnp.arange(nseg)[None, :, None] == (counted - 1)[:, None, :]
    ends = jnp.concatenate([source_starts[:, 1:], jnp.full_like(source_starts[:, :1], MEM)], axis=1)
    start = jnp.sum(jnp.where(pick, source_starts[:, :, None], 0), axis=1)
    end = jnp.sum(jnp.where(pick, ends[:, :, None], 0), axis=1)
    start = jnp.where(live, start, 0)
    end = jnp.where(live, end, MEM)
    bounds = jnp.pad(jnp.stack([start, end], axis=1), ((0, 0), (0, 6), (0, 0)))
    return first[:, None, :], bounds


TB = 256


def norm_parts(values):
    center = values - jnp.mean(values, axis=-1, keepdims=True)
    inverse = lax.rsqrt(jnp.mean(center * center, axis=-1, keepdims=True) + EPSILON)
    return center * inverse, inverse


def norm_back(unit, inverse, gain, gradient):
    scaled = gradient * gain
    return inverse * (
        scaled
        - jnp.mean(scaled, axis=-1, keepdims=True)
        - unit * jnp.mean(scaled * unit, axis=-1, keepdims=True)
    )


def add_norm_grads(ref, unit, gradient):
    @pl.when(pl.program_id(0) == 0)
    def _():
        ref[...] = jnp.zeros_like(ref)

    ref[0:1, :] += jnp.sum(gradient * unit, axis=0, keepdims=True)
    ref[1:2, :] += jnp.sum(gradient, axis=0, keepdims=True)


def tile(rows, columns, at=0):
    return pl.BlockSpec((rows, columns), lambda b: (b, at))


def whole(rows, columns, at=0):
    return pl.BlockSpec((rows, columns), lambda b: (0, at), pipeline_mode=pl.Buffered(1))


def shape(rows, columns, dtype):
    return jax.ShapeDtypeStruct((rows, columns), dtype)


def params(mib):
    return pltpu.CompilerParams(vmem_limit_bytes=mib << 20)


def cost(flops, moved):
    return pl.CostEstimate(flops=int(flops), bytes_accessed=int(moved), transcendentals=0)


def project_kernel(tokens_ref, norms_ref, weight_ref, normed_ref, out_ref):
    unit, _ = norm_parts(tokens_ref[...].astype(F32))
    normed = (unit * norms_ref[0:1, :] + norms_ref[1:2, :]).astype(BF16)
    normed_ref[...] = normed
    for part in range(3):
        at = slice(part * 1024, (part + 1) * 1024)
        out_ref[:, at] = mm(normed, weight_ref[:, at]).astype(BF16)


def project(tokens, norms, early):
    rows, d = tokens.shape
    return pl.pallas_call(
        project_kernel,
        grid=(rows // TB,),
        in_specs=[tile(TB, d), whole(8, d), whole(d, 3 * d)],
        out_specs=[tile(TB, d), tile(TB, 3 * d)],
        out_shape=[shape(rows, d, BF16), shape(rows, 3 * d, BF16)],
        name="project",
        compiler_params=params(40),
        cost_estimate=cost(6 * rows * d * d, 16 << 20),
    )(tokens, norms, early)


def middle_kernel(
    mixed_ref, tokens_ref, memory_ref, norms_ref, wo_ref, wq_ref, wkv_ref, after_ref, normed_ref, q_ref, kv_ref
):
    after = tokens_ref[...].astype(F32) + mm(mixed_ref[...], wo_ref[...])
    after_ref[...] = after
    kv_ref[...] = mm(memory_ref[...], wkv_ref[...]).astype(BF16)
    unit, _ = norm_parts(after)
    normed = (unit * norms_ref[2:3, :] + norms_ref[3:4, :]).astype(BF16)
    normed_ref[...] = normed
    q_ref[...] = mm(normed, wq_ref[...]).astype(BF16)


def middle(mixed, tokens, memory, norms, early):
    rows, d = tokens.shape
    mem_rows = memory.shape[0]
    steps = rows // TB
    mb = mem_rows // steps
    return pl.pallas_call(
        middle_kernel,
        grid=(steps,),
        in_specs=[
            tile(TB, d),
            tile(TB, d),
            tile(mb, d),
            whole(8, d),
            whole(d, d, OUT_SELF),
            whole(d, d, QUERY_CROSS),
            whole(d, 2 * d, KV_CROSS),
        ],
        out_specs=[tile(TB, d), tile(TB, d), tile(TB, d), tile(mb, 2 * d)],
        out_shape=[shape(rows, d, F32), shape(rows, d, BF16), shape(rows, d, BF16), shape(mem_rows, 2 * d, BF16)],
        name="middle",
        compiler_params=params(40),
        cost_estimate=cost(6 * rows * d * d, 20 << 20),
    )(mixed, tokens, memory, norms, early, early, early)


GELU_A = 0.7978845608028654
GELU_B = 0.044715


def hidden_parts(win_ref, wout_ref, part, d):
    if len(win_ref.shape) == 2:
        at = slice(part * d, (part + 1) * d)
        return win_ref[:, at], wout_ref[at, :]
    devices, quad, _ = win_ref.shape
    rows, share = quad // 4, devices // 4
    win = win_ref[:, part * rows : (part + 1) * rows, :].reshape(d, d)
    return win, wout_ref[part * share : (part + 1) * share].reshape(d, d)


def feed_kernel(
    live_ref,
    weight_ref,
    mixed_ref,
    before_ref,
    cot_ref,
    norms_ref,
    wo_ref,
    win_ref,
    wout_ref,
    out_ref,
    normed_ref,
    act_ref,
    hid_ref,
    b3_ref,
    total_ref,
    b2_ref,
    grad_ref,
    ngrad_ref,
):
    block = pl.program_id(0)
    per_row = SEQ // TB
    row = block // per_row
    places = lax.broadcasted_iota(jnp.int32, (TB, 1), 0) + (block % per_row) * TB
    live = (places < live_ref[row]).astype(F32)
    out_grad = cot_ref[...].astype(F32) * live * weight_ref[0]
    branch = out_grad.astype(BF16)
    b3_ref[...] = branch
    after = before_ref[...] + mm(mixed_ref[...], wo_ref[...])
    unit, inverse = norm_parts(after)
    normed = (unit * norms_ref[4:5, :] + norms_ref[5:6, :]).astype(BF16)
    normed_ref[...] = normed
    d = normed.shape[1]
    result, back = after, None
    for part in range(act_ref.shape[1] // d):
        at = slice(part * d, (part + 1) * d)
        win, wout = hidden_parts(win_ref, wout_ref, part, d)
        x = mm(normed, win)
        square = x * x
        t = jnp.tanh(GELU_A * x * (1.0 + GELU_B * square))
        half = 0.5 * (1.0 + t)
        act = (x * half).astype(BF16)
        slope = half + (0.5 * GELU_A) * x * (1.0 - t * t) * (1.0 + (3.0 * GELU_B) * square)
        act_ref[:, at] = act
        hid = (mm_t(branch, wout) * slope).astype(BF16)
        hid_ref[:, at] = hid
        result = result + mm(act, wout)
        term = mm_t(hid, win)
        back = term if back is None else back + term
    out_ref[...] = result.astype(BF16)
    total = out_grad + norm_back(unit, inverse, norms_ref[4:5, :], back)
    total_ref[...] = total
    b2 = total.astype(BF16)
    b2_ref[...] = b2
    grad_ref[...] = mm_t(b2, wo_ref[...]).astype(BF16)
    add_norm_grads(ngrad_ref, unit, back)


def feed(live_length, row_weight, mixed, before, cotangent, norms, early, late):
    rows, d = cotangent.shape
    ff = 4 * d
    if len(late) == 1:
        devices, block, _ = late[0].shape
        late = late * 2
        late_specs = [
            pl.BlockSpec((devices, block // 2, d), lambda b, n=n: (0, n, 0), pipeline_mode=pl.Buffered(1)) for n in range(2)
        ]
    else:
        late_specs = [whole(d, ff), whole(ff, d)]
    smem = pl.BlockSpec(memory_space=pltpu.SMEM)
    return pl.pallas_call(
        feed_kernel,
        grid=(rows // TB,),
        in_specs=[
            smem,
            smem,
            tile(TB, d),
            tile(TB, d),
            tile(TB, d),
            whole(8, d),
            whole(d, d, OUT_CROSS),
            *late_specs,
        ],
        out_specs=[
            tile(TB, d),
            tile(TB, d),
            tile(TB, ff),
            tile(TB, ff),
            tile(TB, d),
            tile(TB, d),
            tile(TB, d),
            tile(TB, d),
            whole(8, d),
        ],
        out_shape=[
            shape(rows, d, BF16),
            shape(rows, d, BF16),
            shape(rows, ff, BF16),
            shape(rows, ff, BF16),
            shape(rows, d, BF16),
            shape(rows, d, F32),
            shape(rows, d, BF16),
            shape(rows, d, BF16),
            shape(8, d, F32),
        ],
        name="feed",
        compiler_params=params(58),
        cost_estimate=cost(38 * rows * d * d, 50 << 20),
    )(live_length, row_weight, mixed, before, cotangent, norms, early, *late)


def cross_close_kernel(
    dq_ref, dkv_ref, before_ref, total_ref, norms_ref, wq_ref, wkv_ref, wo_ref, out_ref, b1_ref, grad_ref, mem_ref, ngrad_ref
):
    gradient = mm_t(dq_ref[...], wq_ref[...])
    mem_ref[...] = mm_t(dkv_ref[...], wkv_ref[...]).astype(BF16)
    unit, inverse = norm_parts(before_ref[...])
    total = total_ref[...] + norm_back(unit, inverse, norms_ref[2:3, :], gradient)
    out_ref[...] = total
    b1 = total.astype(BF16)
    b1_ref[...] = b1
    grad_ref[...] = mm_t(b1, wo_ref[...]).astype(BF16)
    add_norm_grads(ngrad_ref, unit, gradient)


def cross_close(dq, dkv, before, total, norms, early):
    rows, d = dq.shape
    mem_rows = dkv.shape[0]
    steps = rows // TB
    mb = mem_rows // steps
    return pl.pallas_call(
        cross_close_kernel,
        grid=(steps,),
        in_specs=[
            tile(TB, d),
            tile(mb, 2 * d),
            tile(TB, d),
            tile(TB, d),
            whole(8, d),
            whole(d, d, QUERY_CROSS),
            whole(d, 2 * d, KV_CROSS),
            whole(d, d, OUT_SELF),
        ],
        out_specs=[tile(TB, d), tile(TB, d), tile(TB, d), tile(mb, d), whole(8, d)],
        out_shape=[
            shape(rows, d, F32),
            shape(rows, d, BF16),
            shape(rows, d, BF16),
            shape(mem_rows, d, BF16),
            shape(8, d, F32),
        ],
        name="cross_close",
        compiler_params=params(40),
        cost_estimate=cost(6 * rows * d * d, 24 << 20),
    )(dq, dkv, before, total, norms, early, early, early)


def self_close_kernel(dqkv_ref, before_ref, total_ref, norms_ref, w_ref, out_ref, ngrad_ref):
    gradient = mm_t(dqkv_ref[...], w_ref[...])
    unit, inverse = norm_parts(before_ref[...].astype(F32))
    total = total_ref[...] + norm_back(unit, inverse, norms_ref[0:1, :], gradient)
    out_ref[...] = total.astype(BF16)
    add_norm_grads(ngrad_ref, unit, gradient)


def self_close(dqkv, before, total, norms, early):
    rows, d = total.shape
    return pl.pallas_call(
        self_close_kernel,
        grid=(rows // TB,),
        in_specs=[tile(TB, 3 * d), tile(TB, d), tile(TB, d), whole(8, d), whole(d, 3 * d)],
        out_specs=[tile(TB, d), whole(8, d)],
        out_shape=[shape(rows, d, BF16), shape(8, d, F32)],
        name="self_close",
        compiler_params=params(40),
        cost_estimate=cost(6 * rows * d * d, 20 << 20),
    )(dqkv, before, total, norms, early)


OUT_SELF, QUERY_CROSS, KV_CROSS, OUT_CROSS = 0, 1, 1, 4


def greet_all(narrow):
    w, z = lax.axis_index("wide"), lax.axis_index("narrow")
    barrier = pltpu.get_barrier_semaphore()
    others = [(w ^ 1, z), (w ^ 2, z), (w ^ 4, z)] + [(w, z ^ mask) for mask in range(1, narrow)]
    for other in others:
        pl.semaphore_signal(barrier, inc=1, device_id=other, device_id_type=pl.DeviceIdType.MESH)
    pl.semaphore_wait(barrier, len(others))


class Gather:
    def __init__(self, shard_ref, out_ref, send_sems, recv_sems, narrow):
        self.shard_ref, self.out_ref = shard_ref, out_ref
        self.send_sems, self.recv_sems = send_sems, recv_sems
        self.narrow = narrow
        self.rows = shard_ref.shape[0]
        self.half = self.rows // 2
        self.w, self.z = w, z = lax.axis_index("wide"), lax.axis_index("narrow")
        self.core, self.x, self.y, self.xy = w ^ 1, w ^ 2, w ^ 4, w ^ 6
        self.above, self.below = (w, z + 1), (w, z - 1)
        self.at_core, self.at_x, self.at_y = (self.core, z), (self.x, z), (self.y, z)
        self.up, self.down, self.to_x, self.to_y, self.on_y, self.on_x, self.to_core = [k * narrow for k in range(7)]

    def move(self, holder, s, number, target, first=0, count=None, own=False):
        count = self.rows if count is None else count
        at = pl.multiple_of((holder * self.narrow + s) * self.rows + first, self.half)
        place = self.out_ref.at[pl.ds(at, count)]
        return pltpu.make_async_remote_copy(
            src_ref=self.shard_ref.at[pl.ds(first, count)] if own else place,
            dst_ref=place,
            send_sem=self.send_sems.at[number],
            recv_sem=self.recv_sems.at[number],
            device_id=target,
            device_id_type=pl.DeviceIdType.MESH,
        )

    def own_place(self):
        return self.out_ref.at[pl.ds(pl.multiple_of((self.w * self.narrow + self.z) * self.rows, self.rows), self.rows)]

    def spread(self, s, own=False):
        self.move(self.w, s, self.to_x + s, self.at_x, own=own).start()
        self.move(self.w, s, self.to_y + s, self.at_y, own=own).start()
        self.move(self.w, s, self.to_core + s, self.at_core, own=own).start()

    def relay(self, s):
        half = self.half
        self.move(self.x, s, self.to_x + s, self.at_x).wait_recv()
        self.move(self.x, s, self.on_y + s, self.at_y, 0, half).start()
        self.move(self.x, s, self.to_core + self.narrow + s, self.at_core).start()
        self.move(self.y, s, self.to_y + s, self.at_y).wait_recv()
        self.move(self.y, s, self.on_x + s, self.at_x, half, half).start()
        self.move(self.y, s, self.to_core + 2 * self.narrow + s, self.at_core).start()

    def corner(self, s):
        self.move(self.xy, s, self.on_y + s, self.at_y, 0, self.half).wait_recv()
        self.move(self.xy, s, self.on_x + s, self.at_x, self.half, self.half).wait_recv()
        self.move(self.xy, s, self.to_core + 3 * self.narrow + s, self.at_core).start()

    def at_distance(self, r, action):
        if r == 0:
            action(self.z)
        else:
            pl.when(self.z - r >= 0)(lambda: action(self.z - r))
            pl.when(self.z + r < self.narrow)(lambda: action(self.z + r))

    def begin_line(self):
        z = self.z
        pl.when(z < self.narrow - 1)(lambda: self.move(self.w, z, self.up + z, self.above, own=True).start())
        pl.when(z > 0)(lambda: self.move(self.w, z, self.down + z, self.below, own=True).start())

    def begin_spread(self):
        self.spread(self.z, own=True)

    def round(self, r):
        z = self.z

        def from_below():
            s = z - r
            self.move(self.w, s, self.up + s, self.above).wait_recv()
            pl.when(z < self.narrow - 1)(lambda: self.move(self.w, s, self.up + s, self.above).start())
            self.spread(s)

        def from_above():
            s = z + r
            self.move(self.w, s, self.down + s, self.below).wait_recv()
            pl.when(z > 0)(lambda: self.move(self.w, s, self.down + s, self.below).start())
            self.spread(s)

        if r < self.narrow:
            pl.when(z - r >= 0)(from_below)
            pl.when(z + r < self.narrow)(from_above)
        self.at_distance(r - 1, self.relay)

    def corners(self):
        for r in range(self.narrow):
            self.at_distance(r, self.corner)

    def arrive(self):
        for s in range(self.narrow):
            for k, holder in enumerate((self.w, self.x, self.y, self.xy)):
                self.move(holder ^ 1, s, self.to_core + k * self.narrow + s, self.at_core).wait_recv()

    def close(self):
        z, half = self.z, self.half
        for s in range(self.narrow):
            up, down = self.move(self.w, s, self.up + s, self.above), self.move(self.w, s, self.down + s, self.below)
            pl.when((s <= z) & (z < self.narrow - 1))(up.wait_send)
            pl.when((s >= z) & (z > 0))(down.wait_send)
            self.move(self.w, s, self.to_x + s, self.at_x).wait_send()
            self.move(self.w, s, self.to_y + s, self.at_y).wait_send()
            self.move(self.x, s, self.on_y + s, self.at_y, 0, half).wait_send()
            self.move(self.y, s, self.on_x + s, self.at_x, half, half).wait_send()
            for k, holder in enumerate((self.w, self.x, self.y, self.xy)):
                self.move(holder, s, self.to_core + k * self.narrow + s, self.at_core).wait_send()


def place_bounds(live_ref, pairs_ref, sources_ref, first_ref, bounds_ref):
    place = lax.broadcasted_iota(jnp.int32, (1, SEQ), 1)
    live = place < live_ref[0]
    count = pairs_ref.shape[1]
    first, start, end = jnp.zeros_like(place), jnp.zeros_like(place), jnp.zeros_like(place)
    for n in range(count):
        begun = place >= pairs_ref[0, n]
        first = jnp.where(begun, pairs_ref[0, n], first)
        start = jnp.where(begun, sources_ref[0, n], start)
        end = jnp.where(begun, sources_ref[0, n + 1] if n + 1 < count else MEM, end)
    first_ref[0] = jnp.where(live, first, live_ref[0])
    bounds_ref[0, 0:1, :] = jnp.where(live, start, 0)
    bounds_ref[0, 1:2, :] = jnp.where(live, end, MEM)
    bounds_ref[0, 2:8, :] = jnp.zeros((6, SEQ), jnp.int32)


def front_kernel(
    narrow,
    live_ref,
    pairs_ref,
    sources_ref,
    wq_ref,
    wk_ref,
    wv_ref,
    ck_ref,
    cv_ref,
    others_refs,
    hidden_in_ref,
    hidden_out_ref,
    extra_ref,
    tokens_ref,
    memory_ref,
    wide_any,
    later_any,
    late_any,
    normed_any,
    qkv_any,
    mixed_ref,
    log_ref,
    norms_ref,
    first_ref,
    bounds_ref,
    after_ref,
    normed_two_ref,
    cross_q_ref,
    cross_kv_ref,
    cross_mixed_ref,
    cross_log_ref,
    shard_a,
    shard_b,
    shard_c,
    weight,
    later,
    normed,
    qkv,
    a_send,
    a_recv,
    b_send,
    b_recv,
    c_send,
    c_recv,
    local_sems,
):
    d = tokens_ref.shape[1]
    rows = wq_ref.shape[0]
    for p in range(PAIRS):
        lanes = slice(p * 128, (p + 1) * 128)
        for n, ref in enumerate((wq_ref, wk_ref, wv_ref)):
            shard_a[:, (3 * p + n) * 128 : (3 * p + n + 1) * 128] = ref[:, lanes]
        for n, ref in enumerate((ck_ref, cv_ref)):
            at = KV_CROSS * 2 * d + (2 * p + n) * 128
            shard_b[:, at : at + 128] = ref[:, lanes]
    shard_a[:, 3 * d :] = extra_ref[...]

    one = Gather(shard_a, weight, a_send, a_recv, narrow)
    two = Gather(shard_b, later, b_send, b_recv, narrow)
    three = Gather(shard_c, late_any, c_send, c_recv, narrow)
    keeps = [
        pltpu.make_async_copy(gather.shard_ref, gather.own_place(), local_sems.at[n])
        for n, gather in enumerate((one, two, three))
    ]
    greet_all(narrow)
    one.begin_line()
    one.begin_spread()
    keeps[0].start()
    for at, ref in zip((OUT_SELF, QUERY_CROSS, OUT_CROSS), others_refs):
        shard_b[:, at * d : (at + 1) * d] = ref[...]
    for n in range(4):
        shard_c[n * rows : (n + 1) * rows, :] = hidden_in_ref[:, n * d : (n + 1) * d]
    shard_c[4 * rows :, :] = hidden_out_ref[...]
    keeps[1].start()
    keeps[2].start()
    place_bounds(live_ref, pairs_ref, sources_ref, first_ref, bounds_ref)
    one.round(1)
    one.round(2)
    two.begin_line()
    for r in range(3, narrow + 1):
        one.round(r)
    two.begin_spread()
    one.corners()
    one.arrive()
    keeps[0].wait()
    out_wide = pltpu.make_async_copy(weight, wide_any, local_sems.at[3])
    out_wide.start()

    norms_ref[...] = weight[:, 3 * d :].astype(F32).T[0:8, :]

    def project_block(t, carry):
        at = pl.ds(pl.multiple_of(t * TB, TB), TB)
        unit, _ = norm_parts(tokens_ref[at, :].astype(F32))
        value = (unit * norms_ref[0:1, :] + norms_ref[1:2, :]).astype(BF16)
        normed[at, :] = value
        for part in range(3):
            lanes = slice(part * d, (part + 1) * d)
            qkv[at, lanes] = mm(value, weight[:, lanes]).astype(BF16)
        return carry

    def pair_block(p, carry):
        def lanes(n):
            return pl.ds(pl.multiple_of(p * 384 + n * 128, 128), 128)

        attend(
            lambda at: qkv[at, lanes(0)],
            qkv[:, lanes(1)],
            qkv[:, lanes(2)],
            functools.partial(self_visible, first_ref),
            self_extent,
            *pair_keepers(mixed_ref, log_ref, p),
        )
        return carry

    def middle_block(t, carry):
        at = pl.ds(pl.multiple_of(t * TB, TB), TB)
        mb = memory_ref.shape[0] * TB // tokens_ref.shape[0]
        mem_at = pl.ds(pl.multiple_of(t * mb, mb), mb)
        after = tokens_ref[at, :].astype(F32) + mm(mixed_ref[at, :], later[:, OUT_SELF * d : (OUT_SELF + 1) * d])
        after_ref[at, :] = after
        for n in range(2):
            lanes = slice((2 * KV_CROSS + n) * d, (2 * KV_CROSS + n + 1) * d)
            cross_kv_ref[mem_at, n * d : (n + 1) * d] = mm(memory_ref[mem_at, :], later[:, lanes]).astype(BF16)
        unit, _ = norm_parts(after)
        value = (unit * norms_ref[2:3, :] + norms_ref[3:4, :]).astype(BF16)
        normed_two_ref[at, :] = value
        cross_q_ref[at, :] = mm(value, later[:, QUERY_CROSS * d : (QUERY_CROSS + 1) * d]).astype(BF16)
        return carry

    def cross_block(p, carry):
        def lanes(n):
            return pl.ds(pl.multiple_of(p * 256 + n * 128, 128), 128)

        q_lanes = pl.ds(pl.multiple_of(p * 128, 128), 128)
        attend(
            lambda at: cross_q_ref[at, q_lanes],
            cross_kv_ref[:, lanes(0)],
            cross_kv_ref[:, lanes(1)],
            functools.partial(cross_visible, bounds_ref),
            cross_extent,
            *pair_keepers(cross_mixed_ref, cross_log_ref, p),
        )
        return carry

    lax.fori_loop(0, 4, project_block, 0)
    out_normed = pltpu.make_async_copy(normed, normed_any, local_sems.at[4])
    out_qkv = pltpu.make_async_copy(qkv, qkv_any, local_sems.at[5])
    out_normed.start()
    out_qkv.start()
    two.round(1)
    lax.fori_loop(0, 2, pair_block, 0)
    two.round(2)
    lax.fori_loop(2, 5, pair_block, 0)
    for r in range(3, narrow):
        two.round(r)
    three.begin_line()
    lax.fori_loop(5, 8, pair_block, 0)
    two.round(narrow)
    three.begin_spread()
    two.corners()
    two.arrive()
    keeps[1].wait()
    out_later = pltpu.make_async_copy(later, later_any, local_sems.at[6])
    out_later.start()
    lax.fori_loop(0, 4, middle_block, 0)
    three.round(1)
    lax.fori_loop(0, 4, cross_block, 0)
    three.round(2)
    lax.fori_loop(4, 8, cross_block, 0)
    for r in range(3, narrow + 1):
        three.round(r)
    three.corners()
    three.arrive()
    keeps[2].wait()
    for gather in (one, two, three):
        gather.close()
    for copy in (out_wide, out_normed, out_qkv, out_later):
        copy.wait()


def pair_keepers(out_ref, log_ref, p):
    def keep_out(at, value):
        out_ref[at, pl.ds(pl.multiple_of(p * 128, 128), 128)] = value

    def keep_log(h, at, value):
        log_ref[0, p, h : h + 1, at] = value

    return keep_out, keep_log


def front(live_length, pair_starts, source_starts, weights, hidden_in, hidden_out, extra, tokens, memory, narrow):
    self_query, self_key, self_value, self_output, cross_query, cross_key, cross_value, cross_output = weights
    shard_rows, d = self_query.shape
    rows, mem_rows = tokens.shape[0], memory.shape[0]
    block = 4 * shard_rows + hidden_out.shape[0]
    anywhere, vmem = pl.BlockSpec(memory_space=pl.ANY), pl.BlockSpec(memory_space=pltpu.VMEM)
    smem = pl.BlockSpec(memory_space=pltpu.SMEM)
    logs = jax.ShapeDtypeStruct((1, PAIRS, 8, SEQ), F32)

    def kernel(*refs):
        front_kernel(narrow, *refs[:8], refs[8:11], *refs[11:])

    return pl.pallas_call(
        kernel,
        in_specs=[smem] * 3 + [vmem] * 13,
        out_specs=[anywhere] * 5 + [vmem] * 11,
        out_shape=[
            shape(d, 3 * d + 128, BF16),
            shape(d, 5 * d, BF16),
            shape(8 * narrow * block, d, BF16),
            shape(rows, d, BF16),
            shape(rows, 3 * d, BF16),
            shape(rows, d, BF16),
            logs,
            shape(8, d, F32),
            jax.ShapeDtypeStruct((1, 1, SEQ), jnp.int32),
            jax.ShapeDtypeStruct((1, 8, SEQ), jnp.int32),
            shape(rows, d, F32),
            shape(rows, d, BF16),
            shape(rows, d, BF16),
            shape(mem_rows, 2 * d, BF16),
            shape(rows, d, BF16),
            logs,
        ],
        scratch_shapes=[
            pltpu.VMEM((shard_rows, 3 * d + 128), BF16),
            pltpu.VMEM((shard_rows, 5 * d), BF16),
            pltpu.VMEM((block, d), BF16),
            pltpu.VMEM((d, 3 * d + 128), BF16),
            pltpu.VMEM((d, 5 * d), BF16),
            pltpu.VMEM((rows, d), BF16),
            pltpu.VMEM((rows, 3 * d), BF16),
            *[pltpu.SemaphoreType.DMA((10 * narrow,))] * 6,
            pltpu.SemaphoreType.DMA((7,)),
        ],
        name="front",
        compiler_params=pltpu.CompilerParams(collective_id=0, has_side_effects=True, vmem_limit_bytes=60 << 20),
        cost_estimate=cost(30 * rows * d * d, 200 << 20),
    )(
        live_length,
        pair_starts,
        source_starts,
        self_query,
        self_key,
        self_value,
        cross_key,
        cross_value,
        self_output,
        cross_query,
        cross_output,
        hidden_in,
        hidden_out,
        extra,
        tokens,
        memory,
    )


def stages_of(mesh_axes):
    plan = []
    for axis, size in mesh_axes:
        bits = size.bit_length() - 1
        at = 0
        while at < bits:
            take = 1 if (bits - at) % 2 else 2
            plan.append((axis, at, take))
            at += take
    return plan


def trade(value, axis, size, mask):
    return lax.ppermute(value, axis, [(i, i ^ mask) for i in range(size)])


def digit_of(axis, at, take):
    return (lax.axis_index(axis) >> at) & ((1 << take) - 1)


def pick(value, digit, place):
    if isinstance(value, list):
        return jnp.concatenate([pick(v, digit, place) for v in value], axis=0)
    return lax.dynamic_index_in_dim(value, digit, place, keepdims=False)


def add_up(own, pieces):
    total = own.astype(F32)
    for piece in pieces:
        total = total + piece.astype(F32)
    return total


def sum_steps(partial, mesh_axes):
    sizes = dict(mesh_axes)
    plan = stages_of(mesh_axes)
    groups = []
    for axis, _ in mesh_axes:
        groups += sorted((s for s in plan if s[0] == axis), key=lambda s: -s[1])
    devices = 1
    for _, size in mesh_axes:
        devices *= size
    columns = partial[0].shape[1]
    extents = [1 << s[2] for s in groups]
    value = [p.reshape(p.shape[0] // WIDTH, *extents, -1, columns) for p in partial]
    for number, stage in enumerate(plan):
        axis, at, take = stage
        place = 1 + groups.index(stage)
        groups.remove(stage)
        if axis == "wide" and take == 2:
            if isinstance(value, list):
                value = jnp.concatenate(value, axis=0)
            split = value.reshape(*value.shape[:place], 2, 2, *value.shape[place + 1 :])
            a, b = split[..., : columns // 2], split[..., columns // 2 :]
            low, high = digit_of(axis, at, 1), digit_of(axis, at + 1, 1)
            step = ((high, place, 2 << at), (low, place + 1, 1 << at))
            for (digit_a, place_a, mask_a), (digit_b, place_b, mask_b) in (
                step,
                ((low, place, 1 << at), (high, place, 2 << at)),
            ):
                pieces = yield [
                    trade(pick(a, digit_a ^ 1, place_a), axis, sizes[axis], mask_a),
                    trade(pick(b, digit_b ^ 1, place_b), axis, sizes[axis], mask_b),
                ]
                a = add_up(pick(a, digit_a, place_a), pieces[:1]).astype(BF16)
                b = add_up(pick(b, digit_b, place_b), pieces[1:]).astype(BF16)
            value = jnp.concatenate([a, b], axis=-1)
            continue
        digit = digit_of(axis, at, take)
        pieces = yield [
            trade(pick(value, digit ^ mask, place), axis, sizes[axis], mask << at) for mask in range(1, 1 << take)
        ]
        value = add_up(pick(value, digit, place), pieces)
        if number < len(plan) - 1:
            value = value.astype(BF16)
    return value.astype(F32).reshape(-1, columns)


class StagedSum:
    def __init__(self, partial, mesh_axes):
        self.steps = sum_steps(partial, mesh_axes)
        self.under_way = next(self.steps)
        self.value = None

    def go_on(self, pieces):
        try:
            self.under_way = self.steps.send(pieces)
        except StopIteration as stop:
            self.under_way, self.value = None, stop.value

    def result(self):
        while self.under_way is not None:
            self.go_on(self.under_way)
        return self.value


def fence(value, *sums):
    held = [s for s in sums if s.under_way is not None]
    value, arrived = lax.optimization_barrier((value, [s.under_way for s in held]))
    for s, pieces in zip(held, arrived):
        s.go_on(pieces)
    return value


def sum_everywhere(value, mesh_axes):
    sizes = dict(mesh_axes)
    for axis, at, take in stages_of(mesh_axes):
        arrived = [trade(value, axis, sizes[axis], mask << at) for mask in range(1, 1 << take)]
        for piece in arrived:
            value = value + piece
    return value


def by_pairs(*parts):
    rows = parts[0].shape[0]
    return jnp.stack([p.reshape(rows, -1, 128) for p in parts], axis=2).reshape(rows, -1)


def from_pairs(value, count):
    rows = value.shape[0]
    split = value.reshape(rows, -1, count, 128)
    return [split[:, :, c].reshape(rows, -1) for c in range(count)]


def outer_sum(left_side, gradient):
    return jnp.einsum("td,te->de", left_side, gradient, preferred_element_type=F32).astype(BF16)


CHUNKS = 4


class Scatter:
    def __init__(self, own, theirs, buffers, keep, send_sems, recv_sems, narrow):
        self.own, self.theirs, self.keep = own, theirs, keep
        self.from_core, self.a1, self.b1, self.a2, self.b2, self.from_line = buffers
        self.send_sems, self.recv_sems = send_sems, recv_sems
        self.narrow = narrow
        self.half = self.a1.shape[-1]
        self.w, self.z = lax.axis_index("wide"), lax.axis_index("narrow")
        self.c, self.x, self.y = self.w & 1, (self.w >> 1) & 1, (self.w >> 2) & 1
        self.per_chunk = 4 + narrow

    def move(self, i, number, src, dst, target):
        at = i * self.per_chunk + number
        return pltpu.make_async_remote_copy(
            src_ref=src,
            dst_ref=dst,
            send_sem=self.send_sems.at[at],
            recv_sem=self.recv_sems.at[at],
            device_id=target,
            device_id_type=pl.DeviceIdType.MESH,
        )

    def to_core(self, i):
        return self.move(i, 0, self.theirs(i), self.from_core.at[i], (self.w ^ 1, self.z))

    def first(self, i):
        left, right = pl.ds(0, self.half), pl.ds(self.half, self.half)
        to_x, to_y = (self.w ^ 2, self.z), (self.w ^ 4, self.z)
        return (
            self.move(i, 1, self.own.at[i, :, 1 - self.x, :, :, left], self.a1.at[i], to_x),
            self.move(i, 2, self.own.at[i, 1 - self.y, :, :, :, right], self.b1.at[i], to_y),
        )

    def second(self, i):
        left, right = pl.ds(0, self.half), pl.ds(self.half, self.half)
        to_x, to_y = (self.w ^ 2, self.z), (self.w ^ 4, self.z)
        return (
            self.move(i, 3, self.own.at[i, 1 - self.y, self.x, :, :, left], self.a2.at[i], to_y),
            self.move(i, 4, self.own.at[i, self.y, 1 - self.x, :, :, right], self.b2.at[i], to_x),
        )

    def along(self, i):
        return [
            self.move(
                i,
                4 + mask,
                self.own.at[i, self.y, self.x, self.z ^ mask],
                self.from_line.at[i, mask - 1],
                (self.w, self.z ^ mask),
            )
            for mask in range(1, self.narrow)
        ]

    def begin(self, i):
        self.to_core(i).start()

    def add(self, i, y, x, columns, piece):
        now = self.own[i, y, x, :, :, columns]
        self.own[i, y, x, :, :, columns] = now + piece

    def step(self, i, stage):
        both, left, right = slice(None), slice(0, self.half), slice(self.half, None)
        if stage == 0:
            self.to_core(i).wait_recv()
            for a in range(2):
                for b in range(2):
                    self.add(i, a, b, both, self.from_core[i, a, b])
            for copy in self.first(i):
                copy.start()
        elif stage == 1:
            for copy in self.first(i):
                copy.wait_recv()
            for a in range(2):
                self.add(i, a, self.x, left, self.a1[i, a])
                self.add(i, self.y, a, right, self.b1[i, a])
            for copy in self.second(i):
                copy.start()
        elif stage == 2:
            for copy in self.second(i):
                copy.wait_recv()
            self.add(i, self.y, self.x, left, self.a2[i])
            self.add(i, self.y, self.x, right, self.b2[i])
            for copy in self.along(i):
                copy.start()
        else:
            for copy in self.along(i):
                copy.wait_recv()
            total = self.own[i, self.y, self.x, self.z].astype(F32)
            for mask in range(1, self.narrow):
                total = total + self.from_line[i, mask - 1].astype(F32)
            self.keep(i, total)

    def close(self, i):
        for copy in (self.to_core(i), *self.first(i), *self.second(i), *self.along(i)):
            copy.wait_send()


def scatter_scratch(chunks, narrow, rows, width):
    copies = chunks * (4 + narrow)
    return [
        pltpu.VMEM((chunks, 2, 2, narrow, rows, width), BF16),
        pltpu.VMEM((chunks, 2, 2, narrow, rows, width), BF16),
        pltpu.VMEM((chunks, 2, narrow, rows, width // 2), BF16),
        pltpu.VMEM((chunks, 2, narrow, rows, width // 2), BF16),
        pltpu.VMEM((chunks, narrow, rows, width // 2), BF16),
        pltpu.VMEM((chunks, narrow, rows, width // 2), BF16),
        pltpu.VMEM((chunks, narrow - 1, rows, width), BF16),
        pltpu.SemaphoreType.DMA((copies,)),
        pltpu.SemaphoreType.DMA((copies,)),
        pltpu.SemaphoreType.DMA((chunks,)),
    ]


class Carried:
    def __init__(self, shares, scratch, keep, narrow):
        own, *buffers, send_sems, recv_sems, self.load_sems = scratch
        self.shares = shares
        self.scatter = Scatter(own, self.other, buffers, keep, send_sems, recv_sems, narrow)
        self.chunks = own.shape[0]

    def part(self, i, core):
        return self.shares[i](core)

    def other(self, i):
        return self.part(i, 1 - self.scatter.c)

    def load(self, i):
        return pltpu.make_async_copy(self.part(i, self.scatter.c), self.scatter.own.at[i], self.load_sems.at[i])

    def open(self):
        for i in range(self.chunks):
            self.load(i).start()
        greet_all(self.scatter.narrow)
        for i in range(2):
            self.scatter.begin(i)

    def steps(self, plan):
        for i, stage in plan:
            if stage == 0:
                self.load(i).wait()
            self.scatter.step(i, stage)
            if stage == 0 and i + 2 < self.chunks:
                self.scatter.begin(i + 2)

    def close(self):
        for i in range(self.chunks):
            self.scatter.close(i)


def share_views(array, narrow, rows):
    return array.reshape(2, 2, 2, narrow, rows, array.shape[1])


def share_views(array, narrow, rows):
    return array.reshape(2, 2, 2, narrow, rows, array.shape[1])


def columns_of(ref, at, width):
    return lambda core: ref.at[:, :, core, :, :, pl.ds(at, width)]


def tn(a, b):
    return lax.dot_general(a, b, (((0,), (0,)), ((), ())), preferred_element_type=F32)


def outer_into(out_ref, left_ref, right):
    for at in range(0, left_ref.shape[1], 256):
        out_ref[at : at + 256, :] = tn(left_ref[:, at : at + 256], right).astype(BF16)


CROSS_PLAN = (
    ((0, 0), (1, 0)),
    ((2, 0),),
    ((0, 1),),
    ((3, 0),),
    ((1, 1),),
    ((0, 2), (4, 0)),
    ((2, 1),),
    ((1, 2),),
    ((0, 3), (3, 1), (5, 0)),
    ((2, 2),),
    ((1, 3), (4, 1)),
    ((3, 2),),
    ((2, 3),),
    ((5, 1),),
    ((4, 2),),
    ((3, 3),),
    ((5, 2), (4, 3), (5, 3)),
)
CROSS_WIDE = 2


def cross_back_kernel(
    narrow,
    bounds_ref,
    log_ref,
    q_ref,
    kv_ref,
    mixed_pair_ref,
    grad_ref,
    before_ref,
    total_ref,
    norms_ref,
    mixed_ref,
    b2_ref,
    normed_ref,
    memory_ref,
    self_mixed_ref,
    early_any,
    share_any,
    wide_any,
    out_ref,
    next_ref,
    mem_ref,
    ngrad_ref,
    shares_ref,
    shard_ref,
    wide_ref,
    dk_ref,
    dv_ref,
    dq_ref,
    dkv_ref,
    b1_ref,
    wq,
    wkv,
    wo,
    weight_sems,
    *scratch,
):
    step = pl.program_id(0)
    d = wq.shape[0]
    rows = shard_ref.shape[0] // 4

    def keep(i, value):
        if i < 4:
            shard_ref[i * rows : (i + 1) * rows, :] = value
        else:
            wide_ref[:, (i - 4) * d : (i - 3) * d] = value

    def piece(i):
        return lambda core: share_any.at[:, :, core, :, i]

    pieces = [piece(i) for i in range(4)] + [columns_of(wide_any, i * d, d) for i in range(CROSS_WIDE)]
    carried = Carried(pieces, scratch, keep, narrow)
    loads = [
        pltpu.make_async_copy(early_any.at[:, pl.ds(QUERY_CROSS * d, d)], wq, weight_sems.at[0]),
        pltpu.make_async_copy(early_any.at[:, pl.ds(2 * KV_CROSS * d, 2 * d)], wkv, weight_sems.at[1]),
        pltpu.make_async_copy(early_any.at[:, pl.ds(OUT_SELF * d, d)], wo, weight_sems.at[2]),
    ]

    @pl.when(step == 0)
    def _():
        carried.open()
        for load in loads:
            load.start()

    @pl.when(step < PAIRS)
    def _():
        def keep_dq(rows, value):
            dq_ref[rows, pl.ds(pl.multiple_of(step * 128, 128), 128)] = value

        cross_backward_pair(bounds_ref, log_ref, q_ref, kv_ref, mixed_pair_ref, grad_ref, keep_dq, None, dk_ref, dv_ref)
        at = pl.multiple_of(step * 256, 256)
        dkv_ref[:, pl.ds(at, 128)] = (dk_ref[...] * HEAD_DIM**-0.5).astype(BF16)
        dkv_ref[:, pl.ds(pl.multiple_of(at + 128, 128), 128)] = dv_ref[...].astype(BF16)

    @pl.when(step == PAIRS)
    def _():
        for load in loads:
            load.wait()
        ngrad_ref[...] = jnp.zeros_like(ngrad_ref)

    tokens_end = PAIRS + SEQ // TB

    @pl.when((step >= PAIRS) & (step < tokens_end))
    def _():
        t = step - PAIRS
        mb = mem_ref.shape[0]
        at = pl.ds(pl.multiple_of(t * TB, TB), TB)
        gradient = mm_t(dq_ref[at, :], wq[...])
        mem_ref[...] = mm_t(dkv_ref[pl.ds(pl.multiple_of(t * mb, mb), mb), :], wkv[...]).astype(BF16)
        unit, inverse = norm_parts(before_ref[...])
        total = total_ref[...] + norm_back(unit, inverse, norms_ref[2:3, :], gradient)
        out_ref[...] = total
        b1 = total.astype(BF16)
        b1_ref[at, :] = b1
        next_ref[...] = mm_t(b1, wo[...]).astype(BF16)
        ngrad_ref[0:1, :] += jnp.sum(gradient * unit, axis=0, keepdims=True)
        ngrad_ref[1:2, :] += jnp.sum(gradient, axis=0, keepdims=True)

    pl.when(step == tokens_end)(lambda: outer_into(shares_ref, mixed_ref, b2_ref[...]))
    pl.when(step == tokens_end + 1)(lambda: outer_into(shares_ref, normed_ref, dq_ref[...]))
    pl.when(step == tokens_end + 2)(lambda: outer_into(shares_ref, memory_ref, dkv_ref[:, :d]))
    pl.when(step == tokens_end + 3)(lambda: outer_into(shares_ref, memory_ref, dkv_ref[:, d:]))
    pl.when(step == tokens_end + 4)(lambda: outer_into(shares_ref, self_mixed_ref, b1_ref[...]))

    for number, plan in enumerate(CROSS_PLAN):
        pl.when(step == number)(functools.partial(carried.steps, plan))
    pl.when(step == len(CROSS_PLAN) - 1)(carried.close)


def cross_back(bounds, logs, q, kv, mixed, grad, before, total, norms, b2, normed, memory, self_mixed, early, share, wide_share, narrow):
    rows, d = q.shape
    mem_rows = kv.shape[0]
    shard_rows = d // (8 * narrow)
    steps = rows // TB
    mb = mem_rows // steps

    def pair(s):
        return jnp.minimum(s, PAIRS - 1)

    def token(s):
        return jnp.clip(s - PAIRS, 0, steps - 1)

    anywhere = pl.BlockSpec(memory_space=pl.ANY)
    by_pair = pl.BlockSpec((SEQ, 128), lambda s: (0, pair(s)))
    by_token = pl.BlockSpec((TB, d), lambda s: (token(s), 0))
    return pl.pallas_call(
        functools.partial(cross_back_kernel, narrow),
        grid=(PAIRS + steps + 5,),
        in_specs=[
            pl.BlockSpec((1, 8, SEQ), lambda s: (0, 0, 0)),
            pl.BlockSpec((1, 1, 8, SEQ), lambda s: (0, pair(s), 0, 0)),
            by_pair,
            pl.BlockSpec((MEM, 256), lambda s: (0, pair(s))),
            by_pair,
            by_pair,
            by_token,
            by_token,
            whole(8, d),
            whole(rows, d),
            whole(rows, d),
            whole(rows, d),
            whole(mem_rows, d),
            whole(rows, d),
            anywhere,
            anywhere,
            anywhere,
        ],
        out_specs=[
            by_token,
            by_token,
            pl.BlockSpec((mb, d), lambda s: (token(s), 0)),
            whole(8, d),
            pl.BlockSpec((d, d), lambda s: (jnp.maximum(s - PAIRS - steps, 0), 0)),
            whole(4 * shard_rows, d),
            whole(shard_rows, CROSS_WIDE * d),
        ],
        out_shape=[
            shape(rows, d, F32),
            shape(rows, d, BF16),
            shape(mem_rows, d, BF16),
            shape(8, d, F32),
            shape(5 * d, d, BF16),
            shape(4 * shard_rows, d, F32),
            shape(shard_rows, CROSS_WIDE * d, F32),
        ],
        scratch_shapes=[
            pltpu.VMEM((MEM, 128), F32),
            pltpu.VMEM((MEM, 128), F32),
            pltpu.VMEM((rows, d), BF16),
            pltpu.VMEM((mem_rows, 2 * d), BF16),
            pltpu.VMEM((rows, d), BF16),
            pltpu.VMEM((d, d), BF16),
            pltpu.VMEM((d, 2 * d), BF16),
            pltpu.VMEM((d, d), BF16),
            pltpu.SemaphoreType.DMA((3,)),
            *scatter_scratch(4 + CROSS_WIDE, narrow, shard_rows, d),
        ],
        name="cross_back",
        compiler_params=pltpu.CompilerParams(collective_id=2, has_side_effects=True, vmem_limit_bytes=60 << 20),
        cost_estimate=cost(40 * rows * d * d, 100 << 20),
    )(
        bounds,
        logs,
        q,
        kv,
        mixed,
        grad,
        before,
        total,
        norms,
        mixed,
        b2,
        normed,
        memory,
        self_mixed,
        early,
        share.reshape(2, 2, 2, narrow, 4, shard_rows, d),
        share_views(wide_share, narrow, shard_rows),
    )


SELF_PLAN = (
    ((0, 0), (1, 0)),
    ((2, 0),),
    ((0, 1),),
    ((3, 0),),
    ((1, 1),),
    ((0, 2), (4, 0)),
    ((2, 1),),
    ((1, 2), (5, 0), (3, 1)),
    ((0, 3),),
    ((2, 2), (6, 0)),
    ((1, 3), (4, 1)),
    ((3, 2),),
    ((2, 3), (5, 1)),
    ((4, 2),),
    ((3, 3), (6, 1), (5, 2), (4, 3), (6, 2), (5, 3), (6, 3)),
)
SELF_WIDE = 4 - CROSS_WIDE
SELF_CHUNKS = SELF_WIDE + 5


def self_back_kernel(
    narrow,
    first_ref,
    log_ref,
    qkv_ref,
    mixed_ref,
    grad_ref,
    normed_ref,
    tokens_ref,
    total_ref,
    norms_ref,
    early_any,
    wide_any,
    shares_any,
    qkv_share_ref,
    out_ref,
    ngrad_ref,
    expand_ref,
    cross_output_ref,
    cross_query_ref,
    cross_key_ref,
    cross_value_ref,
    self_output_ref,
    dk_ref,
    dv_ref,
    dqkv,
    weight,
    weight_sem,
    *scratch,
):
    step = pl.program_id(0)
    d = normed_ref.shape[1]

    def keep(i, value):
        i -= SELF_WIDE
        if i < 0:
            expand_ref[:, (i + SELF_WIDE) * d : (i + SELF_WIDE + 1) * d] = value
        elif i == 0:
            cross_output_ref[...] = value
        elif i == 1:
            cross_query_ref[...] = value
        elif i == 4:
            self_output_ref[...] = value
        else:
            for n in range(d // 256):
                at = (i - 2) * d // 2 + n * 128
                cross_key_ref[:, at : at + 128] = value[:, n * 256 : n * 256 + 128]
                cross_value_ref[:, at : at + 128] = value[:, n * 256 + 128 : n * 256 + 256]

    def piece(i):
        return lambda core: shares_any.at[i, :, :, core]

    pieces = [columns_of(wide_any, (CROSS_WIDE + i) * d, d) for i in range(SELF_WIDE)] + [piece(i) for i in range(5)]
    carried = Carried(pieces, scratch, keep, narrow)
    load = pltpu.make_async_copy(early_any.at[:, pl.ds(0, 3 * d)], weight, weight_sem)

    @pl.when(step == 0)
    def _():
        carried.open()
        load.start()

    @pl.when(step < PAIRS)
    def _():
        base = step * 384

        def keep_dq(rows, value):
            dqkv[rows, pl.ds(pl.multiple_of(base, 128), 128)] = value

        attend_back(
            lambda rows: qkv_ref[rows, 0:128],
            qkv_ref[:, 128:256],
            qkv_ref[:, 256:384],
            grad_ref,
            mixed_ref,
            log_ref,
            functools.partial(self_visible, first_ref),
            self_extent,
            keep_dq,
            dk_ref,
            dv_ref,
        )
        dqkv[:, pl.ds(pl.multiple_of(base + 128, 128), 128)] = (dk_ref[...] * HEAD_DIM**-0.5).astype(BF16)
        dqkv[:, pl.ds(pl.multiple_of(base + 256, 128), 128)] = dv_ref[...].astype(BF16)

    @pl.when((step >= PAIRS) & (step < PAIRS + 3))
    def _():
        at = pl.ds(pl.multiple_of((step - PAIRS) * d, d), d)
        outer_into(qkv_share_ref, normed_ref, dqkv[:, at])

    @pl.when(step == PAIRS + 3)
    def _():
        load.wait()
        ngrad_ref[...] = jnp.zeros_like(ngrad_ref)

    @pl.when(step >= PAIRS + 3)
    def _():
        at = pl.ds(pl.multiple_of((step - PAIRS - 3) * TB, TB), TB)
        gradient = mm_t(dqkv[at, :], weight[...])
        unit, inverse = norm_parts(tokens_ref[...].astype(F32))
        total = total_ref[...] + norm_back(unit, inverse, norms_ref[0:1, :], gradient)
        out_ref[...] = total.astype(BF16)
        ngrad_ref[0:1, :] += jnp.sum(gradient * unit, axis=0, keepdims=True)
        ngrad_ref[1:2, :] += jnp.sum(gradient, axis=0, keepdims=True)

    for number, plan in enumerate(SELF_PLAN):
        pl.when(step == number)(functools.partial(carried.steps, plan))
    pl.when(step == len(SELF_PLAN) - 1)(carried.close)


def self_back(first, logs, qkv, mixed, grad, normed, tokens, total, norms, early, wide_share, shares, narrow):
    rows, d = mixed.shape
    shard_rows = d // (8 * narrow)

    def pair(s):
        return jnp.minimum(s, PAIRS - 1)

    def token(s):
        return jnp.maximum(s - PAIRS - 3, 0)

    anywhere = pl.BlockSpec(memory_space=pl.ANY)
    by_pair = pl.BlockSpec((SEQ, 128), lambda s: (0, pair(s)))
    by_token = pl.BlockSpec((TB, d), lambda s: (token(s), 0))
    return pl.pallas_call(
        functools.partial(self_back_kernel, narrow),
        grid=(PAIRS + 3 + rows // TB,),
        in_specs=[
            pl.BlockSpec((1, 1, SEQ), lambda s: (0, 0, 0)),
            pl.BlockSpec((1, 1, 8, SEQ), lambda s: (0, pair(s), 0, 0)),
            pl.BlockSpec((SEQ, 384), lambda s: (0, pair(s))),
            by_pair,
            by_pair,
            whole(rows, d),
            by_token,
            by_token,
            whole(8, d),
            anywhere,
            anywhere,
            anywhere,
        ],
        out_specs=[
            pl.BlockSpec((d, d), lambda s: (0, jnp.clip(s - PAIRS, 0, 2))),
            by_token,
            whole(8, d),
            whole(shard_rows, SELF_WIDE * d),
            *[whole(shard_rows, d)] * 5,
        ],
        out_shape=[
            shape(d, 3 * d, BF16),
            shape(rows, d, BF16),
            shape(8, d, F32),
            shape(shard_rows, SELF_WIDE * d, F32),
            *[shape(shard_rows, d, F32)] * 5,
        ],
        scratch_shapes=[
            pltpu.VMEM((SEQ, 128), F32),
            pltpu.VMEM((SEQ, 128), F32),
            pltpu.VMEM((rows, 3 * d), BF16),
            pltpu.VMEM((d, 3 * d), BF16),
            pltpu.SemaphoreType.DMA,
            *scatter_scratch(SELF_CHUNKS, narrow, shard_rows, d),
        ],
        name="self_back",
        compiler_params=pltpu.CompilerParams(collective_id=3, has_side_effects=True, vmem_limit_bytes=60 << 20),
        cost_estimate=cost(40 * rows * d * d, 100 << 20),
    )(
        first,
        logs,
        qkv,
        mixed,
        grad,
        normed,
        tokens,
        total,
        norms,
        early,
        share_views(wide_share, narrow, shard_rows),
        shares.reshape(5, 2, 2, 2, narrow, shard_rows, d),
    )


TAIL_CHUNKS = 6
TAIL_PLAN = [(0, 0), (1, 0)]
for _k in range(TAIL_CHUNKS + 5):
    TAIL_PLAN += [(_k + 2, 0)] if _k + 2 < TAIL_CHUNKS else []
    TAIL_PLAN += [(_k, 1)] if _k < TAIL_CHUNKS else []
    TAIL_PLAN += [(_k - 1, 2)] if 0 <= _k - 1 < TAIL_CHUNKS else []
    TAIL_PLAN += [(_k - 3, 3)] if 0 <= _k - 3 < TAIL_CHUNKS else []


def tail_kernel(
    narrow,
    norm_refs,
    qkv_any,
    query_ref,
    key_ref,
    value_ref,
    norm_out_ref,
    nval,
    nin,
    norm_send_sems,
    norm_recv_sems,
    *scratch,
):
    width = scratch[0].shape[-1]
    outs = (query_ref, key_ref, value_ref)

    def keep(i, value):
        for n in range(width // 128):
            pair, kind = divmod(i * width // 128 + n, 3)
            outs[kind][:, pair * 128 : (pair + 1) * 128] = value[:, n * 128 : (n + 1) * 128]

    carried = Carried([columns_of(qkv_any, i * width, width) for i in range(TAIL_CHUNKS)], scratch, keep, narrow)
    w, z = carried.scatter.w, carried.scatter.z

    def norm_copy(stage, number, target):
        return pltpu.make_async_remote_copy(
            src_ref=nval.at[stage],
            dst_ref=nin.at[number],
            send_sem=norm_send_sems.at[number],
            recv_sem=norm_recv_sems.at[number],
            device_id=target,
            device_id_type=pl.DeviceIdType.MESH,
        )

    norm_copies = [[norm_copy(0, 0, (w ^ 1, z))], [norm_copy(1, 1, (w ^ 2, z))], [norm_copy(2, 2, (w ^ 4, z))]]
    norm_copies.append([norm_copy(3, 2 + mask, (w, z ^ mask)) for mask in range(1, narrow)])

    def norm_step(stage):
        if stage == 0:
            for n, ref in enumerate(norm_refs):
                nval[0, 2 * n : 2 * n + 2, :] = ref[0:2, :]
            nval[0, 6:8, :] = jnp.zeros_like(norm_refs[0][0:2, :])
        else:
            for copy in norm_copies[stage - 1]:
                copy.wait_recv()
            value = nval[stage - 1]
            if stage < 4:
                nval[stage] = value + nin[stage - 1]
            else:
                for mask in range(1, narrow):
                    value = value + nin[2 + mask]
                norm_out_ref[...] = value
        if stage < 4:
            for copy in norm_copies[stage]:
                copy.start()

    carried.open()
    for number, action in enumerate(TAIL_PLAN):
        carried.steps([action])
        if number % 4 == 0 and number // 4 <= 4:
            norm_step(number // 4)
    carried.close()
    for copies in norm_copies:
        for copy in copies:
            copy.wait_send()


def tail(qkv_share, norm_grads, narrow):
    d = qkv_share.shape[0]
    shard_rows = d // (8 * narrow)
    width = 3 * d // TAIL_CHUNKS
    anywhere, vmem = pl.BlockSpec(memory_space=pl.ANY), pl.BlockSpec(memory_space=pltpu.VMEM)

    def kernel(one, two, three, *refs):
        tail_kernel(narrow, (one, two, three), *refs)

    return pl.pallas_call(
        kernel,
        in_specs=[vmem] * 3 + [anywhere],
        out_specs=[vmem] * 4,
        out_shape=[*[shape(shard_rows, d, F32)] * 3, shape(8, d, F32)],
        scratch_shapes=[
            pltpu.VMEM((4, 8, d), F32),
            pltpu.VMEM((2 + narrow, 8, d), F32),
            pltpu.SemaphoreType.DMA((2 + narrow,)),
            pltpu.SemaphoreType.DMA((2 + narrow,)),
            *scatter_scratch(TAIL_CHUNKS, narrow, shard_rows, width),
        ],
        name="tail",
        compiler_params=pltpu.CompilerParams(collective_id=1, has_side_effects=True, vmem_limit_bytes=40 << 20),
        cost_estimate=cost(4 * d * d * d, 100 << 20),
    )(*norm_grads, share_views(qkv_share, narrow, shard_rows))


def on_device(
    mesh_axes,
    tokens,
    memory,
    cotangent,
    live_length,
    pair_starts,
    source_starts,
    group_bounds,
    group_counts,
    self_query,
    self_key,
    self_value,
    self_output,
    cross_query,
    cross_key,
    cross_value,
    cross_output,
    hidden_in,
    hidden_out,
    first_gain,
    first_shift,
    second_gain,
    second_shift,
    third_gain,
    third_shift,
):
    names = tuple(axis for axis, _ in mesh_axes)
    row_count = live_length.shape[0]
    shard_rows = self_query.shape[0]
    device_count = 1
    for _, size in mesh_axes:
        device_count *= size

    def staged(*partial):
        return StagedSum(partial, mesh_axes)

    digits = jnp.stack([live_length // 256, live_length % 256], axis=1).astype(BF16)
    digits = jnp.pad(digits, ((0, shard_rows - row_count), (0, 0)))
    norms = jnp.stack([first_gain, first_shift, second_gain, second_shift, third_gain, third_shift], axis=1)
    extra = jnp.pad(jnp.concatenate([norms, digits], axis=1), ((0, 0), (0, 120)))
    weights = (self_query, self_key, self_value, self_output, cross_query, cross_key, cross_value, cross_output)
    fast = mesh_axes[0][1] == 8 and row_count == 1 and shard_rows % 32 == 0
    if fast:
        (
            early,
            later,
            late,
            normed_one,
            qkv,
            self_mixed,
            self_logs,
            norms,
            first,
            bounds,
            after_self,
            normed_two,
            cross_q,
            cross_kv,
            cross_mixed,
            cross_logs,
        ) = front(
            live_length,
            pair_starts,
            source_starts,
            weights,
            hidden_in,
            hidden_out,
            extra,
            tokens,
            memory,
            mesh_axes[1][1],
        )
        late = [late.reshape(device_count, -1, WIDTH)]
    else:
        shard = [by_pairs(self_query, self_key, self_value), extra, self_output, cross_query]
        shard += [by_pairs(cross_key, cross_value), cross_output]
        early = lax.all_gather(jnp.concatenate(shard, axis=1), names, axis=0, tiled=True)
        late = [lax.all_gather(part, names, axis=0, tiled=True) for part in (hidden_in, hidden_out)]
        early, later = early[:, : 3 * WIDTH + 128], early[:, 3 * WIDTH + 128 :]
        norms = early[:, 3 * WIDTH : 3 * WIDTH + 8].astype(F32).T
        first, bounds = row_bounds(pair_starts, source_starts, live_length)
        normed_one, qkv = project(tokens, norms, early)
        self_mixed, self_logs = self_forward(first, qkv, row_count)
        after_self, normed_two, cross_q, cross_kv = middle(self_mixed, tokens, memory, norms, later)
        cross_mixed, cross_logs = cross_forward(bounds, cross_q, cross_kv, row_count)

    live_total = jnp.sum(norms[6]) * 256.0 + jnp.sum(norms[7])
    device = lax.axis_index(names)
    member = (group_bounds[:-1] <= device) & (device < group_bounds[1:])
    pair_tokens = jnp.sum(jnp.where(member, group_counts, 0))
    token_all = row_count * SEQ * device_count
    row_weight = pair_tokens.astype(F32) * (token_all / 1000.0) / live_total
    layer_output, normed_three, activated, hidden_grad, branch_three, cross_total, branch_two, mixed_grad, norm_three = feed(
        live_length, row_weight[None], cross_mixed, after_self, cotangent, norms, later, late
    )

    reduce_share, expand_share = outer_sum(activated, branch_three), outer_sum(normed_three, hidden_grad)
    if fast:
        narrow = mesh_axes[1][1]
        self_total, mixed_grad, memory_grad, norm_two, shares, reduce_shard, expand_low = cross_back(
            bounds,
            cross_logs,
            cross_q,
            cross_kv,
            cross_mixed,
            mixed_grad,
            after_self,
            cross_total,
            norms,
            branch_two,
            normed_two,
            memory,
            self_mixed,
            later,
            reduce_share,
            expand_share,
            narrow,
        )
        (
            qkv_share,
            tokens_grad,
            norm_one,
            expand_high,
            cross_output_shard,
            cross_query_shard,
            cross_key_shard,
            cross_value_shard,
            output_shard,
        ) = self_back(
            first,
            self_logs,
            qkv,
            self_mixed,
            mixed_grad,
            normed_one,
            tokens,
            self_total,
            norms,
            early,
            expand_share,
            shares,
            narrow,
        )
        query_shard, key_shard, value_shard, norm_grads = tail(qkv_share, (norm_one, norm_two, norm_three), narrow)
        expand_shard = jnp.concatenate([expand_low, expand_high], axis=1)
    else:
        reduce_sum, expand_sum = staged(reduce_share), staged(expand_share)
        cq_grad, ckv_grad = cross_backward(bounds, cross_logs, cross_q, cross_kv, cross_mixed, mixed_grad, row_count)
        cq_grad, ckv_grad = fence((cq_grad, ckv_grad), reduce_sum, expand_sum)
        cross_shares = [outer_sum(cross_mixed, branch_two), outer_sum(normed_two, cq_grad)]
        cross_shares += [outer_sum(memory, part) for part in (ckv_grad[:, :WIDTH], ckv_grad[:, WIDTH:])]
        cross_sum = staged(*cross_shares)
        self_total, branch_one, mixed_grad, memory_grad, norm_two = cross_close(
            cq_grad, ckv_grad, after_self, cross_total, norms, later
        )
        mixed_grad = fence(mixed_grad, reduce_sum, expand_sum, cross_sum)
        qkv_grad = self_backward(first, self_logs, qkv, self_mixed, mixed_grad, row_count)
        qkv_grad = fence(qkv_grad, reduce_sum, expand_sum, cross_sum)
        last_sum = staged(
            outer_sum(self_mixed, branch_one),
            *[outer_sum(normed_one, qkv_grad[:, n * WIDTH : (n + 1) * WIDTH]) for n in range(3)],
        )
        tokens_grad, norm_one = self_close(qkv_grad, tokens, self_total, norms, early)
        norm_grads = sum_everywhere(jnp.concatenate([norm_one[:2], norm_two[:2], norm_three[:2]]), mesh_axes)
        output_shard, *qkv_shards = last_sum.result().reshape(4, shard_rows, WIDTH)
        query_shard, key_shard, value_shard = from_pairs(jnp.concatenate(qkv_shards, axis=1), 3)
        reduce_shard = reduce_sum.result()
        expand_shard = expand_sum.result()
        cross_output_shard, cross_query_shard, *cross_shards = cross_sum.result().reshape(4, shard_rows, WIDTH)
        cross_key_shard, cross_value_shard = from_pairs(jnp.concatenate(cross_shards, axis=1), 2)

    norm_shards = lax.dynamic_slice_in_dim(norm_grads, device * shard_rows, shard_rows, axis=1)
    return (
        layer_output,
        tokens_grad,
        memory_grad,
        query_shard,
        key_shard,
        value_shard,
        output_shard,
        cross_query_shard,
        cross_key_shard,
        cross_value_shard,
        cross_output_shard,
        expand_shard,
        reduce_shard,
        *[norm_shards[n] for n in range(6)],
    )


def solution(mesh):
    names = ("wide", "narrow")
    mesh_axes = tuple((axis, mesh.shape[axis]) for axis in names)
    split, vector = P(names, None), P(names)
    return jax.shard_map(
        functools.partial(on_device, mesh_axes),
        mesh=mesh,
        in_specs=(split,) * 3 + (vector,) + (split,) * 2 + (P(), P()) + (split,) * 10 + (vector,) * 6,
        out_specs=(split,) * 13 + (vector,) * 6,
        check_vma=False,
    )
```

```python
import functools
import jax
import jax.numpy as jnp
from jax import lax
from jax.experimental import pallas as pl
from jax.experimental.pallas import tpu as pltpu
from jax.sharding import PartitionSpec as P

SEQ = 1024
MEM = 512
HEADS = 16
HEAD_DIM = 64
WIDTH = HEADS * HEAD_DIM
EPSILON = 1e-05
BQ = 256
LOG2E = 1.4426950408889634
SCALE2 = HEAD_DIM**-0.5 * LOG2E
FILLER = -1e30
F32, BF16 = jnp.float32, jnp.bfloat16


def mm(a, b):
    return jnp.dot(a, b, preferred_element_type=F32)


def mm_t(a, b):
    return lax.dot_general(a, b, (((1,), (1,)), ((), ())), preferred_element_type=F32)


def halves(x):
    low = lax.broadcasted_iota(jnp.int32, x.shape, 1) < HEAD_DIM
    zero = jnp.zeros_like(x)
    return (jnp.where(low, x, zero), jnp.where(low, zero, x))


def in_turn(tasks, front, back, ahead):
    waiting = []
    for task in tasks:
        waiting.append((task, front(*task)))
        if len(waiting) > ahead:
            task, held = waiting.pop(0)
            back(*task, *held)
    for task, held in waiting:
        back(*task, *held)


BLOCKS = [slice(i * BQ, (i + 1) * BQ) for i in range(SEQ // BQ)]
TASKS = [(i, h) for i in range(SEQ // BQ) for h in range(2)]


def self_extent(i):
    return (i + 1) * BQ


def cross_extent(i):
    return MEM


def self_visible(first_ref, i):
    shape = (self_extent(i), BQ)
    key = lax.broadcasted_iota(jnp.int32, shape, 0)
    return (key >= first_ref[0, :, BLOCKS[i]]) & (key <= lax.broadcasted_iota(jnp.int32, shape, 1) + i * BQ)


def cross_visible(bounds_ref, i):
    key = lax.broadcasted_iota(jnp.int32, (MEM, BQ), 0)
    return (key >= bounds_ref[0, 0:1, BLOCKS[i]]) & (key < bounds_ref[0, 1:2, BLOCKS[i]])


def attend(q_of, k, v, visible, extent, keep_out, keep_log):
    k_parts, v_t = halves(k), v.T
    outs = {}

    def front(i, h):
        s = jnp.where(visible(i), mm_t(k_parts[h][: extent(i)], q_of(BLOCKS[i])) * SCALE2, FILLER)
        return s, jnp.max(s, axis=0, keepdims=True)

    def back(i, h, s, peak):
        p = jnp.exp2(s - peak)
        total = jnp.sum(p, axis=0, keepdims=True)
        keep_log(h, BLOCKS[i], peak + jnp.log2(total))
        outs[h] = mm(v_t[h * 64 : (h + 1) * 64, : extent(i)], p.astype(BF16)) * (1.0 / total)
        if h == 1:
            keep_out(BLOCKS[i], jnp.concatenate([outs[0], outs[1]], axis=0).T.astype(BF16))

    in_turn(TASKS, front, back, 3)


def attend_back(q_of, k, v, g_ref, out_ref, log_ref, visible, extent, keep_dq, dk_ref, dv_ref):
    k_parts, k_t, v_parts = halves(k), k.T, halves(v)
    deltas, dq = {}, {}
    dk_ref[...] = jnp.zeros_like(dk_ref)
    dv_ref[...] = jnp.zeros_like(dv_ref)

    def front(i, h):
        q, g = q_of(BLOCKS[i]), g_ref[BLOCKS[i], :]
        if h == 0:
            prod = (g.astype(F32) * out_ref[BLOCKS[i], :].astype(F32)).T
            deltas[i] = [jnp.sum(prod[n * 64 : (n + 1) * 64], axis=0, keepdims=True) for n in range(2)]
        s = jnp.where(visible(i), mm_t(k_parts[h][: extent(i)], q) * SCALE2, FILLER)
        p = jnp.exp2(s - log_ref[0, 0, h : h + 1, BLOCKS[i]])
        dp = mm_t(v_parts[h][: extent(i)], g)
        return p.astype(BF16), (p * (dp - deltas[i][h])).astype(BF16)

    def back(i, h, p, ds):
        n = extent(i)
        dv_ref[:n, :] += mm(p, halves(g_ref[BLOCKS[i], :])[h])
        dk_ref[:n, :] += mm(ds, halves(q_of(BLOCKS[i]))[h])
        dq[h] = mm(k_t[h * 64 : (h + 1) * 64, :n], ds)
        if h == 1:
            keep_dq(BLOCKS[i], (jnp.concatenate([dq[0], dq[1]], axis=0) * HEAD_DIM**-0.5).T.astype(BF16))

    in_turn(TASKS, front, back, 2)


def keepers(out_ref, log_ref):
    def keep_out(rows, value):
        out_ref[rows, :] = value

    def keep_log(h, rows, value):
        log_ref[0, 0, h : h + 1, rows] = value

    return keep_out, keep_log


def self_forward_kernel(first_ref, qkv_ref, out_ref, log_ref):
    attend(
        lambda rows: qkv_ref[rows, 0:128],
        qkv_ref[:, 128:256],
        qkv_ref[:, 256:384],
        functools.partial(self_visible, first_ref),
        self_extent,
        *keepers(out_ref, log_ref),
    )


def cross_forward_kernel(bounds_ref, q_ref, kv_ref, out_ref, log_ref):
    attend(
        lambda rows: q_ref[rows, :],
        kv_ref[:, 0:128],
        kv_ref[:, 128:256],
        functools.partial(cross_visible, bounds_ref),
        cross_extent,
        *keepers(out_ref, log_ref),
    )


PAIRS = HEADS // 2
LOG_SPEC = pl.BlockSpec((1, 1, 8, SEQ), lambda r, p: (r, p, 0, 0))
ROW_SPEC = pl.BlockSpec((SEQ, 128), lambda r, p: (r, p))
QKV_SPEC = pl.BlockSpec((SEQ, 384), lambda r, p: (r, p))
KV_SPEC = pl.BlockSpec((MEM, 256), lambda r, p: (r, p))
FIRST_SPEC = pl.BlockSpec((1, 1, SEQ), lambda r, p: (r, 0, 0))
BOUNDS_SPEC = pl.BlockSpec((1, 8, SEQ), lambda r, p: (r, 0, 0))


def attention_call(kernel, name, in_specs, args, row_count):
    return pl.pallas_call(
        kernel,
        grid=(row_count, PAIRS),
        in_specs=in_specs,
        out_specs=[ROW_SPEC, LOG_SPEC],
        out_shape=[
            jax.ShapeDtypeStruct((row_count * SEQ, WIDTH), BF16),
            jax.ShapeDtypeStruct((row_count, PAIRS, 8, SEQ), F32),
        ],
        name=name,
        compiler_params=pltpu.CompilerParams(vmem_limit_bytes=40 << 20),
        cost_estimate=pl.CostEstimate(flops=20 << 30, bytes_accessed=row_count * (8 << 20), transcendentals=8 << 20),
    )(*args)


def self_forward(first, qkv, row_count):
    return attention_call(self_forward_kernel, "self_forward", [FIRST_SPEC, QKV_SPEC], (first, qkv), row_count)


def cross_forward(bounds, q, kv, row_count):
    return attention_call(
        cross_forward_kernel, "cross_forward", [BOUNDS_SPEC, ROW_SPEC, KV_SPEC], (bounds, q, kv), row_count
    )


def self_backward_kernel(first_ref, log_ref, qkv_ref, out_ref, grad_ref, dqkv_ref, dk_ref, dv_ref):
    def keep_dq(rows, value):
        dqkv_ref[rows, 0:128] = value

    attend_back(
        lambda rows: qkv_ref[rows, 0:128],
        qkv_ref[:, 128:256],
        qkv_ref[:, 256:384],
        grad_ref,
        out_ref,
        log_ref,
        functools.partial(self_visible, first_ref),
        self_extent,
        keep_dq,
        dk_ref,
        dv_ref,
    )
    dqkv_ref[:, 128:256] = (dk_ref[...] * HEAD_DIM**-0.5).astype(BF16)
    dqkv_ref[:, 256:384] = dv_ref[...].astype(BF16)


def self_backward(first, logs, qkv, out, grad, row_count):
    return pl.pallas_call(
        self_backward_kernel,
        grid=(row_count, PAIRS),
        in_specs=[FIRST_SPEC, LOG_SPEC, QKV_SPEC, ROW_SPEC, ROW_SPEC],
        out_specs=QKV_SPEC,
        scratch_shapes=[pltpu.VMEM((SEQ, 128), F32), pltpu.VMEM((SEQ, 128), F32)],
        out_shape=jax.ShapeDtypeStruct((row_count * SEQ, 3 * WIDTH), BF16),
        name="self_backward",
        compiler_params=pltpu.CompilerParams(vmem_limit_bytes=40 << 20),
        cost_estimate=pl.CostEstimate(flops=40 << 30, bytes_accessed=row_count * (16 << 20), transcendentals=8 << 20),
    )(first, logs, qkv, out, grad)


def cross_backward_pair(bounds_ref, log_ref, q_ref, kv_ref, out_ref, grad_ref, keep_dq, dkv_ref, dk_ref, dv_ref):
    attend_back(
        lambda rows: q_ref[rows, :],
        kv_ref[:, 0:128],
        kv_ref[:, 128:256],
        grad_ref,
        out_ref,
        log_ref,
        functools.partial(cross_visible, bounds_ref),
        cross_extent,
        keep_dq,
        dk_ref,
        dv_ref,
    )


def cross_backward_kernel(bounds_ref, log_ref, q_ref, kv_ref, out_ref, grad_ref, dq_ref, dkv_ref, dk_ref, dv_ref):
    def keep_dq(rows, value):
        dq_ref[rows, :] = value

    cross_backward_pair(bounds_ref, log_ref, q_ref, kv_ref, out_ref, grad_ref, keep_dq, dkv_ref, dk_ref, dv_ref)
    dkv_ref[:, 0:128] = (dk_ref[...] * HEAD_DIM**-0.5).astype(BF16)
    dkv_ref[:, 128:256] = dv_ref[...].astype(BF16)


def cross_backward(bounds, logs, q, kv, out, grad, row_count):
    return pl.pallas_call(
        cross_backward_kernel,
        grid=(row_count, PAIRS),
        in_specs=[BOUNDS_SPEC, LOG_SPEC, ROW_SPEC, KV_SPEC, ROW_SPEC, ROW_SPEC],
        out_specs=[ROW_SPEC, KV_SPEC],
        scratch_shapes=[pltpu.VMEM((MEM, 128), F32), pltpu.VMEM((MEM, 128), F32)],
        out_shape=[
            jax.ShapeDtypeStruct((row_count * SEQ, WIDTH), BF16),
            jax.ShapeDtypeStruct((row_count * MEM, 2 * WIDTH), BF16),
        ],
        name="cross_backward",
        compiler_params=pltpu.CompilerParams(vmem_limit_bytes=40 << 20),
        cost_estimate=pl.CostEstimate(flops=40 << 30, bytes_accessed=row_count * (12 << 20), transcendentals=8 << 20),
    )(bounds, logs, q, kv, out, grad)


def row_bounds(pair_starts, source_starts, live_length):
    places = jnp.arange(SEQ, dtype=jnp.int32)
    counted = jnp.sum((pair_starts[:, :, None] <= places).astype(jnp.int32), axis=1)
    live = places < live_length[:, None]
    begun = jnp.max(jnp.where(pair_starts[:, :, None] <= places, pair_starts[:, :, None], 0), axis=1)
    first = jnp.where(live, begun, live_length[:, None])
    nseg = pair_starts.shape[1]
    pick = jnp.arange(nseg)[None, :, None] == (counted - 1)[:, None, :]
    ends = jnp.concatenate([source_starts[:, 1:], jnp.full_like(source_starts[:, :1], MEM)], axis=1)
    start = jnp.sum(jnp.where(pick, source_starts[:, :, None], 0), axis=1)
    end = jnp.sum(jnp.where(pick, ends[:, :, None], 0), axis=1)
    start = jnp.where(live, start, 0)
    end = jnp.where(live, end, MEM)
    bounds = jnp.pad(jnp.stack([start, end], axis=1), ((0, 0), (0, 6), (0, 0)))
    return first[:, None, :], bounds


TB = 256


def norm_parts(values):
    center = values - jnp.mean(values, axis=-1, keepdims=True)
    inverse = lax.rsqrt(jnp.mean(center * center, axis=-1, keepdims=True) + EPSILON)
    return center * inverse, inverse


def norm_back(unit, inverse, gain, gradient):
    scaled = gradient * gain
    return inverse * (
        scaled
        - jnp.mean(scaled, axis=-1, keepdims=True)
        - unit * jnp.mean(scaled * unit, axis=-1, keepdims=True)
    )


def add_norm_grads(ref, unit, gradient):
    @pl.when(pl.program_id(0) == 0)
    def _():
        ref[...] = jnp.zeros_like(ref)

    ref[0:1, :] += jnp.sum(gradient * unit, axis=0, keepdims=True)
    ref[1:2, :] += jnp.sum(gradient, axis=0, keepdims=True)


def tile(rows, columns, at=0):
    return pl.BlockSpec((rows, columns), lambda b: (b, at))


def whole(rows, columns, at=0):
    return pl.BlockSpec((rows, columns), lambda b: (0, at), pipeline_mode=pl.Buffered(1))


def shape(rows, columns, dtype):
    return jax.ShapeDtypeStruct((rows, columns), dtype)


def params(mib):
    return pltpu.CompilerParams(vmem_limit_bytes=mib << 20)


def cost(flops, moved):
    return pl.CostEstimate(flops=int(flops), bytes_accessed=int(moved), transcendentals=0)


def project_kernel(tokens_ref, norms_ref, weight_ref, normed_ref, out_ref):
    unit, _ = norm_parts(tokens_ref[...].astype(F32))
    normed = (unit * norms_ref[0:1, :] + norms_ref[1:2, :]).astype(BF16)
    normed_ref[...] = normed
    for part in range(3):
        at = slice(part * 1024, (part + 1) * 1024)
        out_ref[:, at] = mm(normed, weight_ref[:, at]).astype(BF16)


def project(tokens, norms, early):
    rows, d = tokens.shape
    return pl.pallas_call(
        project_kernel,
        grid=(rows // TB,),
        in_specs=[tile(TB, d), whole(8, d), whole(d, 3 * d)],
        out_specs=[tile(TB, d), tile(TB, 3 * d)],
        out_shape=[shape(rows, d, BF16), shape(rows, 3 * d, BF16)],
        name="project",
        compiler_params=params(40),
        cost_estimate=cost(6 * rows * d * d, 16 << 20),
    )(tokens, norms, early)


def middle_kernel(
    mixed_ref, tokens_ref, memory_ref, norms_ref, wo_ref, wq_ref, wkv_ref, after_ref, normed_ref, q_ref, kv_ref
):
    after = tokens_ref[...].astype(F32) + mm(mixed_ref[...], wo_ref[...])
    after_ref[...] = after
    kv_ref[...] = mm(memory_ref[...], wkv_ref[...]).astype(BF16)
    unit, _ = norm_parts(after)
    normed = (unit * norms_ref[2:3, :] + norms_ref[3:4, :]).astype(BF16)
    normed_ref[...] = normed
    q_ref[...] = mm(normed, wq_ref[...]).astype(BF16)


def middle(mixed, tokens, memory, norms, early):
    rows, d = tokens.shape
    mem_rows = memory.shape[0]
    steps = rows // TB
    mb = mem_rows // steps
    return pl.pallas_call(
        middle_kernel,
        grid=(steps,),
        in_specs=[
            tile(TB, d),
            tile(TB, d),
            tile(mb, d),
            whole(8, d),
            whole(d, d, OUT_SELF),
            whole(d, d, QUERY_CROSS),
            whole(d, 2 * d, KV_CROSS),
        ],
        out_specs=[tile(TB, d), tile(TB, d), tile(TB, d), tile(mb, 2 * d)],
        out_shape=[shape(rows, d, F32), shape(rows, d, BF16), shape(rows, d, BF16), shape(mem_rows, 2 * d, BF16)],
        name="middle",
        compiler_params=params(40),
        cost_estimate=cost(6 * rows * d * d, 20 << 20),
    )(mixed, tokens, memory, norms, early, early, early)


GELU_A = 0.7978845608028654
GELU_B = 0.044715


def hidden_parts(win_ref, wout_ref, part, d):
    if len(win_ref.shape) == 2:
        at = slice(part * d, (part + 1) * d)
        return win_ref[:, at], wout_ref[at, :]
    devices, quad, _ = win_ref.shape
    rows, share = quad // 4, devices // 4
    win = win_ref[:, part * rows : (part + 1) * rows, :].reshape(d, d)
    return win, wout_ref[part * share : (part + 1) * share].reshape(d, d)


def feed_kernel(
    live_ref,
    weight_ref,
    mixed_ref,
    before_ref,
    cot_ref,
    norms_ref,
    wo_ref,
    win_ref,
    wout_ref,
    out_ref,
    normed_ref,
    act_ref,
    hid_ref,
    b3_ref,
    total_ref,
    b2_ref,
    grad_ref,
    ngrad_ref,
):
    block = pl.program_id(0)
    per_row = SEQ // TB
    row = block // per_row
    places = lax.broadcasted_iota(jnp.int32, (TB, 1), 0) + (block % per_row) * TB
    live = (places < live_ref[row]).astype(F32)
    out_grad = cot_ref[...].astype(F32) * live * weight_ref[0]
    branch = out_grad.astype(BF16)
    b3_ref[...] = branch
    after = before_ref[...] + mm(mixed_ref[...], wo_ref[...])
    unit, inverse = norm_parts(after)
    normed = (unit * norms_ref[4:5, :] + norms_ref[5:6, :]).astype(BF16)
    normed_ref[...] = normed
    d = normed.shape[1]
    result, back = after, None
    for part in range(act_ref.shape[1] // d):
        at = slice(part * d, (part + 1) * d)
        win, wout = hidden_parts(win_ref, wout_ref, part, d)
        x = mm(normed, win)
        square = x * x
        t = jnp.tanh(GELU_A * x * (1.0 + GELU_B * square))
        half = 0.5 * (1.0 + t)
        act = (x * half).astype(BF16)
        slope = half + (0.5 * GELU_A) * x * (1.0 - t * t) * (1.0 + (3.0 * GELU_B) * square)
        act_ref[:, at] = act
        hid = (mm_t(branch, wout) * slope).astype(BF16)
        hid_ref[:, at] = hid
        result = result + mm(act, wout)
        term = mm_t(hid, win)
        back = term if back is None else back + term
    out_ref[...] = result.astype(BF16)
    total = out_grad + norm_back(unit, inverse, norms_ref[4:5, :], back)
    total_ref[...] = total
    b2 = total.astype(BF16)
    b2_ref[...] = b2
    grad_ref[...] = mm_t(b2, wo_ref[...]).astype(BF16)
    add_norm_grads(ngrad_ref, unit, back)


def feed(live_length, row_weight, mixed, before, cotangent, norms, early, late):
    rows, d = cotangent.shape
    ff = 4 * d
    if len(late) == 1:
        devices, block, _ = late[0].shape
        late = late * 2
        late_specs = [
            pl.BlockSpec((devices, block // 2, d), lambda b, n=n: (0, n, 0), pipeline_mode=pl.Buffered(1)) for n in range(2)
        ]
    else:
        late_specs = [whole(d, ff), whole(ff, d)]
    smem = pl.BlockSpec(memory_space=pltpu.SMEM)
    return pl.pallas_call(
        feed_kernel,
        grid=(rows // TB,),
        in_specs=[
            smem,
            smem,
            tile(TB, d),
            tile(TB, d),
            tile(TB, d),
            whole(8, d),
            whole(d, d, OUT_CROSS),
            *late_specs,
        ],
        out_specs=[
            tile(TB, d),
            tile(TB, d),
            tile(TB, ff),
            tile(TB, ff),
            tile(TB, d),
            tile(TB, d),
            tile(TB, d),
            tile(TB, d),
            whole(8, d),
        ],
        out_shape=[
            shape(rows, d, BF16),
            shape(rows, d, BF16),
            shape(rows, ff, BF16),
            shape(rows, ff, BF16),
            shape(rows, d, BF16),
            shape(rows, d, F32),
            shape(rows, d, BF16),
            shape(rows, d, BF16),
            shape(8, d, F32),
        ],
        name="feed",
        compiler_params=params(58),
        cost_estimate=cost(38 * rows * d * d, 50 << 20),
    )(live_length, row_weight, mixed, before, cotangent, norms, early, *late)


def cross_close_kernel(
    dq_ref, dkv_ref, before_ref, total_ref, norms_ref, wq_ref, wkv_ref, wo_ref, out_ref, b1_ref, grad_ref, mem_ref, ngrad_ref
):
    gradient = mm_t(dq_ref[...], wq_ref[...])
    mem_ref[...] = mm_t(dkv_ref[...], wkv_ref[...]).astype(BF16)
    unit, inverse = norm_parts(before_ref[...])
    total = total_ref[...] + norm_back(unit, inverse, norms_ref[2:3, :], gradient)
    out_ref[...] = total
    b1 = total.astype(BF16)
    b1_ref[...] = b1
    grad_ref[...] = mm_t(b1, wo_ref[...]).astype(BF16)
    add_norm_grads(ngrad_ref, unit, gradient)


def cross_close(dq, dkv, before, total, norms, early):
    rows, d = dq.shape
    mem_rows = dkv.shape[0]
    steps = rows // TB
    mb = mem_rows // steps
    return pl.pallas_call(
        cross_close_kernel,
        grid=(steps,),
        in_specs=[
            tile(TB, d),
            tile(mb, 2 * d),
            tile(TB, d),
            tile(TB, d),
            whole(8, d),
            whole(d, d, QUERY_CROSS),
            whole(d, 2 * d, KV_CROSS),
            whole(d, d, OUT_SELF),
        ],
        out_specs=[tile(TB, d), tile(TB, d), tile(TB, d), tile(mb, d), whole(8, d)],
        out_shape=[
            shape(rows, d, F32),
            shape(rows, d, BF16),
            shape(rows, d, BF16),
            shape(mem_rows, d, BF16),
            shape(8, d, F32),
        ],
        name="cross_close",
        compiler_params=params(40),
        cost_estimate=cost(6 * rows * d * d, 24 << 20),
    )(dq, dkv, before, total, norms, early, early, early)


def self_close_kernel(dqkv_ref, before_ref, total_ref, norms_ref, w_ref, out_ref, ngrad_ref):
    gradient = mm_t(dqkv_ref[...], w_ref[...])
    unit, inverse = norm_parts(before_ref[...].astype(F32))
    total = total_ref[...] + norm_back(unit, inverse, norms_ref[0:1, :], gradient)
    out_ref[...] = total.astype(BF16)
    add_norm_grads(ngrad_ref, unit, gradient)


def self_close(dqkv, before, total, norms, early):
    rows, d = total.shape
    return pl.pallas_call(
        self_close_kernel,
        grid=(rows // TB,),
        in_specs=[tile(TB, 3 * d), tile(TB, d), tile(TB, d), whole(8, d), whole(d, 3 * d)],
        out_specs=[tile(TB, d), whole(8, d)],
        out_shape=[shape(rows, d, BF16), shape(8, d, F32)],
        name="self_close",
        compiler_params=params(40),
        cost_estimate=cost(6 * rows * d * d, 20 << 20),
    )(dqkv, before, total, norms, early)


OUT_SELF, QUERY_CROSS, KV_CROSS, OUT_CROSS = 0, 1, 1, 4


def greet_all(narrow):
    w, z = lax.axis_index("wide"), lax.axis_index("narrow")
    barrier = pltpu.get_barrier_semaphore()
    others = [(w ^ 1, z), (w ^ 2, z), (w ^ 4, z)] + [(w, z ^ mask) for mask in range(1, narrow)]
    for other in others:
        pl.semaphore_signal(barrier, inc=1, device_id=other, device_id_type=pl.DeviceIdType.MESH)
    pl.semaphore_wait(barrier, len(others))


class Gather:
    def __init__(self, shard_ref, out_ref, send_sems, recv_sems, narrow):
        self.shard_ref, self.out_ref = shard_ref, out_ref
        self.send_sems, self.recv_sems = send_sems, recv_sems
        self.narrow = narrow
        self.rows = shard_ref.shape[0]
        self.half = self.rows // 2
        self.w, self.z = w, z = lax.axis_index("wide"), lax.axis_index("narrow")
        self.core, self.x, self.y, self.xy = w ^ 1, w ^ 2, w ^ 4, w ^ 6
        self.above, self.below = (w, z + 1), (w, z - 1)
        self.at_core, self.at_x, self.at_y = (self.core, z), (self.x, z), (self.y, z)
        self.up, self.down, self.to_x, self.to_y, self.on_y, self.on_x, self.to_core = [k * narrow for k in range(7)]

    def move(self, holder, s, number, target, first=0, count=None, own=False):
        count = self.rows if count is None else count
        at = pl.multiple_of((holder * self.narrow + s) * self.rows + first, self.half)
        place = self.out_ref.at[pl.ds(at, count)]
        return pltpu.make_async_remote_copy(
            src_ref=self.shard_ref.at[pl.ds(first, count)] if own else place,
            dst_ref=place,
            send_sem=self.send_sems.at[number],
            recv_sem=self.recv_sems.at[number],
            device_id=target,
            device_id_type=pl.DeviceIdType.MESH,
        )

    def own_place(self):
        return self.out_ref.at[pl.ds(pl.multiple_of((self.w * self.narrow + self.z) * self.rows, self.rows), self.rows)]

    def spread(self, s, own=False):
        self.move(self.w, s, self.to_x + s, self.at_x, own=own).start()
        self.move(self.w, s, self.to_y + s, self.at_y, own=own).start()
        self.move(self.w, s, self.to_core + s, self.at_core, own=own).start()

    def relay(self, s):
        half = self.half
        self.move(self.x, s, self.to_x + s, self.at_x).wait_recv()
        self.move(self.x, s, self.on_y + s, self.at_y, 0, half).start()
        self.move(self.x, s, self.to_core + self.narrow + s, self.at_core).start()
        self.move(self.y, s, self.to_y + s, self.at_y).wait_recv()
        self.move(self.y, s, self.on_x + s, self.at_x, half, half).start()
        self.move(self.y, s, self.to_core + 2 * self.narrow + s, self.at_core).start()

    def corner(self, s):
        self.move(self.xy, s, self.on_y + s, self.at_y, 0, self.half).wait_recv()
        self.move(self.xy, s, self.on_x + s, self.at_x, self.half, self.half).wait_recv()
        self.move(self.xy, s, self.to_core + 3 * self.narrow + s, self.at_core).start()

    def at_distance(self, r, action):
        if r == 0:
            action(self.z)
        else:
            pl.when(self.z - r >= 0)(lambda: action(self.z - r))
            pl.when(self.z + r < self.narrow)(lambda: action(self.z + r))

    def begin_line(self):
        z = self.z
        pl.when(z < self.narrow - 1)(lambda: self.move(self.w, z, self.up + z, self.above, own=True).start())
        pl.when(z > 0)(lambda: self.move(self.w, z, self.down + z, self.below, own=True).start())

    def begin_spread(self):
        self.spread(self.z, own=True)

    def round(self, r):
        z = self.z

        def from_below():
            s = z - r
            self.move(self.w, s, self.up + s, self.above).wait_recv()
            pl.when(z < self.narrow - 1)(lambda: self.move(self.w, s, self.up + s, self.above).start())
            self.spread(s)

        def from_above():
            s = z + r
            self.move(self.w, s, self.down + s, self.below).wait_recv()
            pl.when(z > 0)(lambda: self.move(self.w, s, self.down + s, self.below).start())
            self.spread(s)

        if r < self.narrow:
            pl.when(z - r >= 0)(from_below)
            pl.when(z + r < self.narrow)(from_above)
        self.at_distance(r - 1, self.relay)

    def corners(self):
        for r in range(self.narrow):
            self.at_distance(r, self.corner)

    def arrive(self):
        for s in range(self.narrow):
            for k, holder in enumerate((self.w, self.x, self.y, self.xy)):
                self.move(holder ^ 1, s, self.to_core + k * self.narrow + s, self.at_core).wait_recv()

    def close(self):
        z, half = self.z, self.half
        for s in range(self.narrow):
            up, down = self.move(self.w, s, self.up + s, self.above), self.move(self.w, s, self.down + s, self.below)
            pl.when((s <= z) & (z < self.narrow - 1))(up.wait_send)
            pl.when((s >= z) & (z > 0))(down.wait_send)
            self.move(self.w, s, self.to_x + s, self.at_x).wait_send()
            self.move(self.w, s, self.to_y + s, self.at_y).wait_send()
            self.move(self.x, s, self.on_y + s, self.at_y, 0, half).wait_send()
            self.move(self.y, s, self.on_x + s, self.at_x, half, half).wait_send()
            for k, holder in enumerate((self.w, self.x, self.y, self.xy)):
                self.move(holder, s, self.to_core + k * self.narrow + s, self.at_core).wait_send()


def place_bounds(live_ref, pairs_ref, sources_ref, first_ref, bounds_ref):
    place = lax.broadcasted_iota(jnp.int32, (1, SEQ), 1)
    live = place < live_ref[0]
    count = pairs_ref.shape[1]
    first, start, end = jnp.zeros_like(place), jnp.zeros_like(place), jnp.zeros_like(place)
    for n in range(count):
        begun = place >= pairs_ref[0, n]
        first = jnp.where(begun, pairs_ref[0, n], first)
        start = jnp.where(begun, sources_ref[0, n], start)
        end = jnp.where(begun, sources_ref[0, n + 1] if n + 1 < count else MEM, end)
    first_ref[0] = jnp.where(live, first, live_ref[0])
    bounds_ref[0, 0:1, :] = jnp.where(live, start, 0)
    bounds_ref[0, 1:2, :] = jnp.where(live, end, MEM)
    bounds_ref[0, 2:8, :] = jnp.zeros((6, SEQ), jnp.int32)


def front_kernel(
    narrow,
    live_ref,
    pairs_ref,
    sources_ref,
    wq_ref,
    wk_ref,
    wv_ref,
    ck_ref,
    cv_ref,
    others_refs,
    hidden_in_ref,
    hidden_out_ref,
    extra_ref,
    tokens_ref,
    memory_ref,
    wide_any,
    later_any,
    late_any,
    normed_any,
    qkv_any,
    mixed_ref,
    log_ref,
    norms_ref,
    first_ref,
    bounds_ref,
    after_ref,
    normed_two_ref,
    cross_q_ref,
    cross_kv_ref,
    cross_mixed_ref,
    cross_log_ref,
    shard_a,
    shard_b,
    shard_c,
    weight,
    later,
    normed,
    qkv,
    a_send,
    a_recv,
    b_send,
    b_recv,
    c_send,
    c_recv,
    local_sems,
):
    d = tokens_ref.shape[1]
    rows = wq_ref.shape[0]
    for p in range(PAIRS):
        lanes = slice(p * 128, (p + 1) * 128)
        for n, ref in enumerate((wq_ref, wk_ref, wv_ref)):
            shard_a[:, (3 * p + n) * 128 : (3 * p + n + 1) * 128] = ref[:, lanes]
        for n, ref in enumerate((ck_ref, cv_ref)):
            at = KV_CROSS * 2 * d + (2 * p + n) * 128
            shard_b[:, at : at + 128] = ref[:, lanes]
    shard_a[:, 3 * d :] = extra_ref[...]

    one = Gather(shard_a, weight, a_send, a_recv, narrow)
    two = Gather(shard_b, later, b_send, b_recv, narrow)
    three = Gather(shard_c, late_any, c_send, c_recv, narrow)
    keeps = [
        pltpu.make_async_copy(gather.shard_ref, gather.own_place(), local_sems.at[n])
        for n, gather in enumerate((one, two, three))
    ]
    greet_all(narrow)
    one.begin_line()
    one.begin_spread()
    keeps[0].start()
    for at, ref in zip((OUT_SELF, QUERY_CROSS, OUT_CROSS), others_refs):
        shard_b[:, at * d : (at + 1) * d] = ref[...]
    for n in range(4):
        shard_c[n * rows : (n + 1) * rows, :] = hidden_in_ref[:, n * d : (n + 1) * d]
    shard_c[4 * rows :, :] = hidden_out_ref[...]
    keeps[1].start()
    keeps[2].start()
    place_bounds(live_ref, pairs_ref, sources_ref, first_ref, bounds_ref)
    one.round(1)
    one.round(2)
    two.begin_line()
    for r in range(3, narrow + 1):
        one.round(r)
    two.begin_spread()
    one.corners()
    one.arrive()
    keeps[0].wait()
    out_wide = pltpu.make_async_copy(weight, wide_any, local_sems.at[3])
    out_wide.start()

    norms_ref[...] = weight[:, 3 * d :].astype(F32).T[0:8, :]

    def project_block(t, carry):
        at = pl.ds(pl.multiple_of(t * TB, TB), TB)
        unit, _ = norm_parts(tokens_ref[at, :].astype(F32))
        value = (unit * norms_ref[0:1, :] + norms_ref[1:2, :]).astype(BF16)
        normed[at, :] = value
        for part in range(3):
            lanes = slice(part * d, (part + 1) * d)
            qkv[at, lanes] = mm(value, weight[:, lanes]).astype(BF16)
        return carry

    def pair_block(p, carry):
        def lanes(n):
            return pl.ds(pl.multiple_of(p * 384 + n * 128, 128), 128)

        attend(
            lambda at: qkv[at, lanes(0)],
            qkv[:, lanes(1)],
            qkv[:, lanes(2)],
            functools.partial(self_visible, first_ref),
            self_extent,
            *pair_keepers(mixed_ref, log_ref, p),
        )
        return carry

    def middle_block(t, carry):
        at = pl.ds(pl.multiple_of(t * TB, TB), TB)
        mb = memory_ref.shape[0] * TB // tokens_ref.shape[0]
        mem_at = pl.ds(pl.multiple_of(t * mb, mb), mb)
        after = tokens_ref[at, :].astype(F32) + mm(mixed_ref[at, :], later[:, OUT_SELF * d : (OUT_SELF + 1) * d])
        after_ref[at, :] = after
        for n in range(2):
            lanes = slice((2 * KV_CROSS + n) * d, (2 * KV_CROSS + n + 1) * d)
            cross_kv_ref[mem_at, n * d : (n + 1) * d] = mm(memory_ref[mem_at, :], later[:, lanes]).astype(BF16)
        unit, _ = norm_parts(after)
        value = (unit * norms_ref[2:3, :] + norms_ref[3:4, :]).astype(BF16)
        normed_two_ref[at, :] = value
        cross_q_ref[at, :] = mm(value, later[:, QUERY_CROSS * d : (QUERY_CROSS + 1) * d]).astype(BF16)
        return carry

    def cross_block(p, carry):
        def lanes(n):
            return pl.ds(pl.multiple_of(p * 256 + n * 128, 128), 128)

        q_lanes = pl.ds(pl.multiple_of(p * 128, 128), 128)
        attend(
            lambda at: cross_q_ref[at, q_lanes],
            cross_kv_ref[:, lanes(0)],
            cross_kv_ref[:, lanes(1)],
            functools.partial(cross_visible, bounds_ref),
            cross_extent,
            *pair_keepers(cross_mixed_ref, cross_log_ref, p),
        )
        return carry

    lax.fori_loop(0, 4, project_block, 0)
    out_normed = pltpu.make_async_copy(normed, normed_any, local_sems.at[4])
    out_qkv = pltpu.make_async_copy(qkv, qkv_any, local_sems.at[5])
    out_normed.start()
    out_qkv.start()
    two.round(1)
    lax.fori_loop(0, 2, pair_block, 0)
    two.round(2)
    lax.fori_loop(2, 5, pair_block, 0)
    for r in range(3, narrow):
        two.round(r)
    three.begin_line()
    lax.fori_loop(5, 8, pair_block, 0)
    two.round(narrow)
    three.begin_spread()
    two.corners()
    two.arrive()
    keeps[1].wait()
    out_later = pltpu.make_async_copy(later, later_any, local_sems.at[6])
    out_later.start()
    lax.fori_loop(0, 4, middle_block, 0)
    three.round(1)
    lax.fori_loop(0, 4, cross_block, 0)
    three.round(2)
    lax.fori_loop(4, 8, cross_block, 0)
    for r in range(3, narrow + 1):
        three.round(r)
    three.corners()
    three.arrive()
    keeps[2].wait()
    for gather in (one, two, three):
        gather.close()
    for copy in (out_wide, out_normed, out_qkv, out_later):
        copy.wait()


def pair_keepers(out_ref, log_ref, p):
    def keep_out(at, value):
        out_ref[at, pl.ds(pl.multiple_of(p * 128, 128), 128)] = value

    def keep_log(h, at, value):
        log_ref[0, p, h : h + 1, at] = value

    return keep_out, keep_log


def front(live_length, pair_starts, source_starts, weights, hidden_in, hidden_out, extra, tokens, memory, narrow):
    self_query, self_key, self_value, self_output, cross_query, cross_key, cross_value, cross_output = weights
    shard_rows, d = self_query.shape
    rows, mem_rows = tokens.shape[0], memory.shape[0]
    block = 4 * shard_rows + hidden_out.shape[0]
    anywhere, vmem = pl.BlockSpec(memory_space=pl.ANY), pl.BlockSpec(memory_space=pltpu.VMEM)
    smem = pl.BlockSpec(memory_space=pltpu.SMEM)
    logs = jax.ShapeDtypeStruct((1, PAIRS, 8, SEQ), F32)

    def kernel(*refs):
        front_kernel(narrow, *refs[:8], refs[8:11], *refs[11:])

    return pl.pallas_call(
        kernel,
        in_specs=[smem] * 3 + [vmem] * 13,
        out_specs=[anywhere] * 5 + [vmem] * 11,
        out_shape=[
            shape(d, 3 * d + 128, BF16),
            shape(d, 5 * d, BF16),
            shape(8 * narrow * block, d, BF16),
            shape(rows, d, BF16),
            shape(rows, 3 * d, BF16),
            shape(rows, d, BF16),
            logs,
            shape(8, d, F32),
            jax.ShapeDtypeStruct((1, 1, SEQ), jnp.int32),
            jax.ShapeDtypeStruct((1, 8, SEQ), jnp.int32),
            shape(rows, d, F32),
            shape(rows, d, BF16),
            shape(rows, d, BF16),
            shape(mem_rows, 2 * d, BF16),
            shape(rows, d, BF16),
            logs,
        ],
        scratch_shapes=[
            pltpu.VMEM((shard_rows, 3 * d + 128), BF16),
            pltpu.VMEM((shard_rows, 5 * d), BF16),
            pltpu.VMEM((block, d), BF16),
            pltpu.VMEM((d, 3 * d + 128), BF16),
            pltpu.VMEM((d, 5 * d), BF16),
            pltpu.VMEM((rows, d), BF16),
            pltpu.VMEM((rows, 3 * d), BF16),
            *[pltpu.SemaphoreType.DMA((10 * narrow,))] * 6,
            pltpu.SemaphoreType.DMA((7,)),
        ],
        name="front",
        compiler_params=pltpu.CompilerParams(collective_id=0, has_side_effects=True, vmem_limit_bytes=60 << 20),
        cost_estimate=cost(30 * rows * d * d, 200 << 20),
    )(
        live_length,
        pair_starts,
        source_starts,
        self_query,
        self_key,
        self_value,
        cross_key,
        cross_value,
        self_output,
        cross_query,
        cross_output,
        hidden_in,
        hidden_out,
        extra,
        tokens,
        memory,
    )


def stages_of(mesh_axes):
    plan = []
    for axis, size in mesh_axes:
        bits = size.bit_length() - 1
        at = 0
        while at < bits:
            take = 1 if (bits - at) % 2 else 2
            plan.append((axis, at, take))
            at += take
    return plan


def trade(value, axis, size, mask):
    return lax.ppermute(value, axis, [(i, i ^ mask) for i in range(size)])


def digit_of(axis, at, take):
    return (lax.axis_index(axis) >> at) & ((1 << take) - 1)


def pick(value, digit, place):
    if isinstance(value, list):
        return jnp.concatenate([pick(v, digit, place) for v in value], axis=0)
    return lax.dynamic_index_in_dim(value, digit, place, keepdims=False)


def add_up(own, pieces):
    total = own.astype(F32)
    for piece in pieces:
        total = total + piece.astype(F32)
    return total


def sum_steps(partial, mesh_axes):
    sizes = dict(mesh_axes)
    plan = stages_of(mesh_axes)
    groups = []
    for axis, _ in mesh_axes:
        groups += sorted((s for s in plan if s[0] == axis), key=lambda s: -s[1])
    devices = 1
    for _, size in mesh_axes:
        devices *= size
    columns = partial[0].shape[1]
    extents = [1 << s[2] for s in groups]
    value = [p.reshape(p.shape[0] // WIDTH, *extents, -1, columns) for p in partial]
    for number, stage in enumerate(plan):
        axis, at, take = stage
        place = 1 + groups.index(stage)
        groups.remove(stage)
        if axis == "wide" and take == 2:
            if isinstance(value, list):
                value = jnp.concatenate(value, axis=0)
            split = value.reshape(*value.shape[:place], 2, 2, *value.shape[place + 1 :])
            a, b = split[..., : columns // 2], split[..., columns // 2 :]
            low, high = digit_of(axis, at, 1), digit_of(axis, at + 1, 1)
            step = ((high, place, 2 << at), (low, place + 1, 1 << at))
            for (digit_a, place_a, mask_a), (digit_b, place_b, mask_b) in (
                step,
                ((low, place, 1 << at), (high, place, 2 << at)),
            ):
                pieces = yield [
                    trade(pick(a, digit_a ^ 1, place_a), axis, sizes[axis], mask_a),
                    trade(pick(b, digit_b ^ 1, place_b), axis, sizes[axis], mask_b),
                ]
                a = add_up(pick(a, digit_a, place_a), pieces[:1]).astype(BF16)
                b = add_up(pick(b, digit_b, place_b), pieces[1:]).astype(BF16)
            value = jnp.concatenate([a, b], axis=-1)
            continue
        digit = digit_of(axis, at, take)
        pieces = yield [
            trade(pick(value, digit ^ mask, place), axis, sizes[axis], mask << at) for mask in range(1, 1 << take)
        ]
        value = add_up(pick(value, digit, place), pieces)
        if number < len(plan) - 1:
            value = value.astype(BF16)
    return value.astype(F32).reshape(-1, columns)


class StagedSum:
    def __init__(self, partial, mesh_axes):
        self.steps = sum_steps(partial, mesh_axes)
        self.under_way = next(self.steps)
        self.value = None

    def go_on(self, pieces):
        try:
            self.under_way = self.steps.send(pieces)
        except StopIteration as stop:
            self.under_way, self.value = None, stop.value

    def result(self):
        while self.under_way is not None:
            self.go_on(self.under_way)
        return self.value


def fence(value, *sums):
    held = [s for s in sums if s.under_way is not None]
    value, arrived = lax.optimization_barrier((value, [s.under_way for s in held]))
    for s, pieces in zip(held, arrived):
        s.go_on(pieces)
    return value


def sum_everywhere(value, mesh_axes):
    sizes = dict(mesh_axes)
    for axis, at, take in stages_of(mesh_axes):
        arrived = [trade(value, axis, sizes[axis], mask << at) for mask in range(1, 1 << take)]
        for piece in arrived:
            value = value + piece
    return value


def by_pairs(*parts):
    rows = parts[0].shape[0]
    return jnp.stack([p.reshape(rows, -1, 128) for p in parts], axis=2).reshape(rows, -1)


def from_pairs(value, count):
    rows = value.shape[0]
    split = value.reshape(rows, -1, count, 128)
    return [split[:, :, c].reshape(rows, -1) for c in range(count)]


def outer_sum(left_side, gradient):
    return jnp.einsum("td,te->de", left_side, gradient, preferred_element_type=F32).astype(BF16)


CHUNKS = 4


class Scatter:
    def __init__(self, own, theirs, buffers, keep, send_sems, recv_sems, narrow):
        self.own, self.theirs, self.keep = own, theirs, keep
        self.from_core, self.a1, self.b1, self.a2, self.b2, self.from_line = buffers
        self.send_sems, self.recv_sems = send_sems, recv_sems
        self.narrow = narrow
        self.slots = own.shape[0]
        self.half = self.a1.shape[-1]
        self.w, self.z = lax.axis_index("wide"), lax.axis_index("narrow")
        self.c, self.x, self.y = self.w & 1, (self.w >> 1) & 1, (self.w >> 2) & 1
        self.per_chunk = 4 + narrow

    def move(self, i, number, src, dst, target):
        at = i * self.per_chunk + number
        return pltpu.make_async_remote_copy(
            src_ref=src,
            dst_ref=dst,
            send_sem=self.send_sems.at[at],
            recv_sem=self.recv_sems.at[at],
            device_id=target,
            device_id_type=pl.DeviceIdType.MESH,
        )

    def to_core(self, i):
        return self.move(i, 0, self.theirs(i), self.from_core.at[i % self.slots], (self.w ^ 1, self.z))

    def first(self, i):
        left, right = pl.ds(0, self.half), pl.ds(self.half, self.half)
        to_x, to_y = (self.w ^ 2, self.z), (self.w ^ 4, self.z)
        return (
            self.move(i, 1, self.own.at[i % self.slots, :, 1 - self.x, :, :, left], self.a1.at[i % self.slots], to_x),
            self.move(i, 2, self.own.at[i % self.slots, 1 - self.y, :, :, :, right], self.b1.at[i % self.slots], to_y),
        )

    def second(self, i):
        left, right = pl.ds(0, self.half), pl.ds(self.half, self.half)
        to_x, to_y = (self.w ^ 2, self.z), (self.w ^ 4, self.z)
        return (
            self.move(i, 3, self.own.at[i % self.slots, 1 - self.y, self.x, :, :, left], self.a2.at[i % self.slots], to_y),
            self.move(i, 4, self.own.at[i % self.slots, self.y, 1 - self.x, :, :, right], self.b2.at[i % self.slots], to_x),
        )

    def along(self, i):
        return [
            self.move(
                i,
                4 + mask,
                self.own.at[i % self.slots, self.y, self.x, self.z ^ mask],
                self.from_line.at[i % self.slots, mask - 1],
                (self.w, self.z ^ mask),
            )
            for mask in range(1, self.narrow)
        ]

    def begin(self, i):
        self.to_core(i).start()

    def add(self, i, y, x, columns, piece):
        now = self.own[i % self.slots, y, x, :, :, columns]
        self.own[i % self.slots, y, x, :, :, columns] = now + piece

    def step(self, i, stage):
        both, left, right = slice(None), slice(0, self.half), slice(self.half, None)
        if stage == 0:
            self.to_core(i).wait_recv()
            for a in range(2):
                for b in range(2):
                    self.add(i, a, b, both, self.from_core[i % self.slots, a, b])
            for copy in self.first(i):
                copy.start()
        elif stage == 1:
            for copy in self.first(i):
                copy.wait_recv()
            for a in range(2):
                self.add(i, a, self.x, left, self.a1[i % self.slots, a])
                self.add(i, self.y, a, right, self.b1[i % self.slots, a])
            for copy in self.second(i):
                copy.start()
        elif stage == 2:
            for copy in self.second(i):
                copy.wait_recv()
            self.add(i, self.y, self.x, left, self.a2[i % self.slots])
            self.add(i, self.y, self.x, right, self.b2[i % self.slots])
            for copy in self.along(i):
                copy.start()
        else:
            for copy in self.along(i):
                copy.wait_recv()
            total = self.own[i % self.slots, self.y, self.x, self.z].astype(F32)
            for mask in range(1, self.narrow):
                total = total + self.from_line[i % self.slots, mask - 1].astype(F32)
            self.keep(i, total)

    def close(self, i):
        for copy in (self.to_core(i), *self.first(i), *self.second(i), *self.along(i)):
            copy.wait_send()


def scatter_scratch(chunks, narrow, rows, width, more=0):
    copies = (chunks + more) * (4 + narrow)
    return [
        pltpu.VMEM((chunks, 2, 2, narrow, rows, width), BF16),
        pltpu.VMEM((chunks, 2, 2, narrow, rows, width), BF16),
        pltpu.VMEM((chunks, 2, narrow, rows, width // 2), BF16),
        pltpu.VMEM((chunks, 2, narrow, rows, width // 2), BF16),
        pltpu.VMEM((chunks, narrow, rows, width // 2), BF16),
        pltpu.VMEM((chunks, narrow, rows, width // 2), BF16),
        pltpu.VMEM((chunks, narrow - 1, rows, width), BF16),
        pltpu.SemaphoreType.DMA((copies,)),
        pltpu.SemaphoreType.DMA((copies,)),
        pltpu.SemaphoreType.DMA((chunks + more,)),
    ]


class Carried:
    def __init__(self, shares, scratch, keep, narrow):
        own, *buffers, send_sems, recv_sems, self.load_sems = scratch
        self.shares = shares
        self.scatter = Scatter(own, self.other, buffers, keep, send_sems, recv_sems, narrow)
        self.chunks, self.slots = len(shares), own.shape[0]

    def other(self, i):
        return self.shares[i](1 - self.scatter.c)

    def load(self, i):
        return pltpu.make_async_copy(
            self.shares[i](self.scatter.c), self.scatter.own.at[i % self.slots], self.load_sems.at[i]
        )

    def open(self):
        for i in range(self.slots):
            self.load(i).start()
        greet_all(self.scatter.narrow)
        for i in range(2):
            self.scatter.begin(i)

    def reuse(self, i):
        self.scatter.close(i - self.slots)
        self.load(i).start()
        self.scatter.begin(i)

    def steps(self, plan):
        for i, stage in plan:
            if stage == 0:
                self.load(i).wait()
            self.scatter.step(i, stage)
            if stage == 0 and i + 2 < self.slots:
                self.scatter.begin(i + 2)

    def close(self):
        for i in range(self.chunks - self.slots, self.chunks):
            self.scatter.close(i)


def share_views(array, narrow, rows):
    return array.reshape(2, 2, 2, narrow, rows, array.shape[1])


def share_views(array, narrow, rows):
    return array.reshape(2, 2, 2, narrow, rows, array.shape[1])


def columns_of(ref, at, width):
    return lambda core: ref.at[:, :, core, :, :, pl.ds(at, width)]


def tn(a, b):
    return lax.dot_general(a, b, (((0,), (0,)), ((), ())), preferred_element_type=F32)


def outer_into(out_ref, left_ref, right):
    for at in range(0, left_ref.shape[1], 256):
        out_ref[at : at + 256, :] = tn(left_ref[:, at : at + 256], right).astype(BF16)


CROSS_PLAN = (
    ((0, 0),),
    ((1, 0),),
    (),
    ((0, 1), (1, 1)),
    ((2, 0), (3, 0)),
    ((1, 2),),
    ((0, 2),),
    ((2, 1), (4, 0)),
    ((1, 3),),
    ((2, 2), (3, 1), (4, 1)),
    ((3, 2), (5, 0)),
    ((4, 2),),
    ((5, 1),),
    ((5, 2),),
    ((0, 3),),
    (),
    ((2, 3), (3, 3), (4, 3), (5, 3)),
)
CROSS_WIDE = 2


def cross_back_kernel(
    narrow,
    bounds_ref,
    log_ref,
    q_ref,
    kv_ref,
    mixed_pair_ref,
    grad_ref,
    before_ref,
    total_ref,
    norms_ref,
    mixed_ref,
    b2_ref,
    normed_ref,
    memory_ref,
    self_mixed_ref,
    early_any,
    share_any,
    wide_any,
    out_ref,
    next_ref,
    mem_ref,
    ngrad_ref,
    shares_ref,
    shard_ref,
    wide_ref,
    dk_ref,
    dv_ref,
    dq_ref,
    dkv_ref,
    b1_ref,
    wq,
    wkv,
    wo,
    weight_sems,
    *scratch,
):
    step = pl.program_id(0)
    d = wq.shape[0]
    rows = shard_ref.shape[0] // 4

    def keep(i, value):
        if i < 4:
            shard_ref[i * rows : (i + 1) * rows, :] = value
        else:
            wide_ref[:, (i - 4) * d : (i - 3) * d] = value

    def piece(i):
        return lambda core: share_any.at[:, :, core, :, i]

    pieces = [piece(i) for i in range(4)] + [columns_of(wide_any, i * d, d) for i in range(CROSS_WIDE)]
    carried = Carried(pieces, scratch, keep, narrow)
    loads = [
        pltpu.make_async_copy(early_any.at[:, pl.ds(QUERY_CROSS * d, d)], wq, weight_sems.at[0]),
        pltpu.make_async_copy(early_any.at[:, pl.ds(2 * KV_CROSS * d, 2 * d)], wkv, weight_sems.at[1]),
        pltpu.make_async_copy(early_any.at[:, pl.ds(OUT_SELF * d, d)], wo, weight_sems.at[2]),
    ]

    @pl.when(step == 0)
    def _():
        carried.open()
        for load in loads:
            load.start()

    @pl.when(step < PAIRS)
    def _():
        def keep_dq(rows, value):
            dq_ref[rows, pl.ds(pl.multiple_of(step * 128, 128), 128)] = value

        cross_backward_pair(bounds_ref, log_ref, q_ref, kv_ref, mixed_pair_ref, grad_ref, keep_dq, None, dk_ref, dv_ref)
        at = pl.multiple_of(step * 256, 256)
        dkv_ref[:, pl.ds(at, 128)] = (dk_ref[...] * HEAD_DIM**-0.5).astype(BF16)
        dkv_ref[:, pl.ds(pl.multiple_of(at + 128, 128), 128)] = dv_ref[...].astype(BF16)

    @pl.when(step == PAIRS)
    def _():
        for load in loads:
            load.wait()
        ngrad_ref[...] = jnp.zeros_like(ngrad_ref)

    tokens_end = PAIRS + SEQ // TB

    @pl.when((step >= PAIRS) & (step < tokens_end))
    def _():
        t = step - PAIRS
        mb = mem_ref.shape[0]
        at = pl.ds(pl.multiple_of(t * TB, TB), TB)
        gradient = mm_t(dq_ref[at, :], wq[...])
        mem_ref[...] = mm_t(dkv_ref[pl.ds(pl.multiple_of(t * mb, mb), mb), :], wkv[...]).astype(BF16)
        unit, inverse = norm_parts(before_ref[...])
        total = total_ref[...] + norm_back(unit, inverse, norms_ref[2:3, :], gradient)
        out_ref[...] = total
        b1 = total.astype(BF16)
        b1_ref[at, :] = b1
        next_ref[...] = mm_t(b1, wo[...]).astype(BF16)
        ngrad_ref[0:1, :] += jnp.sum(gradient * unit, axis=0, keepdims=True)
        ngrad_ref[1:2, :] += jnp.sum(gradient, axis=0, keepdims=True)

    pl.when(step == tokens_end)(lambda: outer_into(shares_ref, mixed_ref, b2_ref[...]))
    pl.when(step == tokens_end + 1)(lambda: outer_into(shares_ref, normed_ref, dq_ref[...]))
    pl.when(step == tokens_end + 2)(lambda: outer_into(shares_ref, memory_ref, dkv_ref[:, :d]))
    pl.when(step == tokens_end + 3)(lambda: outer_into(shares_ref, memory_ref, dkv_ref[:, d:]))
    pl.when(step == tokens_end + 4)(lambda: outer_into(shares_ref, self_mixed_ref, b1_ref[...]))

    for number, plan in enumerate(CROSS_PLAN):
        pl.when(step == number)(functools.partial(carried.steps, plan))
    pl.when(step == len(CROSS_PLAN) - 1)(carried.close)


def cross_back(bounds, logs, q, kv, mixed, grad, before, total, norms, b2, normed, memory, self_mixed, early, share, wide_share, narrow):
    rows, d = q.shape
    mem_rows = kv.shape[0]
    shard_rows = d // (8 * narrow)
    steps = rows // TB
    mb = mem_rows // steps

    def pair(s):
        return jnp.minimum(s, PAIRS - 1)

    def token(s):
        return jnp.clip(s - PAIRS, 0, steps - 1)

    anywhere = pl.BlockSpec(memory_space=pl.ANY)
    by_pair = pl.BlockSpec((SEQ, 128), lambda s: (0, pair(s)))
    by_token = pl.BlockSpec((TB, d), lambda s: (token(s), 0))
    return pl.pallas_call(
        functools.partial(cross_back_kernel, narrow),
        grid=(PAIRS + steps + 5,),
        in_specs=[
            pl.BlockSpec((1, 8, SEQ), lambda s: (0, 0, 0)),
            pl.BlockSpec((1, 1, 8, SEQ), lambda s: (0, pair(s), 0, 0)),
            by_pair,
            pl.BlockSpec((MEM, 256), lambda s: (0, pair(s))),
            by_pair,
            by_pair,
            by_token,
            by_token,
            whole(8, d),
            whole(rows, d),
            whole(rows, d),
            whole(rows, d),
            whole(mem_rows, d),
            whole(rows, d),
            anywhere,
            anywhere,
            anywhere,
        ],
        out_specs=[
            by_token,
            by_token,
            pl.BlockSpec((mb, d), lambda s: (token(s), 0)),
            whole(8, d),
            pl.BlockSpec((d, d), lambda s: (jnp.maximum(s - PAIRS - steps, 0), 0)),
            whole(4 * shard_rows, d),
            whole(shard_rows, CROSS_WIDE * d),
        ],
        out_shape=[
            shape(rows, d, F32),
            shape(rows, d, BF16),
            shape(mem_rows, d, BF16),
            shape(8, d, F32),
            shape(5 * d, d, BF16),
            shape(4 * shard_rows, d, F32),
            shape(shard_rows, CROSS_WIDE * d, F32),
        ],
        scratch_shapes=[
            pltpu.VMEM((MEM, 128), F32),
            pltpu.VMEM((MEM, 128), F32),
            pltpu.VMEM((rows, d), BF16),
            pltpu.VMEM((mem_rows, 2 * d), BF16),
            pltpu.VMEM((rows, d), BF16),
            pltpu.VMEM((d, d), BF16),
            pltpu.VMEM((d, 2 * d), BF16),
            pltpu.VMEM((d, d), BF16),
            pltpu.SemaphoreType.DMA((3,)),
            *scatter_scratch(4 + CROSS_WIDE, narrow, shard_rows, d),
        ],
        name="cross_back",
        compiler_params=pltpu.CompilerParams(collective_id=2, has_side_effects=True, vmem_limit_bytes=60 << 20),
        cost_estimate=cost(40 * rows * d * d, 100 << 20),
    )(
        bounds,
        logs,
        q,
        kv,
        mixed,
        grad,
        before,
        total,
        norms,
        mixed,
        b2,
        normed,
        memory,
        self_mixed,
        early,
        share.reshape(2, 2, 2, narrow, 4, shard_rows, d),
        share_views(wide_share, narrow, shard_rows),
    )


SELF_PLAN = (
    ((0, 0),),
    ((1, 0),),
    ((2, 0),),
    ((0, 1), (2, 1), (3, 0), (4, 0)),
    ((1, 1),),
    ((0, 2), (2, 2)),
    ((3, 1), (5, 0)),
    ((4, 1), (6, 0)),
    ((0, 3), (2, 3), (1, 2), (3, 2), (5, 1)),
    ((1, 3),),
    ((3, 3), (4, 2), (6, 1), (7, 0)),
    ((8, 0),),
    ((5, 2), (5, 3), (6, 2), (7, 1), (8, 1), (9, 0)),
    ((7, 2), (8, 2), (9, 1), (9, 2)),
    ((4, 3), (6, 3), (7, 3), (8, 3), (9, 3)),
)
SELF_REUSE = {9: 7, 10: 8, 11: 9}
SELF_WIDE = 4 - CROSS_WIDE
SELF_CHUNKS = SELF_WIDE + 5


def self_back_kernel(
    narrow,
    first_ref,
    log_ref,
    qkv_ref,
    mixed_ref,
    grad_ref,
    normed_ref,
    tokens_ref,
    total_ref,
    norms_ref,
    norm_two_ref,
    norm_three_ref,
    early_any,
    wide_any,
    shares_any,
    out_ref,
    norm_out_ref,
    expand_ref,
    cross_output_ref,
    cross_query_ref,
    cross_key_ref,
    cross_value_ref,
    self_output_ref,
    query_ref,
    key_ref,
    value_ref,
    dk_ref,
    dv_ref,
    dqkv,
    weight,
    weight_sem,
    stage,
    nval,
    nin,
    norm_send_sems,
    norm_recv_sems,
    *scratch,
):
    step = pl.program_id(0)
    d = normed_ref.shape[1]

    outs = (query_ref, key_ref, value_ref)

    def keep(i, value):
        i -= SELF_WIDE
        if i < 0:
            expand_ref[:, (i + SELF_WIDE) * d : (i + SELF_WIDE + 1) * d] = value
        elif i == 0:
            cross_output_ref[...] = value
        elif i == 1:
            cross_query_ref[...] = value
        elif i == 4:
            self_output_ref[...] = value
        elif i > 4:
            for n in range(d // 128):
                pair, kind = divmod((i - 5) * d // 128 + n, 3)
                outs[kind][:, pair * 128 : (pair + 1) * 128] = value[:, n * 128 : (n + 1) * 128]
        else:
            for n in range(d // 256):
                at = (i - 2) * d // 2 + n * 128
                cross_key_ref[:, at : at + 128] = value[:, n * 256 : n * 256 + 128]
                cross_value_ref[:, at : at + 128] = value[:, n * 256 + 128 : n * 256 + 256]

    def piece(i):
        return lambda core: shares_any.at[i, :, :, core]

    def staged_piece(i):
        return lambda core: stage.at[i, :, :, core]

    pieces = [columns_of(wide_any, (CROSS_WIDE + i) * d, d) for i in range(SELF_WIDE)] + [piece(i) for i in range(5)]
    pieces += [staged_piece(i) for i in range(3)]
    carried = Carried(pieces, scratch, keep, narrow)
    load = pltpu.make_async_copy(early_any.at[:, pl.ds(0, 3 * d)], weight, weight_sem)

    @pl.when(step == 0)
    def _():
        carried.open()
        load.start()

    @pl.when(step < PAIRS)
    def _():
        base = step * 384

        def keep_dq(rows, value):
            dqkv[rows, pl.ds(pl.multiple_of(base, 128), 128)] = value

        attend_back(
            lambda rows: qkv_ref[rows, 0:128],
            qkv_ref[:, 128:256],
            qkv_ref[:, 256:384],
            grad_ref,
            mixed_ref,
            log_ref,
            functools.partial(self_visible, first_ref),
            self_extent,
            keep_dq,
            dk_ref,
            dv_ref,
        )
        dqkv[:, pl.ds(pl.multiple_of(base + 128, 128), 128)] = (dk_ref[...] * HEAD_DIM**-0.5).astype(BF16)
        dqkv[:, pl.ds(pl.multiple_of(base + 256, 128), 128)] = dv_ref[...].astype(BF16)

    rows = stage.shape[5]
    group = 2 * narrow * rows

    def multiply(m):
        for a in range(2):
            for b in range(2):
                at = (2 * a + b) * group
                product = tn(normed_ref[:, at : at + group], dqkv[:, m * d : (m + 1) * d])
                stage[m, a, b] = product.astype(BF16).reshape(2, narrow, rows, d)

    for m in range(3):
        pl.when(step == PAIRS + m)(functools.partial(multiply, m))

    @pl.when(step == PAIRS + 3)
    def _():
        load.wait()
        nval[0] = jnp.zeros_like(nval[0])
        nval[0, 2:4, :] = norm_two_ref[0:2, :]
        nval[0, 4:6, :] = norm_three_ref[0:2, :]

    @pl.when(step >= PAIRS + 3)
    def _():
        at = pl.ds(pl.multiple_of((step - PAIRS - 3) * TB, TB), TB)
        gradient = mm_t(dqkv[at, :], weight[...])
        unit, inverse = norm_parts(tokens_ref[...].astype(F32))
        total = total_ref[...] + norm_back(unit, inverse, norms_ref[0:1, :], gradient)
        out_ref[...] = total.astype(BF16)
        nval[0, 0:1, :] += jnp.sum(gradient * unit, axis=0, keepdims=True)
        nval[0, 1:2, :] += jnp.sum(gradient, axis=0, keepdims=True)

    w, z = carried.scatter.w, carried.scatter.z

    def norm_copy(stage_number, number, target):
        return pltpu.make_async_remote_copy(
            src_ref=nval.at[stage_number],
            dst_ref=nin.at[number],
            send_sem=norm_send_sems.at[number],
            recv_sem=norm_recv_sems.at[number],
            device_id=target,
            device_id_type=pl.DeviceIdType.MESH,
        )

    norm_copies = [[norm_copy(0, 0, (w ^ 1, z))], [norm_copy(1, 1, (w ^ 2, z))], [norm_copy(2, 2, (w ^ 4, z))]]
    norm_copies.append([norm_copy(3, 2 + mask, (w, z ^ mask)) for mask in range(1, narrow)])

    def norm_step(number):
        if number > 0:
            for copy in norm_copies[number - 1]:
                copy.wait_recv()
            value = nval[number - 1]
            if number < 4:
                nval[number] = value + nin[number - 1]
            else:
                for mask in range(1, narrow):
                    value = value + nin[2 + mask]
                norm_out_ref[...] = value
        if number < 4:
            for copy in norm_copies[number]:
                copy.start()

    last = len(SELF_PLAN) - 1
    for number, plan in enumerate(SELF_PLAN[:last]):
        pl.when(step == number)(functools.partial(carried.steps, plan))
        if number in SELF_REUSE:
            pl.when(step == number)(functools.partial(carried.reuse, SELF_REUSE[number]))

    @pl.when(step == last)
    def _():
        for number in range(5):
            norm_step(number)
            if number < len(SELF_PLAN[last]):
                carried.steps(SELF_PLAN[last][number : number + 1])
        carried.close()
        for copies in norm_copies:
            for copy in copies:
                copy.wait_send()


def self_back(first, logs, qkv, mixed, grad, normed, tokens, total, norms, norm_two, norm_three, early, wide_share, shares, narrow):
    rows, d = mixed.shape
    shard_rows = d // (8 * narrow)

    def pair(s):
        return jnp.minimum(s, PAIRS - 1)

    def token(s):
        return jnp.maximum(s - PAIRS - 3, 0)

    anywhere = pl.BlockSpec(memory_space=pl.ANY)
    by_pair = pl.BlockSpec((SEQ, 128), lambda s: (0, pair(s)))
    by_token = pl.BlockSpec((TB, d), lambda s: (token(s), 0))
    return pl.pallas_call(
        functools.partial(self_back_kernel, narrow),
        grid=(PAIRS + 3 + rows // TB,),
        in_specs=[
            pl.BlockSpec((1, 1, SEQ), lambda s: (0, 0, 0)),
            pl.BlockSpec((1, 1, 8, SEQ), lambda s: (0, pair(s), 0, 0)),
            pl.BlockSpec((SEQ, 384), lambda s: (0, pair(s))),
            by_pair,
            by_pair,
            whole(rows, d),
            by_token,
            by_token,
            whole(8, d),
            whole(8, d),
            whole(8, d),
            anywhere,
            anywhere,
            anywhere,
        ],
        out_specs=[
            by_token,
            whole(8, d),
            whole(shard_rows, SELF_WIDE * d),
            *[whole(shard_rows, d)] * 8,
        ],
        out_shape=[
            shape(rows, d, BF16),
            shape(8, d, F32),
            shape(shard_rows, SELF_WIDE * d, F32),
            *[shape(shard_rows, d, F32)] * 8,
        ],
        scratch_shapes=[
            pltpu.VMEM((SEQ, 128), F32),
            pltpu.VMEM((SEQ, 128), F32),
            pltpu.VMEM((rows, 3 * d), BF16),
            pltpu.VMEM((d, 3 * d), BF16),
            pltpu.SemaphoreType.DMA,
            pltpu.VMEM((3, 2, 2, 2, narrow, shard_rows, d), BF16),
            pltpu.VMEM((4, 8, d), F32),
            pltpu.VMEM((2 + narrow, 8, d), F32),
            pltpu.SemaphoreType.DMA((2 + narrow,)),
            pltpu.SemaphoreType.DMA((2 + narrow,)),
            *scatter_scratch(SELF_CHUNKS, narrow, shard_rows, d, 3),
        ],
        name="self_back",
        compiler_params=pltpu.CompilerParams(collective_id=3, has_side_effects=True, vmem_limit_bytes=60 << 20),
        cost_estimate=cost(40 * rows * d * d, 100 << 20),
    )(
        first,
        logs,
        qkv,
        mixed,
        grad,
        normed,
        tokens,
        total,
        norms,
        norm_two,
        norm_three,
        early,
        share_views(wide_share, narrow, shard_rows),
        shares.reshape(5, 2, 2, 2, narrow, shard_rows, d),
    )


def on_device(
    mesh_axes,
    tokens,
    memory,
    cotangent,
    live_length,
    pair_starts,
    source_starts,
    group_bounds,
    group_counts,
    self_query,
    self_key,
    self_value,
    self_output,
    cross_query,
    cross_key,
    cross_value,
    cross_output,
    hidden_in,
    hidden_out,
    first_gain,
    first_shift,
    second_gain,
    second_shift,
    third_gain,
    third_shift,
):
    names = tuple(axis for axis, _ in mesh_axes)
    row_count = live_length.shape[0]
    shard_rows = self_query.shape[0]
    device_count = 1
    for _, size in mesh_axes:
        device_count *= size

    def staged(*partial):
        return StagedSum(partial, mesh_axes)

    digits = jnp.stack([live_length // 256, live_length % 256], axis=1).astype(BF16)
    digits = jnp.pad(digits, ((0, shard_rows - row_count), (0, 0)))
    norms = jnp.stack([first_gain, first_shift, second_gain, second_shift, third_gain, third_shift], axis=1)
    extra = jnp.pad(jnp.concatenate([norms, digits], axis=1), ((0, 0), (0, 120)))
    weights = (self_query, self_key, self_value, self_output, cross_query, cross_key, cross_value, cross_output)
    fast = mesh_axes[0][1] == 8 and row_count == 1 and shard_rows % 32 == 0
    if fast:
        (
            early,
            later,
            late,
            normed_one,
            qkv,
            self_mixed,
            self_logs,
            norms,
            first,
            bounds,
            after_self,
            normed_two,
            cross_q,
            cross_kv,
            cross_mixed,
            cross_logs,
        ) = front(
            live_length,
            pair_starts,
            source_starts,
            weights,
            hidden_in,
            hidden_out,
            extra,
            tokens,
            memory,
            mesh_axes[1][1],
        )
        late = [late.reshape(device_count, -1, WIDTH)]
    else:
        shard = [by_pairs(self_query, self_key, self_value), extra, self_output, cross_query]
        shard += [by_pairs(cross_key, cross_value), cross_output]
        early = lax.all_gather(jnp.concatenate(shard, axis=1), names, axis=0, tiled=True)
        late = [lax.all_gather(part, names, axis=0, tiled=True) for part in (hidden_in, hidden_out)]
        early, later = early[:, : 3 * WIDTH + 128], early[:, 3 * WIDTH + 128 :]
        norms = early[:, 3 * WIDTH : 3 * WIDTH + 8].astype(F32).T
        first, bounds = row_bounds(pair_starts, source_starts, live_length)
        normed_one, qkv = project(tokens, norms, early)
        self_mixed, self_logs = self_forward(first, qkv, row_count)
        after_self, normed_two, cross_q, cross_kv = middle(self_mixed, tokens, memory, norms, later)
        cross_mixed, cross_logs = cross_forward(bounds, cross_q, cross_kv, row_count)

    live_total = jnp.sum(norms[6]) * 256.0 + jnp.sum(norms[7])
    device = lax.axis_index(names)
    member = (group_bounds[:-1] <= device) & (device < group_bounds[1:])
    pair_tokens = jnp.sum(jnp.where(member, group_counts, 0))
    token_all = row_count * SEQ * device_count
    row_weight = pair_tokens.astype(F32) * (token_all / 1000.0) / live_total
    layer_output, normed_three, activated, hidden_grad, branch_three, cross_total, branch_two, mixed_grad, norm_three = feed(
        live_length, row_weight[None], cross_mixed, after_self, cotangent, norms, later, late
    )

    reduce_share, expand_share = outer_sum(activated, branch_three), outer_sum(normed_three, hidden_grad)
    if fast:
        narrow = mesh_axes[1][1]
        self_total, mixed_grad, memory_grad, norm_two, shares, reduce_shard, expand_low = cross_back(
            bounds,
            cross_logs,
            cross_q,
            cross_kv,
            cross_mixed,
            mixed_grad,
            after_self,
            cross_total,
            norms,
            branch_two,
            normed_two,
            memory,
            self_mixed,
            later,
            reduce_share,
            expand_share,
            narrow,
        )
        (
            tokens_grad,
            norm_grads,
            expand_high,
            cross_output_shard,
            cross_query_shard,
            cross_key_shard,
            cross_value_shard,
            output_shard,
            query_shard,
            key_shard,
            value_shard,
        ) = self_back(
            first,
            self_logs,
            qkv,
            self_mixed,
            mixed_grad,
            normed_one,
            tokens,
            self_total,
            norms,
            norm_two,
            norm_three,
            early,
            expand_share,
            shares,
            narrow,
        )
        expand_shard = jnp.concatenate([expand_low, expand_high], axis=1)
    else:
        reduce_sum, expand_sum = staged(reduce_share), staged(expand_share)
        cq_grad, ckv_grad = cross_backward(bounds, cross_logs, cross_q, cross_kv, cross_mixed, mixed_grad, row_count)
        cq_grad, ckv_grad = fence((cq_grad, ckv_grad), reduce_sum, expand_sum)
        cross_shares = [outer_sum(cross_mixed, branch_two), outer_sum(normed_two, cq_grad)]
        cross_shares += [outer_sum(memory, part) for part in (ckv_grad[:, :WIDTH], ckv_grad[:, WIDTH:])]
        cross_sum = staged(*cross_shares)
        self_total, branch_one, mixed_grad, memory_grad, norm_two = cross_close(
            cq_grad, ckv_grad, after_self, cross_total, norms, later
        )
        mixed_grad = fence(mixed_grad, reduce_sum, expand_sum, cross_sum)
        qkv_grad = self_backward(first, self_logs, qkv, self_mixed, mixed_grad, row_count)
        qkv_grad = fence(qkv_grad, reduce_sum, expand_sum, cross_sum)
        last_sum = staged(
            outer_sum(self_mixed, branch_one),
            *[outer_sum(normed_one, qkv_grad[:, n * WIDTH : (n + 1) * WIDTH]) for n in range(3)],
        )
        tokens_grad, norm_one = self_close(qkv_grad, tokens, self_total, norms, early)
        norm_grads = sum_everywhere(jnp.concatenate([norm_one[:2], norm_two[:2], norm_three[:2]]), mesh_axes)
        output_shard, *qkv_shards = last_sum.result().reshape(4, shard_rows, WIDTH)
        query_shard, key_shard, value_shard = from_pairs(jnp.concatenate(qkv_shards, axis=1), 3)
        reduce_shard = reduce_sum.result()
        expand_shard = expand_sum.result()
        cross_output_shard, cross_query_shard, *cross_shards = cross_sum.result().reshape(4, shard_rows, WIDTH)
        cross_key_shard, cross_value_shard = from_pairs(jnp.concatenate(cross_shards, axis=1), 2)

    norm_shards = lax.dynamic_slice_in_dim(norm_grads, device * shard_rows, shard_rows, axis=1)
    return (
        layer_output,
        tokens_grad,
        memory_grad,
        query_shard,
        key_shard,
        value_shard,
        output_shard,
        cross_query_shard,
        cross_key_shard,
        cross_value_shard,
        cross_output_shard,
        expand_shard,
        reduce_shard,
        *[norm_shards[n] for n in range(6)],
    )


def solution(mesh):
    names = ("wide", "narrow")
    mesh_axes = tuple((axis, mesh.shape[axis]) for axis in names)
    split, vector = P(names, None), P(names)
    return jax.shard_map(
        functools.partial(on_device, mesh_axes),
        mesh=mesh,
        in_specs=(split,) * 3 + (vector,) + (split,) * 2 + (P(), P()) + (split,) * 10 + (vector,) * 6,
        out_specs=(split,) * 13 + (vector,) * 6,
        check_vma=False,
    )
```

```python
import functools
import jax
import jax.numpy as jnp
from jax import lax
from jax.experimental import pallas as pl
from jax.experimental.pallas import tpu as pltpu
from jax.sharding import PartitionSpec as P

SEQ = 1024
MEM = 512
HEADS = 16
HEAD_DIM = 64
WIDTH = HEADS * HEAD_DIM
EPSILON = 1e-05
BQ = 256
LOG2E = 1.4426950408889634
SCALE2 = HEAD_DIM**-0.5 * LOG2E
FILLER = -1e30
F32, BF16 = jnp.float32, jnp.bfloat16


def mm(a, b):
    return jnp.dot(a, b, preferred_element_type=F32)


def mm_t(a, b):
    return lax.dot_general(a, b, (((1,), (1,)), ((), ())), preferred_element_type=F32)


def halves(x):
    low = lax.broadcasted_iota(jnp.int32, x.shape, 1) < HEAD_DIM
    zero = jnp.zeros_like(x)
    return (jnp.where(low, x, zero), jnp.where(low, zero, x))


def in_turn(tasks, front, back, ahead):
    waiting = []
    for task in tasks:
        waiting.append((task, front(*task)))
        if len(waiting) > ahead:
            task, held = waiting.pop(0)
            back(*task, *held)
    for task, held in waiting:
        back(*task, *held)


BLOCKS = [slice(i * BQ, (i + 1) * BQ) for i in range(SEQ // BQ)]
TASKS = [(i, h) for i in range(SEQ // BQ) for h in range(2)]


def self_extent(i):
    return (i + 1) * BQ


def cross_extent(i):
    return MEM


def self_visible(first_ref, i):
    shape = (self_extent(i), BQ)
    key = lax.broadcasted_iota(jnp.int32, shape, 0)
    return (key >= first_ref[0, :, BLOCKS[i]]) & (key <= lax.broadcasted_iota(jnp.int32, shape, 1) + i * BQ)


def cross_visible(bounds_ref, i):
    key = lax.broadcasted_iota(jnp.int32, (MEM, BQ), 0)
    return (key >= bounds_ref[0, 0:1, BLOCKS[i]]) & (key < bounds_ref[0, 1:2, BLOCKS[i]])


def attend(q_of, k, v, visible, extent, keep_out, keep_log):
    k_parts, v_t = halves(k), v.T
    outs = {}

    def front(i, h):
        s = jnp.where(visible(i), mm_t(k_parts[h][: extent(i)], q_of(BLOCKS[i])) * SCALE2, FILLER)
        return s, jnp.max(s, axis=0, keepdims=True)

    def back(i, h, s, peak):
        p = jnp.exp2(s - peak)
        total = jnp.sum(p, axis=0, keepdims=True)
        keep_log(h, BLOCKS[i], peak + jnp.log2(total))
        outs[h] = mm(v_t[h * 64 : (h + 1) * 64, : extent(i)], p.astype(BF16)) * (1.0 / total)
        if h == 1:
            keep_out(BLOCKS[i], jnp.concatenate([outs[0], outs[1]], axis=0).T.astype(BF16))

    in_turn(TASKS, front, back, 3)


def attend_back(q_of, k, v, g_ref, out_ref, log_ref, visible, extent, keep_dq, dk_ref, dv_ref):
    k_parts, k_t, v_parts = halves(k), k.T, halves(v)
    deltas, dq = {}, {}
    dk_ref[...] = jnp.zeros_like(dk_ref)
    dv_ref[...] = jnp.zeros_like(dv_ref)

    def front(i, h):
        q, g = q_of(BLOCKS[i]), g_ref[BLOCKS[i], :]
        if h == 0:
            prod = (g.astype(F32) * out_ref[BLOCKS[i], :].astype(F32)).T
            deltas[i] = [jnp.sum(prod[n * 64 : (n + 1) * 64], axis=0, keepdims=True) for n in range(2)]
        s = jnp.where(visible(i), mm_t(k_parts[h][: extent(i)], q) * SCALE2, FILLER)
        p = jnp.exp2(s - log_ref[0, 0, h : h + 1, BLOCKS[i]])
        dp = mm_t(v_parts[h][: extent(i)], g)
        return p.astype(BF16), (p * (dp - deltas[i][h])).astype(BF16)

    def back(i, h, p, ds):
        n = extent(i)
        dv_ref[:n, :] += mm(p, halves(g_ref[BLOCKS[i], :])[h])
        dk_ref[:n, :] += mm(ds, halves(q_of(BLOCKS[i]))[h])
        dq[h] = mm(k_t[h * 64 : (h + 1) * 64, :n], ds)
        if h == 1:
            keep_dq(BLOCKS[i], (jnp.concatenate([dq[0], dq[1]], axis=0) * HEAD_DIM**-0.5).T.astype(BF16))

    in_turn(TASKS, front, back, 2)


def keepers(out_ref, log_ref):
    def keep_out(rows, value):
        out_ref[rows, :] = value

    def keep_log(h, rows, value):
        log_ref[0, 0, h : h + 1, rows] = value

    return keep_out, keep_log


def self_forward_kernel(first_ref, qkv_ref, out_ref, log_ref):
    attend(
        lambda rows: qkv_ref[rows, 0:128],
        qkv_ref[:, 128:256],
        qkv_ref[:, 256:384],
        functools.partial(self_visible, first_ref),
        self_extent,
        *keepers(out_ref, log_ref),
    )


def cross_forward_kernel(bounds_ref, q_ref, kv_ref, out_ref, log_ref):
    attend(
        lambda rows: q_ref[rows, :],
        kv_ref[:, 0:128],
        kv_ref[:, 128:256],
        functools.partial(cross_visible, bounds_ref),
        cross_extent,
        *keepers(out_ref, log_ref),
    )


PAIRS = HEADS // 2
LOG_SPEC = pl.BlockSpec((1, 1, 8, SEQ), lambda r, p: (r, p, 0, 0))
ROW_SPEC = pl.BlockSpec((SEQ, 128), lambda r, p: (r, p))
QKV_SPEC = pl.BlockSpec((SEQ, 384), lambda r, p: (r, p))
KV_SPEC = pl.BlockSpec((MEM, 256), lambda r, p: (r, p))
FIRST_SPEC = pl.BlockSpec((1, 1, SEQ), lambda r, p: (r, 0, 0))
BOUNDS_SPEC = pl.BlockSpec((1, 8, SEQ), lambda r, p: (r, 0, 0))


def attention_call(kernel, name, in_specs, args, row_count):
    return pl.pallas_call(
        kernel,
        grid=(row_count, PAIRS),
        in_specs=in_specs,
        out_specs=[ROW_SPEC, LOG_SPEC],
        out_shape=[
            jax.ShapeDtypeStruct((row_count * SEQ, WIDTH), BF16),
            jax.ShapeDtypeStruct((row_count, PAIRS, 8, SEQ), F32),
        ],
        name=name,
        compiler_params=pltpu.CompilerParams(vmem_limit_bytes=40 << 20),
        cost_estimate=pl.CostEstimate(flops=20 << 30, bytes_accessed=row_count * (8 << 20), transcendentals=8 << 20),
    )(*args)


def self_forward(first, qkv, row_count):
    return attention_call(self_forward_kernel, "self_forward", [FIRST_SPEC, QKV_SPEC], (first, qkv), row_count)


def cross_forward(bounds, q, kv, row_count):
    return attention_call(
        cross_forward_kernel, "cross_forward", [BOUNDS_SPEC, ROW_SPEC, KV_SPEC], (bounds, q, kv), row_count
    )


def self_backward_kernel(first_ref, log_ref, qkv_ref, out_ref, grad_ref, dqkv_ref, dk_ref, dv_ref):
    def keep_dq(rows, value):
        dqkv_ref[rows, 0:128] = value

    attend_back(
        lambda rows: qkv_ref[rows, 0:128],
        qkv_ref[:, 128:256],
        qkv_ref[:, 256:384],
        grad_ref,
        out_ref,
        log_ref,
        functools.partial(self_visible, first_ref),
        self_extent,
        keep_dq,
        dk_ref,
        dv_ref,
    )
    dqkv_ref[:, 128:256] = (dk_ref[...] * HEAD_DIM**-0.5).astype(BF16)
    dqkv_ref[:, 256:384] = dv_ref[...].astype(BF16)


def self_backward(first, logs, qkv, out, grad, row_count):
    return pl.pallas_call(
        self_backward_kernel,
        grid=(row_count, PAIRS),
        in_specs=[FIRST_SPEC, LOG_SPEC, QKV_SPEC, ROW_SPEC, ROW_SPEC],
        out_specs=QKV_SPEC,
        scratch_shapes=[pltpu.VMEM((SEQ, 128), F32), pltpu.VMEM((SEQ, 128), F32)],
        out_shape=jax.ShapeDtypeStruct((row_count * SEQ, 3 * WIDTH), BF16),
        name="self_backward",
        compiler_params=pltpu.CompilerParams(vmem_limit_bytes=40 << 20),
        cost_estimate=pl.CostEstimate(flops=40 << 30, bytes_accessed=row_count * (16 << 20), transcendentals=8 << 20),
    )(first, logs, qkv, out, grad)


def cross_backward_pair(bounds_ref, log_ref, q_ref, kv_ref, out_ref, grad_ref, keep_dq, dkv_ref, dk_ref, dv_ref):
    attend_back(
        lambda rows: q_ref[rows, :],
        kv_ref[:, 0:128],
        kv_ref[:, 128:256],
        grad_ref,
        out_ref,
        log_ref,
        functools.partial(cross_visible, bounds_ref),
        cross_extent,
        keep_dq,
        dk_ref,
        dv_ref,
    )


def cross_backward_kernel(bounds_ref, log_ref, q_ref, kv_ref, out_ref, grad_ref, dq_ref, dkv_ref, dk_ref, dv_ref):
    def keep_dq(rows, value):
        dq_ref[rows, :] = value

    cross_backward_pair(bounds_ref, log_ref, q_ref, kv_ref, out_ref, grad_ref, keep_dq, dkv_ref, dk_ref, dv_ref)
    dkv_ref[:, 0:128] = (dk_ref[...] * HEAD_DIM**-0.5).astype(BF16)
    dkv_ref[:, 128:256] = dv_ref[...].astype(BF16)


def cross_backward(bounds, logs, q, kv, out, grad, row_count):
    return pl.pallas_call(
        cross_backward_kernel,
        grid=(row_count, PAIRS),
        in_specs=[BOUNDS_SPEC, LOG_SPEC, ROW_SPEC, KV_SPEC, ROW_SPEC, ROW_SPEC],
        out_specs=[ROW_SPEC, KV_SPEC],
        scratch_shapes=[pltpu.VMEM((MEM, 128), F32), pltpu.VMEM((MEM, 128), F32)],
        out_shape=[
            jax.ShapeDtypeStruct((row_count * SEQ, WIDTH), BF16),
            jax.ShapeDtypeStruct((row_count * MEM, 2 * WIDTH), BF16),
        ],
        name="cross_backward",
        compiler_params=pltpu.CompilerParams(vmem_limit_bytes=40 << 20),
        cost_estimate=pl.CostEstimate(flops=40 << 30, bytes_accessed=row_count * (12 << 20), transcendentals=8 << 20),
    )(bounds, logs, q, kv, out, grad)


def row_bounds(pair_starts, source_starts, live_length):
    places = jnp.arange(SEQ, dtype=jnp.int32)
    counted = jnp.sum((pair_starts[:, :, None] <= places).astype(jnp.int32), axis=1)
    live = places < live_length[:, None]
    begun = jnp.max(jnp.where(pair_starts[:, :, None] <= places, pair_starts[:, :, None], 0), axis=1)
    first = jnp.where(live, begun, live_length[:, None])
    nseg = pair_starts.shape[1]
    pick = jnp.arange(nseg)[None, :, None] == (counted - 1)[:, None, :]
    ends = jnp.concatenate([source_starts[:, 1:], jnp.full_like(source_starts[:, :1], MEM)], axis=1)
    start = jnp.sum(jnp.where(pick, source_starts[:, :, None], 0), axis=1)
    end = jnp.sum(jnp.where(pick, ends[:, :, None], 0), axis=1)
    start = jnp.where(live, start, 0)
    end = jnp.where(live, end, MEM)
    bounds = jnp.pad(jnp.stack([start, end], axis=1), ((0, 0), (0, 6), (0, 0)))
    return first[:, None, :], bounds


TB = 256


def norm_parts(values):
    center = values - jnp.mean(values, axis=-1, keepdims=True)
    inverse = lax.rsqrt(jnp.mean(center * center, axis=-1, keepdims=True) + EPSILON)
    return center * inverse, inverse


def norm_back(unit, inverse, gain, gradient):
    scaled = gradient * gain
    return inverse * (
        scaled
        - jnp.mean(scaled, axis=-1, keepdims=True)
        - unit * jnp.mean(scaled * unit, axis=-1, keepdims=True)
    )


def add_norm_grads(ref, unit, gradient):
    @pl.when(pl.program_id(0) == 0)
    def _():
        ref[...] = jnp.zeros_like(ref)

    ref[0:1, :] += jnp.sum(gradient * unit, axis=0, keepdims=True)
    ref[1:2, :] += jnp.sum(gradient, axis=0, keepdims=True)


def tile(rows, columns, at=0):
    return pl.BlockSpec((rows, columns), lambda b: (b, at))


def whole(rows, columns, at=0):
    return pl.BlockSpec((rows, columns), lambda b: (0, at), pipeline_mode=pl.Buffered(1))


def shape(rows, columns, dtype):
    return jax.ShapeDtypeStruct((rows, columns), dtype)


def params(mib):
    return pltpu.CompilerParams(vmem_limit_bytes=mib << 20)


def cost(flops, moved):
    return pl.CostEstimate(flops=int(flops), bytes_accessed=int(moved), transcendentals=0)


def project_kernel(tokens_ref, norms_ref, weight_ref, normed_ref, out_ref):
    unit, _ = norm_parts(tokens_ref[...].astype(F32))
    normed = (unit * norms_ref[0:1, :] + norms_ref[1:2, :]).astype(BF16)
    normed_ref[...] = normed
    for part in range(3):
        at = slice(part * 1024, (part + 1) * 1024)
        out_ref[:, at] = mm(normed, weight_ref[:, at]).astype(BF16)


def project(tokens, norms, early):
    rows, d = tokens.shape
    return pl.pallas_call(
        project_kernel,
        grid=(rows // TB,),
        in_specs=[tile(TB, d), whole(8, d), whole(d, 3 * d)],
        out_specs=[tile(TB, d), tile(TB, 3 * d)],
        out_shape=[shape(rows, d, BF16), shape(rows, 3 * d, BF16)],
        name="project",
        compiler_params=params(40),
        cost_estimate=cost(6 * rows * d * d, 16 << 20),
    )(tokens, norms, early)


def middle_kernel(
    mixed_ref, tokens_ref, memory_ref, norms_ref, wo_ref, wq_ref, wkv_ref, after_ref, normed_ref, q_ref, kv_ref
):
    after = tokens_ref[...].astype(F32) + mm(mixed_ref[...], wo_ref[...])
    after_ref[...] = after
    kv_ref[...] = mm(memory_ref[...], wkv_ref[...]).astype(BF16)
    unit, _ = norm_parts(after)
    normed = (unit * norms_ref[2:3, :] + norms_ref[3:4, :]).astype(BF16)
    normed_ref[...] = normed
    q_ref[...] = mm(normed, wq_ref[...]).astype(BF16)


def middle(mixed, tokens, memory, norms, early):
    rows, d = tokens.shape
    mem_rows = memory.shape[0]
    steps = rows // TB
    mb = mem_rows // steps
    return pl.pallas_call(
        middle_kernel,
        grid=(steps,),
        in_specs=[
            tile(TB, d),
            tile(TB, d),
            tile(mb, d),
            whole(8, d),
            whole(d, d, OUT_SELF),
            whole(d, d, QUERY_CROSS),
            whole(d, 2 * d, KV_CROSS),
        ],
        out_specs=[tile(TB, d), tile(TB, d), tile(TB, d), tile(mb, 2 * d)],
        out_shape=[shape(rows, d, F32), shape(rows, d, BF16), shape(rows, d, BF16), shape(mem_rows, 2 * d, BF16)],
        name="middle",
        compiler_params=params(40),
        cost_estimate=cost(6 * rows * d * d, 20 << 20),
    )(mixed, tokens, memory, norms, early, early, early)


GELU_A = 0.7978845608028654
GELU_B = 0.044715


def hidden_parts(win_ref, wout_ref, part, d):
    if len(win_ref.shape) == 2:
        at = slice(part * d, (part + 1) * d)
        return win_ref[:, at], wout_ref[at, :]
    devices, quad, _ = win_ref.shape
    rows, share = quad // 4, devices // 4
    win = win_ref[:, part * rows : (part + 1) * rows, :].reshape(d, d)
    return win, wout_ref[part * share : (part + 1) * share].reshape(d, d)


def feed_kernel(
    narrow,
    token_all,
    live_ref,
    group_bounds_ref,
    group_counts_ref,
    mixed_ref,
    before_ref,
    cot_ref,
    norms_ref,
    wo_ref,
    win_ref,
    wout_ref,
    out_ref,
    normed_ref,
    act_ref,
    hid_ref,
    b3_ref,
    total_ref,
    b2_ref,
    grad_ref,
    ngrad_ref,
):
    block = pl.program_id(0)
    per_row = SEQ // TB
    row = block // per_row
    places = lax.broadcasted_iota(jnp.int32, (TB, 1), 0) + (block % per_row) * TB
    live = (places < live_ref[row]).astype(F32)
    device = lax.axis_index("wide") * narrow + lax.axis_index("narrow")
    pair_tokens = jnp.int32(0)
    for g in range(group_counts_ref.shape[0]):
        member = (group_bounds_ref[g] <= device) & (device < group_bounds_ref[g + 1])
        pair_tokens += jnp.where(member, group_counts_ref[g], 0)
    live_total = jnp.sum(norms_ref[6:7, :], keepdims=True) * 256.0 + jnp.sum(norms_ref[7:8, :], keepdims=True)
    out_grad = cot_ref[...].astype(F32) * live * (pair_tokens.astype(F32) * (token_all / 1000.0) / live_total)
    branch = out_grad.astype(BF16)
    b3_ref[...] = branch
    after = before_ref[...] + mm(mixed_ref[...], wo_ref[...])
    unit, inverse = norm_parts(after)
    normed = (unit * norms_ref[4:5, :] + norms_ref[5:6, :]).astype(BF16)
    normed_ref[...] = normed
    d = normed.shape[1]
    result, back = after, None
    for part in range(act_ref.shape[1] // d):
        at = slice(part * d, (part + 1) * d)
        win, wout = hidden_parts(win_ref, wout_ref, part, d)
        x = mm(normed, win)
        square = x * x
        t = jnp.tanh(GELU_A * x * (1.0 + GELU_B * square))
        half = 0.5 * (1.0 + t)
        act = (x * half).astype(BF16)
        slope = half + (0.5 * GELU_A) * x * (1.0 - t * t) * (1.0 + (3.0 * GELU_B) * square)
        act_ref[:, at] = act
        hid = (mm_t(branch, wout) * slope).astype(BF16)
        hid_ref[:, at] = hid
        result = result + mm(act, wout)
        term = mm_t(hid, win)
        back = term if back is None else back + term
    out_ref[...] = result.astype(BF16)
    total = out_grad + norm_back(unit, inverse, norms_ref[4:5, :], back)
    total_ref[...] = total
    b2 = total.astype(BF16)
    b2_ref[...] = b2
    grad_ref[...] = mm_t(b2, wo_ref[...]).astype(BF16)
    add_norm_grads(ngrad_ref, unit, back)


def feed(live_length, group_bounds, group_counts, mixed, before, cotangent, norms, early, late, mesh_axes):
    rows, d = cotangent.shape
    (_, wide), (_, narrow) = mesh_axes
    ff = 4 * d
    if len(late) == 1:
        devices, block, _ = late[0].shape
        late = late * 2
        late_specs = [
            pl.BlockSpec((devices, block // 2, d), lambda b, n=n: (0, n, 0), pipeline_mode=pl.Buffered(1)) for n in range(2)
        ]
    else:
        late_specs = [whole(d, ff), whole(ff, d)]
    smem = pl.BlockSpec(memory_space=pltpu.SMEM)
    return pl.pallas_call(
        functools.partial(feed_kernel, narrow, rows * wide * narrow),
        grid=(rows // TB,),
        in_specs=[
            smem,
            smem,
            smem,
            tile(TB, d),
            tile(TB, d),
            tile(TB, d),
            whole(8, d),
            whole(d, d, OUT_CROSS),
            *late_specs,
        ],
        out_specs=[
            tile(TB, d),
            tile(TB, d),
            tile(TB, ff),
            tile(TB, ff),
            tile(TB, d),
            tile(TB, d),
            tile(TB, d),
            tile(TB, d),
            whole(8, d),
        ],
        out_shape=[
            shape(rows, d, BF16),
            shape(rows, d, BF16),
            shape(rows, ff, BF16),
            shape(rows, ff, BF16),
            shape(rows, d, BF16),
            shape(rows, d, F32),
            shape(rows, d, BF16),
            shape(rows, d, BF16),
            shape(8, d, F32),
        ],
        name="feed",
        compiler_params=params(58),
        cost_estimate=cost(38 * rows * d * d, 50 << 20),
    )(live_length, group_bounds, group_counts, mixed, before, cotangent, norms, early, *late)


def cross_close_kernel(
    dq_ref, dkv_ref, before_ref, total_ref, norms_ref, wq_ref, wkv_ref, wo_ref, out_ref, b1_ref, grad_ref, mem_ref, ngrad_ref
):
    gradient = mm_t(dq_ref[...], wq_ref[...])
    mem_ref[...] = mm_t(dkv_ref[...], wkv_ref[...]).astype(BF16)
    unit, inverse = norm_parts(before_ref[...])
    total = total_ref[...] + norm_back(unit, inverse, norms_ref[2:3, :], gradient)
    out_ref[...] = total
    b1 = total.astype(BF16)
    b1_ref[...] = b1
    grad_ref[...] = mm_t(b1, wo_ref[...]).astype(BF16)
    add_norm_grads(ngrad_ref, unit, gradient)


def cross_close(dq, dkv, before, total, norms, early):
    rows, d = dq.shape
    mem_rows = dkv.shape[0]
    steps = rows // TB
    mb = mem_rows // steps
    return pl.pallas_call(
        cross_close_kernel,
        grid=(steps,),
        in_specs=[
            tile(TB, d),
            tile(mb, 2 * d),
            tile(TB, d),
            tile(TB, d),
            whole(8, d),
            whole(d, d, QUERY_CROSS),
            whole(d, 2 * d, KV_CROSS),
            whole(d, d, OUT_SELF),
        ],
        out_specs=[tile(TB, d), tile(TB, d), tile(TB, d), tile(mb, d), whole(8, d)],
        out_shape=[
            shape(rows, d, F32),
            shape(rows, d, BF16),
            shape(rows, d, BF16),
            shape(mem_rows, d, BF16),
            shape(8, d, F32),
        ],
        name="cross_close",
        compiler_params=params(40),
        cost_estimate=cost(6 * rows * d * d, 24 << 20),
    )(dq, dkv, before, total, norms, early, early, early)


def self_close_kernel(dqkv_ref, before_ref, total_ref, norms_ref, w_ref, out_ref, ngrad_ref):
    gradient = mm_t(dqkv_ref[...], w_ref[...])
    unit, inverse = norm_parts(before_ref[...].astype(F32))
    total = total_ref[...] + norm_back(unit, inverse, norms_ref[0:1, :], gradient)
    out_ref[...] = total.astype(BF16)
    add_norm_grads(ngrad_ref, unit, gradient)


def self_close(dqkv, before, total, norms, early):
    rows, d = total.shape
    return pl.pallas_call(
        self_close_kernel,
        grid=(rows // TB,),
        in_specs=[tile(TB, 3 * d), tile(TB, d), tile(TB, d), whole(8, d), whole(d, 3 * d)],
        out_specs=[tile(TB, d), whole(8, d)],
        out_shape=[shape(rows, d, BF16), shape(8, d, F32)],
        name="self_close",
        compiler_params=params(40),
        cost_estimate=cost(6 * rows * d * d, 20 << 20),
    )(dqkv, before, total, norms, early)


OUT_SELF, QUERY_CROSS, KV_CROSS, OUT_CROSS = 0, 1, 1, 4


def greet_all(narrow):
    w, z = lax.axis_index("wide"), lax.axis_index("narrow")
    barrier = pltpu.get_barrier_semaphore()
    others = [(w ^ 1, z), (w ^ 2, z), (w ^ 4, z)] + [(w, z ^ mask) for mask in range(1, narrow)]
    for other in others:
        pl.semaphore_signal(barrier, inc=1, device_id=other, device_id_type=pl.DeviceIdType.MESH)
    pl.semaphore_wait(barrier, len(others))


class Gather:
    def __init__(self, shard_ref, out_ref, send_sems, recv_sems, narrow):
        self.shard_ref, self.out_ref = shard_ref, out_ref
        self.send_sems, self.recv_sems = send_sems, recv_sems
        self.narrow = narrow
        self.rows = shard_ref.shape[0]
        self.half = self.rows // 2
        self.w, self.z = w, z = lax.axis_index("wide"), lax.axis_index("narrow")
        self.core, self.x, self.y, self.xy = w ^ 1, w ^ 2, w ^ 4, w ^ 6
        self.above, self.below = (w, z + 1), (w, z - 1)
        self.at_core, self.at_x, self.at_y = (self.core, z), (self.x, z), (self.y, z)
        self.up, self.down, self.to_x, self.to_y, self.on_y, self.on_x, self.to_core = [k * narrow for k in range(7)]

    def move(self, holder, s, number, target, first=0, count=None, own=False):
        count = self.rows if count is None else count
        at = pl.multiple_of((holder * self.narrow + s) * self.rows + first, self.half)
        place = self.out_ref.at[pl.ds(at, count)]
        return pltpu.make_async_remote_copy(
            src_ref=self.shard_ref.at[pl.ds(first, count)] if own else place,
            dst_ref=place,
            send_sem=self.send_sems.at[number],
            recv_sem=self.recv_sems.at[number],
            device_id=target,
            device_id_type=pl.DeviceIdType.MESH,
        )

    def own_place(self):
        return self.out_ref.at[pl.ds(pl.multiple_of((self.w * self.narrow + self.z) * self.rows, self.rows), self.rows)]

    def spread(self, s, own=False):
        self.move(self.w, s, self.to_x + s, self.at_x, own=own).start()
        self.move(self.w, s, self.to_y + s, self.at_y, own=own).start()
        self.move(self.w, s, self.to_core + s, self.at_core, own=own).start()

    def relay(self, s):
        half = self.half
        self.move(self.x, s, self.to_x + s, self.at_x).wait_recv()
        self.move(self.x, s, self.on_y + s, self.at_y, 0, half).start()
        self.move(self.x, s, self.to_core + self.narrow + s, self.at_core).start()
        self.move(self.y, s, self.to_y + s, self.at_y).wait_recv()
        self.move(self.y, s, self.on_x + s, self.at_x, half, half).start()
        self.move(self.y, s, self.to_core + 2 * self.narrow + s, self.at_core).start()

    def corner(self, s):
        self.move(self.xy, s, self.on_y + s, self.at_y, 0, self.half).wait_recv()
        self.move(self.xy, s, self.on_x + s, self.at_x, self.half, self.half).wait_recv()
        self.move(self.xy, s, self.to_core + 3 * self.narrow + s, self.at_core).start()

    def at_distance(self, r, action):
        if r == 0:
            action(self.z)
        else:
            pl.when(self.z - r >= 0)(lambda: action(self.z - r))
            pl.when(self.z + r < self.narrow)(lambda: action(self.z + r))

    def begin_line(self):
        z = self.z
        pl.when(z < self.narrow - 1)(lambda: self.move(self.w, z, self.up + z, self.above, own=True).start())
        pl.when(z > 0)(lambda: self.move(self.w, z, self.down + z, self.below, own=True).start())

    def begin_spread(self):
        self.spread(self.z, own=True)

    def round(self, r):
        z = self.z

        def from_below():
            s = z - r
            self.move(self.w, s, self.up + s, self.above).wait_recv()
            pl.when(z < self.narrow - 1)(lambda: self.move(self.w, s, self.up + s, self.above).start())
            self.spread(s)

        def from_above():
            s = z + r
            self.move(self.w, s, self.down + s, self.below).wait_recv()
            pl.when(z > 0)(lambda: self.move(self.w, s, self.down + s, self.below).start())
            self.spread(s)

        if r < self.narrow:
            pl.when(z - r >= 0)(from_below)
            pl.when(z + r < self.narrow)(from_above)
        self.at_distance(r - 1, self.relay)

    def corners(self):
        for r in range(self.narrow):
            self.at_distance(r, self.corner)

    def arrive(self):
        for s in range(self.narrow):
            for k, holder in enumerate((self.w, self.x, self.y, self.xy)):
                self.move(holder ^ 1, s, self.to_core + k * self.narrow + s, self.at_core).wait_recv()

    def close(self):
        z, half = self.z, self.half
        for s in range(self.narrow):
            up, down = self.move(self.w, s, self.up + s, self.above), self.move(self.w, s, self.down + s, self.below)
            pl.when((s <= z) & (z < self.narrow - 1))(up.wait_send)
            pl.when((s >= z) & (z > 0))(down.wait_send)
            self.move(self.w, s, self.to_x + s, self.at_x).wait_send()
            self.move(self.w, s, self.to_y + s, self.at_y).wait_send()
            self.move(self.x, s, self.on_y + s, self.at_y, 0, half).wait_send()
            self.move(self.y, s, self.on_x + s, self.at_x, half, half).wait_send()
            for k, holder in enumerate((self.w, self.x, self.y, self.xy)):
                self.move(holder, s, self.to_core + k * self.narrow + s, self.at_core).wait_send()


def place_bounds(live_ref, pairs_ref, sources_ref, first_ref, bounds_ref):
    place = lax.broadcasted_iota(jnp.int32, (1, SEQ), 1)
    live = place < live_ref[0]
    count = pairs_ref.shape[1]
    first, start, end = jnp.zeros_like(place), jnp.zeros_like(place), jnp.zeros_like(place)
    for n in range(count):
        begun = place >= pairs_ref[0, n]
        first = jnp.where(begun, pairs_ref[0, n], first)
        start = jnp.where(begun, sources_ref[0, n], start)
        end = jnp.where(begun, sources_ref[0, n + 1] if n + 1 < count else MEM, end)
    first_ref[0] = jnp.where(live, first, live_ref[0])
    bounds_ref[0, 0:1, :] = jnp.where(live, start, 0)
    bounds_ref[0, 1:2, :] = jnp.where(live, end, MEM)
    bounds_ref[0, 2:8, :] = jnp.zeros((6, SEQ), jnp.int32)


def front_kernel(
    narrow,
    live_ref,
    pairs_ref,
    sources_ref,
    wq_ref,
    wk_ref,
    wv_ref,
    ck_ref,
    cv_ref,
    others_refs,
    hidden_in_ref,
    hidden_out_ref,
    extra_ref,
    tokens_ref,
    memory_ref,
    wide_any,
    later_any,
    late_any,
    normed_any,
    qkv_any,
    mixed_ref,
    log_ref,
    norms_ref,
    first_ref,
    bounds_ref,
    after_ref,
    normed_two_ref,
    cross_q_ref,
    cross_kv_ref,
    cross_mixed_ref,
    cross_log_ref,
    shard_a,
    shard_b,
    shard_c,
    weight,
    later,
    normed,
    qkv,
    a_send,
    a_recv,
    b_send,
    b_recv,
    c_send,
    c_recv,
    local_sems,
):
    d = tokens_ref.shape[1]
    rows = wq_ref.shape[0]
    for p in range(PAIRS):
        lanes = slice(p * 128, (p + 1) * 128)
        for n, ref in enumerate((wq_ref, wk_ref, wv_ref)):
            shard_a[:, (3 * p + n) * 128 : (3 * p + n + 1) * 128] = ref[:, lanes]
        for n, ref in enumerate((ck_ref, cv_ref)):
            at = KV_CROSS * 2 * d + (2 * p + n) * 128
            shard_b[:, at : at + 128] = ref[:, lanes]
    shard_a[:, 3 * d :] = extra_ref[...]

    one = Gather(shard_a, weight, a_send, a_recv, narrow)
    two = Gather(shard_b, later, b_send, b_recv, narrow)
    three = Gather(shard_c, late_any, c_send, c_recv, narrow)
    keeps = [
        pltpu.make_async_copy(gather.shard_ref, gather.own_place(), local_sems.at[n])
        for n, gather in enumerate((one, two, three))
    ]
    greet_all(narrow)
    one.begin_line()
    one.begin_spread()
    keeps[0].start()
    for at, ref in zip((OUT_SELF, QUERY_CROSS, OUT_CROSS), others_refs):
        shard_b[:, at * d : (at + 1) * d] = ref[...]
    for n in range(4):
        shard_c[n * rows : (n + 1) * rows, :] = hidden_in_ref[:, n * d : (n + 1) * d]
    shard_c[4 * rows :, :] = hidden_out_ref[...]
    keeps[1].start()
    keeps[2].start()
    place_bounds(live_ref, pairs_ref, sources_ref, first_ref, bounds_ref)
    one.round(1)
    one.round(2)
    two.begin_line()
    for r in range(3, narrow + 1):
        one.round(r)
    two.begin_spread()
    one.corners()
    one.arrive()
    keeps[0].wait()
    out_wide = pltpu.make_async_copy(weight, wide_any, local_sems.at[3])
    out_wide.start()

    norms_ref[...] = weight[:, 3 * d :].astype(F32).T[0:8, :]

    def project_block(t, carry):
        at = pl.ds(pl.multiple_of(t * TB, TB), TB)
        unit, _ = norm_parts(tokens_ref[at, :].astype(F32))
        value = (unit * norms_ref[0:1, :] + norms_ref[1:2, :]).astype(BF16)
        normed[at, :] = value
        for part in range(3):
            lanes = slice(part * d, (part + 1) * d)
            qkv[at, lanes] = mm(value, weight[:, lanes]).astype(BF16)
        return carry

    def pair_block(p, carry):
        def lanes(n):
            return pl.ds(pl.multiple_of(p * 384 + n * 128, 128), 128)

        attend(
            lambda at: qkv[at, lanes(0)],
            qkv[:, lanes(1)],
            qkv[:, lanes(2)],
            functools.partial(self_visible, first_ref),
            self_extent,
            *pair_keepers(mixed_ref, log_ref, p),
        )
        return carry

    def middle_block(t, carry):
        at = pl.ds(pl.multiple_of(t * TB, TB), TB)
        mb = memory_ref.shape[0] * TB // tokens_ref.shape[0]
        mem_at = pl.ds(pl.multiple_of(t * mb, mb), mb)
        after = tokens_ref[at, :].astype(F32) + mm(mixed_ref[at, :], later[:, OUT_SELF * d : (OUT_SELF + 1) * d])
        after_ref[at, :] = after
        for n in range(2):
            lanes = slice((2 * KV_CROSS + n) * d, (2 * KV_CROSS + n + 1) * d)
            cross_kv_ref[mem_at, n * d : (n + 1) * d] = mm(memory_ref[mem_at, :], later[:, lanes]).astype(BF16)
        unit, _ = norm_parts(after)
        value = (unit * norms_ref[2:3, :] + norms_ref[3:4, :]).astype(BF16)
        normed_two_ref[at, :] = value
        cross_q_ref[at, :] = mm(value, later[:, QUERY_CROSS * d : (QUERY_CROSS + 1) * d]).astype(BF16)
        return carry

    def cross_block(p, carry):
        def lanes(n):
            return pl.ds(pl.multiple_of(p * 256 + n * 128, 128), 128)

        q_lanes = pl.ds(pl.multiple_of(p * 128, 128), 128)
        attend(
            lambda at: cross_q_ref[at, q_lanes],
            cross_kv_ref[:, lanes(0)],
            cross_kv_ref[:, lanes(1)],
            functools.partial(cross_visible, bounds_ref),
            cross_extent,
            *pair_keepers(cross_mixed_ref, cross_log_ref, p),
        )
        return carry

    lax.fori_loop(0, 4, project_block, 0)
    out_normed = pltpu.make_async_copy(normed, normed_any, local_sems.at[4])
    out_qkv = pltpu.make_async_copy(qkv, qkv_any, local_sems.at[5])
    out_normed.start()
    out_qkv.start()
    two.round(1)
    lax.fori_loop(0, 2, pair_block, 0)
    two.round(2)
    lax.fori_loop(2, 5, pair_block, 0)
    for r in range(3, narrow):
        two.round(r)
    three.begin_line()
    lax.fori_loop(5, 8, pair_block, 0)
    two.round(narrow)
    three.begin_spread()
    two.corners()
    two.arrive()
    keeps[1].wait()
    out_later = pltpu.make_async_copy(later, later_any, local_sems.at[6])
    out_later.start()
    three.round(1)
    lax.fori_loop(0, 4, middle_block, 0)
    three.round(2)
    lax.fori_loop(0, 4, cross_block, 0)
    for r in range(3, narrow):
        three.round(r)
    lax.fori_loop(4, 8, cross_block, 0)
    three.round(narrow)
    three.corners()
    three.arrive()
    keeps[2].wait()
    for gather in (one, two, three):
        gather.close()
    for copy in (out_wide, out_normed, out_qkv, out_later):
        copy.wait()


def pair_keepers(out_ref, log_ref, p):
    def keep_out(at, value):
        out_ref[at, pl.ds(pl.multiple_of(p * 128, 128), 128)] = value

    def keep_log(h, at, value):
        log_ref[0, p, h : h + 1, at] = value

    return keep_out, keep_log


def front(live_length, pair_starts, source_starts, weights, hidden_in, hidden_out, extra, tokens, memory, narrow):
    self_query, self_key, self_value, self_output, cross_query, cross_key, cross_value, cross_output = weights
    shard_rows, d = self_query.shape
    rows, mem_rows = tokens.shape[0], memory.shape[0]
    block = 4 * shard_rows + hidden_out.shape[0]
    anywhere, vmem = pl.BlockSpec(memory_space=pl.ANY), pl.BlockSpec(memory_space=pltpu.VMEM)
    smem = pl.BlockSpec(memory_space=pltpu.SMEM)
    logs = jax.ShapeDtypeStruct((1, PAIRS, 8, SEQ), F32)

    def kernel(*refs):
        front_kernel(narrow, *refs[:8], refs[8:11], *refs[11:])

    return pl.pallas_call(
        kernel,
        in_specs=[smem] * 3 + [vmem] * 13,
        out_specs=[anywhere] * 5 + [vmem] * 11,
        out_shape=[
            shape(d, 3 * d + 128, BF16),
            shape(d, 5 * d, BF16),
            shape(8 * narrow * block, d, BF16),
            shape(rows, d, BF16),
            shape(rows, 3 * d, BF16),
            shape(rows, d, BF16),
            logs,
            shape(8, d, F32),
            jax.ShapeDtypeStruct((1, 1, SEQ), jnp.int32),
            jax.ShapeDtypeStruct((1, 8, SEQ), jnp.int32),
            shape(rows, d, F32),
            shape(rows, d, BF16),
            shape(rows, d, BF16),
            shape(mem_rows, 2 * d, BF16),
            shape(rows, d, BF16),
            logs,
        ],
        scratch_shapes=[
            pltpu.VMEM((shard_rows, 3 * d + 128), BF16),
            pltpu.VMEM((shard_rows, 5 * d), BF16),
            pltpu.VMEM((block, d), BF16),
            pltpu.VMEM((d, 3 * d + 128), BF16),
            pltpu.VMEM((d, 5 * d), BF16),
            pltpu.VMEM((rows, d), BF16),
            pltpu.VMEM((rows, 3 * d), BF16),
            *[pltpu.SemaphoreType.DMA((10 * narrow,))] * 6,
            pltpu.SemaphoreType.DMA((7,)),
        ],
        name="front",
        compiler_params=pltpu.CompilerParams(collective_id=0, has_side_effects=True, vmem_limit_bytes=60 << 20),
        cost_estimate=cost(30 * rows * d * d, 200 << 20),
    )(
        live_length,
        pair_starts,
        source_starts,
        self_query,
        self_key,
        self_value,
        cross_key,
        cross_value,
        self_output,
        cross_query,
        cross_output,
        hidden_in,
        hidden_out,
        extra,
        tokens,
        memory,
    )


def stages_of(mesh_axes):
    plan = []
    for axis, size in mesh_axes:
        bits = size.bit_length() - 1
        at = 0
        while at < bits:
            take = 1 if (bits - at) % 2 else 2
            plan.append((axis, at, take))
            at += take
    return plan


def trade(value, axis, size, mask):
    return lax.ppermute(value, axis, [(i, i ^ mask) for i in range(size)])


def digit_of(axis, at, take):
    return (lax.axis_index(axis) >> at) & ((1 << take) - 1)


def pick(value, digit, place):
    if isinstance(value, list):
        return jnp.concatenate([pick(v, digit, place) for v in value], axis=0)
    return lax.dynamic_index_in_dim(value, digit, place, keepdims=False)


def add_up(own, pieces):
    total = own.astype(F32)
    for piece in pieces:
        total = total + piece.astype(F32)
    return total


def sum_steps(partial, mesh_axes):
    sizes = dict(mesh_axes)
    plan = stages_of(mesh_axes)
    groups = []
    for axis, _ in mesh_axes:
        groups += sorted((s for s in plan if s[0] == axis), key=lambda s: -s[1])
    devices = 1
    for _, size in mesh_axes:
        devices *= size
    columns = partial[0].shape[1]
    extents = [1 << s[2] for s in groups]
    value = [p.reshape(p.shape[0] // WIDTH, *extents, -1, columns) for p in partial]
    for number, stage in enumerate(plan):
        axis, at, take = stage
        place = 1 + groups.index(stage)
        groups.remove(stage)
        if axis == "wide" and take == 2:
            if isinstance(value, list):
                value = jnp.concatenate(value, axis=0)
            split = value.reshape(*value.shape[:place], 2, 2, *value.shape[place + 1 :])
            a, b = split[..., : columns // 2], split[..., columns // 2 :]
            low, high = digit_of(axis, at, 1), digit_of(axis, at + 1, 1)
            step = ((high, place, 2 << at), (low, place + 1, 1 << at))
            for (digit_a, place_a, mask_a), (digit_b, place_b, mask_b) in (
                step,
                ((low, place, 1 << at), (high, place, 2 << at)),
            ):
                pieces = yield [
                    trade(pick(a, digit_a ^ 1, place_a), axis, sizes[axis], mask_a),
                    trade(pick(b, digit_b ^ 1, place_b), axis, sizes[axis], mask_b),
                ]
                a = add_up(pick(a, digit_a, place_a), pieces[:1]).astype(BF16)
                b = add_up(pick(b, digit_b, place_b), pieces[1:]).astype(BF16)
            value = jnp.concatenate([a, b], axis=-1)
            continue
        digit = digit_of(axis, at, take)
        pieces = yield [
            trade(pick(value, digit ^ mask, place), axis, sizes[axis], mask << at) for mask in range(1, 1 << take)
        ]
        value = add_up(pick(value, digit, place), pieces)
        if number < len(plan) - 1:
            value = value.astype(BF16)
    return value.astype(F32).reshape(-1, columns)


class StagedSum:
    def __init__(self, partial, mesh_axes):
        self.steps = sum_steps(partial, mesh_axes)
        self.under_way = next(self.steps)
        self.value = None

    def go_on(self, pieces):
        try:
            self.under_way = self.steps.send(pieces)
        except StopIteration as stop:
            self.under_way, self.value = None, stop.value

    def result(self):
        while self.under_way is not None:
            self.go_on(self.under_way)
        return self.value


def fence(value, *sums):
    held = [s for s in sums if s.under_way is not None]
    value, arrived = lax.optimization_barrier((value, [s.under_way for s in held]))
    for s, pieces in zip(held, arrived):
        s.go_on(pieces)
    return value


def sum_everywhere(value, mesh_axes):
    sizes = dict(mesh_axes)
    for axis, at, take in stages_of(mesh_axes):
        arrived = [trade(value, axis, sizes[axis], mask << at) for mask in range(1, 1 << take)]
        for piece in arrived:
            value = value + piece
    return value


def by_pairs(*parts):
    rows = parts[0].shape[0]
    return jnp.stack([p.reshape(rows, -1, 128) for p in parts], axis=2).reshape(rows, -1)


def from_pairs(value, count):
    rows = value.shape[0]
    split = value.reshape(rows, -1, count, 128)
    return [split[:, :, c].reshape(rows, -1) for c in range(count)]


def outer_sum(left_side, gradient):
    return jnp.einsum("td,te->de", left_side, gradient, preferred_element_type=F32).astype(BF16)


CHUNKS = 4


class Scatter:
    def __init__(self, own, theirs, buffers, keep, send_sems, recv_sems, narrow):
        self.own, self.theirs, self.keep = own, theirs, keep
        self.from_core, self.a1, self.b1, self.a2, self.b2, self.from_line = buffers
        self.send_sems, self.recv_sems = send_sems, recv_sems
        self.narrow = narrow
        self.slots = own.shape[0]
        self.half = self.a1.shape[-1]
        self.w, self.z = lax.axis_index("wide"), lax.axis_index("narrow")
        self.c, self.x, self.y = self.w & 1, (self.w >> 1) & 1, (self.w >> 2) & 1
        self.per_chunk = 4 + narrow

    def move(self, i, number, src, dst, target):
        at = i * self.per_chunk + number
        return pltpu.make_async_remote_copy(
            src_ref=src,
            dst_ref=dst,
            send_sem=self.send_sems.at[at],
            recv_sem=self.recv_sems.at[at],
            device_id=target,
            device_id_type=pl.DeviceIdType.MESH,
        )

    def to_core(self, i):
        return self.move(i, 0, self.theirs(i), self.from_core.at[i % self.slots], (self.w ^ 1, self.z))

    def first(self, i):
        left, right = pl.ds(0, self.half), pl.ds(self.half, self.half)
        to_x, to_y = (self.w ^ 2, self.z), (self.w ^ 4, self.z)
        return (
            self.move(i, 1, self.own.at[i % self.slots, :, 1 - self.x, :, :, left], self.a1.at[i % self.slots], to_x),
            self.move(i, 2, self.own.at[i % self.slots, 1 - self.y, :, :, :, right], self.b1.at[i % self.slots], to_y),
        )

    def second(self, i):
        left, right = pl.ds(0, self.half), pl.ds(self.half, self.half)
        to_x, to_y = (self.w ^ 2, self.z), (self.w ^ 4, self.z)
        return (
            self.move(i, 3, self.own.at[i % self.slots, 1 - self.y, self.x, :, :, left], self.a2.at[i % self.slots], to_y),
            self.move(i, 4, self.own.at[i % self.slots, self.y, 1 - self.x, :, :, right], self.b2.at[i % self.slots], to_x),
        )

    def along(self, i):
        return [
            self.move(
                i,
                4 + mask,
                self.own.at[i % self.slots, self.y, self.x, self.z ^ mask],
                self.from_line.at[i % self.slots, mask - 1],
                (self.w, self.z ^ mask),
            )
            for mask in range(1, self.narrow)
        ]

    def begin(self, i):
        self.to_core(i).start()

    def add(self, i, y, x, columns, piece):
        now = self.own[i % self.slots, y, x, :, :, columns]
        self.own[i % self.slots, y, x, :, :, columns] = now + piece

    def step(self, i, stage):
        both, left, right = slice(None), slice(0, self.half), slice(self.half, None)
        if stage == 0:
            self.to_core(i).wait_recv()
            for a in range(2):
                for b in range(2):
                    self.add(i, a, b, both, self.from_core[i % self.slots, a, b])
            for copy in self.first(i):
                copy.start()
        elif stage == 1:
            for copy in self.first(i):
                copy.wait_recv()
            for a in range(2):
                self.add(i, a, self.x, left, self.a1[i % self.slots, a])
                self.add(i, self.y, a, right, self.b1[i % self.slots, a])
            for copy in self.second(i):
                copy.start()
        elif stage == 2:
            for copy in self.second(i):
                copy.wait_recv()
            self.add(i, self.y, self.x, left, self.a2[i % self.slots])
            self.add(i, self.y, self.x, right, self.b2[i % self.slots])
            for copy in self.along(i):
                copy.start()
        else:
            for copy in self.along(i):
                copy.wait_recv()
            total = self.own[i % self.slots, self.y, self.x, self.z].astype(F32)
            for mask in range(1, self.narrow):
                total = total + self.from_line[i % self.slots, mask - 1].astype(F32)
            self.keep(i, total)

    def close(self, i):
        for copy in (self.to_core(i), *self.first(i), *self.second(i), *self.along(i)):
            copy.wait_send()


def scatter_scratch(chunks, narrow, rows, width, more=0):
    copies = (chunks + more) * (4 + narrow)
    return [
        pltpu.VMEM((chunks, 2, 2, narrow, rows, width), BF16),
        pltpu.VMEM((chunks, 2, 2, narrow, rows, width), BF16),
        pltpu.VMEM((chunks, 2, narrow, rows, width // 2), BF16),
        pltpu.VMEM((chunks, 2, narrow, rows, width // 2), BF16),
        pltpu.VMEM((chunks, narrow, rows, width // 2), BF16),
        pltpu.VMEM((chunks, narrow, rows, width // 2), BF16),
        pltpu.VMEM((chunks, narrow - 1, rows, width), BF16),
        pltpu.SemaphoreType.DMA((copies,)),
        pltpu.SemaphoreType.DMA((copies,)),
        pltpu.SemaphoreType.DMA((chunks + more,)),
    ]


class Carried:
    def __init__(self, shares, scratch, keep, narrow):
        own, *buffers, send_sems, recv_sems, self.load_sems = scratch
        self.shares = shares
        self.scatter = Scatter(own, self.other, buffers, keep, send_sems, recv_sems, narrow)
        self.chunks, self.slots = len(shares), own.shape[0]

    def other(self, i):
        return self.shares[i](1 - self.scatter.c)

    def load(self, i):
        return pltpu.make_async_copy(
            self.shares[i](self.scatter.c), self.scatter.own.at[i % self.slots], self.load_sems.at[i]
        )

    def open(self):
        for i in range(self.slots):
            self.load(i).start()
        greet_all(self.scatter.narrow)
        for i in range(2):
            self.scatter.begin(i)

    def reuse(self, i):
        self.scatter.close(i - self.slots)
        self.load(i).start()
        self.scatter.begin(i)

    def steps(self, plan):
        for i, stage in plan:
            if stage == 0:
                self.load(i).wait()
            self.scatter.step(i, stage)
            if stage == 0 and i + 2 < self.slots:
                self.scatter.begin(i + 2)

    def close(self):
        for i in range(self.chunks - self.slots, self.chunks):
            self.scatter.close(i)


def share_views(array, narrow, rows):
    return array.reshape(2, 2, 2, narrow, rows, array.shape[1])


def share_views(array, narrow, rows):
    return array.reshape(2, 2, 2, narrow, rows, array.shape[1])


def columns_of(ref, at, width):
    return lambda core: ref.at[:, :, core, :, :, pl.ds(at, width)]


def tn(a, b):
    return lax.dot_general(a, b, (((0,), (0,)), ((), ())), preferred_element_type=F32)


def outer_into(out_ref, left_ref, right):
    for at in range(0, left_ref.shape[1], 256):
        out_ref[at : at + 256, :] = tn(left_ref[:, at : at + 256], right).astype(BF16)


CROSS_PLAN = (
    ((0, 0),),
    ((1, 0),),
    (),
    ((0, 1), (1, 1)),
    ((2, 0), (3, 0)),
    ((1, 2),),
    ((0, 2),),
    ((2, 1), (4, 0)),
    ((1, 3),),
    ((2, 2), (3, 1), (4, 1)),
    ((3, 2), (5, 0)),
    ((4, 2),),
    ((5, 1),),
    ((5, 2),),
    ((0, 3),),
    (),
    ((2, 3), (3, 3), (4, 3), (5, 3)),
)
CROSS_WIDE = 2


def cross_back_kernel(
    narrow,
    bounds_ref,
    log_ref,
    q_ref,
    kv_ref,
    mixed_pair_ref,
    grad_ref,
    before_ref,
    total_ref,
    norms_ref,
    mixed_ref,
    b2_ref,
    normed_ref,
    memory_ref,
    self_mixed_ref,
    early_any,
    share_any,
    wide_any,
    out_ref,
    next_ref,
    mem_ref,
    ngrad_ref,
    shares_ref,
    shard_ref,
    wide_ref,
    dk_ref,
    dv_ref,
    dq_ref,
    dkv_ref,
    b1_ref,
    wq,
    wkv,
    wo,
    weight_sems,
    *scratch,
):
    step = pl.program_id(0)
    d = wq.shape[0]
    rows = shard_ref.shape[0] // 4

    def keep(i, value):
        if i < 4:
            shard_ref[i * rows : (i + 1) * rows, :] = value
        else:
            wide_ref[:, (i - 4) * d : (i - 3) * d] = value

    def piece(i):
        return lambda core: share_any.at[:, :, core, :, i]

    pieces = [piece(i) for i in range(4)] + [columns_of(wide_any, i * d, d) for i in range(CROSS_WIDE)]
    carried = Carried(pieces, scratch, keep, narrow)
    loads = [
        pltpu.make_async_copy(early_any.at[:, pl.ds(QUERY_CROSS * d, d)], wq, weight_sems.at[0]),
        pltpu.make_async_copy(early_any.at[:, pl.ds(2 * KV_CROSS * d, 2 * d)], wkv, weight_sems.at[1]),
        pltpu.make_async_copy(early_any.at[:, pl.ds(OUT_SELF * d, d)], wo, weight_sems.at[2]),
    ]

    @pl.when(step == 0)
    def _():
        carried.open()
        for load in loads:
            load.start()

    @pl.when(step < PAIRS)
    def _():
        def keep_dq(rows, value):
            dq_ref[rows, pl.ds(pl.multiple_of(step * 128, 128), 128)] = value

        cross_backward_pair(bounds_ref, log_ref, q_ref, kv_ref, mixed_pair_ref, grad_ref, keep_dq, None, dk_ref, dv_ref)
        at = pl.multiple_of(step * 256, 256)
        dkv_ref[:, pl.ds(at, 128)] = (dk_ref[...] * HEAD_DIM**-0.5).astype(BF16)
        dkv_ref[:, pl.ds(pl.multiple_of(at + 128, 128), 128)] = dv_ref[...].astype(BF16)

    @pl.when(step == PAIRS)
    def _():
        for load in loads:
            load.wait()
        ngrad_ref[...] = jnp.zeros_like(ngrad_ref)

    tokens_end = PAIRS + SEQ // TB

    @pl.when((step >= PAIRS) & (step < tokens_end))
    def _():
        t = step - PAIRS
        mb = mem_ref.shape[0]
        at = pl.ds(pl.multiple_of(t * TB, TB), TB)
        gradient = mm_t(dq_ref[at, :], wq[...])
        mem_ref[...] = mm_t(dkv_ref[pl.ds(pl.multiple_of(t * mb, mb), mb), :], wkv[...]).astype(BF16)
        unit, inverse = norm_parts(before_ref[...])
        total = total_ref[...] + norm_back(unit, inverse, norms_ref[2:3, :], gradient)
        out_ref[...] = total
        b1 = total.astype(BF16)
        b1_ref[at, :] = b1
        next_ref[...] = mm_t(b1, wo[...]).astype(BF16)
        ngrad_ref[0:1, :] += jnp.sum(gradient * unit, axis=0, keepdims=True)
        ngrad_ref[1:2, :] += jnp.sum(gradient, axis=0, keepdims=True)

    pl.when(step == tokens_end)(lambda: outer_into(shares_ref, mixed_ref, b2_ref[...]))
    pl.when(step == tokens_end + 1)(lambda: outer_into(shares_ref, normed_ref, dq_ref[...]))
    pl.when(step == tokens_end + 2)(lambda: outer_into(shares_ref, memory_ref, dkv_ref[:, :d]))
    pl.when(step == tokens_end + 3)(lambda: outer_into(shares_ref, memory_ref, dkv_ref[:, d:]))
    pl.when(step == tokens_end + 4)(lambda: outer_into(shares_ref, self_mixed_ref, b1_ref[...]))

    for number, plan in enumerate(CROSS_PLAN):
        pl.when(step == number)(functools.partial(carried.steps, plan))
    pl.when(step == len(CROSS_PLAN) - 1)(carried.close)


def cross_back(bounds, logs, q, kv, mixed, grad, before, total, norms, b2, normed, memory, self_mixed, early, share, wide_share, narrow):
    rows, d = q.shape
    mem_rows = kv.shape[0]
    shard_rows = d // (8 * narrow)
    steps = rows // TB
    mb = mem_rows // steps

    def pair(s):
        return jnp.minimum(s, PAIRS - 1)

    def token(s):
        return jnp.clip(s - PAIRS, 0, steps - 1)

    anywhere = pl.BlockSpec(memory_space=pl.ANY)
    by_pair = pl.BlockSpec((SEQ, 128), lambda s: (0, pair(s)))
    by_token = pl.BlockSpec((TB, d), lambda s: (token(s), 0))
    return pl.pallas_call(
        functools.partial(cross_back_kernel, narrow),
        grid=(PAIRS + steps + 5,),
        in_specs=[
            pl.BlockSpec((1, 8, SEQ), lambda s: (0, 0, 0)),
            pl.BlockSpec((1, 1, 8, SEQ), lambda s: (0, pair(s), 0, 0)),
            by_pair,
            pl.BlockSpec((MEM, 256), lambda s: (0, pair(s))),
            by_pair,
            by_pair,
            by_token,
            by_token,
            whole(8, d),
            whole(rows, d),
            whole(rows, d),
            whole(rows, d),
            whole(mem_rows, d),
            whole(rows, d),
            anywhere,
            anywhere,
            anywhere,
        ],
        out_specs=[
            by_token,
            by_token,
            pl.BlockSpec((mb, d), lambda s: (token(s), 0)),
            whole(8, d),
            pl.BlockSpec((d, d), lambda s: (jnp.maximum(s - PAIRS - steps, 0), 0)),
            whole(4 * shard_rows, d),
            whole(shard_rows, CROSS_WIDE * d),
        ],
        out_shape=[
            shape(rows, d, F32),
            shape(rows, d, BF16),
            shape(mem_rows, d, BF16),
            shape(8, d, F32),
            shape(5 * d, d, BF16),
            shape(4 * shard_rows, d, F32),
            shape(shard_rows, CROSS_WIDE * d, F32),
        ],
        scratch_shapes=[
            pltpu.VMEM((MEM, 128), F32),
            pltpu.VMEM((MEM, 128), F32),
            pltpu.VMEM((rows, d), BF16),
            pltpu.VMEM((mem_rows, 2 * d), BF16),
            pltpu.VMEM((rows, d), BF16),
            pltpu.VMEM((d, d), BF16),
            pltpu.VMEM((d, 2 * d), BF16),
            pltpu.VMEM((d, d), BF16),
            pltpu.SemaphoreType.DMA((3,)),
            *scatter_scratch(4 + CROSS_WIDE, narrow, shard_rows, d),
        ],
        name="cross_back",
        compiler_params=pltpu.CompilerParams(collective_id=2, has_side_effects=True, vmem_limit_bytes=60 << 20),
        cost_estimate=cost(40 * rows * d * d, 100 << 20),
    )(
        bounds,
        logs,
        q,
        kv,
        mixed,
        grad,
        before,
        total,
        norms,
        mixed,
        b2,
        normed,
        memory,
        self_mixed,
        early,
        share.reshape(2, 2, 2, narrow, 4, shard_rows, d),
        share_views(wide_share, narrow, shard_rows),
    )


SELF_PLAN = (
    ((0, 0),),
    ((1, 0),),
    ((2, 0),),
    ((0, 1), (2, 1), (3, 0), (4, 0)),
    ((1, 1),),
    ((0, 2), (2, 2)),
    ((3, 1), (5, 0)),
    ((4, 1), (6, 0)),
    ((0, 3), (2, 3), (1, 2), (3, 2), (5, 1)),
    ((1, 3),),
    ((3, 3), (4, 2), (6, 1), (7, 0)),
    ((8, 0),),
    ((5, 2), (5, 3), (6, 2), (7, 1), (8, 1), (9, 0)),
    ((7, 2), (8, 2), (9, 1), (9, 2)),
    ((4, 3), (6, 3), (7, 3), (8, 3), (9, 3)),
)
SELF_REUSE = {9: 7, 10: 8, 11: 9}
SELF_WIDE = 4 - CROSS_WIDE
SELF_CHUNKS = SELF_WIDE + 5


def self_back_kernel(
    narrow,
    first_ref,
    log_ref,
    qkv_ref,
    mixed_ref,
    grad_ref,
    normed_ref,
    tokens_ref,
    total_ref,
    norms_ref,
    norm_two_ref,
    norm_three_ref,
    expand_low_ref,
    early_any,
    wide_any,
    shares_any,
    out_ref,
    norm_out_ref,
    expand_ref,
    cross_output_ref,
    cross_query_ref,
    cross_key_ref,
    cross_value_ref,
    self_output_ref,
    query_ref,
    key_ref,
    value_ref,
    dk_ref,
    dv_ref,
    dqkv,
    weight,
    weight_sem,
    stage,
    nval,
    nin,
    norm_send_sems,
    norm_recv_sems,
    *scratch,
):
    step = pl.program_id(0)
    d = normed_ref.shape[1]

    outs = (query_ref, key_ref, value_ref)

    def keep(i, value):
        i -= SELF_WIDE
        if i < 0:
            expand_ref[:, (i + 4) * d : (i + 5) * d] = value
        elif i == 0:
            cross_output_ref[...] = value
        elif i == 1:
            cross_query_ref[...] = value
        elif i == 4:
            self_output_ref[...] = value
        elif i > 4:
            for n in range(d // 128):
                pair, kind = divmod((i - 5) * d // 128 + n, 3)
                outs[kind][:, pair * 128 : (pair + 1) * 128] = value[:, n * 128 : (n + 1) * 128]
        else:
            for n in range(d // 256):
                at = (i - 2) * d // 2 + n * 128
                cross_key_ref[:, at : at + 128] = value[:, n * 256 : n * 256 + 128]
                cross_value_ref[:, at : at + 128] = value[:, n * 256 + 128 : n * 256 + 256]

    def piece(i):
        return lambda core: shares_any.at[i, :, :, core]

    def staged_piece(i):
        return lambda core: stage.at[i, :, :, core]

    pieces = [columns_of(wide_any, (CROSS_WIDE + i) * d, d) for i in range(SELF_WIDE)] + [piece(i) for i in range(5)]
    pieces += [staged_piece(i) for i in range(3)]
    carried = Carried(pieces, scratch, keep, narrow)
    load = pltpu.make_async_copy(early_any.at[:, pl.ds(0, 3 * d)], weight, weight_sem)

    @pl.when(step == 0)
    def _():
        carried.open()
        load.start()
        expand_ref[:, : CROSS_WIDE * d] = expand_low_ref[...]

    @pl.when(step < PAIRS)
    def _():
        base = step * 384

        def keep_dq(rows, value):
            dqkv[rows, pl.ds(pl.multiple_of(base, 128), 128)] = value

        attend_back(
            lambda rows: qkv_ref[rows, 0:128],
            qkv_ref[:, 128:256],
            qkv_ref[:, 256:384],
            grad_ref,
            mixed_ref,
            log_ref,
            functools.partial(self_visible, first_ref),
            self_extent,
            keep_dq,
            dk_ref,
            dv_ref,
        )
        dqkv[:, pl.ds(pl.multiple_of(base + 128, 128), 128)] = (dk_ref[...] * HEAD_DIM**-0.5).astype(BF16)
        dqkv[:, pl.ds(pl.multiple_of(base + 256, 128), 128)] = dv_ref[...].astype(BF16)

    rows = stage.shape[5]
    group = 2 * narrow * rows

    def multiply(m):
        for a in range(2):
            for b in range(2):
                at = (2 * a + b) * group
                product = tn(normed_ref[:, at : at + group], dqkv[:, m * d : (m + 1) * d])
                stage[m, a, b] = product.astype(BF16).reshape(2, narrow, rows, d)

    for m in range(3):
        pl.when(step == PAIRS + m)(functools.partial(multiply, m))

    @pl.when(step == PAIRS + 3)
    def _():
        load.wait()
        nval[0] = jnp.zeros_like(nval[0])
        nval[0, 2:4, :] = norm_two_ref[0:2, :]
        nval[0, 4:6, :] = norm_three_ref[0:2, :]

    @pl.when(step >= PAIRS + 3)
    def _():
        at = pl.ds(pl.multiple_of((step - PAIRS - 3) * TB, TB), TB)
        gradient = mm_t(dqkv[at, :], weight[...])
        unit, inverse = norm_parts(tokens_ref[...].astype(F32))
        total = total_ref[...] + norm_back(unit, inverse, norms_ref[0:1, :], gradient)
        out_ref[...] = total.astype(BF16)
        nval[0, 0:1, :] += jnp.sum(gradient * unit, axis=0, keepdims=True)
        nval[0, 1:2, :] += jnp.sum(gradient, axis=0, keepdims=True)

    w, z = carried.scatter.w, carried.scatter.z

    def norm_copy(stage_number, number, target):
        return pltpu.make_async_remote_copy(
            src_ref=nval.at[stage_number],
            dst_ref=nin.at[number],
            send_sem=norm_send_sems.at[number],
            recv_sem=norm_recv_sems.at[number],
            device_id=target,
            device_id_type=pl.DeviceIdType.MESH,
        )

    norm_copies = [[norm_copy(0, 0, (w ^ 1, z))], [norm_copy(1, 1, (w ^ 2, z))], [norm_copy(2, 2, (w ^ 4, z))]]
    norm_copies.append([norm_copy(3, 2 + mask, (w, z ^ mask)) for mask in range(1, narrow)])

    def norm_step(number):
        if number > 0:
            for copy in norm_copies[number - 1]:
                copy.wait_recv()
            value = nval[number - 1]
            if number < 4:
                nval[number] = value + nin[number - 1]
            else:
                for mask in range(1, narrow):
                    value = value + nin[2 + mask]
                norm_out_ref[...] = value
        if number < 4:
            for copy in norm_copies[number]:
                copy.start()

    last = len(SELF_PLAN) - 1
    for number, plan in enumerate(SELF_PLAN[:last]):
        pl.when(step == number)(functools.partial(carried.steps, plan))
        if number in SELF_REUSE:
            pl.when(step == number)(functools.partial(carried.reuse, SELF_REUSE[number]))

    @pl.when(step == last)
    def _():
        for number in range(5):
            norm_step(number)
            if number < len(SELF_PLAN[last]):
                carried.steps(SELF_PLAN[last][number : number + 1])
        carried.close()
        for copies in norm_copies:
            for copy in copies:
                copy.wait_send()


def self_back(first, logs, qkv, mixed, grad, normed, tokens, total, norms, norm_two, norm_three, expand_low, early, wide_share, shares, narrow):
    rows, d = mixed.shape
    shard_rows = d // (8 * narrow)

    def pair(s):
        return jnp.minimum(s, PAIRS - 1)

    def token(s):
        return jnp.maximum(s - PAIRS - 3, 0)

    anywhere = pl.BlockSpec(memory_space=pl.ANY)
    by_pair = pl.BlockSpec((SEQ, 128), lambda s: (0, pair(s)))
    by_token = pl.BlockSpec((TB, d), lambda s: (token(s), 0))
    return pl.pallas_call(
        functools.partial(self_back_kernel, narrow),
        grid=(PAIRS + 3 + rows // TB,),
        in_specs=[
            pl.BlockSpec((1, 1, SEQ), lambda s: (0, 0, 0)),
            pl.BlockSpec((1, 1, 8, SEQ), lambda s: (0, pair(s), 0, 0)),
            pl.BlockSpec((SEQ, 384), lambda s: (0, pair(s))),
            by_pair,
            by_pair,
            whole(rows, d),
            by_token,
            by_token,
            whole(8, d),
            whole(8, d),
            whole(8, d),
            whole(shard_rows, CROSS_WIDE * d),
            anywhere,
            anywhere,
            anywhere,
        ],
        out_specs=[
            by_token,
            whole(8, d),
            whole(shard_rows, 4 * d),
            *[whole(shard_rows, d)] * 8,
        ],
        out_shape=[
            shape(rows, d, BF16),
            shape(8, d, F32),
            shape(shard_rows, 4 * d, F32),
            *[shape(shard_rows, d, F32)] * 8,
        ],
        scratch_shapes=[
            pltpu.VMEM((SEQ, 128), F32),
            pltpu.VMEM((SEQ, 128), F32),
            pltpu.VMEM((rows, 3 * d), BF16),
            pltpu.VMEM((d, 3 * d), BF16),
            pltpu.SemaphoreType.DMA,
            pltpu.VMEM((3, 2, 2, 2, narrow, shard_rows, d), BF16),
            pltpu.VMEM((4, 8, d), F32),
            pltpu.VMEM((2 + narrow, 8, d), F32),
            pltpu.SemaphoreType.DMA((2 + narrow,)),
            pltpu.SemaphoreType.DMA((2 + narrow,)),
            *scatter_scratch(SELF_CHUNKS, narrow, shard_rows, d, 3),
        ],
        name="self_back",
        compiler_params=pltpu.CompilerParams(collective_id=3, has_side_effects=True, vmem_limit_bytes=60 << 20),
        cost_estimate=cost(40 * rows * d * d, 100 << 20),
    )(
        first,
        logs,
        qkv,
        mixed,
        grad,
        normed,
        tokens,
        total,
        norms,
        norm_two,
        norm_three,
        expand_low,
        early,
        share_views(wide_share, narrow, shard_rows),
        shares.reshape(5, 2, 2, 2, narrow, shard_rows, d),
    )


def on_device(
    mesh_axes,
    tokens,
    memory,
    cotangent,
    live_length,
    pair_starts,
    source_starts,
    group_bounds,
    group_counts,
    self_query,
    self_key,
    self_value,
    self_output,
    cross_query,
    cross_key,
    cross_value,
    cross_output,
    hidden_in,
    hidden_out,
    first_gain,
    first_shift,
    second_gain,
    second_shift,
    third_gain,
    third_shift,
):
    names = tuple(axis for axis, _ in mesh_axes)
    row_count = live_length.shape[0]
    shard_rows = self_query.shape[0]
    device_count = 1
    for _, size in mesh_axes:
        device_count *= size

    def staged(*partial):
        return StagedSum(partial, mesh_axes)

    digits = jnp.stack([live_length // 256, live_length % 256], axis=1).astype(BF16)
    digits = jnp.pad(digits, ((0, shard_rows - row_count), (0, 0)))
    norms = jnp.stack([first_gain, first_shift, second_gain, second_shift, third_gain, third_shift], axis=1)
    extra = jnp.pad(jnp.concatenate([norms, digits], axis=1), ((0, 0), (0, 120)))
    weights = (self_query, self_key, self_value, self_output, cross_query, cross_key, cross_value, cross_output)
    fast = mesh_axes[0][1] == 8 and row_count == 1 and shard_rows % 32 == 0
    if fast:
        (
            early,
            later,
            late,
            normed_one,
            qkv,
            self_mixed,
            self_logs,
            norms,
            first,
            bounds,
            after_self,
            normed_two,
            cross_q,
            cross_kv,
            cross_mixed,
            cross_logs,
        ) = front(
            live_length,
            pair_starts,
            source_starts,
            weights,
            hidden_in,
            hidden_out,
            extra,
            tokens,
            memory,
            mesh_axes[1][1],
        )
        late = [late.reshape(device_count, -1, WIDTH)]
    else:
        shard = [by_pairs(self_query, self_key, self_value), extra, self_output, cross_query]
        shard += [by_pairs(cross_key, cross_value), cross_output]
        early = lax.all_gather(jnp.concatenate(shard, axis=1), names, axis=0, tiled=True)
        late = [lax.all_gather(part, names, axis=0, tiled=True) for part in (hidden_in, hidden_out)]
        early, later = early[:, : 3 * WIDTH + 128], early[:, 3 * WIDTH + 128 :]
        norms = early[:, 3 * WIDTH : 3 * WIDTH + 8].astype(F32).T
        first, bounds = row_bounds(pair_starts, source_starts, live_length)
        normed_one, qkv = project(tokens, norms, early)
        self_mixed, self_logs = self_forward(first, qkv, row_count)
        after_self, normed_two, cross_q, cross_kv = middle(self_mixed, tokens, memory, norms, later)
        cross_mixed, cross_logs = cross_forward(bounds, cross_q, cross_kv, row_count)

    device = lax.axis_index(names)
    layer_output, normed_three, activated, hidden_grad, branch_three, cross_total, branch_two, mixed_grad, norm_three = feed(
        live_length, group_bounds, group_counts, cross_mixed, after_self, cotangent, norms, later, late, mesh_axes
    )

    reduce_share, expand_share = outer_sum(activated, branch_three), outer_sum(normed_three, hidden_grad)
    if fast:
        narrow = mesh_axes[1][1]
        self_total, mixed_grad, memory_grad, norm_two, shares, reduce_shard, expand_low = cross_back(
            bounds,
            cross_logs,
            cross_q,
            cross_kv,
            cross_mixed,
            mixed_grad,
            after_self,
            cross_total,
            norms,
            branch_two,
            normed_two,
            memory,
            self_mixed,
            later,
            reduce_share,
            expand_share,
            narrow,
        )
        (
            tokens_grad,
            norm_grads,
            expand_shard,
            cross_output_shard,
            cross_query_shard,
            cross_key_shard,
            cross_value_shard,
            output_shard,
            query_shard,
            key_shard,
            value_shard,
        ) = self_back(
            first,
            self_logs,
            qkv,
            self_mixed,
            mixed_grad,
            normed_one,
            tokens,
            self_total,
            norms,
            norm_two,
            norm_three,
            expand_low,
            early,
            expand_share,
            shares,
            narrow,
        )
    else:
        reduce_sum, expand_sum = staged(reduce_share), staged(expand_share)
        cq_grad, ckv_grad = cross_backward(bounds, cross_logs, cross_q, cross_kv, cross_mixed, mixed_grad, row_count)
        cq_grad, ckv_grad = fence((cq_grad, ckv_grad), reduce_sum, expand_sum)
        cross_shares = [outer_sum(cross_mixed, branch_two), outer_sum(normed_two, cq_grad)]
        cross_shares += [outer_sum(memory, part) for part in (ckv_grad[:, :WIDTH], ckv_grad[:, WIDTH:])]
        cross_sum = staged(*cross_shares)
        self_total, branch_one, mixed_grad, memory_grad, norm_two = cross_close(
            cq_grad, ckv_grad, after_self, cross_total, norms, later
        )
        mixed_grad = fence(mixed_grad, reduce_sum, expand_sum, cross_sum)
        qkv_grad = self_backward(first, self_logs, qkv, self_mixed, mixed_grad, row_count)
        qkv_grad = fence(qkv_grad, reduce_sum, expand_sum, cross_sum)
        last_sum = staged(
            outer_sum(self_mixed, branch_one),
            *[outer_sum(normed_one, qkv_grad[:, n * WIDTH : (n + 1) * WIDTH]) for n in range(3)],
        )
        tokens_grad, norm_one = self_close(qkv_grad, tokens, self_total, norms, early)
        norm_grads = sum_everywhere(jnp.concatenate([norm_one[:2], norm_two[:2], norm_three[:2]]), mesh_axes)
        output_shard, *qkv_shards = last_sum.result().reshape(4, shard_rows, WIDTH)
        query_shard, key_shard, value_shard = from_pairs(jnp.concatenate(qkv_shards, axis=1), 3)
        reduce_shard = reduce_sum.result()
        expand_shard = expand_sum.result()
        cross_output_shard, cross_query_shard, *cross_shards = cross_sum.result().reshape(4, shard_rows, WIDTH)
        cross_key_shard, cross_value_shard = from_pairs(jnp.concatenate(cross_shards, axis=1), 2)

    norm_shards = lax.dynamic_slice_in_dim(norm_grads, device * shard_rows, shard_rows, axis=1)
    return (
        layer_output,
        tokens_grad,
        memory_grad,
        query_shard,
        key_shard,
        value_shard,
        output_shard,
        cross_query_shard,
        cross_key_shard,
        cross_value_shard,
        cross_output_shard,
        expand_shard,
        reduce_shard,
        *[norm_shards[n] for n in range(6)],
    )


def solution(mesh):
    names = ("wide", "narrow")
    mesh_axes = tuple((axis, mesh.shape[axis]) for axis in names)
    split, vector = P(names, None), P(names)
    return jax.shard_map(
        functools.partial(on_device, mesh_axes),
        mesh=mesh,
        in_specs=(split,) * 3 + (vector,) + (split,) * 2 + (P(), P()) + (split,) * 10 + (vector,) * 6,
        out_specs=(split,) * 13 + (vector,) * 6,
        check_vma=False,
    )
```

```python
import functools
import jax
import jax.numpy as jnp
from jax import lax
from jax.experimental import pallas as pl
from jax.experimental.pallas import tpu as pltpu
from jax.sharding import PartitionSpec as P

SEQ = 1024
MEM = 512
HEADS = 16
HEAD_DIM = 64
WIDTH = HEADS * HEAD_DIM
EPSILON = 1e-05
BQ = 256
LOG2E = 1.4426950408889634
SCALE2 = HEAD_DIM**-0.5 * LOG2E
FILLER = -1e30
F32, BF16 = jnp.float32, jnp.bfloat16


def mm(a, b):
    return jnp.dot(a, b, preferred_element_type=F32)


def mm_t(a, b):
    return lax.dot_general(a, b, (((1,), (1,)), ((), ())), preferred_element_type=F32)


def halves(x):
    low = lax.broadcasted_iota(jnp.int32, x.shape, 1) < HEAD_DIM
    zero = jnp.zeros_like(x)
    return (jnp.where(low, x, zero), jnp.where(low, zero, x))


def in_turn(tasks, front, back, ahead):
    waiting = []
    for task in tasks:
        waiting.append((task, front(*task)))
        if len(waiting) > ahead:
            task, held = waiting.pop(0)
            back(*task, *held)
    for task, held in waiting:
        back(*task, *held)


BLOCKS = [slice(i * BQ, (i + 1) * BQ) for i in range(SEQ // BQ)]
TASKS = [(i, h) for i in range(SEQ // BQ) for h in range(2)]


def self_extent(i):
    return (i + 1) * BQ


def cross_extent(i):
    return MEM


def self_visible(first_ref, i):
    shape = (self_extent(i), BQ)
    key = lax.broadcasted_iota(jnp.int32, shape, 0)
    return (key >= first_ref[0, :, BLOCKS[i]]) & (key <= lax.broadcasted_iota(jnp.int32, shape, 1) + i * BQ)


def cross_visible(bounds_ref, i):
    key = lax.broadcasted_iota(jnp.int32, (MEM, BQ), 0)
    return (key >= bounds_ref[0, 0:1, BLOCKS[i]]) & (key < bounds_ref[0, 1:2, BLOCKS[i]])


def attend(q_of, k, v, visible, extent, keep_out, keep_log):
    k_parts, v_t = halves(k), v.T
    outs = {}

    def front(i, h):
        s = jnp.where(visible(i), mm_t(k_parts[h][: extent(i)], q_of(BLOCKS[i])) * SCALE2, FILLER)
        return s, jnp.max(s, axis=0, keepdims=True)

    def back(i, h, s, peak):
        p = jnp.exp2(s - peak)
        total = jnp.sum(p, axis=0, keepdims=True)
        keep_log(h, BLOCKS[i], peak + jnp.log2(total))
        outs[h] = mm(v_t[h * 64 : (h + 1) * 64, : extent(i)], p.astype(BF16)) * (1.0 / total)
        if h == 1:
            keep_out(BLOCKS[i], jnp.concatenate([outs[0], outs[1]], axis=0).T.astype(BF16))

    in_turn(TASKS, front, back, 3)


def attend_back(q_of, k, v, g_ref, out_ref, log_ref, visible, extent, keep_dq, dk_ref, dv_ref):
    k_parts, k_t, v_parts = halves(k), k.T, halves(v)
    deltas, dq = {}, {}
    dk_ref[...] = jnp.zeros_like(dk_ref)
    dv_ref[...] = jnp.zeros_like(dv_ref)

    def front(i, h):
        q, g = q_of(BLOCKS[i]), g_ref[BLOCKS[i], :]
        if h == 0:
            prod = (g.astype(F32) * out_ref[BLOCKS[i], :].astype(F32)).T
            deltas[i] = [jnp.sum(prod[n * 64 : (n + 1) * 64], axis=0, keepdims=True) for n in range(2)]
        s = jnp.where(visible(i), mm_t(k_parts[h][: extent(i)], q) * SCALE2, FILLER)
        p = jnp.exp2(s - log_ref[0, 0, h : h + 1, BLOCKS[i]])
        dp = mm_t(v_parts[h][: extent(i)], g)
        return p.astype(BF16), (p * (dp - deltas[i][h])).astype(BF16)

    def back(i, h, p, ds):
        n = extent(i)
        dv_ref[:n, :] += mm(p, halves(g_ref[BLOCKS[i], :])[h])
        dk_ref[:n, :] += mm(ds, halves(q_of(BLOCKS[i]))[h])
        dq[h] = mm(k_t[h * 64 : (h + 1) * 64, :n], ds)
        if h == 1:
            keep_dq(BLOCKS[i], (jnp.concatenate([dq[0], dq[1]], axis=0) * HEAD_DIM**-0.5).T.astype(BF16))

    in_turn(TASKS, front, back, 2)


def keepers(out_ref, log_ref):
    def keep_out(rows, value):
        out_ref[rows, :] = value

    def keep_log(h, rows, value):
        log_ref[0, 0, h : h + 1, rows] = value

    return keep_out, keep_log


def self_forward_kernel(first_ref, qkv_ref, out_ref, log_ref):
    attend(
        lambda rows: qkv_ref[rows, 0:128],
        qkv_ref[:, 128:256],
        qkv_ref[:, 256:384],
        functools.partial(self_visible, first_ref),
        self_extent,
        *keepers(out_ref, log_ref),
    )


def cross_forward_kernel(bounds_ref, q_ref, kv_ref, out_ref, log_ref):
    attend(
        lambda rows: q_ref[rows, :],
        kv_ref[:, 0:128],
        kv_ref[:, 128:256],
        functools.partial(cross_visible, bounds_ref),
        cross_extent,
        *keepers(out_ref, log_ref),
    )


PAIRS = HEADS // 2
LOG_SPEC = pl.BlockSpec((1, 1, 8, SEQ), lambda r, p: (r, p, 0, 0))
ROW_SPEC = pl.BlockSpec((SEQ, 128), lambda r, p: (r, p))
QKV_SPEC = pl.BlockSpec((SEQ, 384), lambda r, p: (r, p))
KV_SPEC = pl.BlockSpec((MEM, 256), lambda r, p: (r, p))
FIRST_SPEC = pl.BlockSpec((1, 1, SEQ), lambda r, p: (r, 0, 0))
BOUNDS_SPEC = pl.BlockSpec((1, 8, SEQ), lambda r, p: (r, 0, 0))


def attention_call(kernel, name, in_specs, args, row_count):
    return pl.pallas_call(
        kernel,
        grid=(row_count, PAIRS),
        in_specs=in_specs,
        out_specs=[ROW_SPEC, LOG_SPEC],
        out_shape=[
            jax.ShapeDtypeStruct((row_count * SEQ, WIDTH), BF16),
            jax.ShapeDtypeStruct((row_count, PAIRS, 8, SEQ), F32),
        ],
        name=name,
        compiler_params=pltpu.CompilerParams(vmem_limit_bytes=40 << 20),
        cost_estimate=pl.CostEstimate(flops=20 << 30, bytes_accessed=row_count * (8 << 20), transcendentals=8 << 20),
    )(*args)


def self_forward(first, qkv, row_count):
    return attention_call(self_forward_kernel, "self_forward", [FIRST_SPEC, QKV_SPEC], (first, qkv), row_count)


def cross_forward(bounds, q, kv, row_count):
    return attention_call(
        cross_forward_kernel, "cross_forward", [BOUNDS_SPEC, ROW_SPEC, KV_SPEC], (bounds, q, kv), row_count
    )


def self_backward_kernel(first_ref, log_ref, qkv_ref, out_ref, grad_ref, dqkv_ref, dk_ref, dv_ref):
    def keep_dq(rows, value):
        dqkv_ref[rows, 0:128] = value

    attend_back(
        lambda rows: qkv_ref[rows, 0:128],
        qkv_ref[:, 128:256],
        qkv_ref[:, 256:384],
        grad_ref,
        out_ref,
        log_ref,
        functools.partial(self_visible, first_ref),
        self_extent,
        keep_dq,
        dk_ref,
        dv_ref,
    )
    dqkv_ref[:, 128:256] = (dk_ref[...] * HEAD_DIM**-0.5).astype(BF16)
    dqkv_ref[:, 256:384] = dv_ref[...].astype(BF16)


def self_backward(first, logs, qkv, out, grad, row_count):
    return pl.pallas_call(
        self_backward_kernel,
        grid=(row_count, PAIRS),
        in_specs=[FIRST_SPEC, LOG_SPEC, QKV_SPEC, ROW_SPEC, ROW_SPEC],
        out_specs=QKV_SPEC,
        scratch_shapes=[pltpu.VMEM((SEQ, 128), F32), pltpu.VMEM((SEQ, 128), F32)],
        out_shape=jax.ShapeDtypeStruct((row_count * SEQ, 3 * WIDTH), BF16),
        name="self_backward",
        compiler_params=pltpu.CompilerParams(vmem_limit_bytes=40 << 20),
        cost_estimate=pl.CostEstimate(flops=40 << 30, bytes_accessed=row_count * (16 << 20), transcendentals=8 << 20),
    )(first, logs, qkv, out, grad)


def cross_backward_pair(bounds_ref, log_ref, q_ref, kv_ref, out_ref, grad_ref, keep_dq, dkv_ref, dk_ref, dv_ref):
    attend_back(
        lambda rows: q_ref[rows, :],
        kv_ref[:, 0:128],
        kv_ref[:, 128:256],
        grad_ref,
        out_ref,
        log_ref,
        functools.partial(cross_visible, bounds_ref),
        cross_extent,
        keep_dq,
        dk_ref,
        dv_ref,
    )


def cross_backward_kernel(bounds_ref, log_ref, q_ref, kv_ref, out_ref, grad_ref, dq_ref, dkv_ref, dk_ref, dv_ref):
    def keep_dq(rows, value):
        dq_ref[rows, :] = value

    cross_backward_pair(bounds_ref, log_ref, q_ref, kv_ref, out_ref, grad_ref, keep_dq, dkv_ref, dk_ref, dv_ref)
    dkv_ref[:, 0:128] = (dk_ref[...] * HEAD_DIM**-0.5).astype(BF16)
    dkv_ref[:, 128:256] = dv_ref[...].astype(BF16)


def cross_backward(bounds, logs, q, kv, out, grad, row_count):
    return pl.pallas_call(
        cross_backward_kernel,
        grid=(row_count, PAIRS),
        in_specs=[BOUNDS_SPEC, LOG_SPEC, ROW_SPEC, KV_SPEC, ROW_SPEC, ROW_SPEC],
        out_specs=[ROW_SPEC, KV_SPEC],
        scratch_shapes=[pltpu.VMEM((MEM, 128), F32), pltpu.VMEM((MEM, 128), F32)],
        out_shape=[
            jax.ShapeDtypeStruct((row_count * SEQ, WIDTH), BF16),
            jax.ShapeDtypeStruct((row_count * MEM, 2 * WIDTH), BF16),
        ],
        name="cross_backward",
        compiler_params=pltpu.CompilerParams(vmem_limit_bytes=40 << 20),
        cost_estimate=pl.CostEstimate(flops=40 << 30, bytes_accessed=row_count * (12 << 20), transcendentals=8 << 20),
    )(bounds, logs, q, kv, out, grad)


def row_bounds(pair_starts, source_starts, live_length):
    places = jnp.arange(SEQ, dtype=jnp.int32)
    counted = jnp.sum((pair_starts[:, :, None] <= places).astype(jnp.int32), axis=1)
    live = places < live_length[:, None]
    begun = jnp.max(jnp.where(pair_starts[:, :, None] <= places, pair_starts[:, :, None], 0), axis=1)
    first = jnp.where(live, begun, live_length[:, None])
    nseg = pair_starts.shape[1]
    pick = jnp.arange(nseg)[None, :, None] == (counted - 1)[:, None, :]
    ends = jnp.concatenate([source_starts[:, 1:], jnp.full_like(source_starts[:, :1], MEM)], axis=1)
    start = jnp.sum(jnp.where(pick, source_starts[:, :, None], 0), axis=1)
    end = jnp.sum(jnp.where(pick, ends[:, :, None], 0), axis=1)
    start = jnp.where(live, start, 0)
    end = jnp.where(live, end, MEM)
    bounds = jnp.pad(jnp.stack([start, end], axis=1), ((0, 0), (0, 6), (0, 0)))
    return first[:, None, :], bounds


TB = 256


def norm_parts(values):
    center = values - jnp.mean(values, axis=-1, keepdims=True)
    inverse = lax.rsqrt(jnp.mean(center * center, axis=-1, keepdims=True) + EPSILON)
    return center * inverse, inverse


def norm_back(unit, inverse, gain, gradient):
    scaled = gradient * gain
    return inverse * (
        scaled
        - jnp.mean(scaled, axis=-1, keepdims=True)
        - unit * jnp.mean(scaled * unit, axis=-1, keepdims=True)
    )


def add_norm_grads(ref, unit, gradient):
    @pl.when(pl.program_id(0) == 0)
    def _():
        ref[...] = jnp.zeros_like(ref)

    ref[0:1, :] += jnp.sum(gradient * unit, axis=0, keepdims=True)
    ref[1:2, :] += jnp.sum(gradient, axis=0, keepdims=True)


def tile(rows, columns, at=0):
    return pl.BlockSpec((rows, columns), lambda b: (b, at))


def whole(rows, columns, at=0):
    return pl.BlockSpec((rows, columns), lambda b: (0, at), pipeline_mode=pl.Buffered(1))


def shape(rows, columns, dtype):
    return jax.ShapeDtypeStruct((rows, columns), dtype)


def params(mib):
    return pltpu.CompilerParams(vmem_limit_bytes=mib << 20)


def cost(flops, moved):
    return pl.CostEstimate(flops=int(flops), bytes_accessed=int(moved), transcendentals=0)


def project_kernel(tokens_ref, norms_ref, weight_ref, normed_ref, out_ref):
    unit, _ = norm_parts(tokens_ref[...].astype(F32))
    normed = (unit * norms_ref[0:1, :] + norms_ref[1:2, :]).astype(BF16)
    normed_ref[...] = normed
    for part in range(3):
        at = slice(part * 1024, (part + 1) * 1024)
        out_ref[:, at] = mm(normed, weight_ref[:, at]).astype(BF16)


def project(tokens, norms, early):
    rows, d = tokens.shape
    return pl.pallas_call(
        project_kernel,
        grid=(rows // TB,),
        in_specs=[tile(TB, d), whole(8, d), whole(d, 3 * d)],
        out_specs=[tile(TB, d), tile(TB, 3 * d)],
        out_shape=[shape(rows, d, BF16), shape(rows, 3 * d, BF16)],
        name="project",
        compiler_params=params(40),
        cost_estimate=cost(6 * rows * d * d, 16 << 20),
    )(tokens, norms, early)


def middle_kernel(
    mixed_ref, tokens_ref, memory_ref, norms_ref, wo_ref, wq_ref, wkv_ref, after_ref, normed_ref, q_ref, kv_ref
):
    after = tokens_ref[...].astype(F32) + mm(mixed_ref[...], wo_ref[...])
    after_ref[...] = after
    kv_ref[...] = mm(memory_ref[...], wkv_ref[...]).astype(BF16)
    unit, _ = norm_parts(after)
    normed = (unit * norms_ref[2:3, :] + norms_ref[3:4, :]).astype(BF16)
    normed_ref[...] = normed
    q_ref[...] = mm(normed, wq_ref[...]).astype(BF16)


def middle(mixed, tokens, memory, norms, early):
    rows, d = tokens.shape
    mem_rows = memory.shape[0]
    steps = rows // TB
    mb = mem_rows // steps
    return pl.pallas_call(
        middle_kernel,
        grid=(steps,),
        in_specs=[
            tile(TB, d),
            tile(TB, d),
            tile(mb, d),
            whole(8, d),
            whole(d, d, OUT_SELF),
            whole(d, d, QUERY_CROSS),
            whole(d, 2 * d, KV_CROSS),
        ],
        out_specs=[tile(TB, d), tile(TB, d), tile(TB, d), tile(mb, 2 * d)],
        out_shape=[shape(rows, d, F32), shape(rows, d, BF16), shape(rows, d, BF16), shape(mem_rows, 2 * d, BF16)],
        name="middle",
        compiler_params=params(40),
        cost_estimate=cost(6 * rows * d * d, 20 << 20),
    )(mixed, tokens, memory, norms, early, early, early)


GELU_A = 0.7978845608028654
GELU_B = 0.044715


def hidden_parts(win_ref, wout_ref, part, d):
    if len(win_ref.shape) == 2:
        at = slice(part * d, (part + 1) * d)
        return win_ref[:, at], wout_ref[at, :]
    devices, quad, _ = win_ref.shape
    rows, share = quad // 4, devices // 4
    win = win_ref[:, part * rows : (part + 1) * rows, :].reshape(d, d)
    return win, wout_ref[part * share : (part + 1) * share].reshape(d, d)


def feed_kernel(
    narrow,
    token_all,
    live_ref,
    group_bounds_ref,
    group_counts_ref,
    mixed_ref,
    before_ref,
    cot_ref,
    norms_ref,
    wo_ref,
    win_ref,
    wout_ref,
    out_ref,
    normed_ref,
    act_ref,
    hid_ref,
    b3_ref,
    total_ref,
    b2_ref,
    grad_ref,
    ngrad_ref,
    *scratch,
):
    block = pl.program_id(0)
    loads = []
    if scratch:
        late_any = win_ref
        win_ref, wout_ref, sems = scratch
        devices, quad, _ = win_ref.shape
        rows, share = quad // 4, devices // 4
        for n in range(4):
            lane, holders = pl.ds(n * rows, rows), pl.ds(n * share, share)
            loads.append(
                (
                    pltpu.make_async_copy(late_any.at[:, lane], win_ref.at[:, lane], sems.at[2 * n]),
                    pltpu.make_async_copy(
                        late_any.at[holders, pl.ds(quad, quad)], wout_ref.at[holders], sems.at[2 * n + 1]
                    ),
                )
            )

        @pl.when(block == 0)
        def _():
            for pair in loads:
                for load in pair:
                    load.start()

    per_row = SEQ // TB
    row = block // per_row
    places = lax.broadcasted_iota(jnp.int32, (TB, 1), 0) + (block % per_row) * TB
    live = (places < live_ref[row]).astype(F32)
    device = lax.axis_index("wide") * narrow + lax.axis_index("narrow")
    pair_tokens = jnp.int32(0)
    for g in range(group_counts_ref.shape[0]):
        member = (group_bounds_ref[g] <= device) & (device < group_bounds_ref[g + 1])
        pair_tokens += jnp.where(member, group_counts_ref[g], 0)
    live_total = jnp.sum(norms_ref[6:7, :], keepdims=True) * 256.0 + jnp.sum(norms_ref[7:8, :], keepdims=True)
    out_grad = cot_ref[...].astype(F32) * live * (pair_tokens.astype(F32) * (token_all / 1000.0) / live_total)
    branch = out_grad.astype(BF16)
    b3_ref[...] = branch
    after = before_ref[...] + mm(mixed_ref[...], wo_ref[...])
    unit, inverse = norm_parts(after)
    normed = (unit * norms_ref[4:5, :] + norms_ref[5:6, :]).astype(BF16)
    normed_ref[...] = normed
    d = normed.shape[1]
    result, back = after, None
    for part in range(act_ref.shape[1] // d):
        at = slice(part * d, (part + 1) * d)
        for load in loads[part] if loads else ():
            pl.when(block == 0)(load.wait)
        win, wout = hidden_parts(win_ref, wout_ref, part, d)
        x = mm(normed, win)
        square = x * x
        t = jnp.tanh(GELU_A * x * (1.0 + GELU_B * square))
        half = 0.5 * (1.0 + t)
        act = (x * half).astype(BF16)
        slope = half + (0.5 * GELU_A) * x * (1.0 - t * t) * (1.0 + (3.0 * GELU_B) * square)
        act_ref[:, at] = act
        hid = (mm_t(branch, wout) * slope).astype(BF16)
        hid_ref[:, at] = hid
        result = result + mm(act, wout)
        term = mm_t(hid, win)
        back = term if back is None else back + term
    out_ref[...] = result.astype(BF16)
    total = out_grad + norm_back(unit, inverse, norms_ref[4:5, :], back)
    total_ref[...] = total
    b2 = total.astype(BF16)
    b2_ref[...] = b2
    grad_ref[...] = mm_t(b2, wo_ref[...]).astype(BF16)
    add_norm_grads(ngrad_ref, unit, back)


def feed(live_length, group_bounds, group_counts, mixed, before, cotangent, norms, early, late, mesh_axes):
    rows, d = cotangent.shape
    (_, wide), (_, narrow) = mesh_axes
    ff = 4 * d
    if len(late) == 1:
        devices, block, _ = late[0].shape
        late = late * 2
        late_specs = [pl.BlockSpec(memory_space=pl.ANY)] * 2
        scratch = [pltpu.VMEM((devices, block // 2, d), BF16)] * 2 + [pltpu.SemaphoreType.DMA((8,))]
    else:
        late_specs, scratch = [whole(d, ff), whole(ff, d)], []
    smem = pl.BlockSpec(memory_space=pltpu.SMEM)
    return pl.pallas_call(
        functools.partial(feed_kernel, narrow, rows * wide * narrow),
        grid=(rows // TB,),
        in_specs=[
            smem,
            smem,
            smem,
            tile(TB, d),
            tile(TB, d),
            tile(TB, d),
            whole(8, d),
            whole(d, d, OUT_CROSS),
            *late_specs,
        ],
        out_specs=[
            tile(TB, d),
            tile(TB, d),
            tile(TB, ff),
            tile(TB, ff),
            tile(TB, d),
            tile(TB, d),
            tile(TB, d),
            tile(TB, d),
            whole(8, d),
        ],
        out_shape=[
            shape(rows, d, BF16),
            shape(rows, d, BF16),
            shape(rows, ff, BF16),
            shape(rows, ff, BF16),
            shape(rows, d, BF16),
            shape(rows, d, F32),
            shape(rows, d, BF16),
            shape(rows, d, BF16),
            shape(8, d, F32),
        ],
        scratch_shapes=scratch,
        name="feed",
        compiler_params=params(58),
        cost_estimate=cost(38 * rows * d * d, 50 << 20),
    )(live_length, group_bounds, group_counts, mixed, before, cotangent, norms, early, *late)


def cross_close_kernel(
    dq_ref, dkv_ref, before_ref, total_ref, norms_ref, wq_ref, wkv_ref, wo_ref, out_ref, b1_ref, grad_ref, mem_ref, ngrad_ref
):
    gradient = mm_t(dq_ref[...], wq_ref[...])
    mem_ref[...] = mm_t(dkv_ref[...], wkv_ref[...]).astype(BF16)
    unit, inverse = norm_parts(before_ref[...])
    total = total_ref[...] + norm_back(unit, inverse, norms_ref[2:3, :], gradient)
    out_ref[...] = total
    b1 = total.astype(BF16)
    b1_ref[...] = b1
    grad_ref[...] = mm_t(b1, wo_ref[...]).astype(BF16)
    add_norm_grads(ngrad_ref, unit, gradient)


def cross_close(dq, dkv, before, total, norms, early):
    rows, d = dq.shape
    mem_rows = dkv.shape[0]
    steps = rows // TB
    mb = mem_rows // steps
    return pl.pallas_call(
        cross_close_kernel,
        grid=(steps,),
        in_specs=[
            tile(TB, d),
            tile(mb, 2 * d),
            tile(TB, d),
            tile(TB, d),
            whole(8, d),
            whole(d, d, QUERY_CROSS),
            whole(d, 2 * d, KV_CROSS),
            whole(d, d, OUT_SELF),
        ],
        out_specs=[tile(TB, d), tile(TB, d), tile(TB, d), tile(mb, d), whole(8, d)],
        out_shape=[
            shape(rows, d, F32),
            shape(rows, d, BF16),
            shape(rows, d, BF16),
            shape(mem_rows, d, BF16),
            shape(8, d, F32),
        ],
        name="cross_close",
        compiler_params=params(40),
        cost_estimate=cost(6 * rows * d * d, 24 << 20),
    )(dq, dkv, before, total, norms, early, early, early)


def self_close_kernel(dqkv_ref, before_ref, total_ref, norms_ref, w_ref, out_ref, ngrad_ref):
    gradient = mm_t(dqkv_ref[...], w_ref[...])
    unit, inverse = norm_parts(before_ref[...].astype(F32))
    total = total_ref[...] + norm_back(unit, inverse, norms_ref[0:1, :], gradient)
    out_ref[...] = total.astype(BF16)
    add_norm_grads(ngrad_ref, unit, gradient)


def self_close(dqkv, before, total, norms, early):
    rows, d = total.shape
    return pl.pallas_call(
        self_close_kernel,
        grid=(rows // TB,),
        in_specs=[tile(TB, 3 * d), tile(TB, d), tile(TB, d), whole(8, d), whole(d, 3 * d)],
        out_specs=[tile(TB, d), whole(8, d)],
        out_shape=[shape(rows, d, BF16), shape(8, d, F32)],
        name="self_close",
        compiler_params=params(40),
        cost_estimate=cost(6 * rows * d * d, 20 << 20),
    )(dqkv, before, total, norms, early)


OUT_SELF, QUERY_CROSS, KV_CROSS, OUT_CROSS = 0, 1, 1, 4


def greet_all(narrow):
    w, z = lax.axis_index("wide"), lax.axis_index("narrow")
    barrier = pltpu.get_barrier_semaphore()
    others = [(w ^ 1, z), (w ^ 2, z), (w ^ 4, z)] + [(w, z ^ mask) for mask in range(1, narrow)]
    for other in others:
        pl.semaphore_signal(barrier, inc=1, device_id=other, device_id_type=pl.DeviceIdType.MESH)
    pl.semaphore_wait(barrier, len(others))


class Gather:
    def __init__(self, shard_ref, out_ref, send_sems, recv_sems, narrow):
        self.shard_ref, self.out_ref = shard_ref, out_ref
        self.send_sems, self.recv_sems = send_sems, recv_sems
        self.narrow = narrow
        self.rows = shard_ref.shape[0]
        self.half = self.rows // 2
        self.w, self.z = w, z = lax.axis_index("wide"), lax.axis_index("narrow")
        self.core, self.x, self.y, self.xy = w ^ 1, w ^ 2, w ^ 4, w ^ 6
        self.above, self.below = (w, z + 1), (w, z - 1)
        self.at_core, self.at_x, self.at_y = (self.core, z), (self.x, z), (self.y, z)
        self.up, self.down, self.to_x, self.to_y, self.on_y, self.on_x, self.to_core = [k * narrow for k in range(7)]

    def move(self, holder, s, number, target, first=0, count=None, own=False):
        count = self.rows if count is None else count
        at = pl.multiple_of((holder * self.narrow + s) * self.rows + first, self.half)
        place = self.out_ref.at[pl.ds(at, count)]
        return pltpu.make_async_remote_copy(
            src_ref=self.shard_ref.at[pl.ds(first, count)] if own else place,
            dst_ref=place,
            send_sem=self.send_sems.at[number],
            recv_sem=self.recv_sems.at[number],
            device_id=target,
            device_id_type=pl.DeviceIdType.MESH,
        )

    def own_place(self):
        return self.out_ref.at[pl.ds(pl.multiple_of((self.w * self.narrow + self.z) * self.rows, self.rows), self.rows)]

    def spread(self, s, own=False):
        self.move(self.w, s, self.to_x + s, self.at_x, own=own).start()
        self.move(self.w, s, self.to_y + s, self.at_y, own=own).start()
        self.move(self.w, s, self.to_core + s, self.at_core, own=own).start()

    def relay(self, s):
        half = self.half
        self.move(self.x, s, self.to_x + s, self.at_x).wait_recv()
        self.move(self.x, s, self.on_y + s, self.at_y, 0, half).start()
        self.move(self.x, s, self.to_core + self.narrow + s, self.at_core).start()
        self.move(self.y, s, self.to_y + s, self.at_y).wait_recv()
        self.move(self.y, s, self.on_x + s, self.at_x, half, half).start()
        self.move(self.y, s, self.to_core + 2 * self.narrow + s, self.at_core).start()

    def corner(self, s):
        self.move(self.xy, s, self.on_y + s, self.at_y, 0, self.half).wait_recv()
        self.move(self.xy, s, self.on_x + s, self.at_x, self.half, self.half).wait_recv()
        self.move(self.xy, s, self.to_core + 3 * self.narrow + s, self.at_core).start()

    def at_distance(self, r, action):
        if r == 0:
            action(self.z)
        else:
            pl.when(self.z - r >= 0)(lambda: action(self.z - r))
            pl.when(self.z + r < self.narrow)(lambda: action(self.z + r))

    def begin_line(self):
        z = self.z
        pl.when(z < self.narrow - 1)(lambda: self.move(self.w, z, self.up + z, self.above, own=True).start())
        pl.when(z > 0)(lambda: self.move(self.w, z, self.down + z, self.below, own=True).start())

    def begin_spread(self):
        self.spread(self.z, own=True)

    def round(self, r):
        z = self.z

        def from_below():
            s = z - r
            self.move(self.w, s, self.up + s, self.above).wait_recv()
            pl.when(z < self.narrow - 1)(lambda: self.move(self.w, s, self.up + s, self.above).start())
            self.spread(s)

        def from_above():
            s = z + r
            self.move(self.w, s, self.down + s, self.below).wait_recv()
            pl.when(z > 0)(lambda: self.move(self.w, s, self.down + s, self.below).start())
            self.spread(s)

        if r < self.narrow:
            pl.when(z - r >= 0)(from_below)
            pl.when(z + r < self.narrow)(from_above)
        self.at_distance(r - 1, self.relay)

    def corners(self):
        for r in range(self.narrow):
            self.at_distance(r, self.corner)

    def arrive(self):
        for s in range(self.narrow):
            for k, holder in enumerate((self.w, self.x, self.y, self.xy)):
                self.move(holder ^ 1, s, self.to_core + k * self.narrow + s, self.at_core).wait_recv()

    def close(self):
        z, half = self.z, self.half
        for s in range(self.narrow):
            up, down = self.move(self.w, s, self.up + s, self.above), self.move(self.w, s, self.down + s, self.below)
            pl.when((s <= z) & (z < self.narrow - 1))(up.wait_send)
            pl.when((s >= z) & (z > 0))(down.wait_send)
            self.move(self.w, s, self.to_x + s, self.at_x).wait_send()
            self.move(self.w, s, self.to_y + s, self.at_y).wait_send()
            self.move(self.x, s, self.on_y + s, self.at_y, 0, half).wait_send()
            self.move(self.y, s, self.on_x + s, self.at_x, half, half).wait_send()
            for k, holder in enumerate((self.w, self.x, self.y, self.xy)):
                self.move(holder, s, self.to_core + k * self.narrow + s, self.at_core).wait_send()


def place_bounds(live_ref, pairs_ref, sources_ref, first_ref, bounds_ref):
    place = lax.broadcasted_iota(jnp.int32, (1, SEQ), 1)
    live = place < live_ref[0]
    count = pairs_ref.shape[1]
    first, start, end = jnp.zeros_like(place), jnp.zeros_like(place), jnp.zeros_like(place)
    for n in range(count):
        begun = place >= pairs_ref[0, n]
        first = jnp.where(begun, pairs_ref[0, n], first)
        start = jnp.where(begun, sources_ref[0, n], start)
        end = jnp.where(begun, sources_ref[0, n + 1] if n + 1 < count else MEM, end)
    first_ref[0] = jnp.where(live, first, live_ref[0])
    bounds_ref[0, 0:1, :] = jnp.where(live, start, 0)
    bounds_ref[0, 1:2, :] = jnp.where(live, end, MEM)
    bounds_ref[0, 2:8, :] = jnp.zeros((6, SEQ), jnp.int32)


def front_kernel(
    narrow,
    live_ref,
    pairs_ref,
    sources_ref,
    wq_ref,
    wk_ref,
    wv_ref,
    ck_ref,
    cv_ref,
    others_refs,
    hidden_in_ref,
    hidden_out_ref,
    extra_ref,
    tokens_ref,
    memory_ref,
    wide_any,
    later_any,
    late_any,
    normed_any,
    qkv_any,
    mixed_ref,
    log_ref,
    norms_ref,
    first_ref,
    bounds_ref,
    after_ref,
    normed_two_ref,
    cross_q_ref,
    cross_kv_ref,
    cross_mixed_ref,
    cross_log_ref,
    shard_a,
    shard_b,
    shard_c,
    weight,
    later,
    normed,
    qkv,
    a_send,
    a_recv,
    b_send,
    b_recv,
    c_send,
    c_recv,
    local_sems,
):
    d = tokens_ref.shape[1]
    rows = wq_ref.shape[0]
    for p in range(PAIRS):
        lanes = slice(p * 128, (p + 1) * 128)
        for n, ref in enumerate((wq_ref, wk_ref, wv_ref)):
            shard_a[:, (3 * p + n) * 128 : (3 * p + n + 1) * 128] = ref[:, lanes]
        for n, ref in enumerate((ck_ref, cv_ref)):
            at = KV_CROSS * 2 * d + (2 * p + n) * 128
            shard_b[:, at : at + 128] = ref[:, lanes]
    shard_a[:, 3 * d :] = extra_ref[...]

    one = Gather(shard_a, weight, a_send, a_recv, narrow)
    two = Gather(shard_b, later, b_send, b_recv, narrow)
    three = Gather(shard_c, late_any, c_send, c_recv, narrow)
    keeps = [
        pltpu.make_async_copy(gather.shard_ref, gather.own_place(), local_sems.at[n])
        for n, gather in enumerate((one, two, three))
    ]
    greet_all(narrow)
    one.begin_line()
    one.begin_spread()
    keeps[0].start()
    for at, ref in zip((OUT_SELF, QUERY_CROSS, OUT_CROSS), others_refs):
        shard_b[:, at * d : (at + 1) * d] = ref[...]
    for n in range(4):
        shard_c[n * rows : (n + 1) * rows, :] = hidden_in_ref[:, n * d : (n + 1) * d]
    shard_c[4 * rows :, :] = hidden_out_ref[...]
    keeps[1].start()
    keeps[2].start()
    place_bounds(live_ref, pairs_ref, sources_ref, first_ref, bounds_ref)
    one.round(1)
    one.round(2)
    two.begin_line()
    for r in range(3, narrow + 1):
        one.round(r)
    two.begin_spread()
    one.corners()
    one.arrive()
    keeps[0].wait()
    out_wide = pltpu.make_async_copy(weight, wide_any, local_sems.at[3])
    out_wide.start()

    norms_ref[...] = weight[:, 3 * d :].astype(F32).T[0:8, :]

    def project_block(t, carry):
        at = pl.ds(pl.multiple_of(t * TB, TB), TB)
        unit, _ = norm_parts(tokens_ref[at, :].astype(F32))
        value = (unit * norms_ref[0:1, :] + norms_ref[1:2, :]).astype(BF16)
        normed[at, :] = value
        for part in range(3):
            lanes = slice(part * d, (part + 1) * d)
            qkv[at, lanes] = mm(value, weight[:, lanes]).astype(BF16)
        return carry

    def pair_block(p, carry):
        def lanes(n):
            return pl.ds(pl.multiple_of(p * 384 + n * 128, 128), 128)

        attend(
            lambda at: qkv[at, lanes(0)],
            qkv[:, lanes(1)],
            qkv[:, lanes(2)],
            functools.partial(self_visible, first_ref),
            self_extent,
            *pair_keepers(mixed_ref, log_ref, p),
        )
        return carry

    def middle_block(t, carry):
        at = pl.ds(pl.multiple_of(t * TB, TB), TB)
        mb = memory_ref.shape[0] * TB // tokens_ref.shape[0]
        mem_at = pl.ds(pl.multiple_of(t * mb, mb), mb)
        after = tokens_ref[at, :].astype(F32) + mm(mixed_ref[at, :], later[:, OUT_SELF * d : (OUT_SELF + 1) * d])
        after_ref[at, :] = after
        for n in range(2):
            lanes = slice((2 * KV_CROSS + n) * d, (2 * KV_CROSS + n + 1) * d)
            cross_kv_ref[mem_at, n * d : (n + 1) * d] = mm(memory_ref[mem_at, :], later[:, lanes]).astype(BF16)
        unit, _ = norm_parts(after)
        value = (unit * norms_ref[2:3, :] + norms_ref[3:4, :]).astype(BF16)
        normed_two_ref[at, :] = value
        cross_q_ref[at, :] = mm(value, later[:, QUERY_CROSS * d : (QUERY_CROSS + 1) * d]).astype(BF16)
        return carry

    def cross_block(p, carry):
        def lanes(n):
            return pl.ds(pl.multiple_of(p * 256 + n * 128, 128), 128)

        q_lanes = pl.ds(pl.multiple_of(p * 128, 128), 128)
        attend(
            lambda at: cross_q_ref[at, q_lanes],
            cross_kv_ref[:, lanes(0)],
            cross_kv_ref[:, lanes(1)],
            functools.partial(cross_visible, bounds_ref),
            cross_extent,
            *pair_keepers(cross_mixed_ref, cross_log_ref, p),
        )
        return carry

    lax.fori_loop(0, 4, project_block, 0)
    out_normed = pltpu.make_async_copy(normed, normed_any, local_sems.at[4])
    out_qkv = pltpu.make_async_copy(qkv, qkv_any, local_sems.at[5])
    out_normed.start()
    out_qkv.start()
    two.round(1)
    lax.fori_loop(0, 2, pair_block, 0)
    two.round(2)
    lax.fori_loop(2, 5, pair_block, 0)
    for r in range(3, narrow):
        two.round(r)
    three.begin_line()
    lax.fori_loop(5, 8, pair_block, 0)
    two.round(narrow)
    three.begin_spread()
    two.corners()
    two.arrive()
    keeps[1].wait()
    out_later = pltpu.make_async_copy(later, later_any, local_sems.at[6])
    out_later.start()
    three.round(1)
    lax.fori_loop(0, 4, middle_block, 0)
    three.round(2)
    lax.fori_loop(0, 4, cross_block, 0)
    for r in range(3, narrow):
        three.round(r)
    lax.fori_loop(4, 8, cross_block, 0)
    three.round(narrow)
    three.corners()
    three.arrive()
    keeps[2].wait()
    for gather in (one, two, three):
        gather.close()
    for copy in (out_wide, out_normed, out_qkv, out_later):
        copy.wait()


def pair_keepers(out_ref, log_ref, p):
    def keep_out(at, value):
        out_ref[at, pl.ds(pl.multiple_of(p * 128, 128), 128)] = value

    def keep_log(h, at, value):
        log_ref[0, p, h : h + 1, at] = value

    return keep_out, keep_log


def front(live_length, pair_starts, source_starts, weights, hidden_in, hidden_out, extra, tokens, memory, narrow):
    self_query, self_key, self_value, self_output, cross_query, cross_key, cross_value, cross_output = weights
    shard_rows, d = self_query.shape
    rows, mem_rows = tokens.shape[0], memory.shape[0]
    block = 4 * shard_rows + hidden_out.shape[0]
    anywhere, vmem = pl.BlockSpec(memory_space=pl.ANY), pl.BlockSpec(memory_space=pltpu.VMEM)
    smem = pl.BlockSpec(memory_space=pltpu.SMEM)
    logs = jax.ShapeDtypeStruct((1, PAIRS, 8, SEQ), F32)

    def kernel(*refs):
        front_kernel(narrow, *refs[:8], refs[8:11], *refs[11:])

    return pl.pallas_call(
        kernel,
        in_specs=[smem] * 3 + [vmem] * 13,
        out_specs=[anywhere] * 5 + [vmem] * 11,
        out_shape=[
            shape(d, 3 * d + 128, BF16),
            shape(d, 5 * d, BF16),
            shape(8 * narrow * block, d, BF16),
            shape(rows, d, BF16),
            shape(rows, 3 * d, BF16),
            shape(rows, d, BF16),
            logs,
            shape(8, d, F32),
            jax.ShapeDtypeStruct((1, 1, SEQ), jnp.int32),
            jax.ShapeDtypeStruct((1, 8, SEQ), jnp.int32),
            shape(rows, d, F32),
            shape(rows, d, BF16),
            shape(rows, d, BF16),
            shape(mem_rows, 2 * d, BF16),
            shape(rows, d, BF16),
            logs,
        ],
        scratch_shapes=[
            pltpu.VMEM((shard_rows, 3 * d + 128), BF16),
            pltpu.VMEM((shard_rows, 5 * d), BF16),
            pltpu.VMEM((block, d), BF16),
            pltpu.VMEM((d, 3 * d + 128), BF16),
            pltpu.VMEM((d, 5 * d), BF16),
            pltpu.VMEM((rows, d), BF16),
            pltpu.VMEM((rows, 3 * d), BF16),
            *[pltpu.SemaphoreType.DMA((10 * narrow,))] * 6,
            pltpu.SemaphoreType.DMA((7,)),
        ],
        name="front",
        compiler_params=pltpu.CompilerParams(collective_id=0, has_side_effects=True, vmem_limit_bytes=60 << 20),
        cost_estimate=cost(30 * rows * d * d, 200 << 20),
    )(
        live_length,
        pair_starts,
        source_starts,
        self_query,
        self_key,
        self_value,
        cross_key,
        cross_value,
        self_output,
        cross_query,
        cross_output,
        hidden_in,
        hidden_out,
        extra,
        tokens,
        memory,
    )


def stages_of(mesh_axes):
    plan = []
    for axis, size in mesh_axes:
        bits = size.bit_length() - 1
        at = 0
        while at < bits:
            take = 1 if (bits - at) % 2 else 2
            plan.append((axis, at, take))
            at += take
    return plan


def trade(value, axis, size, mask):
    return lax.ppermute(value, axis, [(i, i ^ mask) for i in range(size)])


def digit_of(axis, at, take):
    return (lax.axis_index(axis) >> at) & ((1 << take) - 1)


def pick(value, digit, place):
    if isinstance(value, list):
        return jnp.concatenate([pick(v, digit, place) for v in value], axis=0)
    return lax.dynamic_index_in_dim(value, digit, place, keepdims=False)


def add_up(own, pieces):
    total = own.astype(F32)
    for piece in pieces:
        total = total + piece.astype(F32)
    return total


def sum_steps(partial, mesh_axes):
    sizes = dict(mesh_axes)
    plan = stages_of(mesh_axes)
    groups = []
    for axis, _ in mesh_axes:
        groups += sorted((s for s in plan if s[0] == axis), key=lambda s: -s[1])
    devices = 1
    for _, size in mesh_axes:
        devices *= size
    columns = partial[0].shape[1]
    extents = [1 << s[2] for s in groups]
    value = [p.reshape(p.shape[0] // WIDTH, *extents, -1, columns) for p in partial]
    for number, stage in enumerate(plan):
        axis, at, take = stage
        place = 1 + groups.index(stage)
        groups.remove(stage)
        if axis == "wide" and take == 2:
            if isinstance(value, list):
                value = jnp.concatenate(value, axis=0)
            split = value.reshape(*value.shape[:place], 2, 2, *value.shape[place + 1 :])
            a, b = split[..., : columns // 2], split[..., columns // 2 :]
            low, high = digit_of(axis, at, 1), digit_of(axis, at + 1, 1)
            step = ((high, place, 2 << at), (low, place + 1, 1 << at))
            for (digit_a, place_a, mask_a), (digit_b, place_b, mask_b) in (
                step,
                ((low, place, 1 << at), (high, place, 2 << at)),
            ):
                pieces = yield [
                    trade(pick(a, digit_a ^ 1, place_a), axis, sizes[axis], mask_a),
                    trade(pick(b, digit_b ^ 1, place_b), axis, sizes[axis], mask_b),
                ]
                a = add_up(pick(a, digit_a, place_a), pieces[:1]).astype(BF16)
                b = add_up(pick(b, digit_b, place_b), pieces[1:]).astype(BF16)
            value = jnp.concatenate([a, b], axis=-1)
            continue
        digit = digit_of(axis, at, take)
        pieces = yield [
            trade(pick(value, digit ^ mask, place), axis, sizes[axis], mask << at) for mask in range(1, 1 << take)
        ]
        value = add_up(pick(value, digit, place), pieces)
        if number < len(plan) - 1:
            value = value.astype(BF16)
    return value.astype(F32).reshape(-1, columns)


class StagedSum:
    def __init__(self, partial, mesh_axes):
        self.steps = sum_steps(partial, mesh_axes)
        self.under_way = next(self.steps)
        self.value = None

    def go_on(self, pieces):
        try:
            self.under_way = self.steps.send(pieces)
        except StopIteration as stop:
            self.under_way, self.value = None, stop.value

    def result(self):
        while self.under_way is not None:
            self.go_on(self.under_way)
        return self.value


def fence(value, *sums):
    held = [s for s in sums if s.under_way is not None]
    value, arrived = lax.optimization_barrier((value, [s.under_way for s in held]))
    for s, pieces in zip(held, arrived):
        s.go_on(pieces)
    return value


def sum_everywhere(value, mesh_axes):
    sizes = dict(mesh_axes)
    for axis, at, take in stages_of(mesh_axes):
        arrived = [trade(value, axis, sizes[axis], mask << at) for mask in range(1, 1 << take)]
        for piece in arrived:
            value = value + piece
    return value


def by_pairs(*parts):
    rows = parts[0].shape[0]
    return jnp.stack([p.reshape(rows, -1, 128) for p in parts], axis=2).reshape(rows, -1)


def from_pairs(value, count):
    rows = value.shape[0]
    split = value.reshape(rows, -1, count, 128)
    return [split[:, :, c].reshape(rows, -1) for c in range(count)]


def outer_sum(left_side, gradient):
    return jnp.einsum("td,te->de", left_side, gradient, preferred_element_type=F32).astype(BF16)


CHUNKS = 4


class Scatter:
    def __init__(self, own, theirs, buffers, keep, send_sems, recv_sems, narrow):
        self.own, self.theirs, self.keep = own, theirs, keep
        self.from_core, self.a1, self.b1, self.a2, self.b2, self.from_line = buffers
        self.send_sems, self.recv_sems = send_sems, recv_sems
        self.narrow = narrow
        self.slots = own.shape[0]
        self.half = self.a1.shape[-1]
        self.w, self.z = lax.axis_index("wide"), lax.axis_index("narrow")
        self.c, self.x, self.y = self.w & 1, (self.w >> 1) & 1, (self.w >> 2) & 1
        self.per_chunk = 4 + narrow

    def move(self, i, number, src, dst, target):
        at = i * self.per_chunk + number
        return pltpu.make_async_remote_copy(
            src_ref=src,
            dst_ref=dst,
            send_sem=self.send_sems.at[at],
            recv_sem=self.recv_sems.at[at],
            device_id=target,
            device_id_type=pl.DeviceIdType.MESH,
        )

    def to_core(self, i):
        return self.move(i, 0, self.theirs(i), self.from_core.at[i % self.slots], (self.w ^ 1, self.z))

    def first(self, i):
        left, right = pl.ds(0, self.half), pl.ds(self.half, self.half)
        to_x, to_y = (self.w ^ 2, self.z), (self.w ^ 4, self.z)
        return (
            self.move(i, 1, self.own.at[i % self.slots, :, 1 - self.x, :, :, left], self.a1.at[i % self.slots], to_x),
            self.move(i, 2, self.own.at[i % self.slots, 1 - self.y, :, :, :, right], self.b1.at[i % self.slots], to_y),
        )

    def second(self, i):
        left, right = pl.ds(0, self.half), pl.ds(self.half, self.half)
        to_x, to_y = (self.w ^ 2, self.z), (self.w ^ 4, self.z)
        return (
            self.move(i, 3, self.own.at[i % self.slots, 1 - self.y, self.x, :, :, left], self.a2.at[i % self.slots], to_y),
            self.move(i, 4, self.own.at[i % self.slots, self.y, 1 - self.x, :, :, right], self.b2.at[i % self.slots], to_x),
        )

    def along(self, i):
        return [
            self.move(
                i,
                4 + mask,
                self.own.at[i % self.slots, self.y, self.x, self.z ^ mask],
                self.from_line.at[i % self.slots, mask - 1],
                (self.w, self.z ^ mask),
            )
            for mask in range(1, self.narrow)
        ]

    def begin(self, i):
        self.to_core(i).start()

    def add(self, i, y, x, columns, piece):
        now = self.own[i % self.slots, y, x, :, :, columns]
        self.own[i % self.slots, y, x, :, :, columns] = now + piece

    def step(self, i, stage):
        both, left, right = slice(None), slice(0, self.half), slice(self.half, None)
        if stage == 0:
            self.to_core(i).wait_recv()
            for a in range(2):
                for b in range(2):
                    self.add(i, a, b, both, self.from_core[i % self.slots, a, b])
            for copy in self.first(i):
                copy.start()
        elif stage == 1:
            for copy in self.first(i):
                copy.wait_recv()
            for a in range(2):
                self.add(i, a, self.x, left, self.a1[i % self.slots, a])
                self.add(i, self.y, a, right, self.b1[i % self.slots, a])
            for copy in self.second(i):
                copy.start()
        elif stage == 2:
            for copy in self.second(i):
                copy.wait_recv()
            self.add(i, self.y, self.x, left, self.a2[i % self.slots])
            self.add(i, self.y, self.x, right, self.b2[i % self.slots])
            for copy in self.along(i):
                copy.start()
        else:
            for copy in self.along(i):
                copy.wait_recv()
            total = self.own[i % self.slots, self.y, self.x, self.z].astype(F32)
            for mask in range(1, self.narrow):
                total = total + self.from_line[i % self.slots, mask - 1].astype(F32)
            self.keep(i, total)

    def close(self, i):
        for copy in (self.to_core(i), *self.first(i), *self.second(i), *self.along(i)):
            copy.wait_send()


def scatter_scratch(chunks, narrow, rows, width, more=0):
    copies = (chunks + more) * (4 + narrow)
    return [
        pltpu.VMEM((chunks, 2, 2, narrow, rows, width), BF16),
        pltpu.VMEM((chunks, 2, 2, narrow, rows, width), BF16),
        pltpu.VMEM((chunks, 2, narrow, rows, width // 2), BF16),
        pltpu.VMEM((chunks, 2, narrow, rows, width // 2), BF16),
        pltpu.VMEM((chunks, narrow, rows, width // 2), BF16),
        pltpu.VMEM((chunks, narrow, rows, width // 2), BF16),
        pltpu.VMEM((chunks, narrow - 1, rows, width), BF16),
        pltpu.SemaphoreType.DMA((copies,)),
        pltpu.SemaphoreType.DMA((copies,)),
        pltpu.SemaphoreType.DMA((chunks + more,)),
    ]


class Carried:
    def __init__(self, shares, scratch, keep, narrow):
        own, *buffers, send_sems, recv_sems, self.load_sems = scratch
        self.shares = shares
        self.scatter = Scatter(own, self.other, buffers, keep, send_sems, recv_sems, narrow)
        self.chunks, self.slots = len(shares), own.shape[0]

    def other(self, i):
        return self.shares[i](1 - self.scatter.c)

    def load(self, i):
        return pltpu.make_async_copy(
            self.shares[i](self.scatter.c), self.scatter.own.at[i % self.slots], self.load_sems.at[i]
        )

    def open(self):
        for i in range(self.slots):
            self.load(i).start()
        greet_all(self.scatter.narrow)
        for i in range(2):
            self.scatter.begin(i)

    def reuse(self, i):
        self.scatter.close(i - self.slots)
        self.load(i).start()
        self.scatter.begin(i)

    def steps(self, plan):
        for i, stage in plan:
            if stage == 0:
                self.load(i).wait()
            self.scatter.step(i, stage)
            if stage == 0 and i + 2 < self.slots:
                self.scatter.begin(i + 2)

    def close(self):
        for i in range(self.chunks - self.slots, self.chunks):
            self.scatter.close(i)


def share_views(array, narrow, rows):
    return array.reshape(2, 2, 2, narrow, rows, array.shape[1])


def share_views(array, narrow, rows):
    return array.reshape(2, 2, 2, narrow, rows, array.shape[1])


def columns_of(ref, at, width):
    return lambda core: ref.at[:, :, core, :, :, pl.ds(at, width)]


def tn(a, b):
    return lax.dot_general(a, b, (((0,), (0,)), ((), ())), preferred_element_type=F32)


def outer_into(out_ref, left_ref, right):
    for at in range(0, left_ref.shape[1], 256):
        out_ref[at : at + 256, :] = tn(left_ref[:, at : at + 256], right).astype(BF16)


CROSS_PLAN = (
    ((0, 0),),
    ((1, 0),),
    (),
    ((0, 1), (1, 1)),
    ((2, 0), (3, 0)),
    ((1, 2),),
    ((0, 2),),
    ((2, 1), (4, 0)),
    ((1, 3),),
    ((2, 2), (3, 1), (4, 1)),
    ((3, 2), (5, 0)),
    ((4, 2),),
    ((5, 1),),
    ((5, 2),),
    ((0, 3),),
    (),
    ((2, 3), (3, 3), (4, 3), (5, 3)),
)
CROSS_WIDE = 2


def cross_back_kernel(
    narrow,
    bounds_ref,
    log_ref,
    q_ref,
    kv_ref,
    mixed_pair_ref,
    grad_ref,
    before_ref,
    total_ref,
    norms_ref,
    mixed_any,
    b2_any,
    normed_any,
    memory_any,
    self_mixed_any,
    early_any,
    share_any,
    wide_any,
    out_ref,
    next_ref,
    mem_ref,
    ngrad_ref,
    shares_ref,
    shard_ref,
    wide_ref,
    dk_ref,
    dv_ref,
    dq_ref,
    dkv_ref,
    b1_ref,
    wq,
    wkv,
    wo,
    weight_sems,
    mixed_ref,
    b2_ref,
    normed_ref,
    memory_ref,
    self_mixed_ref,
    *scratch,
):
    step = pl.program_id(0)
    d = wq.shape[0]
    rows = shard_ref.shape[0] // 4

    def keep(i, value):
        if i < 4:
            shard_ref[i * rows : (i + 1) * rows, :] = value
        else:
            wide_ref[:, (i - 4) * d : (i - 3) * d] = value

    def piece(i):
        return lambda core: share_any.at[:, :, core, :, i]

    pieces = [piece(i) for i in range(4)] + [columns_of(wide_any, i * d, d) for i in range(CROSS_WIDE)]
    carried = Carried(pieces, scratch, keep, narrow)
    loads = [
        pltpu.make_async_copy(early_any.at[:, pl.ds(QUERY_CROSS * d, d)], wq, weight_sems.at[0]),
        pltpu.make_async_copy(early_any.at[:, pl.ds(2 * KV_CROSS * d, 2 * d)], wkv, weight_sems.at[1]),
        pltpu.make_async_copy(early_any.at[:, pl.ds(OUT_SELF * d, d)], wo, weight_sems.at[2]),
    ]
    later_loads = [
        pltpu.make_async_copy(source, target, weight_sems.at[3 + n])
        for n, (source, target) in enumerate(
            (
                (mixed_any, mixed_ref),
                (b2_any, b2_ref),
                (normed_any, normed_ref),
                (memory_any, memory_ref),
                (self_mixed_any, self_mixed_ref),
            )
        )
    ]

    @pl.when(step == 0)
    def _():
        carried.open()
        for load in loads + later_loads:
            load.start()

    @pl.when(step < PAIRS)
    def _():
        def keep_dq(rows, value):
            dq_ref[rows, pl.ds(pl.multiple_of(step * 128, 128), 128)] = value

        cross_backward_pair(bounds_ref, log_ref, q_ref, kv_ref, mixed_pair_ref, grad_ref, keep_dq, None, dk_ref, dv_ref)
        at = pl.multiple_of(step * 256, 256)
        dkv_ref[:, pl.ds(at, 128)] = (dk_ref[...] * HEAD_DIM**-0.5).astype(BF16)
        dkv_ref[:, pl.ds(pl.multiple_of(at + 128, 128), 128)] = dv_ref[...].astype(BF16)

    @pl.when(step == PAIRS)
    def _():
        for load in loads:
            load.wait()
        ngrad_ref[...] = jnp.zeros_like(ngrad_ref)

    tokens_end = PAIRS + SEQ // TB

    @pl.when((step >= PAIRS) & (step < tokens_end))
    def _():
        t = step - PAIRS
        mb = mem_ref.shape[0]
        at = pl.ds(pl.multiple_of(t * TB, TB), TB)
        gradient = mm_t(dq_ref[at, :], wq[...])
        mem_ref[...] = mm_t(dkv_ref[pl.ds(pl.multiple_of(t * mb, mb), mb), :], wkv[...]).astype(BF16)
        unit, inverse = norm_parts(before_ref[...])
        total = total_ref[...] + norm_back(unit, inverse, norms_ref[2:3, :], gradient)
        out_ref[...] = total
        b1 = total.astype(BF16)
        b1_ref[at, :] = b1
        next_ref[...] = mm_t(b1, wo[...]).astype(BF16)
        ngrad_ref[0:1, :] += jnp.sum(gradient * unit, axis=0, keepdims=True)
        ngrad_ref[1:2, :] += jnp.sum(gradient, axis=0, keepdims=True)

    @pl.when(step == tokens_end)
    def _():
        for load in later_loads:
            load.wait()
        outer_into(shares_ref, mixed_ref, b2_ref[...])

    pl.when(step == tokens_end + 1)(lambda: outer_into(shares_ref, normed_ref, dq_ref[...]))
    pl.when(step == tokens_end + 2)(lambda: outer_into(shares_ref, memory_ref, dkv_ref[:, :d]))
    pl.when(step == tokens_end + 3)(lambda: outer_into(shares_ref, memory_ref, dkv_ref[:, d:]))
    pl.when(step == tokens_end + 4)(lambda: outer_into(shares_ref, self_mixed_ref, b1_ref[...]))

    for number, plan in enumerate(CROSS_PLAN):
        pl.when(step == number)(functools.partial(carried.steps, plan))
    pl.when(step == len(CROSS_PLAN) - 1)(carried.close)


def cross_back(bounds, logs, q, kv, mixed, grad, before, total, norms, b2, normed, memory, self_mixed, early, share, wide_share, narrow):
    rows, d = q.shape
    mem_rows = kv.shape[0]
    shard_rows = d // (8 * narrow)
    steps = rows // TB
    mb = mem_rows // steps

    def pair(s):
        return jnp.minimum(s, PAIRS - 1)

    def token(s):
        return jnp.clip(s - PAIRS, 0, steps - 1)

    anywhere = pl.BlockSpec(memory_space=pl.ANY)
    by_pair = pl.BlockSpec((SEQ, 128), lambda s: (0, pair(s)))
    by_token = pl.BlockSpec((TB, d), lambda s: (token(s), 0))
    return pl.pallas_call(
        functools.partial(cross_back_kernel, narrow),
        grid=(PAIRS + steps + 5,),
        in_specs=[
            pl.BlockSpec((1, 8, SEQ), lambda s: (0, 0, 0)),
            pl.BlockSpec((1, 1, 8, SEQ), lambda s: (0, pair(s), 0, 0)),
            by_pair,
            pl.BlockSpec((MEM, 256), lambda s: (0, pair(s))),
            by_pair,
            by_pair,
            by_token,
            by_token,
            whole(8, d),
            *[anywhere] * 5,
            anywhere,
            anywhere,
            anywhere,
        ],
        out_specs=[
            by_token,
            by_token,
            pl.BlockSpec((mb, d), lambda s: (token(s), 0)),
            whole(8, d),
            pl.BlockSpec((d, d), lambda s: (jnp.maximum(s - PAIRS - steps, 0), 0)),
            whole(4 * shard_rows, d),
            whole(shard_rows, CROSS_WIDE * d),
        ],
        out_shape=[
            shape(rows, d, F32),
            shape(rows, d, BF16),
            shape(mem_rows, d, BF16),
            shape(8, d, F32),
            shape(5 * d, d, BF16),
            shape(4 * shard_rows, d, F32),
            shape(shard_rows, CROSS_WIDE * d, F32),
        ],
        scratch_shapes=[
            pltpu.VMEM((MEM, 128), F32),
            pltpu.VMEM((MEM, 128), F32),
            pltpu.VMEM((rows, d), BF16),
            pltpu.VMEM((mem_rows, 2 * d), BF16),
            pltpu.VMEM((rows, d), BF16),
            pltpu.VMEM((d, d), BF16),
            pltpu.VMEM((d, 2 * d), BF16),
            pltpu.VMEM((d, d), BF16),
            pltpu.SemaphoreType.DMA((8,)),
            pltpu.VMEM((rows, d), BF16),
            pltpu.VMEM((rows, d), BF16),
            pltpu.VMEM((rows, d), BF16),
            pltpu.VMEM((mem_rows, d), BF16),
            pltpu.VMEM((rows, d), BF16),
            *scatter_scratch(4 + CROSS_WIDE, narrow, shard_rows, d),
        ],
        name="cross_back",
        compiler_params=pltpu.CompilerParams(collective_id=2, has_side_effects=True, vmem_limit_bytes=60 << 20),
        cost_estimate=cost(40 * rows * d * d, 100 << 20),
    )(
        bounds,
        logs,
        q,
        kv,
        mixed,
        grad,
        before,
        total,
        norms,
        mixed,
        b2,
        normed,
        memory,
        self_mixed,
        early,
        share.reshape(2, 2, 2, narrow, 4, shard_rows, d),
        share_views(wide_share, narrow, shard_rows),
    )


SELF_PLAN = (
    ((0, 0),),
    ((1, 0),),
    ((2, 0),),
    ((0, 1), (2, 1), (3, 0), (4, 0)),
    ((1, 1),),
    ((0, 2), (2, 2)),
    ((3, 1), (5, 0)),
    ((4, 1), (6, 0)),
    ((0, 3), (2, 3), (1, 2), (3, 2), (5, 1)),
    ((1, 3),),
    ((3, 3), (4, 2), (6, 1), (7, 0)),
    ((8, 0),),
    ((5, 2), (5, 3), (6, 2), (7, 1), (8, 1), (9, 0)),
    ((7, 2), (8, 2), (9, 1), (9, 2)),
    ((4, 3), (6, 3), (7, 3), (8, 3), (9, 3)),
)
SELF_REUSE = {9: 7, 10: 8, 11: 9}
SELF_WIDE = 4 - CROSS_WIDE
SELF_CHUNKS = SELF_WIDE + 5


def self_back_kernel(
    narrow,
    first_ref,
    log_ref,
    qkv_ref,
    mixed_ref,
    grad_ref,
    normed_ref,
    tokens_ref,
    total_ref,
    norms_ref,
    norm_two_ref,
    norm_three_ref,
    expand_low_ref,
    early_any,
    wide_any,
    shares_any,
    out_ref,
    norm_out_ref,
    expand_ref,
    cross_output_ref,
    cross_query_ref,
    cross_key_ref,
    cross_value_ref,
    self_output_ref,
    query_ref,
    key_ref,
    value_ref,
    dk_ref,
    dv_ref,
    dqkv,
    weight,
    weight_sem,
    stage,
    nval,
    nin,
    norm_send_sems,
    norm_recv_sems,
    *scratch,
):
    step = pl.program_id(0)
    d = normed_ref.shape[1]

    outs = (query_ref, key_ref, value_ref)

    def keep(i, value):
        i -= SELF_WIDE
        if i < 0:
            expand_ref[:, (i + 4) * d : (i + 5) * d] = value
        elif i == 0:
            cross_output_ref[...] = value
        elif i == 1:
            cross_query_ref[...] = value
        elif i == 4:
            self_output_ref[...] = value
        elif i > 4:
            for n in range(d // 128):
                pair, kind = divmod((i - 5) * d // 128 + n, 3)
                outs[kind][:, pair * 128 : (pair + 1) * 128] = value[:, n * 128 : (n + 1) * 128]
        else:
            for n in range(d // 256):
                at = (i - 2) * d // 2 + n * 128
                cross_key_ref[:, at : at + 128] = value[:, n * 256 : n * 256 + 128]
                cross_value_ref[:, at : at + 128] = value[:, n * 256 + 128 : n * 256 + 256]

    def piece(i):
        return lambda core: shares_any.at[i, :, :, core]

    def staged_piece(i):
        return lambda core: stage.at[i, :, :, core]

    pieces = [columns_of(wide_any, (CROSS_WIDE + i) * d, d) for i in range(SELF_WIDE)] + [piece(i) for i in range(5)]
    pieces += [staged_piece(i) for i in range(3)]
    carried = Carried(pieces, scratch, keep, narrow)
    load = pltpu.make_async_copy(early_any.at[:, pl.ds(0, 3 * d)], weight, weight_sem)

    @pl.when(step == 0)
    def _():
        carried.open()
        load.start()
        expand_ref[:, : CROSS_WIDE * d] = expand_low_ref[...]

    @pl.when(step < PAIRS)
    def _():
        base = step * 384

        def keep_dq(rows, value):
            dqkv[rows, pl.ds(pl.multiple_of(base, 128), 128)] = value

        attend_back(
            lambda rows: qkv_ref[rows, 0:128],
            qkv_ref[:, 128:256],
            qkv_ref[:, 256:384],
            grad_ref,
            mixed_ref,
            log_ref,
            functools.partial(self_visible, first_ref),
            self_extent,
            keep_dq,
            dk_ref,
            dv_ref,
        )
        dqkv[:, pl.ds(pl.multiple_of(base + 128, 128), 128)] = (dk_ref[...] * HEAD_DIM**-0.5).astype(BF16)
        dqkv[:, pl.ds(pl.multiple_of(base + 256, 128), 128)] = dv_ref[...].astype(BF16)

    rows = stage.shape[5]
    group = 2 * narrow * rows

    def multiply(m):
        for a in range(2):
            for b in range(2):
                at = (2 * a + b) * group
                product = tn(normed_ref[:, at : at + group], dqkv[:, m * d : (m + 1) * d])
                stage[m, a, b] = product.astype(BF16).reshape(2, narrow, rows, d)

    for m in range(3):
        pl.when(step == PAIRS + m)(functools.partial(multiply, m))

    @pl.when(step == PAIRS + 3)
    def _():
        load.wait()
        nval[0] = jnp.zeros_like(nval[0])
        nval[0, 2:4, :] = norm_two_ref[0:2, :]
        nval[0, 4:6, :] = norm_three_ref[0:2, :]

    @pl.when(step >= PAIRS + 3)
    def _():
        at = pl.ds(pl.multiple_of((step - PAIRS - 3) * TB, TB), TB)
        gradient = mm_t(dqkv[at, :], weight[...])
        unit, inverse = norm_parts(tokens_ref[...].astype(F32))
        total = total_ref[...] + norm_back(unit, inverse, norms_ref[0:1, :], gradient)
        out_ref[...] = total.astype(BF16)
        nval[0, 0:1, :] += jnp.sum(gradient * unit, axis=0, keepdims=True)
        nval[0, 1:2, :] += jnp.sum(gradient, axis=0, keepdims=True)

    w, z = carried.scatter.w, carried.scatter.z

    def norm_copy(stage_number, number, target):
        return pltpu.make_async_remote_copy(
            src_ref=nval.at[stage_number],
            dst_ref=nin.at[number],
            send_sem=norm_send_sems.at[number],
            recv_sem=norm_recv_sems.at[number],
            device_id=target,
            device_id_type=pl.DeviceIdType.MESH,
        )

    norm_copies = [[norm_copy(0, 0, (w ^ 1, z))], [norm_copy(1, 1, (w ^ 2, z))], [norm_copy(2, 2, (w ^ 4, z))]]
    norm_copies.append([norm_copy(3, 2 + mask, (w, z ^ mask)) for mask in range(1, narrow)])

    def norm_step(number):
        if number > 0:
            for copy in norm_copies[number - 1]:
                copy.wait_recv()
            value = nval[number - 1]
            if number < 4:
                nval[number] = value + nin[number - 1]
            else:
                for mask in range(1, narrow):
                    value = value + nin[2 + mask]
                norm_out_ref[...] = value
        if number < 4:
            for copy in norm_copies[number]:
                copy.start()

    last = len(SELF_PLAN) - 1
    for number, plan in enumerate(SELF_PLAN[:last]):
        pl.when(step == number)(functools.partial(carried.steps, plan))
        if number in SELF_REUSE:
            pl.when(step == number)(functools.partial(carried.reuse, SELF_REUSE[number]))

    @pl.when(step == last)
    def _():
        for number in range(5):
            norm_step(number)
            if number < len(SELF_PLAN[last]):
                carried.steps(SELF_PLAN[last][number : number + 1])
        carried.close()
        for copies in norm_copies:
            for copy in copies:
                copy.wait_send()


def self_back(first, logs, qkv, mixed, grad, normed, tokens, total, norms, norm_two, norm_three, expand_low, early, wide_share, shares, narrow):
    rows, d = mixed.shape
    shard_rows = d // (8 * narrow)

    def pair(s):
        return jnp.minimum(s, PAIRS - 1)

    def token(s):
        return jnp.maximum(s - PAIRS - 3, 0)

    anywhere = pl.BlockSpec(memory_space=pl.ANY)
    by_pair = pl.BlockSpec((SEQ, 128), lambda s: (0, pair(s)))
    by_token = pl.BlockSpec((TB, d), lambda s: (token(s), 0))
    return pl.pallas_call(
        functools.partial(self_back_kernel, narrow),
        grid=(PAIRS + 3 + rows // TB,),
        in_specs=[
            pl.BlockSpec((1, 1, SEQ), lambda s: (0, 0, 0)),
            pl.BlockSpec((1, 1, 8, SEQ), lambda s: (0, pair(s), 0, 0)),
            pl.BlockSpec((SEQ, 384), lambda s: (0, pair(s))),
            by_pair,
            by_pair,
            whole(rows, d),
            by_token,
            by_token,
            whole(8, d),
            whole(8, d),
            whole(8, d),
            whole(shard_rows, CROSS_WIDE * d),
            anywhere,
            anywhere,
            anywhere,
        ],
        out_specs=[
            by_token,
            whole(8, d),
            whole(shard_rows, 4 * d),
            *[whole(shard_rows, d)] * 8,
        ],
        out_shape=[
            shape(rows, d, BF16),
            shape(8, d, F32),
            shape(shard_rows, 4 * d, F32),
            *[shape(shard_rows, d, F32)] * 8,
        ],
        scratch_shapes=[
            pltpu.VMEM((SEQ, 128), F32),
            pltpu.VMEM((SEQ, 128), F32),
            pltpu.VMEM((rows, 3 * d), BF16),
            pltpu.VMEM((d, 3 * d), BF16),
            pltpu.SemaphoreType.DMA,
            pltpu.VMEM((3, 2, 2, 2, narrow, shard_rows, d), BF16),
            pltpu.VMEM((4, 8, d), F32),
            pltpu.VMEM((2 + narrow, 8, d), F32),
            pltpu.SemaphoreType.DMA((2 + narrow,)),
            pltpu.SemaphoreType.DMA((2 + narrow,)),
            *scatter_scratch(SELF_CHUNKS, narrow, shard_rows, d, 3),
        ],
        name="self_back",
        compiler_params=pltpu.CompilerParams(collective_id=3, has_side_effects=True, vmem_limit_bytes=60 << 20),
        cost_estimate=cost(40 * rows * d * d, 100 << 20),
    )(
        first,
        logs,
        qkv,
        mixed,
        grad,
        normed,
        tokens,
        total,
        norms,
        norm_two,
        norm_three,
        expand_low,
        early,
        share_views(wide_share, narrow, shard_rows),
        shares.reshape(5, 2, 2, 2, narrow, shard_rows, d),
    )


def on_device(
    mesh_axes,
    tokens,
    memory,
    cotangent,
    live_length,
    pair_starts,
    source_starts,
    group_bounds,
    group_counts,
    self_query,
    self_key,
    self_value,
    self_output,
    cross_query,
    cross_key,
    cross_value,
    cross_output,
    hidden_in,
    hidden_out,
    first_gain,
    first_shift,
    second_gain,
    second_shift,
    third_gain,
    third_shift,
):
    names = tuple(axis for axis, _ in mesh_axes)
    row_count = live_length.shape[0]
    shard_rows = self_query.shape[0]
    device_count = 1
    for _, size in mesh_axes:
        device_count *= size

    def staged(*partial):
        return StagedSum(partial, mesh_axes)

    digits = jnp.stack([live_length // 256, live_length % 256], axis=1).astype(BF16)
    digits = jnp.pad(digits, ((0, shard_rows - row_count), (0, 0)))
    norms = jnp.stack([first_gain, first_shift, second_gain, second_shift, third_gain, third_shift], axis=1)
    extra = jnp.pad(jnp.concatenate([norms, digits], axis=1), ((0, 0), (0, 120)))
    weights = (self_query, self_key, self_value, self_output, cross_query, cross_key, cross_value, cross_output)
    fast = mesh_axes[0][1] == 8 and row_count == 1 and shard_rows % 32 == 0
    if fast:
        (
            early,
            later,
            late,
            normed_one,
            qkv,
            self_mixed,
            self_logs,
            norms,
            first,
            bounds,
            after_self,
            normed_two,
            cross_q,
            cross_kv,
            cross_mixed,
            cross_logs,
        ) = front(
            live_length,
            pair_starts,
            source_starts,
            weights,
            hidden_in,
            hidden_out,
            extra,
            tokens,
            memory,
            mesh_axes[1][1],
        )
        late = [late.reshape(device_count, -1, WIDTH)]
    else:
        shard = [by_pairs(self_query, self_key, self_value), extra, self_output, cross_query]
        shard += [by_pairs(cross_key, cross_value), cross_output]
        early = lax.all_gather(jnp.concatenate(shard, axis=1), names, axis=0, tiled=True)
        late = [lax.all_gather(part, names, axis=0, tiled=True) for part in (hidden_in, hidden_out)]
        early, later = early[:, : 3 * WIDTH + 128], early[:, 3 * WIDTH + 128 :]
        norms = early[:, 3 * WIDTH : 3 * WIDTH + 8].astype(F32).T
        first, bounds = row_bounds(pair_starts, source_starts, live_length)
        normed_one, qkv = project(tokens, norms, early)
        self_mixed, self_logs = self_forward(first, qkv, row_count)
        after_self, normed_two, cross_q, cross_kv = middle(self_mixed, tokens, memory, norms, later)
        cross_mixed, cross_logs = cross_forward(bounds, cross_q, cross_kv, row_count)

    device = lax.axis_index(names)
    layer_output, normed_three, activated, hidden_grad, branch_three, cross_total, branch_two, mixed_grad, norm_three = feed(
        live_length, group_bounds, group_counts, cross_mixed, after_self, cotangent, norms, later, late, mesh_axes
    )

    reduce_share, expand_share = outer_sum(activated, branch_three), outer_sum(normed_three, hidden_grad)
    if fast:
        narrow = mesh_axes[1][1]
        self_total, mixed_grad, memory_grad, norm_two, shares, reduce_shard, expand_low = cross_back(
            bounds,
            cross_logs,
            cross_q,
            cross_kv,
            cross_mixed,
            mixed_grad,
            after_self,
            cross_total,
            norms,
            branch_two,
            normed_two,
            memory,
            self_mixed,
            later,
            reduce_share,
            expand_share,
            narrow,
        )
        (
            tokens_grad,
            norm_grads,
            expand_shard,
            cross_output_shard,
            cross_query_shard,
            cross_key_shard,
            cross_value_shard,
            output_shard,
            query_shard,
            key_shard,
            value_shard,
        ) = self_back(
            first,
            self_logs,
            qkv,
            self_mixed,
            mixed_grad,
            normed_one,
            tokens,
            self_total,
            norms,
            norm_two,
            norm_three,
            expand_low,
            early,
            expand_share,
            shares,
            narrow,
        )
    else:
        reduce_sum, expand_sum = staged(reduce_share), staged(expand_share)
        cq_grad, ckv_grad = cross_backward(bounds, cross_logs, cross_q, cross_kv, cross_mixed, mixed_grad, row_count)
        cq_grad, ckv_grad = fence((cq_grad, ckv_grad), reduce_sum, expand_sum)
        cross_shares = [outer_sum(cross_mixed, branch_two), outer_sum(normed_two, cq_grad)]
        cross_shares += [outer_sum(memory, part) for part in (ckv_grad[:, :WIDTH], ckv_grad[:, WIDTH:])]
        cross_sum = staged(*cross_shares)
        self_total, branch_one, mixed_grad, memory_grad, norm_two = cross_close(
            cq_grad, ckv_grad, after_self, cross_total, norms, later
        )
        mixed_grad = fence(mixed_grad, reduce_sum, expand_sum, cross_sum)
        qkv_grad = self_backward(first, self_logs, qkv, self_mixed, mixed_grad, row_count)
        qkv_grad = fence(qkv_grad, reduce_sum, expand_sum, cross_sum)
        last_sum = staged(
            outer_sum(self_mixed, branch_one),
            *[outer_sum(normed_one, qkv_grad[:, n * WIDTH : (n + 1) * WIDTH]) for n in range(3)],
        )
        tokens_grad, norm_one = self_close(qkv_grad, tokens, self_total, norms, early)
        norm_grads = sum_everywhere(jnp.concatenate([norm_one[:2], norm_two[:2], norm_three[:2]]), mesh_axes)
        output_shard, *qkv_shards = last_sum.result().reshape(4, shard_rows, WIDTH)
        query_shard, key_shard, value_shard = from_pairs(jnp.concatenate(qkv_shards, axis=1), 3)
        reduce_shard = reduce_sum.result()
        expand_shard = expand_sum.result()
        cross_output_shard, cross_query_shard, *cross_shards = cross_sum.result().reshape(4, shard_rows, WIDTH)
        cross_key_shard, cross_value_shard = from_pairs(jnp.concatenate(cross_shards, axis=1), 2)

    norm_shards = lax.dynamic_slice_in_dim(norm_grads, device * shard_rows, shard_rows, axis=1)
    return (
        layer_output,
        tokens_grad,
        memory_grad,
        query_shard,
        key_shard,
        value_shard,
        output_shard,
        cross_query_shard,
        cross_key_shard,
        cross_value_shard,
        cross_output_shard,
        expand_shard,
        reduce_shard,
        *[norm_shards[n] for n in range(6)],
    )


def solution(mesh):
    names = ("wide", "narrow")
    mesh_axes = tuple((axis, mesh.shape[axis]) for axis in names)
    split, vector = P(names, None), P(names)
    return jax.shard_map(
        functools.partial(on_device, mesh_axes),
        mesh=mesh,
        in_specs=(split,) * 3 + (vector,) + (split,) * 2 + (P(), P()) + (split,) * 10 + (vector,) * 6,
        out_specs=(split,) * 13 + (vector,) * 6,
        check_vma=False,
    )
```

```python
import functools
import jax
import jax.numpy as jnp
from jax import lax
from jax.experimental import pallas as pl
from jax.experimental.pallas import tpu as pltpu
from jax.sharding import PartitionSpec as P

SEQ = 1024
MEM = 512
HEADS = 16
HEAD_DIM = 64
WIDTH = HEADS * HEAD_DIM
EPSILON = 1e-05
BQ = 256
LOG2E = 1.4426950408889634
SCALE2 = HEAD_DIM**-0.5 * LOG2E
FILLER = -1e30
F32, BF16 = jnp.float32, jnp.bfloat16


def mm(a, b):
    return jnp.dot(a, b, preferred_element_type=F32)


def mm_t(a, b):
    return lax.dot_general(a, b, (((1,), (1,)), ((), ())), preferred_element_type=F32)


def halves(x):
    low = lax.broadcasted_iota(jnp.int32, x.shape, 1) < HEAD_DIM
    zero = jnp.zeros_like(x)
    return (jnp.where(low, x, zero), jnp.where(low, zero, x))


def in_turn(tasks, front, back, ahead):
    waiting = []
    for task in tasks:
        waiting.append((task, front(*task)))
        if len(waiting) > ahead:
            task, held = waiting.pop(0)
            back(*task, *held)
    for task, held in waiting:
        back(*task, *held)


BLOCKS = [slice(i * BQ, (i + 1) * BQ) for i in range(SEQ // BQ)]
TASKS = [(i, h) for i in range(SEQ // BQ) for h in range(2)]


def self_extent(i):
    return (i + 1) * BQ


def cross_extent(i):
    return MEM


def self_visible(first_ref, i):
    shape = (self_extent(i), BQ)
    key = lax.broadcasted_iota(jnp.int32, shape, 0)
    return (key >= first_ref[0, :, BLOCKS[i]]) & (key <= lax.broadcasted_iota(jnp.int32, shape, 1) + i * BQ)


def cross_visible(bounds_ref, i):
    key = lax.broadcasted_iota(jnp.int32, (MEM, BQ), 0)
    return (key >= bounds_ref[0, 0:1, BLOCKS[i]]) & (key < bounds_ref[0, 1:2, BLOCKS[i]])


def attend(q_of, k, v, visible, extent, keep_out, keep_log):
    k_parts, v_t = halves(k), v.T
    outs = {}

    def front(i, h):
        s = jnp.where(visible(i), mm_t(k_parts[h][: extent(i)], q_of(BLOCKS[i])) * SCALE2, FILLER)
        return s, jnp.max(s, axis=0, keepdims=True)

    def back(i, h, s, peak):
        p = jnp.exp2(s - peak)
        total = jnp.sum(p, axis=0, keepdims=True)
        keep_log(h, BLOCKS[i], peak + jnp.log2(total))
        outs[h] = mm(v_t[h * 64 : (h + 1) * 64, : extent(i)], p.astype(BF16)) * (1.0 / total)
        if h == 1:
            keep_out(BLOCKS[i], jnp.concatenate([outs[0], outs[1]], axis=0).T.astype(BF16))

    in_turn(TASKS, front, back, 3)


def attend_back(q_of, k, v, g_ref, out_ref, log_ref, visible, extent, keep_dq, dk_ref, dv_ref):
    k_parts, k_t, v_parts = halves(k), k.T, halves(v)
    deltas, dq = {}, {}
    dk_ref[...] = jnp.zeros_like(dk_ref)
    dv_ref[...] = jnp.zeros_like(dv_ref)

    def front(i, h):
        q, g = q_of(BLOCKS[i]), g_ref[BLOCKS[i], :]
        if h == 0:
            prod = (g.astype(F32) * out_ref[BLOCKS[i], :].astype(F32)).T
            deltas[i] = [jnp.sum(prod[n * 64 : (n + 1) * 64], axis=0, keepdims=True) for n in range(2)]
        s = jnp.where(visible(i), mm_t(k_parts[h][: extent(i)], q) * SCALE2, FILLER)
        p = jnp.exp2(s - log_ref[0, 0, h : h + 1, BLOCKS[i]])
        dp = mm_t(v_parts[h][: extent(i)], g)
        return p.astype(BF16), (p * (dp - deltas[i][h])).astype(BF16)

    def back(i, h, p, ds):
        n = extent(i)
        dv_ref[:n, :] += mm(p, halves(g_ref[BLOCKS[i], :])[h])
        dk_ref[:n, :] += mm(ds, halves(q_of(BLOCKS[i]))[h])
        dq[h] = mm(k_t[h * 64 : (h + 1) * 64, :n], ds)
        if h == 1:
            keep_dq(BLOCKS[i], (jnp.concatenate([dq[0], dq[1]], axis=0) * HEAD_DIM**-0.5).T.astype(BF16))

    in_turn(TASKS, front, back, 2)


def keepers(out_ref, log_ref):
    def keep_out(rows, value):
        out_ref[rows, :] = value

    def keep_log(h, rows, value):
        log_ref[0, 0, h : h + 1, rows] = value

    return keep_out, keep_log


def self_forward_kernel(first_ref, qkv_ref, out_ref, log_ref):
    attend(
        lambda rows: qkv_ref[rows, 0:128],
        qkv_ref[:, 128:256],
        qkv_ref[:, 256:384],
        functools.partial(self_visible, first_ref),
        self_extent,
        *keepers(out_ref, log_ref),
    )


def cross_forward_kernel(bounds_ref, q_ref, kv_ref, out_ref, log_ref):
    attend(
        lambda rows: q_ref[rows, :],
        kv_ref[:, 0:128],
        kv_ref[:, 128:256],
        functools.partial(cross_visible, bounds_ref),
        cross_extent,
        *keepers(out_ref, log_ref),
    )


PAIRS = HEADS // 2
LOG_SPEC = pl.BlockSpec((1, 1, 8, SEQ), lambda r, p: (r, p, 0, 0))
ROW_SPEC = pl.BlockSpec((SEQ, 128), lambda r, p: (r, p))
QKV_SPEC = pl.BlockSpec((SEQ, 384), lambda r, p: (r, p))
KV_SPEC = pl.BlockSpec((MEM, 256), lambda r, p: (r, p))
FIRST_SPEC = pl.BlockSpec((1, 1, SEQ), lambda r, p: (r, 0, 0))
BOUNDS_SPEC = pl.BlockSpec((1, 8, SEQ), lambda r, p: (r, 0, 0))


def attention_call(kernel, name, in_specs, args, row_count):
    return pl.pallas_call(
        kernel,
        grid=(row_count, PAIRS),
        in_specs=in_specs,
        out_specs=[ROW_SPEC, LOG_SPEC],
        out_shape=[
            jax.ShapeDtypeStruct((row_count * SEQ, WIDTH), BF16),
            jax.ShapeDtypeStruct((row_count, PAIRS, 8, SEQ), F32),
        ],
        name=name,
        compiler_params=pltpu.CompilerParams(vmem_limit_bytes=40 << 20),
        cost_estimate=pl.CostEstimate(flops=20 << 30, bytes_accessed=row_count * (8 << 20), transcendentals=8 << 20),
    )(*args)


def self_forward(first, qkv, row_count):
    return attention_call(self_forward_kernel, "self_forward", [FIRST_SPEC, QKV_SPEC], (first, qkv), row_count)


def cross_forward(bounds, q, kv, row_count):
    return attention_call(
        cross_forward_kernel, "cross_forward", [BOUNDS_SPEC, ROW_SPEC, KV_SPEC], (bounds, q, kv), row_count
    )


def self_backward_kernel(first_ref, log_ref, qkv_ref, out_ref, grad_ref, dqkv_ref, dk_ref, dv_ref):
    def keep_dq(rows, value):
        dqkv_ref[rows, 0:128] = value

    attend_back(
        lambda rows: qkv_ref[rows, 0:128],
        qkv_ref[:, 128:256],
        qkv_ref[:, 256:384],
        grad_ref,
        out_ref,
        log_ref,
        functools.partial(self_visible, first_ref),
        self_extent,
        keep_dq,
        dk_ref,
        dv_ref,
    )
    dqkv_ref[:, 128:256] = (dk_ref[...] * HEAD_DIM**-0.5).astype(BF16)
    dqkv_ref[:, 256:384] = dv_ref[...].astype(BF16)


def self_backward(first, logs, qkv, out, grad, row_count):
    return pl.pallas_call(
        self_backward_kernel,
        grid=(row_count, PAIRS),
        in_specs=[FIRST_SPEC, LOG_SPEC, QKV_SPEC, ROW_SPEC, ROW_SPEC],
        out_specs=QKV_SPEC,
        scratch_shapes=[pltpu.VMEM((SEQ, 128), F32), pltpu.VMEM((SEQ, 128), F32)],
        out_shape=jax.ShapeDtypeStruct((row_count * SEQ, 3 * WIDTH), BF16),
        name="self_backward",
        compiler_params=pltpu.CompilerParams(vmem_limit_bytes=40 << 20),
        cost_estimate=pl.CostEstimate(flops=40 << 30, bytes_accessed=row_count * (16 << 20), transcendentals=8 << 20),
    )(first, logs, qkv, out, grad)


def cross_backward_pair(bounds_ref, log_ref, q_ref, kv_ref, out_ref, grad_ref, keep_dq, dkv_ref, dk_ref, dv_ref):
    attend_back(
        lambda rows: q_ref[rows, :],
        kv_ref[:, 0:128],
        kv_ref[:, 128:256],
        grad_ref,
        out_ref,
        log_ref,
        functools.partial(cross_visible, bounds_ref),
        cross_extent,
        keep_dq,
        dk_ref,
        dv_ref,
    )


def cross_backward_kernel(bounds_ref, log_ref, q_ref, kv_ref, out_ref, grad_ref, dq_ref, dkv_ref, dk_ref, dv_ref):
    def keep_dq(rows, value):
        dq_ref[rows, :] = value

    cross_backward_pair(bounds_ref, log_ref, q_ref, kv_ref, out_ref, grad_ref, keep_dq, dkv_ref, dk_ref, dv_ref)
    dkv_ref[:, 0:128] = (dk_ref[...] * HEAD_DIM**-0.5).astype(BF16)
    dkv_ref[:, 128:256] = dv_ref[...].astype(BF16)


def cross_backward(bounds, logs, q, kv, out, grad, row_count):
    return pl.pallas_call(
        cross_backward_kernel,
        grid=(row_count, PAIRS),
        in_specs=[BOUNDS_SPEC, LOG_SPEC, ROW_SPEC, KV_SPEC, ROW_SPEC, ROW_SPEC],
        out_specs=[ROW_SPEC, KV_SPEC],
        scratch_shapes=[pltpu.VMEM((MEM, 128), F32), pltpu.VMEM((MEM, 128), F32)],
        out_shape=[
            jax.ShapeDtypeStruct((row_count * SEQ, WIDTH), BF16),
            jax.ShapeDtypeStruct((row_count * MEM, 2 * WIDTH), BF16),
        ],
        name="cross_backward",
        compiler_params=pltpu.CompilerParams(vmem_limit_bytes=40 << 20),
        cost_estimate=pl.CostEstimate(flops=40 << 30, bytes_accessed=row_count * (12 << 20), transcendentals=8 << 20),
    )(bounds, logs, q, kv, out, grad)


def row_bounds(pair_starts, source_starts, live_length):
    places = jnp.arange(SEQ, dtype=jnp.int32)
    counted = jnp.sum((pair_starts[:, :, None] <= places).astype(jnp.int32), axis=1)
    live = places < live_length[:, None]
    begun = jnp.max(jnp.where(pair_starts[:, :, None] <= places, pair_starts[:, :, None], 0), axis=1)
    first = jnp.where(live, begun, live_length[:, None])
    nseg = pair_starts.shape[1]
    pick = jnp.arange(nseg)[None, :, None] == (counted - 1)[:, None, :]
    ends = jnp.concatenate([source_starts[:, 1:], jnp.full_like(source_starts[:, :1], MEM)], axis=1)
    start = jnp.sum(jnp.where(pick, source_starts[:, :, None], 0), axis=1)
    end = jnp.sum(jnp.where(pick, ends[:, :, None], 0), axis=1)
    start = jnp.where(live, start, 0)
    end = jnp.where(live, end, MEM)
    bounds = jnp.pad(jnp.stack([start, end], axis=1), ((0, 0), (0, 6), (0, 0)))
    return first[:, None, :], bounds


TB = 256


def norm_parts(values):
    center = values - jnp.mean(values, axis=-1, keepdims=True)
    inverse = lax.rsqrt(jnp.mean(center * center, axis=-1, keepdims=True) + EPSILON)
    return center * inverse, inverse


def norm_back(unit, inverse, gain, gradient):
    scaled = gradient * gain
    return inverse * (
        scaled
        - jnp.mean(scaled, axis=-1, keepdims=True)
        - unit * jnp.mean(scaled * unit, axis=-1, keepdims=True)
    )


def add_norm_grads(ref, unit, gradient):
    @pl.when(pl.program_id(0) == 0)
    def _():
        ref[...] = jnp.zeros_like(ref)

    ref[0:1, :] += jnp.sum(gradient * unit, axis=0, keepdims=True)
    ref[1:2, :] += jnp.sum(gradient, axis=0, keepdims=True)


def tile(rows, columns, at=0):
    return pl.BlockSpec((rows, columns), lambda b: (b, at))


def whole(rows, columns, at=0):
    return pl.BlockSpec((rows, columns), lambda b: (0, at), pipeline_mode=pl.Buffered(1))


def shape(rows, columns, dtype):
    return jax.ShapeDtypeStruct((rows, columns), dtype)


def params(mib):
    return pltpu.CompilerParams(vmem_limit_bytes=mib << 20)


def cost(flops, moved):
    return pl.CostEstimate(flops=int(flops), bytes_accessed=int(moved), transcendentals=0)


def project_kernel(tokens_ref, norms_ref, weight_ref, normed_ref, out_ref):
    unit, _ = norm_parts(tokens_ref[...].astype(F32))
    normed = (unit * norms_ref[0:1, :] + norms_ref[1:2, :]).astype(BF16)
    normed_ref[...] = normed
    for part in range(3):
        at = slice(part * 1024, (part + 1) * 1024)
        out_ref[:, at] = mm(normed, weight_ref[:, at]).astype(BF16)


def project(tokens, norms, early):
    rows, d = tokens.shape
    return pl.pallas_call(
        project_kernel,
        grid=(rows // TB,),
        in_specs=[tile(TB, d), whole(8, d), whole(d, 3 * d)],
        out_specs=[tile(TB, d), tile(TB, 3 * d)],
        out_shape=[shape(rows, d, BF16), shape(rows, 3 * d, BF16)],
        name="project",
        compiler_params=params(40),
        cost_estimate=cost(6 * rows * d * d, 16 << 20),
    )(tokens, norms, early)


def middle_kernel(
    mixed_ref, tokens_ref, memory_ref, norms_ref, wo_ref, wq_ref, wkv_ref, after_ref, normed_ref, q_ref, kv_ref
):
    after = tokens_ref[...].astype(F32) + mm(mixed_ref[...], wo_ref[...])
    after_ref[...] = after
    kv_ref[...] = mm(memory_ref[...], wkv_ref[...]).astype(BF16)
    unit, _ = norm_parts(after)
    normed = (unit * norms_ref[2:3, :] + norms_ref[3:4, :]).astype(BF16)
    normed_ref[...] = normed
    q_ref[...] = mm(normed, wq_ref[...]).astype(BF16)


def middle(mixed, tokens, memory, norms, early):
    rows, d = tokens.shape
    mem_rows = memory.shape[0]
    steps = rows // TB
    mb = mem_rows // steps
    return pl.pallas_call(
        middle_kernel,
        grid=(steps,),
        in_specs=[
            tile(TB, d),
            tile(TB, d),
            tile(mb, d),
            whole(8, d),
            whole(d, d, OUT_SELF),
            whole(d, d, QUERY_CROSS),
            whole(d, 2 * d, KV_CROSS),
        ],
        out_specs=[tile(TB, d), tile(TB, d), tile(TB, d), tile(mb, 2 * d)],
        out_shape=[shape(rows, d, F32), shape(rows, d, BF16), shape(rows, d, BF16), shape(mem_rows, 2 * d, BF16)],
        name="middle",
        compiler_params=params(40),
        cost_estimate=cost(6 * rows * d * d, 20 << 20),
    )(mixed, tokens, memory, norms, early, early, early)


GELU_A = 0.7978845608028654
GELU_B = 0.044715


def hidden_parts(win_ref, wout_ref, part, d):
    if len(win_ref.shape) == 2:
        at = slice(part * d, (part + 1) * d)
        return win_ref[:, at], wout_ref[at, :]
    devices, quad, _ = win_ref.shape
    rows, share = quad // 4, devices // 4
    win = win_ref[:, part * rows : (part + 1) * rows, :].reshape(d, d)
    return win, wout_ref[part * share : (part + 1) * share].reshape(d, d)


def feed_kernel(
    narrow,
    token_all,
    live_ref,
    group_bounds_ref,
    group_counts_ref,
    mixed_ref,
    before_ref,
    cot_ref,
    norms_ref,
    wo_ref,
    win_ref,
    wout_ref,
    out_ref,
    normed_ref,
    act_ref,
    hid_ref,
    b3_ref,
    total_ref,
    b2_ref,
    grad_ref,
    ngrad_ref,
    *scratch,
):
    block = pl.program_id(0)
    loads = []
    if scratch:
        late_any = win_ref
        win_ref, wout_ref, sems = scratch
        devices, quad, _ = win_ref.shape
        rows, share = quad // 4, devices // 4
        for n in range(4):
            lane, holders = pl.ds(n * rows, rows), pl.ds(n * share, share)
            loads.append(
                (
                    pltpu.make_async_copy(late_any.at[:, lane], win_ref.at[:, lane], sems.at[2 * n]),
                    pltpu.make_async_copy(
                        late_any.at[holders, pl.ds(quad, quad)], wout_ref.at[holders], sems.at[2 * n + 1]
                    ),
                )
            )

        @pl.when(block == 0)
        def _():
            for pair in loads:
                for load in pair:
                    load.start()

    per_row = SEQ // TB
    row = block // per_row
    places = lax.broadcasted_iota(jnp.int32, (TB, 1), 0) + (block % per_row) * TB
    live = (places < live_ref[row]).astype(F32)
    device = lax.axis_index("wide") * narrow + lax.axis_index("narrow")
    pair_tokens = jnp.int32(0)
    for g in range(group_counts_ref.shape[0]):
        member = (group_bounds_ref[g] <= device) & (device < group_bounds_ref[g + 1])
        pair_tokens += jnp.where(member, group_counts_ref[g], 0)
    live_total = jnp.sum(norms_ref[6:7, :], keepdims=True) * 256.0 + jnp.sum(norms_ref[7:8, :], keepdims=True)
    out_grad = cot_ref[...].astype(F32) * live * (pair_tokens.astype(F32) * (token_all / 1000.0) / live_total)
    branch = out_grad.astype(BF16)
    b3_ref[...] = branch
    after = before_ref[...] + mm(mixed_ref[...], wo_ref[...])
    unit, inverse = norm_parts(after)
    normed = (unit * norms_ref[4:5, :] + norms_ref[5:6, :]).astype(BF16)
    normed_ref[...] = normed
    d = normed.shape[1]
    result, back = after, None
    for part in range(act_ref.shape[1] // d):
        at = slice(part * d, (part + 1) * d)
        for load in loads[part] if loads else ():
            pl.when(block == 0)(load.wait)
        win, wout = hidden_parts(win_ref, wout_ref, part, d)
        x = mm(normed, win)
        square = x * x
        t = jnp.tanh(GELU_A * x * (1.0 + GELU_B * square))
        half = 0.5 * (1.0 + t)
        act = (x * half).astype(BF16)
        slope = half + (0.5 * GELU_A) * x * (1.0 - t * t) * (1.0 + (3.0 * GELU_B) * square)
        act_ref[:, at] = act
        hid = (mm_t(branch, wout) * slope).astype(BF16)
        hid_ref[:, at] = hid
        result = result + mm(act, wout)
        term = mm_t(hid, win)
        back = term if back is None else back + term
    out_ref[...] = result.astype(BF16)
    total = out_grad + norm_back(unit, inverse, norms_ref[4:5, :], back)
    total_ref[...] = total
    b2 = total.astype(BF16)
    b2_ref[...] = b2
    grad_ref[...] = mm_t(b2, wo_ref[...]).astype(BF16)
    add_norm_grads(ngrad_ref, unit, back)


def feed(live_length, group_bounds, group_counts, mixed, before, cotangent, norms, early, late, mesh_axes):
    rows, d = cotangent.shape
    (_, wide), (_, narrow) = mesh_axes
    ff = 4 * d
    if len(late) == 1:
        devices, block, _ = late[0].shape
        late = late * 2
        late_specs = [pl.BlockSpec(memory_space=pl.ANY)] * 2
        scratch = [pltpu.VMEM((devices, block // 2, d), BF16)] * 2 + [pltpu.SemaphoreType.DMA((8,))]
    else:
        late_specs, scratch = [whole(d, ff), whole(ff, d)], []
    smem = pl.BlockSpec(memory_space=pltpu.SMEM)
    return pl.pallas_call(
        functools.partial(feed_kernel, narrow, rows * wide * narrow),
        grid=(rows // TB,),
        in_specs=[
            smem,
            smem,
            smem,
            tile(TB, d),
            tile(TB, d),
            tile(TB, d),
            whole(8, d),
            whole(d, d, OUT_CROSS),
            *late_specs,
        ],
        out_specs=[
            tile(TB, d),
            tile(TB, d),
            tile(TB, ff),
            tile(TB, ff),
            tile(TB, d),
            tile(TB, d),
            tile(TB, d),
            tile(TB, d),
            whole(8, d),
        ],
        out_shape=[
            shape(rows, d, BF16),
            shape(rows, d, BF16),
            shape(rows, ff, BF16),
            shape(rows, ff, BF16),
            shape(rows, d, BF16),
            shape(rows, d, F32),
            shape(rows, d, BF16),
            shape(rows, d, BF16),
            shape(8, d, F32),
        ],
        scratch_shapes=scratch,
        name="feed",
        compiler_params=params(58),
        cost_estimate=cost(38 * rows * d * d, 50 << 20),
    )(live_length, group_bounds, group_counts, mixed, before, cotangent, norms, early, *late)


def cross_close_kernel(
    dq_ref, dkv_ref, before_ref, total_ref, norms_ref, wq_ref, wkv_ref, wo_ref, out_ref, b1_ref, grad_ref, mem_ref, ngrad_ref
):
    gradient = mm_t(dq_ref[...], wq_ref[...])
    mem_ref[...] = mm_t(dkv_ref[...], wkv_ref[...]).astype(BF16)
    unit, inverse = norm_parts(before_ref[...])
    total = total_ref[...] + norm_back(unit, inverse, norms_ref[2:3, :], gradient)
    out_ref[...] = total
    b1 = total.astype(BF16)
    b1_ref[...] = b1
    grad_ref[...] = mm_t(b1, wo_ref[...]).astype(BF16)
    add_norm_grads(ngrad_ref, unit, gradient)


def cross_close(dq, dkv, before, total, norms, early):
    rows, d = dq.shape
    mem_rows = dkv.shape[0]
    steps = rows // TB
    mb = mem_rows // steps
    return pl.pallas_call(
        cross_close_kernel,
        grid=(steps,),
        in_specs=[
            tile(TB, d),
            tile(mb, 2 * d),
            tile(TB, d),
            tile(TB, d),
            whole(8, d),
            whole(d, d, QUERY_CROSS),
            whole(d, 2 * d, KV_CROSS),
            whole(d, d, OUT_SELF),
        ],
        out_specs=[tile(TB, d), tile(TB, d), tile(TB, d), tile(mb, d), whole(8, d)],
        out_shape=[
            shape(rows, d, F32),
            shape(rows, d, BF16),
            shape(rows, d, BF16),
            shape(mem_rows, d, BF16),
            shape(8, d, F32),
        ],
        name="cross_close",
        compiler_params=params(40),
        cost_estimate=cost(6 * rows * d * d, 24 << 20),
    )(dq, dkv, before, total, norms, early, early, early)


def self_close_kernel(dqkv_ref, before_ref, total_ref, norms_ref, w_ref, out_ref, ngrad_ref):
    gradient = mm_t(dqkv_ref[...], w_ref[...])
    unit, inverse = norm_parts(before_ref[...].astype(F32))
    total = total_ref[...] + norm_back(unit, inverse, norms_ref[0:1, :], gradient)
    out_ref[...] = total.astype(BF16)
    add_norm_grads(ngrad_ref, unit, gradient)


def self_close(dqkv, before, total, norms, early):
    rows, d = total.shape
    return pl.pallas_call(
        self_close_kernel,
        grid=(rows // TB,),
        in_specs=[tile(TB, 3 * d), tile(TB, d), tile(TB, d), whole(8, d), whole(d, 3 * d)],
        out_specs=[tile(TB, d), whole(8, d)],
        out_shape=[shape(rows, d, BF16), shape(8, d, F32)],
        name="self_close",
        compiler_params=params(40),
        cost_estimate=cost(6 * rows * d * d, 20 << 20),
    )(dqkv, before, total, norms, early)


OUT_SELF, QUERY_CROSS, KV_CROSS, OUT_CROSS = 0, 1, 1, 4


def greet_all(narrow):
    w, z = lax.axis_index("wide"), lax.axis_index("narrow")
    barrier = pltpu.get_barrier_semaphore()
    others = [(w ^ 1, z), (w ^ 2, z), (w ^ 4, z)] + [(w, z ^ mask) for mask in range(1, narrow)]
    for other in others:
        pl.semaphore_signal(barrier, inc=1, device_id=other, device_id_type=pl.DeviceIdType.MESH)
    pl.semaphore_wait(barrier, len(others))


class Gather:
    def __init__(self, shard_ref, out_ref, send_sems, recv_sems, narrow):
        self.shard_ref, self.out_ref = shard_ref, out_ref
        self.send_sems, self.recv_sems = send_sems, recv_sems
        self.narrow = narrow
        self.rows = shard_ref.shape[0]
        self.half = self.rows // 2
        self.w, self.z = w, z = lax.axis_index("wide"), lax.axis_index("narrow")
        self.core, self.x, self.y, self.xy = w ^ 1, w ^ 2, w ^ 4, w ^ 6
        self.above, self.below = (w, z + 1), (w, z - 1)
        self.at_core, self.at_x, self.at_y = (self.core, z), (self.x, z), (self.y, z)
        self.up, self.down, self.to_x, self.to_y, self.on_y, self.on_x, self.to_core = [k * narrow for k in range(7)]

    def move(self, holder, s, number, target, first=0, count=None, own=False):
        count = self.rows if count is None else count
        at = pl.multiple_of((holder * self.narrow + s) * self.rows + first, self.half)
        place = self.out_ref.at[pl.ds(at, count)]
        return pltpu.make_async_remote_copy(
            src_ref=self.shard_ref.at[pl.ds(first, count)] if own else place,
            dst_ref=place,
            send_sem=self.send_sems.at[number],
            recv_sem=self.recv_sems.at[number],
            device_id=target,
            device_id_type=pl.DeviceIdType.MESH,
        )

    def own_place(self):
        return self.out_ref.at[pl.ds(pl.multiple_of((self.w * self.narrow + self.z) * self.rows, self.rows), self.rows)]

    def spread(self, s, own=False):
        self.move(self.w, s, self.to_x + s, self.at_x, own=own).start()
        self.move(self.w, s, self.to_y + s, self.at_y, own=own).start()
        self.move(self.w, s, self.to_core + s, self.at_core, own=own).start()

    def relay(self, s):
        half = self.half
        self.move(self.x, s, self.to_x + s, self.at_x).wait_recv()
        self.move(self.x, s, self.on_y + s, self.at_y, 0, half).start()
        self.move(self.x, s, self.to_core + self.narrow + s, self.at_core).start()
        self.move(self.y, s, self.to_y + s, self.at_y).wait_recv()
        self.move(self.y, s, self.on_x + s, self.at_x, half, half).start()
        self.move(self.y, s, self.to_core + 2 * self.narrow + s, self.at_core).start()

    def corner(self, s):
        self.move(self.xy, s, self.on_y + s, self.at_y, 0, self.half).wait_recv()
        self.move(self.xy, s, self.on_x + s, self.at_x, self.half, self.half).wait_recv()
        self.move(self.xy, s, self.to_core + 3 * self.narrow + s, self.at_core).start()

    def at_distance(self, r, action):
        if r == 0:
            action(self.z)
        else:
            pl.when(self.z - r >= 0)(lambda: action(self.z - r))
            pl.when(self.z + r < self.narrow)(lambda: action(self.z + r))

    def begin_line(self):
        z = self.z
        pl.when(z < self.narrow - 1)(lambda: self.move(self.w, z, self.up + z, self.above, own=True).start())
        pl.when(z > 0)(lambda: self.move(self.w, z, self.down + z, self.below, own=True).start())

    def begin_spread(self):
        self.spread(self.z, own=True)

    def round(self, r):
        z = self.z

        def from_below():
            s = z - r
            self.move(self.w, s, self.up + s, self.above).wait_recv()
            pl.when(z < self.narrow - 1)(lambda: self.move(self.w, s, self.up + s, self.above).start())
            self.spread(s)

        def from_above():
            s = z + r
            self.move(self.w, s, self.down + s, self.below).wait_recv()
            pl.when(z > 0)(lambda: self.move(self.w, s, self.down + s, self.below).start())
            self.spread(s)

        if r < self.narrow:
            pl.when(z - r >= 0)(from_below)
            pl.when(z + r < self.narrow)(from_above)
        self.at_distance(r - 1, self.relay)

    def corners(self):
        for r in range(self.narrow):
            self.at_distance(r, self.corner)

    def arrive(self):
        for s in range(self.narrow):
            for k, holder in enumerate((self.w, self.x, self.y, self.xy)):
                self.move(holder ^ 1, s, self.to_core + k * self.narrow + s, self.at_core).wait_recv()

    def close(self):
        z, half = self.z, self.half
        for s in range(self.narrow):
            up, down = self.move(self.w, s, self.up + s, self.above), self.move(self.w, s, self.down + s, self.below)
            pl.when((s <= z) & (z < self.narrow - 1))(up.wait_send)
            pl.when((s >= z) & (z > 0))(down.wait_send)
            self.move(self.w, s, self.to_x + s, self.at_x).wait_send()
            self.move(self.w, s, self.to_y + s, self.at_y).wait_send()
            self.move(self.x, s, self.on_y + s, self.at_y, 0, half).wait_send()
            self.move(self.y, s, self.on_x + s, self.at_x, half, half).wait_send()
            for k, holder in enumerate((self.w, self.x, self.y, self.xy)):
                self.move(holder, s, self.to_core + k * self.narrow + s, self.at_core).wait_send()


def place_bounds(live_ref, pairs_ref, sources_ref, first_ref, bounds_ref):
    place = lax.broadcasted_iota(jnp.int32, (1, SEQ), 1)
    live = place < live_ref[0]
    count = pairs_ref.shape[1]
    first, start, end = jnp.zeros_like(place), jnp.zeros_like(place), jnp.zeros_like(place)
    for n in range(count):
        begun = place >= pairs_ref[0, n]
        first = jnp.where(begun, pairs_ref[0, n], first)
        start = jnp.where(begun, sources_ref[0, n], start)
        end = jnp.where(begun, sources_ref[0, n + 1] if n + 1 < count else MEM, end)
    first_ref[0] = jnp.where(live, first, live_ref[0])
    bounds_ref[0, 0:1, :] = jnp.where(live, start, 0)
    bounds_ref[0, 1:2, :] = jnp.where(live, end, MEM)
    bounds_ref[0, 2:8, :] = jnp.zeros((6, SEQ), jnp.int32)


def front_kernel(
    narrow,
    live_ref,
    pairs_ref,
    sources_ref,
    wq_ref,
    wk_ref,
    wv_ref,
    ck_ref,
    cv_ref,
    others_refs,
    hidden_in_ref,
    hidden_out_ref,
    extra_ref,
    tokens_ref,
    memory_ref,
    wide_any,
    later_any,
    late_any,
    normed_any,
    qkv_any,
    mixed_ref,
    log_ref,
    norms_ref,
    first_ref,
    bounds_ref,
    after_ref,
    normed_two_ref,
    cross_q_ref,
    cross_kv_ref,
    cross_mixed_ref,
    cross_log_ref,
    shard_a,
    shard_b,
    shard_c,
    weight,
    later,
    normed,
    qkv,
    a_send,
    a_recv,
    b_send,
    b_recv,
    c_send,
    c_recv,
    local_sems,
):
    d = tokens_ref.shape[1]
    rows = wq_ref.shape[0]
    for p in range(PAIRS):
        lanes = slice(p * 128, (p + 1) * 128)
        for n, ref in enumerate((wq_ref, wk_ref, wv_ref)):
            shard_a[:, (3 * p + n) * 128 : (3 * p + n + 1) * 128] = ref[:, lanes]
        for n, ref in enumerate((ck_ref, cv_ref)):
            at = KV_CROSS * 2 * d + (2 * p + n) * 128
            shard_b[:, at : at + 128] = ref[:, lanes]
    shard_a[:, 3 * d :] = extra_ref[...]

    one = Gather(shard_a, weight, a_send, a_recv, narrow)
    two = Gather(shard_b, later, b_send, b_recv, narrow)
    three = Gather(shard_c, late_any, c_send, c_recv, narrow)
    keeps = [
        pltpu.make_async_copy(gather.shard_ref, gather.own_place(), local_sems.at[n])
        for n, gather in enumerate((one, two, three))
    ]
    greet_all(narrow)
    one.begin_line()
    one.begin_spread()
    keeps[0].start()
    for at, ref in zip((OUT_SELF, QUERY_CROSS, OUT_CROSS), others_refs):
        shard_b[:, at * d : (at + 1) * d] = ref[...]
    for n in range(4):
        shard_c[n * rows : (n + 1) * rows, :] = hidden_in_ref[:, n * d : (n + 1) * d]
    shard_c[4 * rows :, :] = hidden_out_ref[...]
    keeps[1].start()
    keeps[2].start()
    place_bounds(live_ref, pairs_ref, sources_ref, first_ref, bounds_ref)
    one.round(1)
    one.round(2)
    two.begin_line()
    for r in range(3, narrow + 1):
        one.round(r)
    two.begin_spread()
    one.corners()
    one.arrive()
    keeps[0].wait()
    out_wide = pltpu.make_async_copy(weight, wide_any, local_sems.at[3])
    out_wide.start()

    norms_ref[...] = weight[:, 3 * d :].astype(F32).T[0:8, :]

    def project_block(t, carry):
        at = pl.ds(pl.multiple_of(t * TB, TB), TB)
        unit, _ = norm_parts(tokens_ref[at, :].astype(F32))
        value = (unit * norms_ref[0:1, :] + norms_ref[1:2, :]).astype(BF16)
        normed[at, :] = value
        for part in range(3):
            lanes = slice(part * d, (part + 1) * d)
            qkv[at, lanes] = mm(value, weight[:, lanes]).astype(BF16)
        return carry

    def pair_block(p, carry):
        def lanes(n):
            return pl.ds(pl.multiple_of(p * 384 + n * 128, 128), 128)

        attend(
            lambda at: qkv[at, lanes(0)],
            qkv[:, lanes(1)],
            qkv[:, lanes(2)],
            functools.partial(self_visible, first_ref),
            self_extent,
            *pair_keepers(mixed_ref, log_ref, p),
        )
        return carry

    def middle_block(t, carry):
        at = pl.ds(pl.multiple_of(t * TB, TB), TB)
        mb = memory_ref.shape[0] * TB // tokens_ref.shape[0]
        mem_at = pl.ds(pl.multiple_of(t * mb, mb), mb)
        after = tokens_ref[at, :].astype(F32) + mm(mixed_ref[at, :], later[:, OUT_SELF * d : (OUT_SELF + 1) * d])
        after_ref[at, :] = after
        for n in range(2):
            lanes = slice((2 * KV_CROSS + n) * d, (2 * KV_CROSS + n + 1) * d)
            cross_kv_ref[mem_at, n * d : (n + 1) * d] = mm(memory_ref[mem_at, :], later[:, lanes]).astype(BF16)
        unit, _ = norm_parts(after)
        value = (unit * norms_ref[2:3, :] + norms_ref[3:4, :]).astype(BF16)
        normed_two_ref[at, :] = value
        cross_q_ref[at, :] = mm(value, later[:, QUERY_CROSS * d : (QUERY_CROSS + 1) * d]).astype(BF16)
        return carry

    def cross_block(p, carry):
        def lanes(n):
            return pl.ds(pl.multiple_of(p * 256 + n * 128, 128), 128)

        q_lanes = pl.ds(pl.multiple_of(p * 128, 128), 128)
        attend(
            lambda at: cross_q_ref[at, q_lanes],
            cross_kv_ref[:, lanes(0)],
            cross_kv_ref[:, lanes(1)],
            functools.partial(cross_visible, bounds_ref),
            cross_extent,
            *pair_keepers(cross_mixed_ref, cross_log_ref, p),
        )
        return carry

    lax.fori_loop(0, 4, project_block, 0)
    out_normed = pltpu.make_async_copy(normed, normed_any, local_sems.at[4])
    out_qkv = pltpu.make_async_copy(qkv, qkv_any, local_sems.at[5])
    out_normed.start()
    out_qkv.start()
    two.round(1)
    lax.fori_loop(0, 2, pair_block, 0)
    two.round(2)
    lax.fori_loop(2, 5, pair_block, 0)
    for r in range(3, narrow):
        two.round(r)
    three.begin_line()
    lax.fori_loop(5, 8, pair_block, 0)
    two.round(narrow)
    three.begin_spread()
    two.corners()
    two.arrive()
    keeps[1].wait()
    out_later = pltpu.make_async_copy(later, later_any, local_sems.at[6])
    out_later.start()
    three.round(1)
    lax.fori_loop(0, 4, middle_block, 0)
    three.round(2)
    lax.fori_loop(0, 4, cross_block, 0)
    for r in range(3, narrow):
        three.round(r)
    lax.fori_loop(4, 8, cross_block, 0)
    three.round(narrow)
    three.corners()
    three.arrive()
    keeps[2].wait()
    for gather in (one, two, three):
        gather.close()
    for copy in (out_wide, out_normed, out_qkv, out_later):
        copy.wait()


def pair_keepers(out_ref, log_ref, p):
    def keep_out(at, value):
        out_ref[at, pl.ds(pl.multiple_of(p * 128, 128), 128)] = value

    def keep_log(h, at, value):
        log_ref[0, p, h : h + 1, at] = value

    return keep_out, keep_log


def front(live_length, pair_starts, source_starts, weights, hidden_in, hidden_out, extra, tokens, memory, narrow):
    self_query, self_key, self_value, self_output, cross_query, cross_key, cross_value, cross_output = weights
    shard_rows, d = self_query.shape
    rows, mem_rows = tokens.shape[0], memory.shape[0]
    block = 4 * shard_rows + hidden_out.shape[0]
    anywhere, vmem = pl.BlockSpec(memory_space=pl.ANY), pl.BlockSpec(memory_space=pltpu.VMEM)
    smem = pl.BlockSpec(memory_space=pltpu.SMEM)
    logs = jax.ShapeDtypeStruct((1, PAIRS, 8, SEQ), F32)

    def kernel(*refs):
        front_kernel(narrow, *refs[:8], refs[8:11], *refs[11:])

    return pl.pallas_call(
        kernel,
        in_specs=[smem] * 3 + [vmem] * 13,
        out_specs=[anywhere] * 5 + [vmem] * 11,
        out_shape=[
            shape(d, 3 * d + 128, BF16),
            shape(d, 5 * d, BF16),
            shape(8 * narrow * block, d, BF16),
            shape(rows, d, BF16),
            shape(rows, 3 * d, BF16),
            shape(rows, d, BF16),
            logs,
            shape(8, d, F32),
            jax.ShapeDtypeStruct((1, 1, SEQ), jnp.int32),
            jax.ShapeDtypeStruct((1, 8, SEQ), jnp.int32),
            shape(rows, d, F32),
            shape(rows, d, BF16),
            shape(rows, d, BF16),
            shape(mem_rows, 2 * d, BF16),
            shape(rows, d, BF16),
            logs,
        ],
        scratch_shapes=[
            pltpu.VMEM((shard_rows, 3 * d + 128), BF16),
            pltpu.VMEM((shard_rows, 5 * d), BF16),
            pltpu.VMEM((block, d), BF16),
            pltpu.VMEM((d, 3 * d + 128), BF16),
            pltpu.VMEM((d, 5 * d), BF16),
            pltpu.VMEM((rows, d), BF16),
            pltpu.VMEM((rows, 3 * d), BF16),
            *[pltpu.SemaphoreType.DMA((10 * narrow,))] * 6,
            pltpu.SemaphoreType.DMA((7,)),
        ],
        name="front",
        compiler_params=pltpu.CompilerParams(collective_id=0, has_side_effects=True, vmem_limit_bytes=60 << 20),
        cost_estimate=cost(30 * rows * d * d, 200 << 20),
    )(
        live_length,
        pair_starts,
        source_starts,
        self_query,
        self_key,
        self_value,
        cross_key,
        cross_value,
        self_output,
        cross_query,
        cross_output,
        hidden_in,
        hidden_out,
        extra,
        tokens,
        memory,
    )


def stages_of(mesh_axes):
    plan = []
    for axis, size in mesh_axes:
        bits = size.bit_length() - 1
        at = 0
        while at < bits:
            take = 1 if (bits - at) % 2 else 2
            plan.append((axis, at, take))
            at += take
    return plan


def trade(value, axis, size, mask):
    return lax.ppermute(value, axis, [(i, i ^ mask) for i in range(size)])


def digit_of(axis, at, take):
    return (lax.axis_index(axis) >> at) & ((1 << take) - 1)


def pick(value, digit, place):
    if isinstance(value, list):
        return jnp.concatenate([pick(v, digit, place) for v in value], axis=0)
    return lax.dynamic_index_in_dim(value, digit, place, keepdims=False)


def add_up(own, pieces):
    total = own.astype(F32)
    for piece in pieces:
        total = total + piece.astype(F32)
    return total


def sum_steps(partial, mesh_axes):
    sizes = dict(mesh_axes)
    plan = stages_of(mesh_axes)
    groups = []
    for axis, _ in mesh_axes:
        groups += sorted((s for s in plan if s[0] == axis), key=lambda s: -s[1])
    devices = 1
    for _, size in mesh_axes:
        devices *= size
    columns = partial[0].shape[1]
    extents = [1 << s[2] for s in groups]
    value = [p.reshape(p.shape[0] // WIDTH, *extents, -1, columns) for p in partial]
    for number, stage in enumerate(plan):
        axis, at, take = stage
        place = 1 + groups.index(stage)
        groups.remove(stage)
        if axis == "wide" and take == 2:
            if isinstance(value, list):
                value = jnp.concatenate(value, axis=0)
            split = value.reshape(*value.shape[:place], 2, 2, *value.shape[place + 1 :])
            a, b = split[..., : columns // 2], split[..., columns // 2 :]
            low, high = digit_of(axis, at, 1), digit_of(axis, at + 1, 1)
            step = ((high, place, 2 << at), (low, place + 1, 1 << at))
            for (digit_a, place_a, mask_a), (digit_b, place_b, mask_b) in (
                step,
                ((low, place, 1 << at), (high, place, 2 << at)),
            ):
                pieces = yield [
                    trade(pick(a, digit_a ^ 1, place_a), axis, sizes[axis], mask_a),
                    trade(pick(b, digit_b ^ 1, place_b), axis, sizes[axis], mask_b),
                ]
                a = add_up(pick(a, digit_a, place_a), pieces[:1]).astype(BF16)
                b = add_up(pick(b, digit_b, place_b), pieces[1:]).astype(BF16)
            value = jnp.concatenate([a, b], axis=-1)
            continue
        digit = digit_of(axis, at, take)
        pieces = yield [
            trade(pick(value, digit ^ mask, place), axis, sizes[axis], mask << at) for mask in range(1, 1 << take)
        ]
        value = add_up(pick(value, digit, place), pieces)
        if number < len(plan) - 1:
            value = value.astype(BF16)
    return value.astype(F32).reshape(-1, columns)


class StagedSum:
    def __init__(self, partial, mesh_axes):
        self.steps = sum_steps(partial, mesh_axes)
        self.under_way = next(self.steps)
        self.value = None

    def go_on(self, pieces):
        try:
            self.under_way = self.steps.send(pieces)
        except StopIteration as stop:
            self.under_way, self.value = None, stop.value

    def result(self):
        while self.under_way is not None:
            self.go_on(self.under_way)
        return self.value


def fence(value, *sums):
    held = [s for s in sums if s.under_way is not None]
    value, arrived = lax.optimization_barrier((value, [s.under_way for s in held]))
    for s, pieces in zip(held, arrived):
        s.go_on(pieces)
    return value


def sum_everywhere(value, mesh_axes):
    sizes = dict(mesh_axes)
    for axis, at, take in stages_of(mesh_axes):
        arrived = [trade(value, axis, sizes[axis], mask << at) for mask in range(1, 1 << take)]
        for piece in arrived:
            value = value + piece
    return value


def by_pairs(*parts):
    rows = parts[0].shape[0]
    return jnp.stack([p.reshape(rows, -1, 128) for p in parts], axis=2).reshape(rows, -1)


def from_pairs(value, count):
    rows = value.shape[0]
    split = value.reshape(rows, -1, count, 128)
    return [split[:, :, c].reshape(rows, -1) for c in range(count)]


def outer_sum(left_side, gradient):
    return jnp.einsum("td,te->de", left_side, gradient, preferred_element_type=F32).astype(BF16)


CHUNKS = 4


class Scatter:
    def __init__(self, own, theirs, buffers, keep, send_sems, recv_sems, narrow):
        self.own, self.theirs, self.keep = own, theirs, keep
        self.from_core, self.a1, self.b1, self.a2, self.b2, self.from_line = buffers
        self.send_sems, self.recv_sems = send_sems, recv_sems
        self.narrow = narrow
        self.slots = own.shape[0]
        self.half = self.a1.shape[-1]
        self.w, self.z = lax.axis_index("wide"), lax.axis_index("narrow")
        self.c, self.x, self.y = self.w & 1, (self.w >> 1) & 1, (self.w >> 2) & 1
        self.per_chunk = 4 + narrow

    def move(self, i, number, src, dst, target):
        at = i * self.per_chunk + number
        return pltpu.make_async_remote_copy(
            src_ref=src,
            dst_ref=dst,
            send_sem=self.send_sems.at[at],
            recv_sem=self.recv_sems.at[at],
            device_id=target,
            device_id_type=pl.DeviceIdType.MESH,
        )

    def to_core(self, i):
        return self.move(i, 0, self.theirs(i), self.from_core.at[i % self.slots], (self.w ^ 1, self.z))

    def first(self, i):
        left, right = pl.ds(0, self.half), pl.ds(self.half, self.half)
        to_x, to_y = (self.w ^ 2, self.z), (self.w ^ 4, self.z)
        return (
            self.move(i, 1, self.own.at[i % self.slots, :, 1 - self.x, :, :, left], self.a1.at[i % self.slots], to_x),
            self.move(i, 2, self.own.at[i % self.slots, 1 - self.y, :, :, :, right], self.b1.at[i % self.slots], to_y),
        )

    def second(self, i):
        left, right = pl.ds(0, self.half), pl.ds(self.half, self.half)
        to_x, to_y = (self.w ^ 2, self.z), (self.w ^ 4, self.z)
        return (
            self.move(i, 3, self.own.at[i % self.slots, 1 - self.y, self.x, :, :, left], self.a2.at[i % self.slots], to_y),
            self.move(i, 4, self.own.at[i % self.slots, self.y, 1 - self.x, :, :, right], self.b2.at[i % self.slots], to_x),
        )

    def along(self, i):
        return [
            self.move(
                i,
                4 + mask,
                self.own.at[i % self.slots, self.y, self.x, self.z ^ mask],
                self.from_line.at[i % self.slots, mask - 1],
                (self.w, self.z ^ mask),
            )
            for mask in range(1, self.narrow)
        ]

    def begin(self, i):
        self.to_core(i).start()

    def add(self, i, y, x, columns, piece):
        now = self.own[i % self.slots, y, x, :, :, columns]
        self.own[i % self.slots, y, x, :, :, columns] = now + piece

    def step(self, i, stage):
        both, left, right = slice(None), slice(0, self.half), slice(self.half, None)
        if stage == 0:
            self.to_core(i).wait_recv()
            for a in range(2):
                for b in range(2):
                    self.add(i, a, b, both, self.from_core[i % self.slots, a, b])
            for copy in self.first(i):
                copy.start()
        elif stage == 1:
            for copy in self.first(i):
                copy.wait_recv()
            for a in range(2):
                self.add(i, a, self.x, left, self.a1[i % self.slots, a])
                self.add(i, self.y, a, right, self.b1[i % self.slots, a])
            for copy in self.second(i):
                copy.start()
        elif stage == 2:
            for copy in self.second(i):
                copy.wait_recv()
            self.add(i, self.y, self.x, left, self.a2[i % self.slots])
            self.add(i, self.y, self.x, right, self.b2[i % self.slots])
            for copy in self.along(i):
                copy.start()
        else:
            for copy in self.along(i):
                copy.wait_recv()
            total = self.own[i % self.slots, self.y, self.x, self.z].astype(F32)
            for mask in range(1, self.narrow):
                total = total + self.from_line[i % self.slots, mask - 1].astype(F32)
            self.keep(i, total)

    def close(self, i):
        for copy in (self.to_core(i), *self.first(i), *self.second(i), *self.along(i)):
            copy.wait_send()


def scatter_scratch(chunks, narrow, rows, width, more=0):
    copies = (chunks + more) * (4 + narrow)
    return [
        pltpu.VMEM((chunks, 2, 2, narrow, rows, width), BF16),
        pltpu.VMEM((chunks, 2, 2, narrow, rows, width), BF16),
        pltpu.VMEM((chunks, 2, narrow, rows, width // 2), BF16),
        pltpu.VMEM((chunks, 2, narrow, rows, width // 2), BF16),
        pltpu.VMEM((chunks, narrow, rows, width // 2), BF16),
        pltpu.VMEM((chunks, narrow, rows, width // 2), BF16),
        pltpu.VMEM((chunks, narrow - 1, rows, width), BF16),
        pltpu.SemaphoreType.DMA((copies,)),
        pltpu.SemaphoreType.DMA((copies,)),
        pltpu.SemaphoreType.DMA((chunks + more,)),
    ]


class Carried:
    def __init__(self, shares, scratch, keep, narrow):
        own, *buffers, send_sems, recv_sems, self.load_sems = scratch
        self.shares = shares
        self.scatter = Scatter(own, self.other, buffers, keep, send_sems, recv_sems, narrow)
        self.chunks, self.slots = len(shares), own.shape[0]

    def other(self, i):
        return self.shares[i](1 - self.scatter.c)

    def load(self, i):
        return pltpu.make_async_copy(
            self.shares[i](self.scatter.c), self.scatter.own.at[i % self.slots], self.load_sems.at[i]
        )

    def open(self):
        for i in range(self.slots):
            self.load(i).start()
        greet_all(self.scatter.narrow)
        for i in range(2):
            self.scatter.begin(i)

    def reuse(self, i):
        self.scatter.close(i - self.slots)
        self.load(i).start()
        self.scatter.begin(i)

    def steps(self, plan):
        for i, stage in plan:
            if stage == 0:
                self.load(i).wait()
            self.scatter.step(i, stage)
            if stage == 0 and i + 2 < self.slots:
                self.scatter.begin(i + 2)

    def close(self):
        for i in range(self.chunks - self.slots, self.chunks):
            self.scatter.close(i)


def share_views(array, narrow, rows):
    return array.reshape(2, 2, 2, narrow, rows, array.shape[1])


def share_views(array, narrow, rows):
    return array.reshape(2, 2, 2, narrow, rows, array.shape[1])


def columns_of(ref, at, width):
    return lambda core: ref.at[:, :, core, :, :, pl.ds(at, width)]


def tn(a, b):
    return lax.dot_general(a, b, (((0,), (0,)), ((), ())), preferred_element_type=F32)


def outer_into(out_ref, left_ref, right):
    for at in range(0, left_ref.shape[1], 256):
        out_ref[at : at + 256, :] = tn(left_ref[:, at : at + 256], right).astype(BF16)


CROSS_PLAN = (
    ((0, 0),),
    ((1, 0),),
    (),
    ((0, 1), (1, 1)),
    ((2, 0), (3, 0)),
    ((1, 2),),
    ((0, 2),),
    ((2, 1), (4, 0)),
    ((1, 3),),
    ((2, 2), (3, 1), (4, 1)),
    ((3, 2), (5, 0)),
    ((4, 2),),
    ((5, 1),),
    ((5, 2),),
    ((0, 3),),
    (),
    ((2, 3), (3, 3), (4, 3), (5, 3)),
)
CROSS_WIDE = 2


def cross_back_kernel(
    narrow,
    bounds_ref,
    log_ref,
    q_ref,
    kv_ref,
    mixed_pair_ref,
    grad_ref,
    before_ref,
    total_ref,
    norms_ref,
    mixed_any,
    b2_any,
    normed_any,
    memory_any,
    self_mixed_any,
    early_any,
    share_any,
    wide_any,
    out_ref,
    next_ref,
    mem_ref,
    ngrad_ref,
    shares_ref,
    shard_ref,
    wide_ref,
    dk_ref,
    dv_ref,
    dq_ref,
    dkv_ref,
    b1_ref,
    wq,
    wkv,
    wo,
    weight_sems,
    mixed_ref,
    b2_ref,
    normed_ref,
    memory_ref,
    self_mixed_ref,
    *scratch,
):
    step = pl.program_id(0)
    d = wq.shape[0]
    rows = shard_ref.shape[0] // 4

    def keep(i, value):
        if i < 4:
            shard_ref[i * rows : (i + 1) * rows, :] = value
        else:
            wide_ref[:, (i - 4) * d : (i - 3) * d] = value

    def piece(i):
        return lambda core: share_any.at[:, :, core, :, i]

    pieces = [piece(i) for i in range(4)] + [columns_of(wide_any, i * d, d) for i in range(CROSS_WIDE)]
    carried = Carried(pieces, scratch, keep, narrow)
    loads = [
        pltpu.make_async_copy(early_any.at[:, pl.ds(QUERY_CROSS * d, d)], wq, weight_sems.at[0]),
        pltpu.make_async_copy(early_any.at[:, pl.ds(2 * KV_CROSS * d, 2 * d)], wkv, weight_sems.at[1]),
        pltpu.make_async_copy(early_any.at[:, pl.ds(OUT_SELF * d, d)], wo, weight_sems.at[2]),
    ]
    later_loads = [
        pltpu.make_async_copy(source, target, weight_sems.at[3 + n])
        for n, (source, target) in enumerate(
            (
                (mixed_any, mixed_ref),
                (b2_any, b2_ref),
                (normed_any, normed_ref),
                (memory_any, memory_ref),
                (self_mixed_any, self_mixed_ref),
            )
        )
    ]

    @pl.when(step == 0)
    def _():
        carried.open()
        for load in loads + later_loads:
            load.start()

    @pl.when(step < PAIRS)
    def _():
        def keep_dq(rows, value):
            dq_ref[rows, pl.ds(pl.multiple_of(step * 128, 128), 128)] = value

        cross_backward_pair(bounds_ref, log_ref, q_ref, kv_ref, mixed_pair_ref, grad_ref, keep_dq, None, dk_ref, dv_ref)
        at = pl.multiple_of(step * 256, 256)
        dkv_ref[:, pl.ds(at, 128)] = (dk_ref[...] * HEAD_DIM**-0.5).astype(BF16)
        dkv_ref[:, pl.ds(pl.multiple_of(at + 128, 128), 128)] = dv_ref[...].astype(BF16)

    @pl.when(step == PAIRS)
    def _():
        for load in loads:
            load.wait()
        ngrad_ref[...] = jnp.zeros_like(ngrad_ref)

    tokens_end = PAIRS + SEQ // TB

    @pl.when((step >= PAIRS) & (step < tokens_end))
    def _():
        t = step - PAIRS
        mb = mem_ref.shape[0]
        at = pl.ds(pl.multiple_of(t * TB, TB), TB)
        gradient = mm_t(dq_ref[at, :], wq[...])
        mem_ref[...] = mm_t(dkv_ref[pl.ds(pl.multiple_of(t * mb, mb), mb), :], wkv[...]).astype(BF16)
        unit, inverse = norm_parts(before_ref[...])
        total = total_ref[...] + norm_back(unit, inverse, norms_ref[2:3, :], gradient)
        out_ref[...] = total
        b1 = total.astype(BF16)
        b1_ref[at, :] = b1
        next_ref[...] = mm_t(b1, wo[...]).astype(BF16)
        ngrad_ref[0:1, :] += jnp.sum(gradient * unit, axis=0, keepdims=True)
        ngrad_ref[1:2, :] += jnp.sum(gradient, axis=0, keepdims=True)

    @pl.when(step == tokens_end)
    def _():
        for load in later_loads:
            load.wait()
        outer_into(shares_ref, mixed_ref, b2_ref[...])

    pl.when(step == tokens_end + 1)(lambda: outer_into(shares_ref, normed_ref, dq_ref[...]))
    pl.when(step == tokens_end + 2)(lambda: outer_into(shares_ref, memory_ref, dkv_ref[:, :d]))
    pl.when(step == tokens_end + 3)(lambda: outer_into(shares_ref, memory_ref, dkv_ref[:, d:]))
    pl.when(step == tokens_end + 4)(lambda: outer_into(shares_ref, self_mixed_ref, b1_ref[...]))

    for number, plan in enumerate(CROSS_PLAN):
        pl.when(step == number)(functools.partial(carried.steps, plan))
    pl.when(step == len(CROSS_PLAN) - 1)(carried.close)


def cross_back(bounds, logs, q, kv, mixed, grad, before, total, norms, b2, normed, memory, self_mixed, early, share, wide_share, narrow):
    rows, d = q.shape
    mem_rows = kv.shape[0]
    shard_rows = d // (8 * narrow)
    steps = rows // TB
    mb = mem_rows // steps

    def pair(s):
        return jnp.minimum(s, PAIRS - 1)

    def token(s):
        return jnp.clip(s - PAIRS, 0, steps - 1)

    anywhere = pl.BlockSpec(memory_space=pl.ANY)
    by_pair = pl.BlockSpec((SEQ, 128), lambda s: (0, pair(s)))
    by_token = pl.BlockSpec((TB, d), lambda s: (token(s), 0))
    return pl.pallas_call(
        functools.partial(cross_back_kernel, narrow),
        grid=(PAIRS + steps + 5,),
        in_specs=[
            pl.BlockSpec((1, 8, SEQ), lambda s: (0, 0, 0)),
            pl.BlockSpec((1, 1, 8, SEQ), lambda s: (0, pair(s), 0, 0)),
            by_pair,
            pl.BlockSpec((MEM, 256), lambda s: (0, pair(s))),
            by_pair,
            by_pair,
            by_token,
            by_token,
            whole(8, d),
            *[anywhere] * 5,
            anywhere,
            anywhere,
            anywhere,
        ],
        out_specs=[
            by_token,
            by_token,
            pl.BlockSpec((mb, d), lambda s: (token(s), 0)),
            whole(8, d),
            pl.BlockSpec((d, d), lambda s: (jnp.maximum(s - PAIRS - steps, 0), 0)),
            whole(4 * shard_rows, d),
            whole(shard_rows, CROSS_WIDE * d),
        ],
        out_shape=[
            shape(rows, d, F32),
            shape(rows, d, BF16),
            shape(mem_rows, d, BF16),
            shape(8, d, F32),
            shape(5 * d, d, BF16),
            shape(4 * shard_rows, d, F32),
            shape(shard_rows, CROSS_WIDE * d, F32),
        ],
        scratch_shapes=[
            pltpu.VMEM((MEM, 128), F32),
            pltpu.VMEM((MEM, 128), F32),
            pltpu.VMEM((rows, d), BF16),
            pltpu.VMEM((mem_rows, 2 * d), BF16),
            pltpu.VMEM((rows, d), BF16),
            pltpu.VMEM((d, d), BF16),
            pltpu.VMEM((d, 2 * d), BF16),
            pltpu.VMEM((d, d), BF16),
            pltpu.SemaphoreType.DMA((8,)),
            pltpu.VMEM((rows, d), BF16),
            pltpu.VMEM((rows, d), BF16),
            pltpu.VMEM((rows, d), BF16),
            pltpu.VMEM((mem_rows, d), BF16),
            pltpu.VMEM((rows, d), BF16),
            *scatter_scratch(4 + CROSS_WIDE, narrow, shard_rows, d),
        ],
        name="cross_back",
        compiler_params=pltpu.CompilerParams(collective_id=2, has_side_effects=True, vmem_limit_bytes=60 << 20),
        cost_estimate=cost(40 * rows * d * d, 100 << 20),
    )(
        bounds,
        logs,
        q,
        kv,
        mixed,
        grad,
        before,
        total,
        norms,
        mixed,
        b2,
        normed,
        memory,
        self_mixed,
        early,
        share.reshape(2, 2, 2, narrow, 4, shard_rows, d),
        share_views(wide_share, narrow, shard_rows),
    )


SELF_PLAN = (
    ((0, 0),),
    ((1, 0),),
    ((2, 0),),
    ((0, 1), (2, 1), (3, 0), (4, 0)),
    ((1, 1),),
    ((0, 2), (2, 2)),
    ((3, 1), (5, 0)),
    ((4, 1), (6, 0)),
    ((0, 3), (2, 3), (1, 2), (3, 2), (5, 1)),
    ((1, 3),),
    ((3, 3), (4, 2), (6, 1), (7, 0)),
    ((8, 0),),
    ((5, 2), (5, 3), (6, 2), (7, 1), (8, 1), (9, 0)),
    ((7, 2), (8, 2), (9, 1), (9, 2)),
    ((4, 3), (6, 3), (7, 3), (8, 3), (9, 3)),
)
SELF_REUSE = {9: 7, 10: 8, 11: 9}
SELF_WIDE = 4 - CROSS_WIDE
SELF_CHUNKS = SELF_WIDE + 5


def self_back_kernel(
    narrow,
    first_ref,
    log_ref,
    qkv_ref,
    mixed_ref,
    grad_ref,
    normed_ref,
    tokens_ref,
    total_ref,
    norms_ref,
    norm_two_ref,
    norm_three_ref,
    expand_low_ref,
    early_any,
    wide_any,
    shares_any,
    out_ref,
    norm_out_ref,
    expand_ref,
    cross_output_ref,
    cross_query_ref,
    cross_key_ref,
    cross_value_ref,
    self_output_ref,
    query_ref,
    key_ref,
    value_ref,
    dk_ref,
    dv_ref,
    dqkv,
    weight,
    weight_sem,
    stage,
    nval,
    nin,
    norm_send_sems,
    norm_recv_sems,
    *scratch,
):
    step = pl.program_id(0)
    d = normed_ref.shape[1]

    outs = (query_ref, key_ref, value_ref)

    def keep(i, value):
        i -= SELF_WIDE
        if i < 0:
            expand_ref[:, (i + 4) * d : (i + 5) * d] = value
        elif i == 0:
            cross_output_ref[...] = value
        elif i == 1:
            cross_query_ref[...] = value
        elif i == 4:
            self_output_ref[...] = value
        elif i > 4:
            for n in range(d // 128):
                pair, kind = divmod((i - 5) * d // 128 + n, 3)
                outs[kind][:, pair * 128 : (pair + 1) * 128] = value[:, n * 128 : (n + 1) * 128]
        else:
            for n in range(d // 256):
                at = (i - 2) * d // 2 + n * 128
                cross_key_ref[:, at : at + 128] = value[:, n * 256 : n * 256 + 128]
                cross_value_ref[:, at : at + 128] = value[:, n * 256 + 128 : n * 256 + 256]

    def piece(i):
        return lambda core: shares_any.at[i, :, :, core]

    def staged_piece(i):
        return lambda core: stage.at[i, :, :, core]

    pieces = [columns_of(wide_any, (CROSS_WIDE + i) * d, d) for i in range(SELF_WIDE)] + [piece(i) for i in range(5)]
    pieces += [staged_piece(i) for i in range(3)]
    carried = Carried(pieces, scratch, keep, narrow)
    load = pltpu.make_async_copy(early_any.at[:, pl.ds(0, 3 * d)], weight, weight_sem)

    @pl.when(step == 0)
    def _():
        carried.open()
        load.start()
        expand_ref[:, : CROSS_WIDE * d] = expand_low_ref[...]

    @pl.when(step < PAIRS)
    def _():
        base = step * 384

        def keep_dq(rows, value):
            dqkv[rows, pl.ds(pl.multiple_of(base, 128), 128)] = value

        attend_back(
            lambda rows: qkv_ref[rows, 0:128],
            qkv_ref[:, 128:256],
            qkv_ref[:, 256:384],
            grad_ref,
            mixed_ref,
            log_ref,
            functools.partial(self_visible, first_ref),
            self_extent,
            keep_dq,
            dk_ref,
            dv_ref,
        )
        dqkv[:, pl.ds(pl.multiple_of(base + 128, 128), 128)] = (dk_ref[...] * HEAD_DIM**-0.5).astype(BF16)
        dqkv[:, pl.ds(pl.multiple_of(base + 256, 128), 128)] = dv_ref[...].astype(BF16)

    rows = stage.shape[5]
    group = 2 * narrow * rows

    def multiply(m):
        for a in range(2):
            for b in range(2):
                at = (2 * a + b) * group
                product = tn(normed_ref[:, at : at + group], dqkv[:, m * d : (m + 1) * d])
                stage[m, a, b] = product.astype(BF16).reshape(2, narrow, rows, d)

    for m in range(3):
        pl.when(step == PAIRS + m)(functools.partial(multiply, m))

    @pl.when(step == PAIRS + 3)
    def _():
        load.wait()
        nval[0] = jnp.zeros_like(nval[0])
        nval[0, 2:4, :] = norm_two_ref[0:2, :]
        nval[0, 4:6, :] = norm_three_ref[0:2, :]

    @pl.when(step >= PAIRS + 3)
    def _():
        at = pl.ds(pl.multiple_of((step - PAIRS - 3) * TB, TB), TB)
        gradient = mm_t(dqkv[at, :], weight[...])
        unit, inverse = norm_parts(tokens_ref[...].astype(F32))
        total = total_ref[...] + norm_back(unit, inverse, norms_ref[0:1, :], gradient)
        out_ref[...] = total.astype(BF16)
        nval[0, 0:1, :] += jnp.sum(gradient * unit, axis=0, keepdims=True)
        nval[0, 1:2, :] += jnp.sum(gradient, axis=0, keepdims=True)

    w, z = carried.scatter.w, carried.scatter.z

    def norm_copy(stage_number, number, target):
        return pltpu.make_async_remote_copy(
            src_ref=nval.at[stage_number],
            dst_ref=nin.at[number],
            send_sem=norm_send_sems.at[number],
            recv_sem=norm_recv_sems.at[number],
            device_id=target,
            device_id_type=pl.DeviceIdType.MESH,
        )

    norm_copies = [[norm_copy(0, 0, (w ^ 1, z))], [norm_copy(1, 1, (w ^ 2, z))], [norm_copy(2, 2, (w ^ 4, z))]]
    norm_copies.append([norm_copy(3, 2 + mask, (w, z ^ mask)) for mask in range(1, narrow)])

    def norm_step(number):
        if number > 0:
            for copy in norm_copies[number - 1]:
                copy.wait_recv()
            value = nval[number - 1]
            if number < 4:
                nval[number] = value + nin[number - 1]
            else:
                for mask in range(1, narrow):
                    value = value + nin[2 + mask]
                norm_out_ref[...] = value
        if number < 4:
            for copy in norm_copies[number]:
                copy.start()

    last = len(SELF_PLAN) - 1
    for number, plan in enumerate(SELF_PLAN[:last]):
        pl.when(step == number)(functools.partial(carried.steps, plan))
        if number in SELF_REUSE:
            pl.when(step == number)(functools.partial(carried.reuse, SELF_REUSE[number]))

    @pl.when(step == last)
    def _():
        for number in range(5):
            norm_step(number)
            if number < len(SELF_PLAN[last]):
                carried.steps(SELF_PLAN[last][number : number + 1])
        carried.close()
        for copies in norm_copies:
            for copy in copies:
                copy.wait_send()


def self_back(first, logs, qkv, mixed, grad, normed, tokens, total, norms, norm_two, norm_three, expand_low, early, wide_share, shares, narrow):
    rows, d = mixed.shape
    shard_rows = d // (8 * narrow)

    def pair(s):
        return jnp.minimum(s, PAIRS - 1)

    def token(s):
        return jnp.maximum(s - PAIRS - 3, 0)

    anywhere = pl.BlockSpec(memory_space=pl.ANY)
    by_pair = pl.BlockSpec((SEQ, 128), lambda s: (0, pair(s)))
    by_token = pl.BlockSpec((TB, d), lambda s: (token(s), 0))
    return pl.pallas_call(
        functools.partial(self_back_kernel, narrow),
        grid=(PAIRS + 3 + rows // TB,),
        in_specs=[
            pl.BlockSpec((1, 1, SEQ), lambda s: (0, 0, 0)),
            pl.BlockSpec((1, 1, 8, SEQ), lambda s: (0, pair(s), 0, 0)),
            pl.BlockSpec((SEQ, 384), lambda s: (0, pair(s))),
            by_pair,
            by_pair,
            whole(rows, d),
            by_token,
            by_token,
            whole(8, d),
            whole(8, d),
            whole(8, d),
            whole(shard_rows, CROSS_WIDE * d),
            anywhere,
            anywhere,
            anywhere,
        ],
        out_specs=[
            by_token,
            whole(8, d),
            whole(shard_rows, 4 * d),
            *[whole(shard_rows, d)] * 8,
        ],
        out_shape=[
            shape(rows, d, BF16),
            shape(8, d, F32),
            shape(shard_rows, 4 * d, F32),
            *[shape(shard_rows, d, F32)] * 8,
        ],
        scratch_shapes=[
            pltpu.VMEM((SEQ, 128), F32),
            pltpu.VMEM((SEQ, 128), F32),
            pltpu.VMEM((rows, 3 * d), BF16),
            pltpu.VMEM((d, 3 * d), BF16),
            pltpu.SemaphoreType.DMA,
            pltpu.VMEM((3, 2, 2, 2, narrow, shard_rows, d), BF16),
            pltpu.VMEM((4, 8, d), F32),
            pltpu.VMEM((2 + narrow, 8, d), F32),
            pltpu.SemaphoreType.DMA((2 + narrow,)),
            pltpu.SemaphoreType.DMA((2 + narrow,)),
            *scatter_scratch(SELF_CHUNKS, narrow, shard_rows, d, 3),
        ],
        name="self_back",
        compiler_params=pltpu.CompilerParams(collective_id=3, has_side_effects=True, vmem_limit_bytes=60 << 20),
        cost_estimate=cost(40 * rows * d * d, 100 << 20),
    )(
        first,
        logs,
        qkv,
        mixed,
        grad,
        normed,
        tokens,
        total,
        norms,
        norm_two,
        norm_three,
        expand_low,
        early,
        share_views(wide_share, narrow, shard_rows),
        shares.reshape(5, 2, 2, 2, narrow, shard_rows, d),
    )


def on_device(
    mesh_axes,
    tokens,
    memory,
    cotangent,
    live_length,
    pair_starts,
    source_starts,
    group_bounds,
    group_counts,
    self_query,
    self_key,
    self_value,
    self_output,
    cross_query,
    cross_key,
    cross_value,
    cross_output,
    hidden_in,
    hidden_out,
    first_gain,
    first_shift,
    second_gain,
    second_shift,
    third_gain,
    third_shift,
):
    names = tuple(axis for axis, _ in mesh_axes)
    row_count = live_length.shape[0]
    shard_rows = self_query.shape[0]
    device_count = 1
    for _, size in mesh_axes:
        device_count *= size

    def staged(*partial):
        return StagedSum(partial, mesh_axes)

    digits = jnp.stack([live_length // 256, live_length % 256], axis=1).astype(BF16)
    digits = jnp.pad(digits, ((0, shard_rows - row_count), (0, 0)))
    norms = jnp.stack([first_gain, first_shift, second_gain, second_shift, third_gain, third_shift], axis=1)
    extra = jnp.pad(jnp.concatenate([norms, digits], axis=1), ((0, 0), (0, 120)))
    weights = (self_query, self_key, self_value, self_output, cross_query, cross_key, cross_value, cross_output)
    fast = mesh_axes[0][1] == 8 and row_count == 1 and shard_rows % 32 == 0
    if fast:
        (
            early,
            later,
            late,
            normed_one,
            qkv,
            self_mixed,
            self_logs,
            norms,
            first,
            bounds,
            after_self,
            normed_two,
            cross_q,
            cross_kv,
            cross_mixed,
            cross_logs,
        ) = front(
            live_length,
            pair_starts,
            source_starts,
            weights,
            hidden_in,
            hidden_out,
            extra,
            tokens,
            memory,
            mesh_axes[1][1],
        )
        late = [late.reshape(device_count, -1, WIDTH)]
    else:
        shard = [by_pairs(self_query, self_key, self_value), extra, self_output, cross_query]
        shard += [by_pairs(cross_key, cross_value), cross_output]
        early = lax.all_gather(jnp.concatenate(shard, axis=1), names, axis=0, tiled=True)
        late = [lax.all_gather(part, names, axis=0, tiled=True) for part in (hidden_in, hidden_out)]
        early, later = early[:, : 3 * WIDTH + 128], early[:, 3 * WIDTH + 128 :]
        norms = early[:, 3 * WIDTH : 3 * WIDTH + 8].astype(F32).T
        first, bounds = row_bounds(pair_starts, source_starts, live_length)
        normed_one, qkv = project(tokens, norms, early)
        self_mixed, self_logs = self_forward(first, qkv, row_count)
        after_self, normed_two, cross_q, cross_kv = middle(self_mixed, tokens, memory, norms, later)
        cross_mixed, cross_logs = cross_forward(bounds, cross_q, cross_kv, row_count)

    device = lax.axis_index(names)
    layer_output, normed_three, activated, hidden_grad, branch_three, cross_total, branch_two, mixed_grad, norm_three = feed(
        live_length, group_bounds, group_counts, cross_mixed, after_self, cotangent, norms, later, late, mesh_axes
    )

    reduce_share, expand_share = outer_sum(activated, branch_three), outer_sum(normed_three, hidden_grad)
    if fast:
        narrow = mesh_axes[1][1]
        self_total, mixed_grad, memory_grad, norm_two, shares, reduce_shard, expand_low = cross_back(
            bounds,
            cross_logs,
            cross_q,
            cross_kv,
            cross_mixed,
            mixed_grad,
            after_self,
            cross_total,
            norms,
            branch_two,
            normed_two,
            memory,
            self_mixed,
            later,
            reduce_share,
            expand_share,
            narrow,
        )
        (
            tokens_grad,
            norm_grads,
            expand_shard,
            cross_output_shard,
            cross_query_shard,
            cross_key_shard,
            cross_value_shard,
            output_shard,
            query_shard,
            key_shard,
            value_shard,
        ) = self_back(
            first,
            self_logs,
            qkv,
            self_mixed,
            mixed_grad,
            normed_one,
            tokens,
            self_total,
            norms,
            norm_two,
            norm_three,
            expand_low,
            early,
            expand_share,
            shares,
            narrow,
        )
    else:
        reduce_sum, expand_sum = staged(reduce_share), staged(expand_share)
        cq_grad, ckv_grad = cross_backward(bounds, cross_logs, cross_q, cross_kv, cross_mixed, mixed_grad, row_count)
        cq_grad, ckv_grad = fence((cq_grad, ckv_grad), reduce_sum, expand_sum)
        cross_shares = [outer_sum(cross_mixed, branch_two), outer_sum(normed_two, cq_grad)]
        cross_shares += [outer_sum(memory, part) for part in (ckv_grad[:, :WIDTH], ckv_grad[:, WIDTH:])]
        cross_sum = staged(*cross_shares)
        self_total, branch_one, mixed_grad, memory_grad, norm_two = cross_close(
            cq_grad, ckv_grad, after_self, cross_total, norms, later
        )
        mixed_grad = fence(mixed_grad, reduce_sum, expand_sum, cross_sum)
        qkv_grad = self_backward(first, self_logs, qkv, self_mixed, mixed_grad, row_count)
        qkv_grad = fence(qkv_grad, reduce_sum, expand_sum, cross_sum)
        last_sum = staged(
            outer_sum(self_mixed, branch_one),
            *[outer_sum(normed_one, qkv_grad[:, n * WIDTH : (n + 1) * WIDTH]) for n in range(3)],
        )
        tokens_grad, norm_one = self_close(qkv_grad, tokens, self_total, norms, early)
        norm_grads = sum_everywhere(jnp.concatenate([norm_one[:2], norm_two[:2], norm_three[:2]]), mesh_axes)
        output_shard, *qkv_shards = last_sum.result().reshape(4, shard_rows, WIDTH)
        query_shard, key_shard, value_shard = from_pairs(jnp.concatenate(qkv_shards, axis=1), 3)
        reduce_shard = reduce_sum.result()
        expand_shard = expand_sum.result()
        cross_output_shard, cross_query_shard, *cross_shards = cross_sum.result().reshape(4, shard_rows, WIDTH)
        cross_key_shard, cross_value_shard = from_pairs(jnp.concatenate(cross_shards, axis=1), 2)

    live = (jnp.arange(SEQ, dtype=jnp.int32)[None, :] < live_length[:, None]).reshape(-1, 1)
    tokens_grad = jnp.where(live, tokens_grad, jnp.zeros_like(tokens_grad))
    norm_shards = lax.dynamic_slice_in_dim(norm_grads, device * shard_rows, shard_rows, axis=1)
    return (
        layer_output,
        tokens_grad,
        memory_grad,
        query_shard,
        key_shard,
        value_shard,
        output_shard,
        cross_query_shard,
        cross_key_shard,
        cross_value_shard,
        cross_output_shard,
        expand_shard,
        reduce_shard,
        *[norm_shards[n] for n in range(6)],
    )


def solution(mesh):
    names = ("wide", "narrow")
    mesh_axes = tuple((axis, mesh.shape[axis]) for axis in names)
    split, vector = P(names, None), P(names)
    return jax.shard_map(
        functools.partial(on_device, mesh_axes),
        mesh=mesh,
        in_specs=(split,) * 3 + (vector,) + (split,) * 2 + (P(), P()) + (split,) * 10 + (vector,) * 6,
        out_specs=(split,) * 13 + (vector,) * 6,
        check_vma=False,
    )
```
